32 devices in a mesh: dp: 16 (over z, y, x), rows: 2 (over core).
Axes of the slice: x: 2, y: 2, z: 4, core: 2. Of those that a mesh axis runs over, the one named last changes fastest.
Arguments:
- images: bfloat16 [512, 8, 7, 2048], P('dp', 'rows'), may hold values from -6 to 6
- row_split: int32 [512], P('dp'), may hold values from 3 to 4
- labels: int32 [512], P('dp'), may hold values from 0 to 999
- partners: int32 [512], replicated, may hold values from 0 to 511
- image_weight: int32 [512], replicated, may hold values from 1 to 7
- owner_slot: int32 [2176], replicated, may hold values from 0 to 2175, each once
- conv_master: float32 [2176, 4096], P('dp'), may hold values from -0.125 to 0.125
- conv_stats: float32 [2176, 64, 128], P('dp')
- conv_roots: float32 [2176, 64, 128], P('dp')
- head_master: float32 [2048, 1000], P('dp'), may hold values from -0.25 to 0.25
- head_moment_one: float32 [2048, 1000], P('dp'), may hold values from -0.0008544922 to 0.0008544922
- head_moment_two: float32 [2048, 1000], P('dp'), may hold values from 1.315e-08 to 5.26e-08
- small_params: float32 [13288], replicated
- small_moment_one: float32 [13288], replicated, may hold values from -0.0034179688 to 0.0034179688
- small_moment_two: float32 [13288], replicated, may hold values from 2.104e-07 to 8.416e-07
Outputs:
- loss_sum: float32 [], replicated
- weight_total: float32 [], replicated
- conv_grad: float32 [2176, 4096], P('dp')
- conv_stats_new: float32 [2176, 64, 128], P('dp')
- conv_master_new: float32 [2176, 4096], P('dp')
- conv_copy: bfloat16 [2176, 4096], P('dp')
- head_moment_one_new: float32 [2048, 1000], P('dp')
- head_moment_two_new: float32 [2048, 1000], P('dp')
- head_master_new: float32 [2048, 1000], P('dp')
- head_copy: bfloat16 [2048, 1000], P('dp')
- small_moment_one_new: float32 [13288], replicated
- small_moment_two_new: float32 [13288], replicated
- small_params_new: float32 [13288], replicated
The draws below stay inside these ranges and needn't reach their ends.
Inputs may be any that keep to these rules, and one draw needn't show every extreme that they name: Image i's first row_split[i] rows lie on the first index of rows, right-aligned in its slots, the others on the second, left-aligned. `owner_slot`: a permutation of the 2176 blocks.
All inputs are finite; a program needn't handle non-finite values.
Results may differ from the reference program's by a relative error of at most 0.02.
Values may be sent and summed in bfloat16 or wider, within the bound.
A program may use at most 320 MiB of HBM per device.

```python
import jax
import jax.numpy as jnp
from jax import lax

C = 2048
M = 512
CLASSES = 1000
HEIGHT = 7
WIDTH = 7
ROW_SLOTS = 4
LAYERS = 2
BLOCK = 64
STEP = 5
B_DEV = 32
IMAGES = 512
NBLK = 2176
SMALL = 13288


def draw_image_weight(key, part):
    key = jax.random.fold_in(key, 5)
    image_ids = jnp.arange(IMAGES, dtype=jnp.int32)
    group_at = image_ids // B_DEV
    group_count = IMAGES // B_DEV
    upper_half = (image_ids % B_DEV >= B_DEV // 2).astype(jnp.int32)
    ceiling = 2 + 4 * group_at // max(group_count - 1, 1) + 2 * upper_half
    return jax.random.randint(key, (IMAGES,), 1, ceiling).astype(jnp.int32)


def square_side(key_diag, key_noise, lower, upper, mixing, scale_of):
    identity = jnp.eye(BLOCK, dtype=jnp.float32)
    diagonal = jax.random.uniform(key_diag, (NBLK, BLOCK), jnp.float32, lower, upper)
    noise = jax.random.normal(key_noise, (NBLK, BLOCK, BLOCK), jnp.float32)
    offdiag = mixing * (noise + jnp.swapaxes(noise, 1, 2)) * (1.0 - identity)
    return scale_of * (diagonal[:, :, None] * identity + offdiag)


def draw_conv_stats(key, part):
    key = jax.random.fold_in(key, 11)
    keys = jax.random.split(key, 4)
    scale_of = BLOCK * 0.0001 / IMAGES
    left_side = square_side(keys[0], keys[1], 1.0, 4.0, 0.05, scale_of)
    right_side = square_side(keys[2], keys[3], 1.0, 4.0, 0.05, scale_of)
    return jnp.concatenate([left_side, right_side], axis=2)


def draw_conv_roots(key, part):
    key = jax.random.fold_in(key, 17)
    keys = jax.random.split(key, 4)
    scale_of = (BLOCK * 0.0001 / IMAGES) ** (-0.25)
    mixing = 0.18 / BLOCK ** 0.5
    left_side = square_side(keys[0], keys[1], 0.7, 1.4, mixing, scale_of)
    right_side = square_side(keys[2], keys[3], 0.7, 1.4, mixing, scale_of)
    return jnp.concatenate([left_side, right_side], axis=2)


def draw_small_params(key, part):
    key = jax.random.fold_in(key, 21)
    key_gain, key_shift = jax.random.split(key)
    entry_ids = jnp.arange(SMALL, dtype=jnp.int32)
    stride = 4 * M + 2 * C
    inner = entry_ids % stride
    is_gain = ((inner < M) | (inner >= 2 * M) & (inner < 3 * M) | (inner >= 4 * M) & (inner < 4 * M + C)) & (entry_ids < LAYERS * stride)
    gains = jax.random.uniform(key_gain, (SMALL,), jnp.float32, 0.6, 1.4)
    shifts = 0.3 * jnp.clip(jax.random.normal(key_shift, (SMALL,), jnp.float32), -4.0, 4.0)
    return jnp.where(is_gain, gains, shifts)


def touch_ends(drawn, rng, least, largest):
    place = [jax.random.randint(jax.random.fold_in(rng, axis), (), 0, length) for axis, length in enumerate(drawn.shape)]
    widest = drawn.shape.index(max(drawn.shape))
    next_to = place[:widest] + [(place[widest] + 1) % drawn.shape[widest]] + place[widest + 1:]
    return drawn.at[tuple(place)].set(least).at[tuple(next_to)].set(largest)


def steps_of(stream_key, extent, cuts, smallest, largest):
    factor_of = 1.0
    for position, parts in cuts:
        draws = jax.random.uniform(jax.random.fold_in(jax.random.fold_in(stream_key, 6), position), (parts,), jnp.float32, smallest / len(cuts), largest / len(cuts))
        factor_of = factor_of * jnp.repeat(jnp.exp(draws), extent[position] // parts).reshape((-1,) + (1,) * (len(extent) - 1 - position))
    return factor_of


def scatter_about(key, extent, width, bound, cuts=(), kind=jnp.bfloat16):
    entries = width * jax.random.normal(key, extent, jnp.float32)
    if cuts:
        entries = entries * steps_of(key, extent, cuts, -0.22, 0.18)
    return jnp.clip(entries, -bound, bound).astype(kind)


def setup_inputs(seed: int = 0) -> dict:
    streams_of = jax.random.split(jax.random.key(seed), 16)
    return {
        "images": scatter_about(streams_of[0], (IMAGES, 2 * ROW_SLOTS, WIDTH, C), 1.0, 6.0, ((0, 16), (1, 2))),
        "row_split": touch_ends(jax.random.randint(streams_of[1], (IMAGES,), 3, 5), jax.random.fold_in(streams_of[1], 1), 3, 4).astype(jnp.int32),
        "labels": touch_ends(jax.random.randint(streams_of[2], (IMAGES,), 0, CLASSES), jax.random.fold_in(streams_of[2], 1), 0, CLASSES - 1).astype(jnp.int32),
        "partners": touch_ends(jax.random.randint(streams_of[3], (IMAGES,), 0, IMAGES), jax.random.fold_in(streams_of[3], 1), 0, IMAGES - 1).astype(jnp.int32),
        "image_weight": draw_image_weight(jax.random.fold_in(streams_of[15], 71), 0),
        "owner_slot": jax.random.permutation(streams_of[5], NBLK).astype(jnp.int32),
        "conv_master": scatter_about(streams_of[6], (NBLK, BLOCK * BLOCK), C ** -0.5, 0.125, ((0, 16),), jnp.float32),
        "conv_stats": draw_conv_stats(jax.random.fold_in(streams_of[15], 71), 0),
        "conv_roots": draw_conv_roots(jax.random.fold_in(streams_of[15], 71), 0),
        "head_master": scatter_about(streams_of[9], (C, CLASSES), M ** -0.5, 0.25, ((0, 16),), jnp.float32),
        "head_moment_one": scatter_about(streams_of[10], (C, CLASSES), (0.11 * 0.0005), 0.0008544922, ((0, 16),), jnp.float32),
        "head_moment_two": jnp.clip(1.3150000199857459e-08 + 3.945000059957238e-08 * jax.random.uniform(streams_of[11], (C, CLASSES), jnp.float32) ** steps_of(streams_of[11], (C, CLASSES), ((0, 16),), -0.2, 0.2), 1.3150000199857459e-08, 5.2600000799429836e-08),
        "small_params": draw_small_params(jax.random.fold_in(streams_of[15], 71), 0),
        "small_moment_one": scatter_about(streams_of[13], (SMALL,), (0.11 * 0.002), 0.0034179688, (), jnp.float32),
        "small_moment_two": jnp.clip(jax.random.uniform(streams_of[14], (SMALL,), jnp.float32, 2.1040000319771934e-07, 8.416000127908774e-07), 2.1040000319771934e-07, 8.416000127908774e-07),
    }


EPS_NORM = 1e-05
MATCH_WEIGHT = 4.0
DECAY_STATS = 0.5
RATE_SHAMPOO = 0.15
RATE_HEAD = 0.03
RATE_SMALL = 0.2
BETA_FIRST = 0.9
BETA_SECOND = 0.95
EPS_ADAM = 1e-08
DECAY_WEIGHT = 0.01
HIGHEST = lax.Precision.HIGHEST

@jax.custom_vjp
def low(v):
    return lax.optimization_barrier(v.astype(jnp.bfloat16)).astype(jnp.float32)

@jax.custom_vjp
def low_back(v):
    return v

def low_keep(v):
    return (low(v), None)

def low_pass(kept, grad):
    return (grad,)

def back_keep(v):
    return (v, None)

def back_low(kept, grad):
    return (low(grad),)
low.defvjp(low_keep, low_pass)
low_back.defvjp(back_keep, back_low)

def from_blocks(pieces, height_rows, width_cols):
    return pieces.reshape(height_rows // BLOCK, width_cols // BLOCK, BLOCK, BLOCK).transpose(0, 2, 1, 3).reshape(height_rows, width_cols)

def layer_matrices(pieces):
    first_count = C // BLOCK * (M // BLOCK)
    middle_count = 9 * (M // BLOCK) * (M // BLOCK)
    w_in = from_blocks(pieces[:first_count], C, M)
    w_mid = from_blocks(pieces[first_count:first_count + middle_count], 9 * M, M)
    w_out = from_blocks(pieces[first_count + middle_count:], M, C)
    return (w_in, w_mid, w_out)

def layer_params(small, layer_at):
    stride = 4 * M + 2 * C
    span_of = small[layer_at * stride:(layer_at + 1) * stride]
    return (span_of[:M], span_of[M:2 * M], span_of[2 * M:3 * M], span_of[3 * M:4 * M], span_of[4 * M:4 * M + C], span_of[4 * M + C:])

def batch_norm(values, gain_of, offset, live_mask):
    live_count = IMAGES * HEIGHT * WIDTH
    mean_of = lax.optimization_barrier(jnp.sum(values, axis=(0, 1, 2))) / live_count
    centered = (values - mean_of) * live_mask
    spread = lax.optimization_barrier(jnp.sum(centered * centered, axis=(0, 1, 2))) / live_count
    return (values - mean_of) * lax.rsqrt(spread + EPS_NORM) * gain_of + offset

def conv_mid(values, w_mid):
    slot_count = values.shape[1]
    padded = jnp.pad(values, ((0, 0), (1, 1), (1, 1), (0, 0)))
    result = jnp.zeros(values.shape[:3] + (w_mid.shape[1],), jnp.float32)
    for tap_row in range(3):
        for tap_col in range(3):
            tap_at = 3 * tap_row + tap_col
            window = padded[:, tap_row:tap_row + slot_count, tap_col:tap_col + WIDTH, :]
            result = result + jnp.einsum('nrcm,mk->nrck', window, w_mid[tap_at * M:(tap_at + 1) * M], precision=HIGHEST)
    return result

def residual_block(inputs, matrices, params, live_mask):
    w_in, w_mid, w_out = matrices
    gain_a, shift_a, gain_b, shift_b, gain_c, shift_c = params
    conv_a = low_back(jnp.einsum('nrcd,dm->nrcm', low(inputs), w_in, precision=HIGHEST))
    hidden_a = low(live_mask * jax.nn.silu(batch_norm(conv_a, gain_a, shift_a, live_mask)))
    conv_b = low_back(live_mask * conv_mid(hidden_a, w_mid))
    hidden_b = low(live_mask * jax.nn.silu(batch_norm(conv_b, gain_b, shift_b, live_mask)))
    conv_c = low_back(jnp.einsum('nrcm,md->nrcd', hidden_b, w_out, precision=HIGHEST))
    return live_mask * jax.nn.silu(batch_norm(conv_c, gain_c, shift_c, live_mask) + inputs)

def shampoo(master, gradient, statistics, root_pairs):
    block_side = statistics.shape[1]
    tile_grads = gradient.reshape(-1, block_side, block_side)
    left_new = DECAY_STATS * statistics[:, :, :block_side] + (1.0 - DECAY_STATS) * jnp.einsum('sij,skj->sik', tile_grads, tile_grads, precision=HIGHEST)
    right_new = DECAY_STATS * statistics[:, :, block_side:] + (1.0 - DECAY_STATS) * jnp.einsum('sji,sjk->sik', tile_grads, tile_grads, precision=HIGHEST)
    turned = jnp.einsum('sij,sjk->sik', root_pairs[:, :, :block_side], tile_grads, precision=HIGHEST)
    turned = jnp.einsum('sij,sjk->sik', turned, root_pairs[:, :, block_side:], precision=HIGHEST)
    return (jnp.concatenate([left_new, right_new], axis=2), master - RATE_SHAMPOO * turned.reshape(master.shape))

def adamw(values_old, gradient, moment_one, moment_two, step_rate):
    one_new = BETA_FIRST * moment_one + (1.0 - BETA_FIRST) * gradient
    two_new = BETA_SECOND * moment_two + (1.0 - BETA_SECOND) * gradient * gradient
    fixed_one = 1.0 - BETA_FIRST ** STEP
    fixed_two = 1.0 - BETA_SECOND ** STEP
    update = one_new / fixed_one / (jnp.sqrt(two_new / fixed_two) + EPS_ADAM)
    return (one_new, two_new, values_old - step_rate * (update + DECAY_WEIGHT * values_old))

def reference(images, row_split, labels, partners, image_weight, owner_slot, conv_master, conv_stats, conv_roots, head_master, head_moment_one, head_moment_two, small_params, small_moment_one, small_moment_two):
    slot_ids = jnp.arange(2 * ROW_SLOTS, dtype=jnp.int32)[None, :]
    first_live = (ROW_SLOTS - row_split)[:, None]
    live_mask = ((slot_ids >= first_live) & (slot_ids < first_live + HEIGHT)).astype(jnp.float32)[:, :, None, None]
    inputs = images.astype(jnp.float32) * live_mask
    weight_f = image_weight.astype(jnp.float32)
    weight_total = jnp.sum(weight_f)
    conv_blocks = jnp.take(conv_master.astype(jnp.bfloat16).astype(jnp.float32), owner_slot, axis=0)
    head_w = head_master.astype(jnp.bfloat16).astype(jnp.float32)
    per_layer = conv_blocks.shape[0] // LAYERS
    class_hot = (labels[:, None] == jnp.arange(CLASSES, dtype=jnp.int32)[None, :]).astype(jnp.float32)

    def loss_fn(blocks_in, head_in, small_in):
        state = inputs
        for layer_at in range(LAYERS):
            matrices = layer_matrices(blocks_in[layer_at * per_layer:(layer_at + 1) * per_layer])
            state = residual_block(state, matrices, layer_params(small_in, layer_at), live_mask)
        pooled = lax.optimization_barrier(jnp.sum(state, axis=(1, 2))) / (HEIGHT * WIDTH)
        head_bias = small_in[LAYERS * (4 * M + 2 * C):]
        logits = low_back(jnp.dot(low(pooled), head_in, precision=HIGHEST) + head_bias)
        log_total = jax.nn.logsumexp(logits, axis=1)
        picked = lax.optimization_barrier(jnp.sum(logits * class_hot, axis=1))
        partner_logits = jnp.take(logits, partners, axis=0)
        matched = lax.optimization_barrier(jnp.mean((logits - partner_logits) ** 2, axis=1))
        summed = jnp.sum(weight_f * (log_total - picked + MATCH_WEIGHT * matched))
        return (summed / weight_total, summed)
    loss_value, back_fn, loss_sum = jax.vjp(loss_fn, conv_blocks, head_w, small_params, has_aux=True)
    grad_blocks, grad_head, grad_small = back_fn(jnp.ones_like(loss_value))
    conv_grad = jnp.zeros_like(grad_blocks).at[owner_slot].set(grad_blocks)
    stats_new, master_new = shampoo(conv_master, conv_grad, conv_stats, conv_roots)
    head_one, head_two, head_new = adamw(head_master, grad_head, head_moment_one, head_moment_two, RATE_HEAD)
    small_one, small_two, small_new = adamw(small_params, grad_small, small_moment_one, small_moment_two, RATE_SMALL)
    return (loss_sum, weight_total, conv_grad, stats_new, master_new, master_new.astype(jnp.bfloat16), head_one, head_two, head_new, head_new.astype(jnp.bfloat16), small_one, small_two, small_new)
```

```python
import functools

import jax
import jax.numpy as jnp
from jax import lax
from jax.experimental import pallas as pl
from jax.experimental.pallas import tpu as pltpu
from jax.sharding import PartitionSpec as P

C = 2048
M = 512
CLASSES = 1000
HEIGHT = 7
WIDTH = 7
ROW_SLOTS = 4
LAYERS = 2
BLOCK = 64
STEP = 5


EPS_NORM = 1e-05
MATCH_WEIGHT = 4.0
DECAY_STATS = 0.5
RATE_SHAMPOO = 0.15
RATE_HEAD = 0.03
RATE_SMALL = 0.2
BETA_FIRST = 0.9
BETA_SECOND = 0.95
EPS_ADAM = 1e-08
DECAY_WEIGHT = 0.01
HIGHEST = lax.Precision.HIGHEST


C = 2048
M = 512
CLASSES = 1000
HEIGHT = 7
WIDTH = 7
ROW_SLOTS = 4
LAYERS = 2
BLOCK = 64
STEP = 5


EPS_NORM = 1e-05
MATCH_WEIGHT = 4.0
DECAY_STATS = 0.5
RATE_SHAMPOO = 0.15
RATE_HEAD = 0.03
RATE_SMALL = 0.2
BETA_FIRST = 0.9
BETA_SECOND = 0.95
EPS_ADAM = 1e-08
DECAY_WEIGHT = 0.01
HIGHEST = lax.Precision.HIGHEST


MESH_IDS = pl.DeviceIdType.MESH
HALF = 16
LANES = 128


def bit_split(devices):
    bits = devices.bit_length() - 1
    first = bits // 3
    second = (bits - first) // 2
    return first, second, bits - first - second


def greet(peers):
    barrier = pltpu.get_barrier_semaphore()
    for peer in peers:
        pl.semaphore_signal(barrier, inc=1, device_id=peer, device_id_type=MESH_IDS)
    pl.semaphore_wait(barrier, len(peers))


def axis_masks(devices, core):
    first, second, third = bit_split(devices)
    low = [m for m in range(1, 1 << first)]
    high = [m << first for m in range(1, 1 << second)]
    if first == second:
        one = [jnp.where(core == 0, h, l) for h, l in zip(high, low)]
        two = [jnp.where(core == 0, l, h) for h, l in zip(high, low)]
    else:
        one, two = low, high
    far = [m << (first + second) for m in range(1, 1 << third)]
    return [0] + one, [0] + two, [0] + far


def chunks_of(count):
    for parts in (8, 4, 2):
        if count % parts == 0:
            return parts
    return 1


def gather_kernel(devices, parts, x_ref, o_ref, local_sem, send_sem, recv_sem):
    me = lax.axis_index("dp")
    core = lax.axis_index("rows")
    per = x_ref.shape[1] // parts
    mid, last, far = axis_masks(devices, core)
    partner = (me, 1 - core)
    greet(
        [(me ^ m, core) for m in far[1:]]
        + [(me ^ m, core) for m in mid[1:]]
        + [(me ^ m, core) for m in last[1:]]
        + [partner]
    )
    sent = []

    def piece(owner, half, part):
        return o_ref.at[owner, half, pl.ds(part * per, per)]

    def send(src_ref, owner, part, device):
        copy = pltpu.make_async_remote_copy(
            src_ref=src_ref,
            dst_ref=piece(owner, core, part),
            send_sem=send_sem.at[len(sent)],
            recv_sem=recv_sem.at[owner, core, part],
            device_id=device,
            device_id_type=MESH_IDS,
        )
        copy.start()
        sent.append(copy)

    def arrived(owner, half, part):
        ref = piece(owner, half, part)
        pltpu.make_async_copy(ref, ref, recv_sem.at[owner, half, part]).wait()

    def onward(owner, part, masks):
        arrived(owner, core, part)
        for m in masks:
            send(piece(owner, core, part), owner, part, (me ^ m, core))
        send(piece(owner, core, part), owner, part, partner)

    early = parts - parts // 4
    own_copy = pltpu.make_async_copy(x_ref, o_ref.at[me], local_sem)
    own_copy.start()
    for part in range(parts):
        order = far[1:] + last[1:] + mid[1:] if part < early else mid[1:] + far[1:] + last[1:]
        for m in order:
            send(x_ref.at[core, pl.ds(part * per, per)], me, part, (me ^ m, core))
    for tick in range(parts + 2):
        part = tick
        if part < parts:
            if part < early:
                for z in far[1:]:
                    onward(me ^ z, part, last[1:] + mid[1:])
            else:
                for m in mid[1:]:
                    onward(me ^ m, part, far[1:] + last[1:])
        part = tick - 1
        if 0 <= part < parts:
            if part < early:
                for m in mid[1:]:
                    for z in far:
                        onward(me ^ m ^ z, part, last[1:])
            else:
                for z in far[1:]:
                    onward(me ^ z, part, last[1:])
                for z in far[1:]:
                    for m in mid[1:]:
                        onward(me ^ z ^ m, part, last[1:])
        part = tick - 2
        if 0 <= part < parts:
            for q in last[1:]:
                for z in far:
                    for m in mid:
                        onward(me ^ q ^ z ^ m, part, [])
    for step in range(1, devices):
        for part in range(parts):
            arrived(me ^ step, 1 - core, part)
    own_copy.wait()
    for copy in sent:
        copy.wait_send()


def gather_blocks(own, devices):
    count = own.shape[1]
    parts = chunks_of(count)
    return pl.pallas_call(
        functools.partial(gather_kernel, devices, parts),
        out_shape=jax.ShapeDtypeStruct((devices,) + own.shape, own.dtype),
        in_specs=[pl.BlockSpec(memory_space=pl.ANY)],
        out_specs=pl.BlockSpec(memory_space=pl.ANY),
        scratch_shapes=[
            pltpu.SemaphoreType.DMA(()),
            pltpu.SemaphoreType.DMA((3 * devices * parts,)),
            pltpu.SemaphoreType.DMA((devices, 2, parts)),
        ],
        compiler_params=pltpu.CompilerParams(
            collective_id=1, has_side_effects=True, vmem_limit_bytes=56 * 2**20
        ),
    )(own)


def slab_shape(shape):
    return (shape[1] // LANES, shape[0], LANES)


def matrix_list():
    shapes = []
    for _ in range(LAYERS):
        shapes += [(C, M), (9 * M, M), (M, C)]
    return shapes


def assemble_kernel(count, idx_ref, g_hbm, *refs):
    shapes = matrix_list()
    n = len(shapes)
    outs, bufs, (g_ref, in_sem, out_sem) = refs[:n], refs[n : 2 * n], refs[2 * n :]
    load = pltpu.make_async_copy(g_hbm, g_ref, in_sem)
    load.start()
    load.wait()
    base = 0
    copies = []
    for at, (rows, cols) in enumerate(shapes):
        pairs = cols // LANES
        buf = bufs[at]

        def strip(r, carry, base=base, pairs=pairs, buf=buf):
            for m in range(pairs):
                even = idx_ref[base + r * (2 * pairs) + 2 * m]
                odd = idx_ref[base + r * (2 * pairs) + 2 * m + 1]
                for h in range(2):
                    e = g_ref[even + h * count]
                    o = g_ref[odd + h * count]
                    buf[m, pl.ds(r * BLOCK + h * HALF, HALF)] = jnp.concatenate(
                        [e[:, :BLOCK], o[:, :BLOCK]], axis=1
                    )
                    buf[m, pl.ds(r * BLOCK + 2 * HALF + h * HALF, HALF)] = jnp.concatenate(
                        [e[:, BLOCK:], o[:, BLOCK:]], axis=1
                    )
            return carry

        lax.fori_loop(0, rows // BLOCK, strip, 0)
        copy = pltpu.make_async_copy(buf, outs[at], out_sem.at[at])
        copy.start()
        copies.append(copy)
        base += (rows // BLOCK) * (cols // BLOCK)
    for copy in copies:
        copy.wait()


def assemble(gathered, index):
    devices, _, count = gathered.shape[:3]
    flat = gathered.reshape(devices * 2 * count, HALF, LANES)
    shapes = matrix_list()
    return pl.pallas_call(
        functools.partial(assemble_kernel, count),
        out_shape=[jax.ShapeDtypeStruct(slab_shape(s), jnp.bfloat16) for s in shapes],
        in_specs=[
            pl.BlockSpec(memory_space=pltpu.SMEM),
            pl.BlockSpec(memory_space=pl.ANY),
        ],
        out_specs=[pl.BlockSpec(memory_space=pl.ANY)] * len(shapes),
        scratch_shapes=[pltpu.VMEM(slab_shape(s), jnp.bfloat16) for s in shapes]
        + [
            pltpu.VMEM(flat.shape, jnp.bfloat16),
            pltpu.SemaphoreType.DMA(()),
            pltpu.SemaphoreType.DMA((len(shapes),)),
        ],
        compiler_params=pltpu.CompilerParams(vmem_limit_bytes=56 * 2**20),
    )(index, flat)


def slots_kernel(count, idx_ref, *refs):
    shapes = matrix_list()
    n = len(shapes)
    grads, o_hbm, bufs, (o_ref, in_sem, out_sem) = (
        refs[:n],
        refs[n],
        refs[n + 1 : 2 * n + 1],
        refs[2 * n + 1 :],
    )
    loads = []
    for at in range(n):
        load = pltpu.make_async_copy(grads[at], bufs[at], in_sem.at[at])
        load.start()
        loads.append(load)
    base = 0
    for at, (rows, cols) in enumerate(shapes):
        pairs = cols // LANES
        buf = bufs[at]
        loads[at].wait()

        def strip(r, carry, base=base, pairs=pairs, buf=buf):
            for m in range(pairs):
                even = idx_ref[base + r * (2 * pairs) + 2 * m]
                odd = idx_ref[base + r * (2 * pairs) + 2 * m + 1]
                for h in range(2):
                    top = buf[m, pl.ds(r * BLOCK + h * HALF, HALF)]
                    low = buf[m, pl.ds(r * BLOCK + 2 * HALF + h * HALF, HALF)]
                    o_ref[even + h * count] = jnp.concatenate(
                        [top[:, :BLOCK], low[:, :BLOCK]], axis=1
                    )
                    o_ref[odd + h * count] = jnp.concatenate(
                        [top[:, BLOCK:], low[:, BLOCK:]], axis=1
                    )
            return carry

        lax.fori_loop(0, rows // BLOCK, strip, 0)
        base += (rows // BLOCK) * (cols // BLOCK)
    store = pltpu.make_async_copy(o_ref, o_hbm, out_sem)
    store.start()
    store.wait()


def to_slots(grads, index, devices):
    shapes = matrix_list()
    total = index.shape[0]
    count = total // devices
    flat = (total * 2, HALF, LANES)
    out = pl.pallas_call(
        functools.partial(slots_kernel, count),
        out_shape=jax.ShapeDtypeStruct(flat, jnp.bfloat16),
        in_specs=[pl.BlockSpec(memory_space=pltpu.SMEM)]
        + [pl.BlockSpec(memory_space=pl.ANY)] * len(shapes),
        out_specs=pl.BlockSpec(memory_space=pl.ANY),
        scratch_shapes=[pltpu.VMEM(slab_shape(s), jnp.bfloat16) for s in shapes]
        + [
            pltpu.VMEM(flat, jnp.bfloat16),
            pltpu.SemaphoreType.DMA((len(shapes),)),
            pltpu.SemaphoreType.DMA(()),
        ],
        compiler_params=pltpu.CompilerParams(vmem_limit_bytes=56 * 2**20),
    )(index, *grads)
    return out.reshape(devices, 2, count, HALF, LANES)


def scatter_kernel(
    devices, parts, g_ref, o_ref, acc, other, land_last, land_mid, land_far, final,
    local_sem, pair_send, pair_recv, send_sem, last_recv, mid_recv, far_recv, end_send, end_recv, out_sem,
):
    me = lax.axis_index("dp")
    core = lax.axis_index("rows")
    count = g_ref.shape[2]
    per = count // parts
    mid, last, far = axis_masks(devices, core)
    partner = (me, 1 - core)
    greet(
        [(me ^ m, core) for m in far[1:]]
        + [(me ^ m, core) for m in mid[1:]]
        + [(me ^ m, core) for m in last[1:]]
        + [partner]
    )

    def span(part):
        return pl.ds(part * per, per)

    pair = []
    local = []
    for part in range(parts):
        copy = pltpu.make_async_remote_copy(
            src_ref=g_ref.at[:, 1 - core, span(part)],
            dst_ref=other.at[:, span(part)],
            send_sem=pair_send.at[part],
            recv_sem=pair_recv.at[part],
            device_id=partner,
            device_id_type=MESH_IDS,
        )
        copy.start()
        pair.append(copy)
        copy = pltpu.make_async_copy(
            g_ref.at[:, core, span(part)], acc.at[:, span(part)], local_sem.at[part]
        )
        copy.start()
        local.append(copy)

    sent = []

    def send(owner, part, land, sems, at, device):
        copy = pltpu.make_async_remote_copy(
            src_ref=acc.at[owner, span(part)],
            dst_ref=land.at[at, span(part)],
            send_sem=send_sem.at[len(sent)],
            recv_sem=sems.at[at, part],
            device_id=device,
            device_id_type=MESH_IDS,
        )
        copy.start()
        sent.append(copy)

    def arrived(land, sems, at, part):
        ref = land.at[at, span(part)]
        pltpu.make_async_copy(ref, ref, sems.at[at, part]).wait()

    def add(owners, lands, part):
        def step(i, carry):
            at = part * per + i
            for owner, (land, j) in zip(owners, lands):
                acc[owner, at] = (
                    acc[owner, at].astype(jnp.float32) + land[j, at].astype(jnp.float32)
                ).astype(jnp.bfloat16)
            return carry

        lax.fori_loop(0, per, step, 0)

    ends = []
    for tick in range(parts + 3):
        part = tick
        if part < parts:
            pair[part].wait_recv()
            local[part].wait()

            def step(i, carry, part=part):
                at = part * per + i
                acc[:, at] = (
                    acc[:, at].astype(jnp.float32) + other[:, at].astype(jnp.float32)
                ).astype(jnp.bfloat16)
                return carry

            lax.fori_loop(0, per, step, 0)
            at = 0
            for q in last[1:]:
                for m in mid[::-1]:
                    for z in far[::-1]:
                        send(me ^ q ^ m ^ z, part, land_last, last_recv, at, (me ^ q, core))
                        at += 1
        part = tick - 1
        if 0 <= part < parts:
            at = 0
            owners, lands = [], []
            per_q = len(mid) * len(far)
            for j in range(len(last) - 1):
                for i, (m, z) in enumerate([(m, z) for m in mid[::-1] for z in far[::-1]]):
                    arrived(land_last, last_recv, j * per_q + i, part)
                    owners.append(me ^ m ^ z)
                    lands.append((land_last, j * per_q + i))
            add(owners, lands, part)
            at = 0
            for m in mid[1:]:
                for z in far[::-1]:
                    send(me ^ m ^ z, part, land_mid, mid_recv, at, (me ^ m, core))
                    at += 1
        part = tick - 2
        if 0 <= part < parts:
            owners, lands = [], []
            for j in range(len(mid) - 1):
                for i, z in enumerate(far[::-1]):
                    at = j * len(far) + i
                    arrived(land_mid, mid_recv, at, part)
                    owners.append(me ^ z)
                    lands.append((land_mid, at))
            add(owners, lands, part)
            for at, z in enumerate(far[1:]):
                send(me ^ z, part, land_far, far_recv, at, (me ^ z, core))
        part = tick - 3
        if 0 <= part < parts:
            for at in range(len(far) - 1):
                arrived(land_far, far_recv, at, part)

            def finish(i, carry, part=part):
                at = part * per + i
                total = acc[me, at].astype(jnp.float32)
                for j in range(len(far) - 1):
                    total = total + land_far[j, at].astype(jnp.float32)
                final[core, at] = total.astype(jnp.bfloat16)
                return carry

            lax.fori_loop(0, per, finish, 0)
            copy = pltpu.make_async_remote_copy(
                src_ref=final.at[core, span(part)],
                dst_ref=final.at[core, span(part)],
                send_sem=end_send.at[part],
                recv_sem=end_recv.at[part],
                device_id=partner,
                device_id_type=MESH_IDS,
            )
            copy.start()
            ends.append(copy)
    for part in range(parts):
        ref = final.at[1 - core, span(part)]
        pltpu.make_async_copy(ref, ref, end_recv.at[part]).wait()
    store = pltpu.make_async_copy(final, o_ref, out_sem)
    store.start()
    for copy in pair + sent + ends:
        copy.wait_send()
    store.wait()


def scatter_blocks(slotted):
    devices, _, count = slotted.shape[:3]
    parts = chunks_of(count) if devices <= 16 else 1
    parts = min(parts, 4)
    first, second, third = bit_split(devices)
    n_mid, n_last, n_far = 1 << first, 1 << second, 1 << third
    tile = (count, HALF, LANES)
    dma = pltpu.SemaphoreType.DMA
    lands = [(n_last - 1) * n_mid * n_far, (n_mid - 1) * n_far, n_far - 1]
    return pl.pallas_call(
        functools.partial(scatter_kernel, devices, parts),
        out_shape=jax.ShapeDtypeStruct((2,) + tile, jnp.bfloat16),
        in_specs=[pl.BlockSpec(memory_space=pl.ANY)],
        out_specs=pl.BlockSpec(memory_space=pl.ANY),
        scratch_shapes=[
            pltpu.VMEM((devices,) + tile, jnp.bfloat16),
            pltpu.VMEM((devices,) + tile, jnp.bfloat16),
        ]
        + [pltpu.VMEM((k,) + tile, jnp.bfloat16) for k in lands]
        + [
            pltpu.VMEM((2,) + tile, jnp.bfloat16),
            dma((parts,)),
            dma((parts,)),
            dma((parts,)),
            dma((sum(lands) * parts,)),
            dma((lands[0], parts)),
            dma((lands[1], parts)),
            dma((lands[2], parts)),
            dma((parts,)),
            dma((parts,)),
            dma(()),
        ],
        compiler_params=pltpu.CompilerParams(
            collective_id=2, has_side_effects=True, vmem_limit_bytes=56 * 2**20
        ),
    )(slotted)


ROWS = ROW_SLOTS * WIDTH
N_IN = C // LANES
N_MID = M // LANES
WIDE = 1024
F32 = jnp.float32
BF16 = jnp.bfloat16


def dot(a, b, ca, cb):
    return lax.dot_general(a, b, (((ca,), (cb,)), ((), ())), preferred_element_type=F32)


def lanes_of(ref, first, count):
    return jnp.concatenate([ref[first + i] for i in range(count)], axis=-1)


def half_tanh(v):
    return 0.5 * (1.0 + jnp.tanh(0.5 * v))


class Net:
    def __init__(self, devices):
        first, second, third = bit_split(devices)
        self.me = lax.axis_index("dp")
        self.core = lax.axis_index("rows")
        self.near, self.far = 1 << (first + second), 1 << third
        self.near_at = lax.rem(self.me, self.near)
        self.far_at = self.me // self.near
        self.partner = (self.me, 1 - self.core)
        self.near_peers = [(self.me ^ m, self.core) for m in range(1, self.near)]
        self.near_slots = [self.near_at ^ m for m in range(1, self.near)]
        self.far_peers = [(self.me ^ (m * self.near), self.core) for m in range(1, self.far)]
        self.far_slots = [self.far_at ^ m for m in range(1, self.far)]

    def hello(self):
        barrier = pltpu.get_barrier_semaphore()
        for peer in [self.partner] + self.near_peers + self.far_peers:
            pl.semaphore_signal(barrier, inc=1, device_id=peer, device_id_type=MESH_IDS)

    def ready(self):
        pl.semaphore_wait(
            pltpu.get_barrier_semaphore(), 1 + len(self.near_peers) + len(self.far_peers)
        )


def slots_total(devices):
    first, second, third = bit_split(devices)
    return 2 + (1 << (first + second)) + (1 << third)


def remote(src, dst, send_sem, recv_sem, device):
    copy = pltpu.make_async_remote_copy(
        src_ref=src,
        dst_ref=dst,
        send_sem=send_sem,
        recv_sem=recv_sem,
        device_id=device,
        device_id_type=MESH_IDS,
    )
    copy.start()
    return copy


def landed(ref, sem):
    pltpu.make_async_copy(ref, ref, sem).wait()


def plain_sum(values, counts):
    total = values[0]
    for value in values[1:]:
        total = total + value
    return total


def pooled_moments(rows):
    def merge(values, counts):
        n = counts[0]
        for more in counts[1:]:
            n = n + more
        sums = values[0][:rows]
        spread = values[0][rows:]
        for value in values[1:]:
            sums = sums + value[:rows]
            spread = spread + value[rows:]
        mean = sums / n
        for value, own in zip(values, counts):
            gap = value[:rows] / own - mean
            spread = spread + own * gap * gap
        return jnp.concatenate([sums, spread], axis=0)

    return merge


def reduce_all(net, value, bufs, send_sem, recv_sem, merge, own_count=None, pair_count=0.0, fillers=()):
    fillers = list(fillers) + [None] * 3
    copies = []
    stages = [
        (0, net.core, [net.partner], [1 - net.core], 2),
        (2, net.near_at, net.near_peers, net.near_slots, net.near),
        (2 + net.near, net.far_at, net.far_peers, net.far_slots, net.far),
    ]
    for step, (base, mine, peers, slots, size) in enumerate(stages):
        bufs[base + mine] = value
        for i, peer in enumerate(peers):
            copies.append(
                remote(
                    bufs.at[base + mine],
                    bufs.at[base + mine],
                    send_sem.at[base + i],
                    recv_sem.at[base + mine],
                    peer,
                )
            )
        if fillers[step] is not None:
            fillers[step]()
        for slot in slots:
            landed(bufs.at[base + slot], recv_sem.at[base + slot])
        if own_count is None:
            counts = [None] * size
        elif step == 0:
            rest = pair_count - own_count
            first = net.core == 0
            counts = [jnp.where(first, own_count, rest), jnp.where(first, rest, own_count)]
        else:
            counts = [pair_count * (1 if step == 1 else net.near)] * size
        value = merge([bufs[base + j] for j in range(size)], counts)
    return value, copies


def column_sum(value):
    return jnp.sum(value.reshape(-1, 8, LANES), axis=0)


def local_moments(z, count, live, own_count, stage, masked):
    quarter = z.shape[1] // 4

    def slab(j, carry):
        total = jnp.zeros((8, LANES), F32)
        for q in range(4):
            rows = pl.ds(q * quarter, quarter)
            v = z[j, rows]
            if masked:
                v = v * live[rows]
                z[j, rows] = v
            total = total + column_sum(v)
        sums = jnp.sum(total, axis=0, keepdims=True)
        mean = sums / own_count
        spread = jnp.zeros((8, LANES), F32)
        for q in range(4):
            rows = pl.ds(q * quarter, quarter)
            d = (z[j, rows] - mean) * live[rows]
            spread = spread + column_sum(d * d)
        stage[pl.ds(j, 1)] = sums
        stage[pl.ds(count + j, 1)] = jnp.sum(spread, axis=0, keepdims=True)
        return carry

    lax.fori_loop(0, count, slab, 0)


def window(ref, down, right):
    batch = ref.shape[3]
    parts = [
        ref[j, pl.ds(down, ROW_SLOTS), pl.ds(right, WIDTH)].reshape(ROWS * batch, LANES)
        for j in range(N_MID)
    ]
    return jnp.concatenate(parts, axis=-1)


def clear_edges(ref, core):
    shape = ref.shape
    zero = jnp.zeros((shape[0], 1) + shape[2:], ref.dtype)
    ref[:, pl.ds(jnp.where(core == 0, 0, ROW_SLOTS + 1), 1)] = zero
    column = jnp.zeros(shape[:2] + (1,) + shape[3:], ref.dtype)
    ref[:, :, 0:1] = column
    ref[:, :, WIDTH + 1 : WIDTH + 2] = column


def send_edge(ref, net, send_sem, recv_sem):
    edge = jnp.where(net.core == 0, ROW_SLOTS, 1)
    there = jnp.where(net.core == 0, 0, ROW_SLOTS + 1)
    return remote(
        ref.at[:, edge, pl.ds(1, WIDTH)],
        ref.at[:, there, pl.ds(1, WIDTH)],
        send_sem,
        recv_sem,
        net.partner,
    )


def edge_landed(ref, net, recv_sem):
    here = jnp.where(net.core == 0, ROW_SLOTS + 1, 0)
    landed(ref.at[:, here, pl.ds(1, WIDTH)], recv_sem)


def edge_first(net, fill, send):
    edge = jnp.where(net.core == 0, ROW_SLOTS - 1, 0)
    fill(edge)
    copy = send()
    for step in range(1, ROW_SLOTS):
        fill(lax.rem(edge + step, ROW_SLOTS))
    return copy


def load_all(pairs, sems):
    copies = []
    for i, (src, dst) in enumerate(pairs):
        copy = pltpu.make_async_copy(src, dst, sems.at[i])
        copy.start()
        copies.append(copy)
    return copies


def forward_kernel(devices, top, total_count, *refs):
    refs = list(refs)
    take = lambda n: [refs.pop(0) for _ in range(n)]
    xb_h, = take(1)
    xf_h, = take(1) if top else [None]
    wi_h, wm_h, wo_h, params, live, count = take(6)
    za_h, hp_h, zb_h, hb_h, zc_h, stat_a, stat_b, stat_c = take(8)
    if top:
        pooled, = take(1)
    else:
        xn_h, xnb_h = take(2)
    xb, = take(1)
    xf, = take(1) if top else [None]
    wi, wm, wo, za, hp, zb, hb, zc = take(8)
    if not top:
        xn, xnb = take(2)
    stage_m, stage_c, buf_a, buf_b, buf_c = take(5)
    in_sem, out_sem, send_sem, recv_sem, halo_sem = take(5)

    net = Net(devices)
    net.hello()
    loads = load_all(
        [(xb_h, xb), (wi_h, wi), (wm_h, wm), (wo_h, wo)] + ([(xf_h, xf)] if top else []), in_sem
    )
    clear_edges(hp, net.core)
    zb[...] = jnp.zeros(zb.shape, F32)
    own_count = count[0:1, :]
    pair_count = total_count / devices
    quarter = za.shape[1] // ROW_SLOTS
    batch = quarter // WIDTH
    stores = []
    sends = []

    def store(src, dst):
        copy = pltpu.make_async_copy(src, dst, out_sem.at[len(stores)])
        copy.start()
        stores.append(copy)

    def norm(z, n, stage, bufs, which, masked, stat):
        local_moments(z, n, live, own_count, stage, masked)
        if which == 0:
            net.ready()
        total, copies = reduce_all(
            net,
            stage[...],
            bufs,
            send_sem.at[which],
            recv_sem.at[which],
            pooled_moments(n),
            own_count,
            pair_count,
        )
        sends.extend(copies)
        stat[0:n] = total[:n] / total_count
        stat[n : 2 * n] = lax.rsqrt(total[n:] / total_count + EPS_NORM)

    def affine(stat, n, gain_at, j):
        mean = stat[pl.ds(j, 1)]
        scale = stat[pl.ds(n + j, 1)] * params[pl.ds(gain_at + j, 1)]
        return mean, scale, params[pl.ds(gain_at + n + j, 1)]

    loads[0].wait()
    loads[1].wait()
    product = dot(lanes_of(xb, 0, N_IN), lanes_of(wi, 0, N_MID), 1, 0)
    for j in range(N_MID):
        za[j] = product[:, j * LANES : (j + 1) * LANES]
    store(za, za_h)
    norm(za, N_MID, stage_m, buf_a, 0, False, stat_a)

    def fill_hidden(slot):
        rows = pl.ds(slot * quarter, quarter)

        def slab(j, carry):
            mean, scale, shift = affine(stat_a, N_MID, 0, j)
            y = (za[j, rows] - mean) * scale + shift
            h = (live[rows] * (y * half_tanh(y))).astype(BF16)
            hp[j, pl.ds(slot + 1, 1), pl.ds(1, WIDTH)] = h.reshape(1, WIDTH, batch, LANES)
            return carry

        lax.fori_loop(0, N_MID, slab, 0)

    sends.append(
        edge_first(net, fill_hidden, lambda: send_edge(hp, net, halo_sem.at[0], halo_sem.at[1]))
    )
    loads[2].wait()

    def tap(t):
        k = pl.ds(pl.multiple_of(t * M, M), M)
        part = dot(
            window(hp, t // 3, lax.rem(t, 3)),
            jnp.concatenate([wm[j, k] for j in range(N_MID)], axis=-1),
            1,
            0,
        )
        for j in range(N_MID):
            zb[j] = zb[j] + part[:, j * LANES : (j + 1) * LANES]

    def middle(i, carry):
        tap(i + 3)
        return carry

    def outer(i, carry):
        tap(jnp.where(i < 3, i, i + 3))
        return carry

    lax.fori_loop(0, 3, middle, 0)
    edge_landed(hp, net, halo_sem.at[1])
    store(hp, hp_h)
    lax.fori_loop(0, 6, outer, 0)
    norm(zb, N_MID, stage_m, buf_b, 1, True, stat_b)
    store(zb, zb_h)

    def fill_second(j, carry):
        mean, scale, shift = affine(stat_b, N_MID, 2 * N_MID, j)
        for q in range(4):
            rows = pl.ds(q * quarter, quarter)
            y = (zb[j, rows] - mean) * scale + shift
            hb[j, rows] = (live[rows] * (y * half_tanh(y))).astype(BF16)
        return carry

    lax.fori_loop(0, N_MID, fill_second, 0)
    store(hb, hb_h)
    loads[3].wait()

    def expand(g, carry):
        part = dot(lanes_of(hb, 0, N_MID), lanes_of(wo, g * N_MID, N_MID), 1, 0)
        for j in range(N_MID):
            zc[g * N_MID + j] = part[:, j * LANES : (j + 1) * LANES]
        return carry

    lax.fori_loop(0, N_IN // N_MID, expand, 0)
    store(zc, zc_h)
    norm(zc, N_IN, stage_c, buf_c, 2, False, stat_c)
    if top:
        loads[4].wait()

    def finish(j, carry):
        mean, scale, shift = affine(stat_c, N_IN, 4 * N_MID, j)
        pool = jnp.zeros((batch, LANES), F32)
        for q in range(4):
            rows = pl.ds(q * quarter, quarter)
            x = xf[j, rows] if top else xb[j, rows].astype(F32)
            y = (zc[j, rows] - mean) * scale + shift + x
            out = live[rows] * (y * half_tanh(y))
            if top:
                pool = pool + jnp.sum(out.reshape(WIDTH, batch, LANES), axis=0)
            else:
                xn[j, rows] = out
                xnb[j, rows] = out.astype(BF16)
        if top:
            pooled[j] = pool
        return carry

    lax.fori_loop(0, N_IN, finish, 0)
    if not top:
        store(xn, xn_h)
        store(xnb, xnb_h)
    for copy in stores:
        copy.wait()
    for copy in sends:
        copy.wait_send()


def forward_layer(devices, top, total_count, ident, xb, xf, weights, params, live, count):
    rows = xb.shape[1]
    batch = rows // ROWS
    shape = jax.ShapeDtypeStruct
    any_space = pl.BlockSpec(memory_space=pl.ANY)
    vmem = pl.BlockSpec(memory_space=pltpu.VMEM)
    fields = [
        shape((N_MID, rows, LANES), F32),
        shape((N_MID, ROW_SLOTS + 2, WIDTH + 2, batch, LANES), BF16),
        shape((N_MID, rows, LANES), F32),
        shape((N_MID, rows, LANES), BF16),
        shape((N_IN, rows, LANES), F32),
    ]
    stats = [shape((2 * n, LANES), F32) for n in (N_MID, N_MID, N_IN)]
    if top:
        last = [shape((N_IN, batch, LANES), F32)]
        last_specs = [vmem]
    else:
        last = [shape((N_IN, rows, LANES), F32), shape((N_IN, rows, LANES), BF16)]
        last_specs = [any_space] * 2
    big = lambda s: pltpu.VMEM(s.shape, s.dtype)
    total = slots_total(devices)
    dma = pltpu.SemaphoreType.DMA
    ins = [xb] + ([xf] if top else []) + list(weights) + [params, live, count]
    return pl.pallas_call(
        functools.partial(forward_kernel, devices, top, total_count),
        out_shape=fields + stats + last,
        in_specs=[any_space] * (len(ins) - 3) + [vmem] * 3,
        out_specs=[any_space] * 5 + [vmem] * 3 + last_specs,
        scratch_shapes=[big(a) for a in ins[:-3]]
        + [big(s) for s in fields]
        + ([] if top else [big(s) for s in last])
        + [
            pltpu.VMEM((2 * N_MID, LANES), F32),
            pltpu.VMEM((2 * N_IN, LANES), F32),
            pltpu.VMEM((total, 2 * N_MID, LANES), F32),
            pltpu.VMEM((total, 2 * N_MID, LANES), F32),
            pltpu.VMEM((total, 2 * N_IN, LANES), F32),
            dma((5,)),
            dma((8,)),
            dma((3, total)),
            dma((3, total)),
            dma((2,)),
        ],
        compiler_params=pltpu.CompilerParams(
            collective_id=ident, has_side_effects=True, vmem_limit_bytes=60 * 2**20
        ),
    )(*ins)


def head_kernel(
    devices, area, pooled, head_h, bias, pick, point, own_weight, in_weight, hot, total,
    extra, gtop, gh_h,
    head, send_pool, recv_pool, low, logits_all, logits, g_low, gh, gt,
    in_sem, out_sem, send_sem, recv_sem,
):
    net = Net(devices)
    net.hello()
    load = pltpu.make_async_copy(head_h, head, in_sem)
    load.start()
    half = send_pool.shape[1]
    mine = pl.ds(pl.multiple_of(net.core * half, half), half)
    theirs = pl.ds(pl.multiple_of((1 - net.core) * half, half), half)
    for j in range(N_IN):
        send_pool[j] = pooled[j, theirs].astype(BF16)
    net.ready()
    sends = [remote(send_pool, recv_pool, send_sem.at[0], recv_sem.at[0], net.partner)]
    load.wait()
    landed(recv_pool, recv_sem.at[0])
    for j in range(N_IN):
        low[j] = ((pooled[j, mine] + recv_pool[j].astype(F32)) / area).astype(BF16)
    logits[...] = dot(lanes_of(low, 0, N_IN), lanes_of(head, 0, N_IN), 1, 1) + bias[0:1, :]
    logits_all[net.core, net.me] = logits[...].astype(BF16)
    at = 1
    for peer, slot in zip(net.near_peers, net.near_slots):
        ref = logits_all.at[net.core, net.me]
        sends.append(remote(ref, ref, send_sem.at[at], recv_sem.at[1 + net.near_at], peer))
        at += 1

    own = logits[...]
    keep = lax.broadcasted_iota(jnp.int32, own.shape, 1) < CLASSES
    peak = jnp.max(jnp.where(keep, own, -3.0e38), axis=1, keepdims=True)
    powers = jnp.where(keep, jnp.exp(jnp.where(keep, own - peak, 0.0)), 0.0)
    log_total = peak + jnp.log(jnp.sum(powers, axis=1, keepdims=True))
    softmax = jnp.where(keep, jnp.exp(jnp.where(keep, own - log_total, 0.0)), 0.0)
    picked = jnp.sum(own * hot[...], axis=1, keepdims=True)

    base = net.me - net.near_at
    for slot in net.near_slots:
        landed(logits_all.at[net.core, base + slot], recv_sem.at[1 + slot])
    group = logits_all.at[net.core, pl.ds(base, net.near)]
    for peer in net.far_peers:
        sends.append(
            remote(group, group, send_sem.at[at], recv_sem.at[1 + net.near + net.far_at], peer)
        )
        at += 1
    for slot in net.far_slots:
        landed(
            logits_all.at[net.core, pl.ds(slot * net.near, net.near)],
            recv_sem.at[1 + net.near + slot],
        )
    ref = logits_all.at[net.core]
    sends.append(
        remote(ref, ref, send_sem.at[at], recv_sem.at[1 + net.near + net.far], net.partner)
    )
    at += 1
    landed(logits_all.at[1 - net.core], recv_sem.at[1 + net.near + net.far])
    every = logits_all[...].reshape(-1, WIDE)
    gap = jnp.where(keep, own - dot(pick[...], every, 1, 0), 0.0)
    incoming = dot(point[...], every, 1, 0)
    weight = own_weight[:, 0:1]
    terms = weight * (
        log_total - picked + MATCH_WEIGHT * (jnp.sum(gap * gap, axis=1, keepdims=True) / CLASSES)
    )
    grad = (
        weight * (softmax - hot[...])
        + MATCH_WEIGHT
        * (2.0 / CLASSES)
        * (weight * gap - (incoming - in_weight[:, 0:1] * own))
    ) / total[0:1, 0:1]
    g_low[...] = jnp.where(keep, grad, 0.0).astype(BF16)
    bias_sum = jnp.sum(g_low[...].astype(F32), axis=0, keepdims=True)
    extra[...] = jnp.zeros(extra.shape, F32)
    for j in range(WIDE // LANES):
        extra[j : j + 1] = bias_sum[:, j * LANES : (j + 1) * LANES]
    extra[WIDE // LANES : WIDE // LANES + 1] = jnp.zeros((1, LANES), F32) + jnp.sum(
        terms, axis=0, keepdims=True
    )
    gt_view = gt.at[:, net.core]
    for j in range(N_IN):
        gt[j, net.core] = (dot(g_low[...], head[j], 1, 0) / area).astype(BF16)
    sends.append(
        remote(
            gt_view, gt_view, send_sem.at[at], recv_sem.at[2 + net.near + net.far], net.partner
        )
    )

    def outer(j, carry):
        gh[j] = dot(g_low[...], low[j], 0, 0)
        return carry

    lax.fori_loop(0, N_IN, outer, 0)
    store = pltpu.make_async_copy(gh, gh_h, out_sem)
    store.start()
    landed(gt.at[:, 1 - net.core], recv_sem.at[2 + net.near + net.far])
    for j in range(N_IN):
        gtop[j] = jnp.concatenate([gt[j, 0], gt[j, 1]], axis=0).astype(F32)
    store.wait()
    for copy in sends:
        copy.wait_send()


def head_step(devices, pooled, head, bias, pick, point, own_weight, in_weight, hot, total):
    batch = pooled.shape[1]
    half = batch // 2
    shape = jax.ShapeDtypeStruct
    any_space = pl.BlockSpec(memory_space=pl.ANY)
    vmem = pl.BlockSpec(memory_space=pltpu.VMEM)
    dma = pltpu.SemaphoreType.DMA
    count = 4 + slots_total(devices)
    return pl.pallas_call(
        functools.partial(head_kernel, devices, float(HEIGHT * WIDTH)),
        out_shape=[
            shape((16, LANES), F32),
            shape((N_IN, batch, LANES), F32),
            shape((N_IN, WIDE, LANES), F32),
        ],
        in_specs=[vmem, any_space] + [vmem] * 7,
        out_specs=[vmem, vmem, any_space],
        scratch_shapes=[
            pltpu.VMEM((N_IN, WIDE, LANES), BF16),
            pltpu.VMEM((N_IN, half, LANES), BF16),
            pltpu.VMEM((N_IN, half, LANES), BF16),
            pltpu.VMEM((N_IN, half, LANES), BF16),
            pltpu.VMEM((2, devices, half, WIDE), BF16),
            pltpu.VMEM((half, WIDE), F32),
            pltpu.VMEM((half, WIDE), BF16),
            pltpu.VMEM((N_IN, WIDE, LANES), F32),
            pltpu.VMEM((N_IN, 2, half, LANES), BF16),
            dma(()),
            dma(()),
            dma((count,)),
            dma((count,)),
        ],
        compiler_params=pltpu.CompilerParams(
            collective_id=5, has_side_effects=True, vmem_limit_bytes=60 * 2**20
        ),
    )(pooled, head, bias, pick, point, own_weight, in_weight, hot, total)


def backward_kernel(devices, top, total_count, *refs):
    refs = list(refs)
    take = lambda n: [refs.pop(0) for _ in range(n)]
    field_h, xb_h, zc_h, hb_h, hp_h, zb_h, za_h, wi_h, wm_h, wo_h = take(10)
    gtop, stat_a, stat_b, stat_c, params, live, extra = take(7)
    gi_h, gm_h, go_h = take(3)
    gout_h, = take(1) if top else [None]
    small, = take(1)
    field, xb, zc, hb, hp, zb, za, wi, wm, wo = take(10)
    gi, gm, go = take(3)
    ec, ep, ea, ub, ua = take(5)
    stage_m, stage_c, buf_a, buf_b, buf_c = take(5)
    in_sem, out_sem, send_sem, recv_sem, halo_sem = take(5)

    net = Net(devices)
    net.hello()
    loads = load_all(
        [
            (zc_h, zc), (field_h, field), (xb_h, xb), (wo_h, wo), (zb_h, zb), (hb_h, hb),
            (hp_h, hp), (wm_h, wm), (za_h, za), (wi_h, wi),
        ],
        in_sem,
    )
    clear_edges(ep, net.core)
    quarter = za.shape[1] // ROW_SLOTS
    batch = quarter // WIDTH
    stores = []
    sends = []

    def store(src, dst):
        copy = pltpu.make_async_copy(src, dst, out_sem.at[len(stores)])
        copy.start()
        stores.append(copy)

    def slope(y):
        sigma = half_tanh(y)
        return sigma * (1.0 + y * (1.0 - sigma))

    def row(ref, j):
        return ref[pl.ds(j, 1)]

    def totals(stage, bufs, which, small_at, n, fillers=()):
        total, copies = reduce_all(
            net, stage[...], bufs, send_sem.at[which], recv_sem.at[which], plain_sum, fillers=fillers
        )
        sends.extend(copies)
        small[small_at : small_at + 2 * n] = total[: 2 * n]
        return total

    loads[0].wait()
    loads[1].wait()
    if not top:
        loads[2].wait()

    def slab_c(j, carry):
        mean, scale = row(stat_c, j), row(stat_c, N_IN + j)
        gain, shift = row(params, 4 * N_MID + j), row(params, 4 * N_MID + N_IN + j)
        total = jnp.zeros((8, LANES), F32)
        crossed = jnp.zeros((8, LANES), F32)
        for q in range(4):
            rows = pl.ds(q * quarter, quarter)
            normed = (zc[j, rows] - mean) * scale
            if top:
                x = field[j, rows]
                g = jnp.concatenate([gtop[j]] * WIDTH, axis=0)
            else:
                x = xb[j, rows].astype(F32)
                g = field[j, rows]
            u = g * live[rows] * slope(normed * gain + shift + x)
            field[j, rows] = u
            total = total + column_sum(u)
            crossed = crossed + column_sum(u * normed)
        stage_c[pl.ds(j, 1)] = jnp.sum(crossed, axis=0, keepdims=True)
        stage_c[pl.ds(N_IN + j, 1)] = jnp.sum(total, axis=0, keepdims=True)
        return carry

    lax.fori_loop(0, N_IN, slab_c, 0)
    stage_c[2 * N_IN :] = extra[...]
    net.ready()
    total_c = totals(stage_c, buf_c, 2, 4 * N_MID, N_IN)
    small[4 * N_MID + 2 * N_IN :] = total_c[2 * N_IN :]

    def back_c(j, carry):
        mean, scale = row(stat_c, j), row(stat_c, N_IN + j)
        gain = row(params, 4 * N_MID + j)
        cross = row(small, 4 * N_MID + j) / total_count
        plain = row(small, 4 * N_MID + N_IN + j) / total_count
        for q in range(4):
            rows = pl.ds(q * quarter, quarter)
            normed = (zc[j, rows] - mean) * scale
            e = live[rows] * ((gain * scale) * (field[j, rows] - plain - normed * cross))
            ec[j, rows] = e.astype(BF16)
        return carry

    lax.fori_loop(0, N_IN, back_c, 0)
    loads[3].wait()
    product = dot(lanes_of(ec, 0, N_IN), lanes_of(wo, 0, N_IN), 1, 1)
    for j in range(N_MID):
        ub[j] = product[:, j * LANES : (j + 1) * LANES]
    loads[4].wait()

    def sums_of(u_ref, z_ref, stat, gain_at, stage):
        def slab(j, carry):
            mean, scale = row(stat, j), row(stat, N_MID + j)
            gain, shift = row(params, gain_at + j), row(params, gain_at + N_MID + j)
            total = jnp.zeros((8, LANES), F32)
            crossed = jnp.zeros((8, LANES), F32)
            for q in range(4):
                rows = pl.ds(q * quarter, quarter)
                normed = (z_ref[j, rows] - mean) * scale
                u = u_ref[j, rows] * live[rows] * slope(normed * gain + shift)
                u_ref[j, rows] = u
                total = total + column_sum(u)
                crossed = crossed + column_sum(u * normed)
            stage[pl.ds(j, 1)] = jnp.sum(crossed, axis=0, keepdims=True)
            stage[pl.ds(N_MID + j, 1)] = jnp.sum(total, axis=0, keepdims=True)
            return carry

        lax.fori_loop(0, N_MID, slab, 0)

    def back_of(u_ref, z_ref, stat, gain_at, small_at, j, rows):
        normed = (z_ref[j, rows] - row(stat, j)) * row(stat, N_MID + j)
        cross = row(small, small_at + j) / total_count
        plain = row(small, small_at + N_MID + j) / total_count
        factor = row(params, gain_at + j) * row(stat, N_MID + j)
        return (live[rows] * (factor * (u_ref[j, rows] - plain - normed * cross))).astype(BF16)

    sums_of(ub, zb, stat_b, 2 * N_MID, stage_m)
    loads[5].wait()

    def grad_out(first, last):
        def group(g, carry):
            part = dot(lanes_of(hb, 0, N_MID), lanes_of(ec, g * N_MID, N_MID), 0, 0)
            for j in range(N_MID):
                go[g * N_MID + j] = part[:, j * LANES : (j + 1) * LANES].astype(BF16)
            return carry

        return lambda: lax.fori_loop(first, last, group, 0)

    groups = N_IN // N_MID
    totals(
        stage_m, buf_b, 1, 2 * N_MID, N_MID,
        [grad_out(0, 1), grad_out(1, groups - 1), grad_out(groups - 1, groups)],
    )
    store(go, go_h)

    def fill_b(slot):
        rows = pl.ds(slot * quarter, quarter)

        def slab(j, carry):
            e = back_of(ub, zb, stat_b, 2 * N_MID, 2 * N_MID, j, rows)
            ep[j, pl.ds(slot + 1, 1), pl.ds(1, WIDTH)] = e.reshape(1, WIDTH, batch, LANES)
            return carry

        lax.fori_loop(0, N_MID, slab, 0)

    sends.append(
        edge_first(net, fill_b, lambda: send_edge(ep, net, halo_sem.at[0], halo_sem.at[1]))
    )
    loads[6].wait()
    loads[7].wait()
    ua[...] = jnp.zeros(ua.shape, F32)

    def grad_mid(first, last):
        def one(t, carry):
            part = dot(window(hp, t // 3, lax.rem(t, 3)), window(ep, 1, 1), 0, 0)
            k = pl.ds(pl.multiple_of(t * M, M), M)
            for j in range(N_MID):
                gm[j, k] = part[:, j * LANES : (j + 1) * LANES].astype(BF16)
            return carry

        return lambda: lax.fori_loop(first, last, one, 0)

    def tap(t):
        k = pl.ds(pl.multiple_of(t * M, M), M)
        part = dot(
            window(ep, 2 - t // 3, 2 - lax.rem(t, 3)),
            jnp.concatenate([wm[j, k] for j in range(N_MID)], axis=-1),
            1,
            1,
        )
        for j in range(N_MID):
            ua[j] = ua[j] + part[:, j * LANES : (j + 1) * LANES]

    def middle(i, carry):
        tap(i + 3)
        return carry

    def outer(i, carry):
        tap(jnp.where(i < 3, i, i + 3))
        return carry

    lax.fori_loop(0, 3, middle, 0)
    edge_landed(ep, net, halo_sem.at[1])
    lax.fori_loop(0, 6, outer, 0)
    loads[8].wait()
    sums_of(ua, za, stat_a, 0, stage_m)
    totals(
        stage_m, buf_a, 0, 0, N_MID, [grad_mid(0, 2), grad_mid(2, 5), grad_mid(5, 9)]
    )
    store(gm, gm_h)

    def fill_a(j, carry):
        for q in range(4):
            rows = pl.ds(q * quarter, quarter)
            ea[j, rows] = back_of(ua, za, stat_a, 0, 0, j, rows)
        return carry

    lax.fori_loop(0, N_MID, fill_a, 0)
    loads[9].wait()
    if top:
        loads[2].wait()

        def grad_field(g, carry):
            k = pl.ds(pl.multiple_of(g * M, M), M)
            part = dot(
                lanes_of(ea, 0, N_MID),
                jnp.concatenate([wi[j, k] for j in range(N_MID)], axis=-1),
                1,
                1,
            )
            for j in range(N_MID):
                at = g * N_MID + j
                field[at] = field[at] + part[:, j * LANES : (j + 1) * LANES]
            return carry

        lax.fori_loop(0, groups, grad_field, 0)
        store(field, gout_h)

    def grad_in(g, carry):
        part = dot(lanes_of(xb, g * N_MID, N_MID), lanes_of(ea, 0, N_MID), 0, 0)
        k = pl.ds(pl.multiple_of(g * M, M), M)
        for j in range(N_MID):
            gi[j, k] = part[:, j * LANES : (j + 1) * LANES].astype(BF16)
        return carry

    lax.fori_loop(0, groups, grad_in, 0)
    store(gi, gi_h)
    for copy in stores:
        copy.wait()
    for copy in sends:
        copy.wait_send()


def backward_layer(
    devices, top, total_count, ident, field, xb, kept, weights, gtop, params, live, extra
):
    za, hp, zb, hb, zc, stat_a, stat_b, stat_c = kept
    wi, wm, wo = weights
    shape = jax.ShapeDtypeStruct
    any_space = pl.BlockSpec(memory_space=pl.ANY)
    vmem = pl.BlockSpec(memory_space=pltpu.VMEM)
    dma = pltpu.SemaphoreType.DMA
    total = slots_total(devices)
    rows = xb.shape[1]
    big = lambda s: pltpu.VMEM(s.shape, s.dtype)
    ins = [field, xb, zc, hb, hp, zb, za, wi, wm, wo]
    small_ins = [gtop, stat_a, stat_b, stat_c, params, live, extra]
    grads = [shape(w.shape, BF16) for w in weights]
    more = [shape(field.shape, F32)] if top else []
    small_rows = 4 * N_MID + 2 * N_IN + extra.shape[0]
    return pl.pallas_call(
        functools.partial(backward_kernel, devices, top, total_count),
        out_shape=grads + more + [shape((small_rows, LANES), F32)],
        in_specs=[any_space] * len(ins) + [vmem] * len(small_ins),
        out_specs=[any_space] * (3 + len(more)) + [vmem],
        scratch_shapes=[big(a) for a in ins]
        + [big(g) for g in grads]
        + [
            pltpu.VMEM((N_IN, rows, LANES), BF16),
            pltpu.VMEM(hp.shape, BF16),
            pltpu.VMEM((N_MID, rows, LANES), BF16),
            pltpu.VMEM((N_MID, rows, LANES), F32),
            pltpu.VMEM((N_MID, rows, LANES), F32),
            pltpu.VMEM((2 * N_MID, LANES), F32),
            pltpu.VMEM((2 * N_IN + extra.shape[0], LANES), F32),
            pltpu.VMEM((total, 2 * N_MID, LANES), F32),
            pltpu.VMEM((total, 2 * N_MID, LANES), F32),
            pltpu.VMEM((total, 2 * N_IN + extra.shape[0], LANES), F32),
            dma((10,)),
            dma((4,)),
            dma((3, total)),
            dma((3, total)),
            dma((2,)),
        ],
        compiler_params=pltpu.CompilerParams(
            collective_id=ident, has_side_effects=True, vmem_limit_bytes=60 * 2**20
        ),
    )(*ins, *small_ins)


def shampoo(master, gradient, statistics, root_pairs):
    block_side = statistics.shape[1]
    tile_grads = gradient.reshape(-1, block_side, block_side)
    left_new = DECAY_STATS * statistics[:, :, :block_side] + (1.0 - DECAY_STATS) * jnp.einsum(
        "sij,skj->sik", tile_grads, tile_grads, precision=HIGHEST
    )
    right_new = DECAY_STATS * statistics[:, :, block_side:] + (1.0 - DECAY_STATS) * jnp.einsum(
        "sji,sjk->sik", tile_grads, tile_grads, precision=HIGHEST
    )
    turned = jnp.einsum(
        "sij,sjk->sik", root_pairs[:, :, :block_side], tile_grads, precision=HIGHEST
    )
    turned = jnp.einsum("sij,sjk->sik", turned, root_pairs[:, :, block_side:], precision=HIGHEST)
    return (
        jnp.concatenate([left_new, right_new], axis=2),
        master - RATE_SHAMPOO * turned.reshape(master.shape),
    )


def adamw(values_old, gradient, moment_one, moment_two, step_rate):
    one_new = BETA_FIRST * moment_one + (1.0 - BETA_FIRST) * gradient
    two_new = BETA_SECOND * moment_two + (1.0 - BETA_SECOND) * gradient * gradient
    fixed_one = 1.0 - BETA_FIRST**STEP
    fixed_two = 1.0 - BETA_SECOND**STEP
    update = one_new / fixed_one / (jnp.sqrt(two_new / fixed_two) + EPS_ADAM)
    return (one_new, two_new, values_old - step_rate * (update + DECAY_WEIGHT * values_old))


def body(
    images,
    row_split,
    labels,
    partners,
    image_weight,
    owner_slot,
    conv_master,
    conv_stats,
    conv_roots,
    head_master,
    head_moment_one,
    head_moment_two,
    small_params,
    small_moment_one,
    small_moment_two,
):
    devices = lax.axis_size("dp")
    core_index = lax.axis_index("rows")
    batch_size = images.shape[0]
    half_batch = batch_size // 2
    slot_count = images.shape[1]
    total_images = partners.shape[0]
    live_count = float(total_images * HEIGHT * WIDTH)
    owned = conv_master.shape[0]
    head_rows = head_master.shape[0]

    halves = (
        conv_master.astype(BF16)
        .reshape(owned, 2, 2, HALF, BLOCK)
        .transpose(2, 0, 3, 1, 4)
        .reshape(2, owned, HALF, LANES)
    )
    slot_index = (owner_slot // owned) * (2 * owned) + owner_slot % owned
    weights = assemble(gather_blocks(halves, devices), slot_index)
    head_t = jnp.pad(head_master.T.astype(BF16), ((0, WIDE - CLASSES), (0, 0)))
    head_all = lax.all_gather(head_t, "dp", axis=0)
    if head_rows != LANES:
        head_all = head_all.transpose(1, 0, 2).reshape(WIDE, N_IN, LANES).transpose(1, 0, 2)

    slot_ids = core_index * slot_count + jnp.arange(slot_count, dtype=jnp.int32)
    first_live = (ROW_SLOTS - row_split)[:, None]
    live = (slot_ids[None, :] >= first_live) & (slot_ids[None, :] < first_live + HEIGHT)
    own_count = jnp.sum(live.astype(F32)) * WIDTH
    counts = jnp.broadcast_to(own_count, (8, LANES))
    rows = slot_count * WIDTH * batch_size
    live_rows = jnp.broadcast_to(
        live.T.astype(F32)[:, None, :, None], (slot_count, WIDTH, batch_size, LANES)
    ).reshape(rows, LANES)
    first = (
        jnp.where(live[:, :, None, None], images, 0)
        .reshape(batch_size, slot_count, WIDTH, N_IN, LANES)
        .transpose(3, 1, 2, 0, 4)
        .reshape(N_IN, rows, LANES)
    )
    stride = 4 * M + 2 * C
    params = [
        small_params[at * stride : (at + 1) * stride].reshape(-1, LANES) for at in range(LAYERS)
    ]
    bias = jnp.broadcast_to(
        jnp.pad(small_params[LAYERS * stride :], (0, WIDE - CLASSES)), (8, WIDE)
    )

    kept = []
    field, low = None, first
    lows = []
    for at in range(LAYERS):
        last = at == LAYERS - 1
        lows.append(low)
        out = forward_layer(
            devices,
            at > 0,
            live_count,
            3 + at,
            low,
            field,
            weights[3 * at : 3 * at + 3],
            params[at],
            live_rows,
            counts,
        )
        kept.append(out[:8])
        if last:
            pooled = out[8]
        else:
            field, low = out[8], out[9]

    def by_core(v):
        return v.reshape(devices, 2, half_batch).transpose(1, 0, 2).reshape(-1)

    weight_f = image_weight.astype(F32)
    weight_total = jnp.sum(weight_f)
    own_start = (lax.axis_index("dp") * 2 + core_index) * half_batch
    own_ids = own_start + jnp.arange(half_batch, dtype=jnp.int32)
    own_weight = lax.dynamic_slice_in_dim(weight_f, own_start, half_batch)
    own_partner = lax.dynamic_slice_in_dim(partners, own_start, half_batch)
    own_label = lax.dynamic_slice_in_dim(labels, core_index * half_batch, half_batch)
    ids = by_core(jnp.arange(total_images, dtype=jnp.int32))
    pick = (own_partner[:, None] == ids[None, :]).astype(BF16)
    point = (by_core(partners)[None, :] == own_ids[:, None]).astype(F32) * by_core(weight_f)[None, :]
    in_weight = jnp.sum(point, axis=1)
    hot = (own_label[:, None] == jnp.arange(WIDE, dtype=jnp.int32)[None, :]).astype(F32)
    spread = lambda v: jnp.broadcast_to(v[:, None], (half_batch, LANES))
    extra, g_top, grad_head = head_step(
        devices,
        pooled,
        head_all,
        bias,
        pick,
        point.astype(BF16),
        spread(own_weight),
        spread(in_weight),
        hot,
        jnp.broadcast_to(weight_total, (8, LANES)),
    )
    if head_rows != LANES:
        grad_head = (
            grad_head.transpose(1, 0, 2).reshape(WIDE, devices, head_rows).transpose(1, 0, 2)
        )
    owned_head = lax.psum_scatter(grad_head, "dp", scatter_dimension=0, tiled=False)
    head_grad = lax.psum(owned_head.astype(BF16), "rows").astype(F32)[:CLASSES].T

    no_extra = jnp.zeros_like(extra)
    top = backward_layer(
        devices, True, live_count, 6, field, lows[1], kept[1], weights[3:], g_top, params[1],
        live_rows, extra,
    )
    bottom = backward_layer(
        devices, False, live_count, 7, top[3], lows[0], kept[0], weights[:3], no_extra, params[0],
        live_rows, no_extra,
    )
    small_top, small_bottom = top[4], bottom[3]
    slotted = to_slots(list(bottom[:3]) + list(top[:3]), slot_index, devices)
    tiles = scatter_blocks(slotted)
    conv_grad = (
        tiles.reshape(2, owned, HALF, 2, BLOCK)
        .transpose(1, 3, 0, 2, 4)
        .reshape(owned, BLOCK * BLOCK)
        .astype(F32)
    )
    stats_new, master_new = shampoo(conv_master, conv_grad, conv_stats, conv_roots)
    head_one, head_two, head_new = adamw(
        head_master, head_grad, head_moment_one, head_moment_two, RATE_HEAD
    )
    layer_rows = stride // LANES
    grad_bias = small_top[layer_rows : layer_rows + WIDE // LANES].reshape(-1)[:CLASSES]
    loss_sum = small_top[layer_rows + WIDE // LANES, 0]
    grad_small = jnp.concatenate(
        [small_bottom[:layer_rows].reshape(-1), small_top[:layer_rows].reshape(-1), grad_bias]
    )
    small_one, small_two, small_new = adamw(
        small_params, grad_small, small_moment_one, small_moment_two, RATE_SMALL
    )
    return (
        loss_sum,
        weight_total,
        conv_grad,
        stats_new,
        master_new,
        master_new.astype(BF16),
        head_one,
        head_two,
        head_new,
        head_new.astype(BF16),
        small_one,
        small_two,
        small_new,
    )


def solution(mesh):
    in_specs = (
        P("dp", "rows", None, None),
        P("dp"),
        P("dp"),
        P(),
        P(),
        P(),
        P("dp", None),
        P("dp", None, None),
        P("dp", None, None),
        P("dp", None),
        P("dp", None),
        P("dp", None),
        P(),
        P(),
        P(),
    )
    out_specs = (
        P(),
        P(),
        P("dp", None),
        P("dp", None, None),
        P("dp", None),
        P("dp", None),
        P("dp", None),
        P("dp", None),
        P("dp", None),
        P("dp", None),
        P(),
        P(),
        P(),
    )
    return jax.shard_map(body, mesh=mesh, in_specs=in_specs, out_specs=out_specs, check_vma=False)
```

```python
import functools

import jax
import jax.numpy as jnp
from jax import lax
from jax.experimental import pallas as pl
from jax.experimental.pallas import tpu as pltpu
from jax.sharding import PartitionSpec as P

C = 2048
M = 512
CLASSES = 1000
HEIGHT = 7
WIDTH = 7
ROW_SLOTS = 4
LAYERS = 2
BLOCK = 64
STEP = 5


EPS_NORM = 1e-05
MATCH_WEIGHT = 4.0
DECAY_STATS = 0.5
RATE_SHAMPOO = 0.15
RATE_HEAD = 0.03
RATE_SMALL = 0.2
BETA_FIRST = 0.9
BETA_SECOND = 0.95
EPS_ADAM = 1e-08
DECAY_WEIGHT = 0.01


C = 2048
M = 512
CLASSES = 1000
HEIGHT = 7
WIDTH = 7
ROW_SLOTS = 4
LAYERS = 2
BLOCK = 64
STEP = 5


EPS_NORM = 1e-05
MATCH_WEIGHT = 4.0
DECAY_STATS = 0.5
RATE_SHAMPOO = 0.15
RATE_HEAD = 0.03
RATE_SMALL = 0.2
BETA_FIRST = 0.9
BETA_SECOND = 0.95
EPS_ADAM = 1e-08
DECAY_WEIGHT = 0.01


MESH_IDS = pl.DeviceIdType.MESH
HALF = 16
LANES = 128


def bit_split(devices):
    bits = devices.bit_length() - 1
    first = bits // 3
    second = (bits - first) // 2
    return first, second, bits - first - second


def greet(peers):
    barrier = pltpu.get_barrier_semaphore()
    for peer in peers:
        pl.semaphore_signal(barrier, inc=1, device_id=peer, device_id_type=MESH_IDS)
    pl.semaphore_wait(barrier, len(peers))


def axis_masks(devices, core):
    first, second, third = bit_split(devices)
    low = [m for m in range(1, 1 << first)]
    high = [m << first for m in range(1, 1 << second)]
    if first == second:
        one = [jnp.where(core == 0, h, l) for h, l in zip(high, low)]
        two = [jnp.where(core == 0, l, h) for h, l in zip(high, low)]
    else:
        one, two = low, high
    far = [m << (first + second) for m in range(1, 1 << third)]
    return [0] + one, [0] + two, [0] + far


def chunks_of(count):
    for parts in (8, 4, 2):
        if count % parts == 0:
            return parts
    return 1


def gather_kernel(devices, parts, x_ref, o_ref, local_sem, send_sem, recv_sem):
    me = lax.axis_index("dp")
    core = lax.axis_index("rows")
    per = x_ref.shape[1] // parts
    mid, last, far = axis_masks(devices, core)
    partner = (me, 1 - core)
    greet(
        [(me ^ m, core) for m in far[1:]]
        + [(me ^ m, core) for m in mid[1:]]
        + [(me ^ m, core) for m in last[1:]]
        + [partner]
    )
    sent = []

    def piece(owner, half, part):
        return o_ref.at[owner, half, pl.ds(part * per, per)]

    def send(src_ref, owner, part, device):
        copy = pltpu.make_async_remote_copy(
            src_ref=src_ref,
            dst_ref=piece(owner, core, part),
            send_sem=send_sem.at[len(sent)],
            recv_sem=recv_sem.at[owner, core, part],
            device_id=device,
            device_id_type=MESH_IDS,
        )
        copy.start()
        sent.append(copy)

    def arrived(owner, half, part):
        ref = piece(owner, half, part)
        pltpu.make_async_copy(ref, ref, recv_sem.at[owner, half, part]).wait()

    def onward(owner, part, masks):
        arrived(owner, core, part)
        for m in masks:
            send(piece(owner, core, part), owner, part, (me ^ m, core))
        send(piece(owner, core, part), owner, part, partner)

    early = parts - parts // 4
    own_copy = pltpu.make_async_copy(x_ref, o_ref.at[me], local_sem)
    own_copy.start()
    for part in range(parts):
        order = far[1:] + last[1:] + mid[1:] if part < early else mid[1:] + far[1:] + last[1:]
        for m in order:
            send(x_ref.at[core, pl.ds(part * per, per)], me, part, (me ^ m, core))
    for tick in range(parts + 2):
        part = tick
        if part < parts:
            if part < early:
                for z in far[1:]:
                    onward(me ^ z, part, last[1:] + mid[1:])
            else:
                for m in mid[1:]:
                    onward(me ^ m, part, far[1:] + last[1:])
        part = tick - 1
        if 0 <= part < parts:
            if part < early:
                for m in mid[1:]:
                    for z in far:
                        onward(me ^ m ^ z, part, last[1:])
            else:
                for z in far[1:]:
                    onward(me ^ z, part, last[1:])
                for z in far[1:]:
                    for m in mid[1:]:
                        onward(me ^ z ^ m, part, last[1:])
        part = tick - 2
        if 0 <= part < parts:
            for q in last[1:]:
                for z in far:
                    for m in mid:
                        onward(me ^ q ^ z ^ m, part, [])
    for step in range(1, devices):
        for part in range(parts):
            arrived(me ^ step, 1 - core, part)
    own_copy.wait()
    for copy in sent:
        copy.wait_send()


def gather_blocks(own, devices):
    count = own.shape[1]
    parts = chunks_of(count)
    return pl.pallas_call(
        functools.partial(gather_kernel, devices, parts),
        out_shape=jax.ShapeDtypeStruct((devices,) + own.shape, own.dtype),
        in_specs=[pl.BlockSpec(memory_space=pl.ANY)],
        out_specs=pl.BlockSpec(memory_space=pl.ANY),
        scratch_shapes=[
            pltpu.SemaphoreType.DMA(()),
            pltpu.SemaphoreType.DMA((3 * devices * parts,)),
            pltpu.SemaphoreType.DMA((devices, 2, parts)),
        ],
        compiler_params=pltpu.CompilerParams(
            collective_id=1, has_side_effects=True, vmem_limit_bytes=56 * 2**20
        ),
    )(own)


def slab_shape(shape):
    return (shape[1] // LANES, shape[0], LANES)


def matrix_list():
    shapes = []
    for _ in range(LAYERS):
        shapes += [(C, M), (9 * M, M), (M, C)]
    return shapes


def assemble_kernel(count, idx_ref, g_hbm, *refs):
    shapes = matrix_list()
    n = len(shapes)
    outs, bufs, (g_ref, in_sem, out_sem) = refs[:n], refs[n : 2 * n], refs[2 * n :]
    load = pltpu.make_async_copy(g_hbm, g_ref, in_sem)
    load.start()
    load.wait()
    base = 0
    copies = []
    for at, (rows, cols) in enumerate(shapes):
        pairs = cols // LANES
        buf = bufs[at]

        def strip(r, carry, base=base, pairs=pairs, buf=buf):
            for m in range(pairs):
                even = idx_ref[base + r * (2 * pairs) + 2 * m]
                odd = idx_ref[base + r * (2 * pairs) + 2 * m + 1]
                for h in range(2):
                    e = g_ref[even + h * count]
                    o = g_ref[odd + h * count]
                    buf[m, pl.ds(r * BLOCK + h * HALF, HALF)] = jnp.concatenate(
                        [e[:, :BLOCK], o[:, :BLOCK]], axis=1
                    )
                    buf[m, pl.ds(r * BLOCK + 2 * HALF + h * HALF, HALF)] = jnp.concatenate(
                        [e[:, BLOCK:], o[:, BLOCK:]], axis=1
                    )
            return carry

        lax.fori_loop(0, rows // BLOCK, strip, 0, unroll=8 // (pairs // 4))
        copy = pltpu.make_async_copy(buf, outs[at], out_sem.at[at])
        copy.start()
        copies.append(copy)
        base += (rows // BLOCK) * (cols // BLOCK)
    for copy in copies:
        copy.wait()


def assemble(gathered, index):
    devices, _, count = gathered.shape[:3]
    flat = gathered.reshape(devices * 2 * count, HALF, LANES)
    shapes = matrix_list()
    return pl.pallas_call(
        functools.partial(assemble_kernel, count),
        out_shape=[jax.ShapeDtypeStruct(slab_shape(s), jnp.bfloat16) for s in shapes],
        in_specs=[
            pl.BlockSpec(memory_space=pltpu.SMEM),
            pl.BlockSpec(memory_space=pl.ANY),
        ],
        out_specs=[pl.BlockSpec(memory_space=pl.ANY)] * len(shapes),
        scratch_shapes=[pltpu.VMEM(slab_shape(s), jnp.bfloat16) for s in shapes]
        + [
            pltpu.VMEM(flat.shape, jnp.bfloat16),
            pltpu.SemaphoreType.DMA(()),
            pltpu.SemaphoreType.DMA((len(shapes),)),
        ],
        compiler_params=pltpu.CompilerParams(vmem_limit_bytes=56 * 2**20),
    )(index, flat)


def slots_kernel(count, idx_ref, *refs):
    shapes = matrix_list()
    n = len(shapes)
    grads, o_hbm, bufs, (o_ref, in_sem, out_sem) = (
        refs[:n],
        refs[n],
        refs[n + 1 : 2 * n + 1],
        refs[2 * n + 1 :],
    )
    loads = []
    for at in range(n):
        load = pltpu.make_async_copy(grads[at], bufs[at], in_sem.at[at])
        load.start()
        loads.append(load)
    base = 0
    for at, (rows, cols) in enumerate(shapes):
        pairs = cols // LANES
        buf = bufs[at]
        loads[at].wait()

        def strip(r, carry, base=base, pairs=pairs, buf=buf):
            for m in range(pairs):
                even = idx_ref[base + r * (2 * pairs) + 2 * m]
                odd = idx_ref[base + r * (2 * pairs) + 2 * m + 1]
                for h in range(2):
                    top = buf[m, pl.ds(r * BLOCK + h * HALF, HALF)]
                    low = buf[m, pl.ds(r * BLOCK + 2 * HALF + h * HALF, HALF)]
                    o_ref[even + h * count] = jnp.concatenate(
                        [top[:, :BLOCK], low[:, :BLOCK]], axis=1
                    )
                    o_ref[odd + h * count] = jnp.concatenate(
                        [top[:, BLOCK:], low[:, BLOCK:]], axis=1
                    )
            return carry

        lax.fori_loop(0, rows // BLOCK, strip, 0, unroll=8 // (pairs // 4))
        base += (rows // BLOCK) * (cols // BLOCK)
    store = pltpu.make_async_copy(o_ref, o_hbm, out_sem)
    store.start()
    store.wait()


def to_slots(grads, index, devices):
    shapes = matrix_list()
    total = index.shape[0]
    count = total // devices
    flat = (total * 2, HALF, LANES)
    out = pl.pallas_call(
        functools.partial(slots_kernel, count),
        out_shape=jax.ShapeDtypeStruct(flat, jnp.bfloat16),
        in_specs=[pl.BlockSpec(memory_space=pltpu.SMEM)]
        + [pl.BlockSpec(memory_space=pl.ANY)] * len(shapes),
        out_specs=pl.BlockSpec(memory_space=pl.ANY),
        scratch_shapes=[pltpu.VMEM(slab_shape(s), jnp.bfloat16) for s in shapes]
        + [
            pltpu.VMEM(flat, jnp.bfloat16),
            pltpu.SemaphoreType.DMA((len(shapes),)),
            pltpu.SemaphoreType.DMA(()),
        ],
        compiler_params=pltpu.CompilerParams(vmem_limit_bytes=56 * 2**20),
    )(index, *grads)
    return out.reshape(devices, 2, count, HALF, LANES)


def scatter_kernel(
    devices, parts, g_ref, o_ref, acc, other, land_last, land_mid, land_far, final,
    local_sem, pair_send, pair_recv, send_sem, last_recv, mid_recv, far_recv, end_send, end_recv, out_sem,
):
    me = lax.axis_index("dp")
    core = lax.axis_index("rows")
    count = g_ref.shape[2]
    per = count // parts
    mid, last, far = axis_masks(devices, core)
    partner = (me, 1 - core)
    greet(
        [(me ^ m, core) for m in far[1:]]
        + [(me ^ m, core) for m in mid[1:]]
        + [(me ^ m, core) for m in last[1:]]
        + [partner]
    )

    def span(part):
        return pl.ds(part * per, per)

    pair = []
    local = []
    for part in range(parts):
        copy = pltpu.make_async_remote_copy(
            src_ref=g_ref.at[:, 1 - core, span(part)],
            dst_ref=other.at[:, span(part)],
            send_sem=pair_send.at[part],
            recv_sem=pair_recv.at[part],
            device_id=partner,
            device_id_type=MESH_IDS,
        )
        copy.start()
        pair.append(copy)
        copy = pltpu.make_async_copy(
            g_ref.at[:, core, span(part)], acc.at[:, span(part)], local_sem.at[part]
        )
        copy.start()
        local.append(copy)

    sent = []

    def send(owner, part, land, sems, at, device):
        copy = pltpu.make_async_remote_copy(
            src_ref=acc.at[owner, span(part)],
            dst_ref=land.at[at, span(part)],
            send_sem=send_sem.at[len(sent)],
            recv_sem=sems.at[at, part],
            device_id=device,
            device_id_type=MESH_IDS,
        )
        copy.start()
        sent.append(copy)

    def arrived(land, sems, at, part):
        ref = land.at[at, span(part)]
        pltpu.make_async_copy(ref, ref, sems.at[at, part]).wait()

    def add(owners, lands, part):
        def step(i, carry):
            at = part * per + i
            for owner, (land, j) in zip(owners, lands):
                acc[owner, at] = (
                    acc[owner, at].astype(jnp.float32) + land[j, at].astype(jnp.float32)
                ).astype(jnp.bfloat16)
            return carry

        lax.fori_loop(0, per, step, 0)

    ends = []
    for tick in range(parts + 3):
        part = tick
        if part < parts:
            pair[part].wait_recv()
            local[part].wait()

            def step(i, carry, part=part):
                at = part * per + i
                acc[:, at] = (
                    acc[:, at].astype(jnp.float32) + other[:, at].astype(jnp.float32)
                ).astype(jnp.bfloat16)
                return carry

            lax.fori_loop(0, per, step, 0)
            at = 0
            for q in last[1:]:
                for m in mid[::-1]:
                    for z in far[::-1]:
                        send(me ^ q ^ m ^ z, part, land_last, last_recv, at, (me ^ q, core))
                        at += 1
        part = tick - 1
        if 0 <= part < parts:
            at = 0
            owners, lands = [], []
            per_q = len(mid) * len(far)
            for j in range(len(last) - 1):
                for i, (m, z) in enumerate([(m, z) for m in mid[::-1] for z in far[::-1]]):
                    arrived(land_last, last_recv, j * per_q + i, part)
                    owners.append(me ^ m ^ z)
                    lands.append((land_last, j * per_q + i))
            add(owners, lands, part)
            at = 0
            for m in mid[1:]:
                for z in far[::-1]:
                    send(me ^ m ^ z, part, land_mid, mid_recv, at, (me ^ m, core))
                    at += 1
        part = tick - 2
        if 0 <= part < parts:
            owners, lands = [], []
            for j in range(len(mid) - 1):
                for i, z in enumerate(far[::-1]):
                    at = j * len(far) + i
                    arrived(land_mid, mid_recv, at, part)
                    owners.append(me ^ z)
                    lands.append((land_mid, at))
            add(owners, lands, part)
            for at, z in enumerate(far[1:]):
                send(me ^ z, part, land_far, far_recv, at, (me ^ z, core))
        part = tick - 3
        if 0 <= part < parts:
            for at in range(len(far) - 1):
                arrived(land_far, far_recv, at, part)

            def finish(i, carry, part=part):
                at = part * per + i
                total = acc[me, at].astype(jnp.float32)
                for j in range(len(far) - 1):
                    total = total + land_far[j, at].astype(jnp.float32)
                final[core, at] = total.astype(jnp.bfloat16)
                return carry

            lax.fori_loop(0, per, finish, 0)
            copy = pltpu.make_async_remote_copy(
                src_ref=final.at[core, span(part)],
                dst_ref=final.at[core, span(part)],
                send_sem=end_send.at[part],
                recv_sem=end_recv.at[part],
                device_id=partner,
                device_id_type=MESH_IDS,
            )
            copy.start()
            ends.append(copy)
    for part in range(parts):
        ref = final.at[1 - core, span(part)]
        pltpu.make_async_copy(ref, ref, end_recv.at[part]).wait()
    store = pltpu.make_async_copy(final, o_ref, out_sem)
    store.start()
    for copy in pair + sent + ends:
        copy.wait_send()
    store.wait()


def scatter_blocks(slotted):
    devices, _, count = slotted.shape[:3]
    parts = chunks_of(count) if devices <= 16 else 1
    parts = min(parts, 4)
    first, second, third = bit_split(devices)
    n_mid, n_last, n_far = 1 << first, 1 << second, 1 << third
    tile = (count, HALF, LANES)
    dma = pltpu.SemaphoreType.DMA
    lands = [(n_last - 1) * n_mid * n_far, (n_mid - 1) * n_far, n_far - 1]
    return pl.pallas_call(
        functools.partial(scatter_kernel, devices, parts),
        out_shape=jax.ShapeDtypeStruct((2,) + tile, jnp.bfloat16),
        in_specs=[pl.BlockSpec(memory_space=pl.ANY)],
        out_specs=pl.BlockSpec(memory_space=pl.ANY),
        scratch_shapes=[
            pltpu.VMEM((devices,) + tile, jnp.bfloat16),
            pltpu.VMEM((devices,) + tile, jnp.bfloat16),
        ]
        + [pltpu.VMEM((k,) + tile, jnp.bfloat16) for k in lands]
        + [
            pltpu.VMEM((2,) + tile, jnp.bfloat16),
            dma((parts,)),
            dma((parts,)),
            dma((parts,)),
            dma((sum(lands) * parts,)),
            dma((lands[0], parts)),
            dma((lands[1], parts)),
            dma((lands[2], parts)),
            dma((parts,)),
            dma((parts,)),
            dma(()),
        ],
        compiler_params=pltpu.CompilerParams(
            collective_id=2, has_side_effects=True, vmem_limit_bytes=56 * 2**20
        ),
    )(slotted)


ROWS = ROW_SLOTS * WIDTH
N_IN = C // LANES
N_MID = M // LANES
WIDE = 1024
F32 = jnp.float32
BF16 = jnp.bfloat16


def dot(a, b, ca, cb):
    return lax.dot_general(a, b, (((ca,), (cb,)), ((), ())), preferred_element_type=F32)


def lanes_of(ref, first, count):
    return jnp.concatenate([ref[first + i] for i in range(count)], axis=-1)


def half_tanh(v):
    return 0.5 * (1.0 + jnp.tanh(0.5 * v))


class Net:
    def __init__(self, devices):
        first, second, third = bit_split(devices)
        self.me = lax.axis_index("dp")
        self.core = lax.axis_index("rows")
        self.near, self.far = 1 << (first + second), 1 << third
        self.near_at = lax.rem(self.me, self.near)
        self.far_at = self.me // self.near
        self.partner = (self.me, 1 - self.core)
        self.near_peers = [(self.me ^ m, self.core) for m in range(1, self.near)]
        self.near_slots = [self.near_at ^ m for m in range(1, self.near)]
        self.far_peers = [(self.me ^ (m * self.near), self.core) for m in range(1, self.far)]
        self.far_slots = [self.far_at ^ m for m in range(1, self.far)]

    def hello(self):
        barrier = pltpu.get_barrier_semaphore()
        for peer in [self.partner] + self.near_peers + self.far_peers:
            pl.semaphore_signal(barrier, inc=1, device_id=peer, device_id_type=MESH_IDS)

    def ready(self):
        pl.semaphore_wait(
            pltpu.get_barrier_semaphore(), 1 + len(self.near_peers) + len(self.far_peers)
        )


def slots_total(devices):
    first, second, third = bit_split(devices)
    return 2 + (1 << (first + second)) + (1 << third)


def remote(src, dst, send_sem, recv_sem, device):
    copy = pltpu.make_async_remote_copy(
        src_ref=src,
        dst_ref=dst,
        send_sem=send_sem,
        recv_sem=recv_sem,
        device_id=device,
        device_id_type=MESH_IDS,
    )
    copy.start()
    return copy


def landed(ref, sem):
    pltpu.make_async_copy(ref, ref, sem).wait()


def plain_sum(values, counts):
    total = values[0]
    for value in values[1:]:
        total = total + value
    return total


def pooled_moments(rows):
    def merge(values, counts):
        n = counts[0]
        for more in counts[1:]:
            n = n + more
        sums = values[0][:rows]
        spread = values[0][rows:]
        for value in values[1:]:
            sums = sums + value[:rows]
            spread = spread + value[rows:]
        mean = sums / n
        for value, own in zip(values, counts):
            gap = value[:rows] / own - mean
            spread = spread + own * gap * gap
        return jnp.concatenate([sums, spread], axis=0)

    return merge


def reduce_all(net, value, bufs, send_sem, recv_sem, merge, own_count=None, pair_count=0.0, fillers=()):
    fillers = list(fillers) + [None] * 3
    copies = []
    stages = [
        (0, net.core, [net.partner], [1 - net.core], 2),
        (2, net.near_at, net.near_peers, net.near_slots, net.near),
        (2 + net.near, net.far_at, net.far_peers, net.far_slots, net.far),
    ]
    for step, (base, mine, peers, slots, size) in enumerate(stages):
        bufs[base + mine] = value
        for i, peer in enumerate(peers):
            copies.append(
                remote(
                    bufs.at[base + mine],
                    bufs.at[base + mine],
                    send_sem.at[base + i],
                    recv_sem.at[base + mine],
                    peer,
                )
            )
        if fillers[step] is not None:
            fillers[step]()
        for slot in slots:
            landed(bufs.at[base + slot], recv_sem.at[base + slot])
        if own_count is None:
            counts = [None] * size
        elif step == 0:
            rest = pair_count - own_count
            first = net.core == 0
            counts = [jnp.where(first, own_count, rest), jnp.where(first, rest, own_count)]
        else:
            counts = [pair_count * (1 if step == 1 else net.near)] * size
        value = merge([bufs[base + j] for j in range(size)], counts)
    return value, copies


def column_sum(value):
    return jnp.sum(value.reshape(-1, 8, LANES), axis=0)


def local_moments(z, count, live, own_count, stage, masked):
    quarter = z.shape[1] // 4

    def slab(j, carry):
        total = jnp.zeros((8, LANES), F32)
        for q in range(4):
            rows = pl.ds(q * quarter, quarter)
            v = z[j, rows]
            if masked:
                v = v * live[rows]
                z[j, rows] = v
            total = total + column_sum(v)
        sums = jnp.sum(total, axis=0, keepdims=True)
        mean = sums / own_count
        spread = jnp.zeros((8, LANES), F32)
        for q in range(4):
            rows = pl.ds(q * quarter, quarter)
            d = (z[j, rows] - mean) * live[rows]
            spread = spread + column_sum(d * d)
        stage[pl.ds(j, 1)] = sums
        stage[pl.ds(count + j, 1)] = jnp.sum(spread, axis=0, keepdims=True)
        return carry

    lax.fori_loop(0, count, slab, 0)


def window(ref, down, right):
    batch = ref.shape[3]
    parts = [
        ref[j, pl.ds(down, ROW_SLOTS), pl.ds(right, WIDTH)].reshape(ROWS * batch, LANES)
        for j in range(N_MID)
    ]
    return jnp.concatenate(parts, axis=-1)


def clear_edges(ref, core):
    shape = ref.shape
    zero = jnp.zeros((shape[0], 1) + shape[2:], ref.dtype)
    ref[:, pl.ds(jnp.where(core == 0, 0, ROW_SLOTS + 1), 1)] = zero
    column = jnp.zeros(shape[:2] + (1,) + shape[3:], ref.dtype)
    ref[:, :, 0:1] = column
    ref[:, :, WIDTH + 1 : WIDTH + 2] = column


def send_edge(ref, net, send_sem, recv_sem):
    edge = jnp.where(net.core == 0, ROW_SLOTS, 1)
    there = jnp.where(net.core == 0, 0, ROW_SLOTS + 1)
    return remote(
        ref.at[:, edge, pl.ds(1, WIDTH)],
        ref.at[:, there, pl.ds(1, WIDTH)],
        send_sem,
        recv_sem,
        net.partner,
    )


def edge_landed(ref, net, recv_sem):
    here = jnp.where(net.core == 0, ROW_SLOTS + 1, 0)
    landed(ref.at[:, here, pl.ds(1, WIDTH)], recv_sem)


def edge_first(net, fill, send):
    edge = jnp.where(net.core == 0, ROW_SLOTS - 1, 0)
    fill(edge)
    copy = send()
    for step in range(1, ROW_SLOTS):
        fill(lax.rem(edge + step, ROW_SLOTS))
    return copy


def load_all(pairs, sems):
    copies = []
    for i, (src, dst) in enumerate(pairs):
        copy = pltpu.make_async_copy(src, dst, sems.at[i])
        copy.start()
        copies.append(copy)
    return copies


def forward_kernel(devices, top, total_count, *refs):
    refs = list(refs)
    take = lambda n: [refs.pop(0) for _ in range(n)]
    xb_h, = take(1)
    xf_h, = take(1) if top else [None]
    wi_h, wm_h, wo_h, params, live, count = take(6)
    za_h, hp_h, zb_h, hb_h, zc_h, stat_a, stat_b, stat_c = take(8)
    if top:
        pooled, = take(1)
    else:
        xn_h, xnb_h = take(2)
    xb, = take(1)
    xf, = take(1) if top else [None]
    wi, wm, wo, za, hp, zb, hb, zc = take(8)
    if not top:
        xn, xnb = take(2)
    stage_m, stage_c, buf_a, buf_b, buf_c = take(5)
    in_sem, out_sem, send_sem, recv_sem, halo_sem = take(5)

    net = Net(devices)
    net.hello()
    loads = load_all(
        [(xb_h, xb), (wi_h, wi), (wm_h, wm), (wo_h, wo)] + ([(xf_h, xf)] if top else []), in_sem
    )
    clear_edges(hp, net.core)
    zb[...] = jnp.zeros(zb.shape, F32)
    own_count = count[0:1, :]
    pair_count = total_count / devices
    quarter = za.shape[1] // ROW_SLOTS
    batch = quarter // WIDTH
    stores = []
    sends = []

    def store(src, dst):
        copy = pltpu.make_async_copy(src, dst, out_sem.at[len(stores)])
        copy.start()
        stores.append(copy)

    def norm(z, n, stage, bufs, which, masked, stat):
        local_moments(z, n, live, own_count, stage, masked)
        if which == 0:
            net.ready()
        total, copies = reduce_all(
            net,
            stage[...],
            bufs,
            send_sem.at[which],
            recv_sem.at[which],
            pooled_moments(n),
            own_count,
            pair_count,
        )
        sends.extend(copies)
        stat[0:n] = total[:n] / total_count
        stat[n : 2 * n] = lax.rsqrt(total[n:] / total_count + EPS_NORM)

    def affine(stat, n, gain_at, j):
        mean = stat[pl.ds(j, 1)]
        scale = stat[pl.ds(n + j, 1)] * params[pl.ds(gain_at + j, 1)]
        return mean, scale, params[pl.ds(gain_at + n + j, 1)]

    loads[0].wait()
    loads[1].wait()
    product = dot(lanes_of(xb, 0, N_IN), lanes_of(wi, 0, N_MID), 1, 0)
    for j in range(N_MID):
        za[j] = product[:, j * LANES : (j + 1) * LANES]
    store(za, za_h)
    norm(za, N_MID, stage_m, buf_a, 0, False, stat_a)

    def fill_hidden(slot):
        rows = pl.ds(slot * quarter, quarter)

        def slab(j, carry):
            mean, scale, shift = affine(stat_a, N_MID, 0, j)
            y = (za[j, rows] - mean) * scale + shift
            h = (live[rows] * (y * half_tanh(y))).astype(BF16)
            hp[j, pl.ds(slot + 1, 1), pl.ds(1, WIDTH)] = h.reshape(1, WIDTH, batch, LANES)
            return carry

        lax.fori_loop(0, N_MID, slab, 0)

    sends.append(
        edge_first(net, fill_hidden, lambda: send_edge(hp, net, halo_sem.at[0], halo_sem.at[1]))
    )
    loads[2].wait()

    def tap(t):
        k = pl.ds(pl.multiple_of(t * M, M), M)
        part = dot(
            window(hp, t // 3, lax.rem(t, 3)),
            jnp.concatenate([wm[j, k] for j in range(N_MID)], axis=-1),
            1,
            0,
        )
        for j in range(N_MID):
            zb[j] = zb[j] + part[:, j * LANES : (j + 1) * LANES]

    def middle(i, carry):
        tap(i + 3)
        return carry

    def outer(i, carry):
        tap(jnp.where(i < 3, i, i + 3))
        return carry

    lax.fori_loop(0, 3, middle, 0)
    edge_landed(hp, net, halo_sem.at[1])
    store(hp, hp_h)
    lax.fori_loop(0, 6, outer, 0)
    norm(zb, N_MID, stage_m, buf_b, 1, True, stat_b)
    store(zb, zb_h)

    def fill_second(j, carry):
        mean, scale, shift = affine(stat_b, N_MID, 2 * N_MID, j)
        for q in range(4):
            rows = pl.ds(q * quarter, quarter)
            y = (zb[j, rows] - mean) * scale + shift
            hb[j, rows] = (live[rows] * (y * half_tanh(y))).astype(BF16)
        return carry

    lax.fori_loop(0, N_MID, fill_second, 0)
    store(hb, hb_h)
    loads[3].wait()

    def expand(g, carry):
        part = dot(lanes_of(hb, 0, N_MID), lanes_of(wo, g * N_MID, N_MID), 1, 0)
        for j in range(N_MID):
            zc[g * N_MID + j] = part[:, j * LANES : (j + 1) * LANES]
        return carry

    lax.fori_loop(0, N_IN // N_MID, expand, 0)
    store(zc, zc_h)
    norm(zc, N_IN, stage_c, buf_c, 2, False, stat_c)
    if top:
        loads[4].wait()

    def finish(j, carry):
        mean, scale, shift = affine(stat_c, N_IN, 4 * N_MID, j)
        pool = jnp.zeros((batch, LANES), F32)
        for q in range(4):
            rows = pl.ds(q * quarter, quarter)
            x = xf[j, rows] if top else xb[j, rows].astype(F32)
            y = (zc[j, rows] - mean) * scale + shift + x
            out = live[rows] * (y * half_tanh(y))
            if top:
                pool = pool + jnp.sum(out.reshape(WIDTH, batch, LANES), axis=0)
            else:
                xn[j, rows] = out
                xnb[j, rows] = out.astype(BF16)
        if top:
            pooled[j] = pool
        return carry

    lax.fori_loop(0, N_IN, finish, 0)
    if not top:
        store(xn, xn_h)
        store(xnb, xnb_h)
    for copy in stores:
        copy.wait()
    for copy in sends:
        copy.wait_send()


def forward_layer(devices, top, total_count, ident, xb, xf, weights, params, live, count):
    rows = xb.shape[1]
    batch = rows // ROWS
    shape = jax.ShapeDtypeStruct
    any_space = pl.BlockSpec(memory_space=pl.ANY)
    vmem = pl.BlockSpec(memory_space=pltpu.VMEM)
    fields = [
        shape((N_MID, rows, LANES), F32),
        shape((N_MID, ROW_SLOTS + 2, WIDTH + 2, batch, LANES), BF16),
        shape((N_MID, rows, LANES), F32),
        shape((N_MID, rows, LANES), BF16),
        shape((N_IN, rows, LANES), F32),
    ]
    stats = [shape((2 * n, LANES), F32) for n in (N_MID, N_MID, N_IN)]
    if top:
        last = [shape((N_IN, batch, LANES), F32)]
        last_specs = [vmem]
    else:
        last = [shape((N_IN, rows, LANES), F32), shape((N_IN, rows, LANES), BF16)]
        last_specs = [any_space] * 2
    big = lambda s: pltpu.VMEM(s.shape, s.dtype)
    total = slots_total(devices)
    dma = pltpu.SemaphoreType.DMA
    ins = [xb] + ([xf] if top else []) + list(weights) + [params, live, count]
    return pl.pallas_call(
        functools.partial(forward_kernel, devices, top, total_count),
        out_shape=fields + stats + last,
        in_specs=[any_space] * (len(ins) - 3) + [vmem] * 3,
        out_specs=[any_space] * 5 + [vmem] * 3 + last_specs,
        scratch_shapes=[big(a) for a in ins[:-3]]
        + [big(s) for s in fields]
        + ([] if top else [big(s) for s in last])
        + [
            pltpu.VMEM((2 * N_MID, LANES), F32),
            pltpu.VMEM((2 * N_IN, LANES), F32),
            pltpu.VMEM((total, 2 * N_MID, LANES), F32),
            pltpu.VMEM((total, 2 * N_MID, LANES), F32),
            pltpu.VMEM((total, 2 * N_IN, LANES), F32),
            dma((5,)),
            dma((8,)),
            dma((3, total)),
            dma((3, total)),
            dma((2,)),
        ],
        compiler_params=pltpu.CompilerParams(
            collective_id=ident, has_side_effects=True, vmem_limit_bytes=60 * 2**20
        ),
    )(*ins)


def head_kernel(
    devices, area, pooled, head_h, bias, pick, point, own_weight, in_weight, hot, total,
    extra, gtop, gh_h,
    head, send_pool, recv_pool, low, logits_all, logits, g_low, gh, gt,
    in_sem, out_sem, send_sem, recv_sem,
):
    net = Net(devices)
    net.hello()
    load = pltpu.make_async_copy(head_h, head, in_sem)
    load.start()
    half = send_pool.shape[1]
    mine = pl.ds(pl.multiple_of(net.core * half, half), half)
    theirs = pl.ds(pl.multiple_of((1 - net.core) * half, half), half)
    for j in range(N_IN):
        send_pool[j] = pooled[j, theirs].astype(BF16)
    net.ready()
    sends = [remote(send_pool, recv_pool, send_sem.at[0], recv_sem.at[0], net.partner)]
    load.wait()
    landed(recv_pool, recv_sem.at[0])
    for j in range(N_IN):
        low[j] = ((pooled[j, mine] + recv_pool[j].astype(F32)) / area).astype(BF16)
    logits[...] = dot(lanes_of(low, 0, N_IN), lanes_of(head, 0, N_IN), 1, 1) + bias[0:1, :]
    logits_all[net.core, net.me] = logits[...].astype(BF16)
    at = 1
    for peer, slot in zip(net.near_peers, net.near_slots):
        ref = logits_all.at[net.core, net.me]
        sends.append(remote(ref, ref, send_sem.at[at], recv_sem.at[1 + net.near_at], peer))
        at += 1

    own = logits[...]
    keep = lax.broadcasted_iota(jnp.int32, own.shape, 1) < CLASSES
    peak = jnp.max(jnp.where(keep, own, -3.0e38), axis=1, keepdims=True)
    powers = jnp.where(keep, jnp.exp(jnp.where(keep, own - peak, 0.0)), 0.0)
    log_total = peak + jnp.log(jnp.sum(powers, axis=1, keepdims=True))
    softmax = jnp.where(keep, jnp.exp(jnp.where(keep, own - log_total, 0.0)), 0.0)
    picked = jnp.sum(own * hot[...], axis=1, keepdims=True)

    base = net.me - net.near_at
    for slot in net.near_slots:
        landed(logits_all.at[net.core, base + slot], recv_sem.at[1 + slot])
    group = logits_all.at[net.core, pl.ds(base, net.near)]
    for peer in net.far_peers:
        sends.append(
            remote(group, group, send_sem.at[at], recv_sem.at[1 + net.near + net.far_at], peer)
        )
        at += 1
    for slot in net.far_slots:
        landed(
            logits_all.at[net.core, pl.ds(slot * net.near, net.near)],
            recv_sem.at[1 + net.near + slot],
        )
    ref = logits_all.at[net.core]
    sends.append(
        remote(ref, ref, send_sem.at[at], recv_sem.at[1 + net.near + net.far], net.partner)
    )
    at += 1
    landed(logits_all.at[1 - net.core], recv_sem.at[1 + net.near + net.far])
    every = logits_all[...].reshape(-1, WIDE)
    gap = jnp.where(keep, own - dot(pick[...], every, 1, 0), 0.0)
    incoming = dot(point[...], every, 1, 0)
    weight = own_weight[:, 0:1]
    terms = weight * (
        log_total - picked + MATCH_WEIGHT * (jnp.sum(gap * gap, axis=1, keepdims=True) / CLASSES)
    )
    grad = (
        weight * (softmax - hot[...])
        + MATCH_WEIGHT
        * (2.0 / CLASSES)
        * (weight * gap - (incoming - in_weight[:, 0:1] * own))
    ) / total[0:1, 0:1]
    g_low[...] = jnp.where(keep, grad, 0.0).astype(BF16)
    bias_sum = jnp.sum(g_low[...].astype(F32), axis=0, keepdims=True)
    extra[...] = jnp.zeros(extra.shape, F32)
    for j in range(WIDE // LANES):
        extra[j : j + 1] = bias_sum[:, j * LANES : (j + 1) * LANES]
    extra[WIDE // LANES : WIDE // LANES + 1] = jnp.zeros((1, LANES), F32) + jnp.sum(
        terms, axis=0, keepdims=True
    )
    gt_view = gt.at[:, net.core]
    for j in range(N_IN):
        gt[j, net.core] = (dot(g_low[...], head[j], 1, 0) / area).astype(BF16)
    sends.append(
        remote(
            gt_view, gt_view, send_sem.at[at], recv_sem.at[2 + net.near + net.far], net.partner
        )
    )

    def outer(j, carry):
        gh[j] = dot(g_low[...], low[j], 0, 0)
        return carry

    lax.fori_loop(0, N_IN, outer, 0)
    store = pltpu.make_async_copy(gh, gh_h, out_sem)
    store.start()
    landed(gt.at[:, 1 - net.core], recv_sem.at[2 + net.near + net.far])
    for j in range(N_IN):
        gtop[j] = jnp.concatenate([gt[j, 0], gt[j, 1]], axis=0).astype(F32)
    store.wait()
    for copy in sends:
        copy.wait_send()


def head_step(devices, pooled, head, bias, pick, point, own_weight, in_weight, hot, total):
    batch = pooled.shape[1]
    half = batch // 2
    shape = jax.ShapeDtypeStruct
    any_space = pl.BlockSpec(memory_space=pl.ANY)
    vmem = pl.BlockSpec(memory_space=pltpu.VMEM)
    dma = pltpu.SemaphoreType.DMA
    count = 4 + slots_total(devices)
    return pl.pallas_call(
        functools.partial(head_kernel, devices, float(HEIGHT * WIDTH)),
        out_shape=[
            shape((16, LANES), F32),
            shape((N_IN, batch, LANES), F32),
            shape((N_IN, WIDE, LANES), F32),
        ],
        in_specs=[vmem, any_space] + [vmem] * 7,
        out_specs=[vmem, vmem, any_space],
        scratch_shapes=[
            pltpu.VMEM((N_IN, WIDE, LANES), BF16),
            pltpu.VMEM((N_IN, half, LANES), BF16),
            pltpu.VMEM((N_IN, half, LANES), BF16),
            pltpu.VMEM((N_IN, half, LANES), BF16),
            pltpu.VMEM((2, devices, half, WIDE), BF16),
            pltpu.VMEM((half, WIDE), F32),
            pltpu.VMEM((half, WIDE), BF16),
            pltpu.VMEM((N_IN, WIDE, LANES), F32),
            pltpu.VMEM((N_IN, 2, half, LANES), BF16),
            dma(()),
            dma(()),
            dma((count,)),
            dma((count,)),
        ],
        compiler_params=pltpu.CompilerParams(
            collective_id=5, has_side_effects=True, vmem_limit_bytes=60 * 2**20
        ),
    )(pooled, head, bias, pick, point, own_weight, in_weight, hot, total)


def backward_kernel(devices, top, total_count, *refs):
    refs = list(refs)
    take = lambda n: [refs.pop(0) for _ in range(n)]
    field_h, xb_h, zc_h, hb_h, hp_h, zb_h, za_h, wi_h, wm_h, wo_h = take(10)
    gtop, stat_a, stat_b, stat_c, params, live, extra = take(7)
    gi_h, gm_h, go_h = take(3)
    gout_h, = take(1) if top else [None]
    small, = take(1)
    field, xb, zc, hb, hp, zb, za, wi, wm, wo = take(10)
    gi, gm, go = take(3)
    ec, ep, ea, ub, ua = take(5)
    stage_m, stage_c, buf_a, buf_b, buf_c = take(5)
    in_sem, out_sem, send_sem, recv_sem, halo_sem = take(5)

    net = Net(devices)
    net.hello()
    loads = load_all(
        [
            (zc_h, zc), (field_h, field), (xb_h, xb), (wo_h, wo), (zb_h, zb), (hb_h, hb),
            (hp_h, hp), (wm_h, wm), (za_h, za), (wi_h, wi),
        ],
        in_sem,
    )
    clear_edges(ep, net.core)
    quarter = za.shape[1] // ROW_SLOTS
    batch = quarter // WIDTH
    stores = []
    sends = []

    def store(src, dst):
        copy = pltpu.make_async_copy(src, dst, out_sem.at[len(stores)])
        copy.start()
        stores.append(copy)

    def slope(y):
        sigma = half_tanh(y)
        return sigma * (1.0 + y * (1.0 - sigma))

    def row(ref, j):
        return ref[pl.ds(j, 1)]

    def totals(stage, bufs, which, small_at, n, fillers=()):
        total, copies = reduce_all(
            net, stage[...], bufs, send_sem.at[which], recv_sem.at[which], plain_sum, fillers=fillers
        )
        sends.extend(copies)
        small[small_at : small_at + 2 * n] = total[: 2 * n]
        return total

    loads[0].wait()
    loads[1].wait()
    if not top:
        loads[2].wait()

    def slab_c(j, carry):
        mean, scale = row(stat_c, j), row(stat_c, N_IN + j)
        gain, shift = row(params, 4 * N_MID + j), row(params, 4 * N_MID + N_IN + j)
        total = jnp.zeros((8, LANES), F32)
        crossed = jnp.zeros((8, LANES), F32)
        for q in range(4):
            rows = pl.ds(q * quarter, quarter)
            normed = (zc[j, rows] - mean) * scale
            if top:
                x = field[j, rows]
                g = jnp.concatenate([gtop[j]] * WIDTH, axis=0)
            else:
                x = xb[j, rows].astype(F32)
                g = field[j, rows]
            u = g * live[rows] * slope(normed * gain + shift + x)
            field[j, rows] = u
            total = total + column_sum(u)
            crossed = crossed + column_sum(u * normed)
        stage_c[pl.ds(j, 1)] = jnp.sum(crossed, axis=0, keepdims=True)
        stage_c[pl.ds(N_IN + j, 1)] = jnp.sum(total, axis=0, keepdims=True)
        return carry

    lax.fori_loop(0, N_IN, slab_c, 0)
    stage_c[2 * N_IN :] = extra[...]
    net.ready()
    total_c = totals(stage_c, buf_c, 2, 4 * N_MID, N_IN)
    small[4 * N_MID + 2 * N_IN :] = total_c[2 * N_IN :]

    def back_c(j, carry):
        mean, scale = row(stat_c, j), row(stat_c, N_IN + j)
        gain = row(params, 4 * N_MID + j)
        cross = row(small, 4 * N_MID + j) / total_count
        plain = row(small, 4 * N_MID + N_IN + j) / total_count
        for q in range(4):
            rows = pl.ds(q * quarter, quarter)
            normed = (zc[j, rows] - mean) * scale
            e = live[rows] * ((gain * scale) * (field[j, rows] - plain - normed * cross))
            ec[j, rows] = e.astype(BF16)
        return carry

    lax.fori_loop(0, N_IN, back_c, 0)
    loads[3].wait()
    product = dot(lanes_of(ec, 0, N_IN), lanes_of(wo, 0, N_IN), 1, 1)
    for j in range(N_MID):
        ub[j] = product[:, j * LANES : (j + 1) * LANES]
    loads[4].wait()

    def sums_of(u_ref, z_ref, stat, gain_at, stage):
        def slab(j, carry):
            mean, scale = row(stat, j), row(stat, N_MID + j)
            gain, shift = row(params, gain_at + j), row(params, gain_at + N_MID + j)
            total = jnp.zeros((8, LANES), F32)
            crossed = jnp.zeros((8, LANES), F32)
            for q in range(4):
                rows = pl.ds(q * quarter, quarter)
                normed = (z_ref[j, rows] - mean) * scale
                u = u_ref[j, rows] * live[rows] * slope(normed * gain + shift)
                u_ref[j, rows] = u
                total = total + column_sum(u)
                crossed = crossed + column_sum(u * normed)
            stage[pl.ds(j, 1)] = jnp.sum(crossed, axis=0, keepdims=True)
            stage[pl.ds(N_MID + j, 1)] = jnp.sum(total, axis=0, keepdims=True)
            return carry

        lax.fori_loop(0, N_MID, slab, 0)

    def back_of(u_ref, z_ref, stat, gain_at, small_at, j, rows):
        normed = (z_ref[j, rows] - row(stat, j)) * row(stat, N_MID + j)
        cross = row(small, small_at + j) / total_count
        plain = row(small, small_at + N_MID + j) / total_count
        factor = row(params, gain_at + j) * row(stat, N_MID + j)
        return (live[rows] * (factor * (u_ref[j, rows] - plain - normed * cross))).astype(BF16)

    sums_of(ub, zb, stat_b, 2 * N_MID, stage_m)
    loads[5].wait()

    def grad_out(first, last):
        def group(g, carry):
            part = dot(lanes_of(hb, 0, N_MID), lanes_of(ec, g * N_MID, N_MID), 0, 0)
            for j in range(N_MID):
                go[g * N_MID + j] = part[:, j * LANES : (j + 1) * LANES].astype(BF16)
            return carry

        return lambda: lax.fori_loop(first, last, group, 0)

    groups = N_IN // N_MID
    totals(
        stage_m, buf_b, 1, 2 * N_MID, N_MID,
        [grad_out(0, 1), grad_out(1, groups - 1), grad_out(groups - 1, groups)],
    )
    store(go, go_h)

    def fill_b(slot):
        rows = pl.ds(slot * quarter, quarter)

        def slab(j, carry):
            e = back_of(ub, zb, stat_b, 2 * N_MID, 2 * N_MID, j, rows)
            ep[j, pl.ds(slot + 1, 1), pl.ds(1, WIDTH)] = e.reshape(1, WIDTH, batch, LANES)
            return carry

        lax.fori_loop(0, N_MID, slab, 0)

    sends.append(
        edge_first(net, fill_b, lambda: send_edge(ep, net, halo_sem.at[0], halo_sem.at[1]))
    )
    loads[6].wait()
    loads[7].wait()
    ua[...] = jnp.zeros(ua.shape, F32)

    def grad_mid(first, last):
        def one(t, carry):
            part = dot(window(hp, t // 3, lax.rem(t, 3)), window(ep, 1, 1), 0, 0)
            k = pl.ds(pl.multiple_of(t * M, M), M)
            for j in range(N_MID):
                gm[j, k] = part[:, j * LANES : (j + 1) * LANES].astype(BF16)
            return carry

        return lambda: lax.fori_loop(first, last, one, 0)

    def tap(t):
        k = pl.ds(pl.multiple_of(t * M, M), M)
        part = dot(
            window(ep, 2 - t // 3, 2 - lax.rem(t, 3)),
            jnp.concatenate([wm[j, k] for j in range(N_MID)], axis=-1),
            1,
            1,
        )
        for j in range(N_MID):
            ua[j] = ua[j] + part[:, j * LANES : (j + 1) * LANES]

    def middle(i, carry):
        tap(i + 3)
        return carry

    def outer(i, carry):
        tap(jnp.where(i < 3, i, i + 3))
        return carry

    lax.fori_loop(0, 3, middle, 0)
    edge_landed(ep, net, halo_sem.at[1])
    lax.fori_loop(0, 6, outer, 0)
    loads[8].wait()
    sums_of(ua, za, stat_a, 0, stage_m)
    totals(
        stage_m, buf_a, 0, 0, N_MID, [grad_mid(0, 2), grad_mid(2, 5), grad_mid(5, 9)]
    )
    store(gm, gm_h)

    def fill_a(j, carry):
        for q in range(4):
            rows = pl.ds(q * quarter, quarter)
            ea[j, rows] = back_of(ua, za, stat_a, 0, 0, j, rows)
        return carry

    lax.fori_loop(0, N_MID, fill_a, 0)
    loads[9].wait()
    if top:
        loads[2].wait()

        def grad_field(g, carry):
            k = pl.ds(pl.multiple_of(g * M, M), M)
            part = dot(
                lanes_of(ea, 0, N_MID),
                jnp.concatenate([wi[j, k] for j in range(N_MID)], axis=-1),
                1,
                1,
            )
            for j in range(N_MID):
                at = g * N_MID + j
                field[at] = field[at] + part[:, j * LANES : (j + 1) * LANES]
            return carry

        lax.fori_loop(0, groups, grad_field, 0)
        store(field, gout_h)

    def grad_in(g, carry):
        part = dot(lanes_of(xb, g * N_MID, N_MID), lanes_of(ea, 0, N_MID), 0, 0)
        k = pl.ds(pl.multiple_of(g * M, M), M)
        for j in range(N_MID):
            gi[j, k] = part[:, j * LANES : (j + 1) * LANES].astype(BF16)
        return carry

    lax.fori_loop(0, groups, grad_in, 0)
    store(gi, gi_h)
    for copy in stores:
        copy.wait()
    for copy in sends:
        copy.wait_send()


def backward_layer(
    devices, top, total_count, ident, field, xb, kept, weights, gtop, params, live, extra
):
    za, hp, zb, hb, zc, stat_a, stat_b, stat_c = kept
    wi, wm, wo = weights
    shape = jax.ShapeDtypeStruct
    any_space = pl.BlockSpec(memory_space=pl.ANY)
    vmem = pl.BlockSpec(memory_space=pltpu.VMEM)
    dma = pltpu.SemaphoreType.DMA
    total = slots_total(devices)
    rows = xb.shape[1]
    big = lambda s: pltpu.VMEM(s.shape, s.dtype)
    ins = [field, xb, zc, hb, hp, zb, za, wi, wm, wo]
    small_ins = [gtop, stat_a, stat_b, stat_c, params, live, extra]
    grads = [shape(w.shape, BF16) for w in weights]
    more = [shape(field.shape, F32)] if top else []
    small_rows = 4 * N_MID + 2 * N_IN + extra.shape[0]
    return pl.pallas_call(
        functools.partial(backward_kernel, devices, top, total_count),
        out_shape=grads + more + [shape((small_rows, LANES), F32)],
        in_specs=[any_space] * len(ins) + [vmem] * len(small_ins),
        out_specs=[any_space] * (3 + len(more)) + [vmem],
        scratch_shapes=[big(a) for a in ins]
        + [big(g) for g in grads]
        + [
            pltpu.VMEM((N_IN, rows, LANES), BF16),
            pltpu.VMEM(hp.shape, BF16),
            pltpu.VMEM((N_MID, rows, LANES), BF16),
            pltpu.VMEM((N_MID, rows, LANES), F32),
            pltpu.VMEM((N_MID, rows, LANES), F32),
            pltpu.VMEM((2 * N_MID, LANES), F32),
            pltpu.VMEM((2 * N_IN + extra.shape[0], LANES), F32),
            pltpu.VMEM((total, 2 * N_MID, LANES), F32),
            pltpu.VMEM((total, 2 * N_MID, LANES), F32),
            pltpu.VMEM((total, 2 * N_IN + extra.shape[0], LANES), F32),
            dma((10,)),
            dma((4,)),
            dma((3, total)),
            dma((3, total)),
            dma((2,)),
        ],
        compiler_params=pltpu.CompilerParams(
            collective_id=ident, has_side_effects=True, vmem_limit_bytes=60 * 2**20
        ),
    )(*ins, *small_ins)


def split_two(v):
    high = v.astype(BF16)
    return high, (v - high.astype(F32)).astype(BF16)


def shampoo_kernel(t_ref, m_ref, s_ref, r_ref, g_ref, s_new, m_new, flat, turn):
    group = t_ref.shape[1]
    left = pl.ds(0, BLOCK)
    right = pl.ds(BLOCK, BLOCK)
    for k in range(group):
        rows = pl.ds(k * HALF, HALF)
        parts = [t_ref[h, k].astype(F32) for h in range(2)]
        for h in range(2):
            flat[h, rows] = parts[h]
        tile = jnp.concatenate([p[:, :BLOCK] for p in parts] + [p[:, BLOCK:] for p in parts], axis=0)
        low = tile.astype(BF16)
        old = s_ref[k]
        roots = r_ref[k]
        high, rest = split_two(roots[:, :BLOCK])
        both = dot(jnp.concatenate([high, rest, tile.T.astype(BF16)], axis=0), low, 1, 0)
        s_new[k] = DECAY_STATS * old + (1.0 - DECAY_STATS) * jnp.concatenate(
            [dot(low, low, 1, 1), both[2 * BLOCK :]], axis=1
        )
        turned = both[:BLOCK] + both[BLOCK : 2 * BLOCK]
        t_high, t_rest = split_two(turned)
        high, rest = split_two(roots)
        wide = jnp.concatenate([high[:, BLOCK:], rest[:, BLOCK:]], axis=1)
        both = dot(jnp.concatenate([t_high, t_rest], axis=0), wide, 1, 0)
        turned = both[:BLOCK, :BLOCK] + both[BLOCK:, :BLOCK] + both[:BLOCK, BLOCK:]
        for h in range(2):
            turn[h, rows] = jnp.concatenate(
                [
                    turned[h * HALF : (h + 1) * HALF],
                    turned[2 * HALF + h * HALF : 2 * HALF + (h + 1) * HALF],
                ],
                axis=1,
            )
    for m in range(2 * HALF // 2):
        h, r = m // (HALF // 2), 2 * (m % (HALF // 2))
        grads = [flat[h, pl.ds(r + i, group, stride=HALF)] for i in range(2)]
        steps = [turn[h, pl.ds(r + i, group, stride=HALF)] for i in range(2)]
        for p in range(2):
            lanes = pl.ds(p * (BLOCK * BLOCK // 2) + m * LANES, LANES)
            cut = slice(p * BLOCK, (p + 1) * BLOCK)
            g_ref[:, lanes] = jnp.concatenate([v[:, cut] for v in grads], axis=1)
            m_new[:, lanes] = m_ref[:, lanes] - RATE_SHAMPOO * jnp.concatenate(
                [v[:, cut] for v in steps], axis=1
            )


def shampoo(tiles, master, statistics, root_pairs):
    owned = master.shape[0]
    group = 8
    whole = (owned + group - 1) // group
    shape = jax.ShapeDtypeStruct
    flat_spec = pl.BlockSpec((group, BLOCK * BLOCK), lambda i: (i, 0))
    pair_spec = pl.BlockSpec((group, BLOCK, 2 * BLOCK), lambda i: (i, 0, 0))
    return pl.pallas_call(
        shampoo_kernel,
        grid=(whole,),
        out_shape=[
            shape(master.shape, F32),
            shape(statistics.shape, F32),
            shape(master.shape, F32),
        ],
        in_specs=[
            pl.BlockSpec((2, group, HALF, LANES), lambda i: (0, i, 0, 0)),
            flat_spec,
            pair_spec,
            pair_spec,
        ],
        out_specs=[flat_spec, pair_spec, flat_spec],
        scratch_shapes=[pltpu.VMEM((2, group * HALF, LANES), F32)] * 2,
        compiler_params=pltpu.CompilerParams(vmem_limit_bytes=32 * 2**20),
    )(tiles, master, statistics, root_pairs)


def adamw(values_old, gradient, moment_one, moment_two, step_rate):
    one_new = BETA_FIRST * moment_one + (1.0 - BETA_FIRST) * gradient
    two_new = BETA_SECOND * moment_two + (1.0 - BETA_SECOND) * gradient * gradient
    fixed_one = 1.0 - BETA_FIRST**STEP
    fixed_two = 1.0 - BETA_SECOND**STEP
    update = one_new / fixed_one / (jnp.sqrt(two_new / fixed_two) + EPS_ADAM)
    return (one_new, two_new, values_old - step_rate * (update + DECAY_WEIGHT * values_old))


def body(
    images,
    row_split,
    labels,
    partners,
    image_weight,
    owner_slot,
    conv_master,
    conv_stats,
    conv_roots,
    head_master,
    head_moment_one,
    head_moment_two,
    small_params,
    small_moment_one,
    small_moment_two,
):
    devices = lax.axis_size("dp")
    core_index = lax.axis_index("rows")
    batch_size = images.shape[0]
    half_batch = batch_size // 2
    slot_count = images.shape[1]
    total_images = partners.shape[0]
    live_count = float(total_images * HEIGHT * WIDTH)
    owned = conv_master.shape[0]
    head_rows = head_master.shape[0]

    halves = (
        conv_master.astype(BF16)
        .reshape(owned, 2, 2, HALF, BLOCK)
        .transpose(2, 0, 3, 1, 4)
        .reshape(2, owned, HALF, LANES)
    )
    slot_index = (owner_slot // owned) * (2 * owned) + owner_slot % owned
    weights = list(assemble(gather_blocks(halves, devices), slot_index))
    head_t = jnp.pad(head_master.T.astype(BF16), ((0, WIDE - CLASSES), (0, 0)))
    head_t, weights[0] = lax.optimization_barrier((head_t, weights[0]))
    head_all = lax.all_gather(head_t, "dp", axis=0)
    if head_rows != LANES:
        head_all = head_all.transpose(1, 0, 2).reshape(WIDE, N_IN, LANES).transpose(1, 0, 2)

    slot_ids = core_index * slot_count + jnp.arange(slot_count, dtype=jnp.int32)
    first_live = (ROW_SLOTS - row_split)[:, None]
    live = (slot_ids[None, :] >= first_live) & (slot_ids[None, :] < first_live + HEIGHT)
    own_count = jnp.sum(live.astype(F32)) * WIDTH
    counts = jnp.broadcast_to(own_count, (8, LANES))
    rows = slot_count * WIDTH * batch_size
    live_rows = jnp.broadcast_to(
        live.T.astype(F32)[:, None, :, None], (slot_count, WIDTH, batch_size, LANES)
    ).reshape(rows, LANES)
    first = (
        jnp.where(live[:, :, None, None], images, 0)
        .reshape(batch_size, slot_count, WIDTH, N_IN, LANES)
        .transpose(3, 1, 2, 0, 4)
        .reshape(N_IN, rows, LANES)
    )
    stride = 4 * M + 2 * C
    params = [
        small_params[at * stride : (at + 1) * stride].reshape(-1, LANES) for at in range(LAYERS)
    ]
    bias = jnp.broadcast_to(
        jnp.pad(small_params[LAYERS * stride :], (0, WIDE - CLASSES)), (8, WIDE)
    )

    kept = []
    field, low = None, first
    lows = []
    for at in range(LAYERS):
        last = at == LAYERS - 1
        lows.append(low)
        out = forward_layer(
            devices,
            at > 0,
            live_count,
            3 + at,
            low,
            field,
            weights[3 * at : 3 * at + 3],
            params[at],
            live_rows,
            counts,
        )
        kept.append(out[:8])
        if last:
            pooled = out[8]
        else:
            field, low = out[8], out[9]

    def by_core(v):
        return v.reshape(devices, 2, half_batch).transpose(1, 0, 2).reshape(-1)

    weight_f = image_weight.astype(F32)
    weight_total = jnp.sum(weight_f)
    own_start = (lax.axis_index("dp") * 2 + core_index) * half_batch
    own_ids = own_start + jnp.arange(half_batch, dtype=jnp.int32)
    own_weight = lax.dynamic_slice_in_dim(weight_f, own_start, half_batch)
    own_partner = lax.dynamic_slice_in_dim(partners, own_start, half_batch)
    own_label = lax.dynamic_slice_in_dim(labels, core_index * half_batch, half_batch)
    ids = by_core(jnp.arange(total_images, dtype=jnp.int32))
    pick = (own_partner[:, None] == ids[None, :]).astype(BF16)
    point = (by_core(partners)[None, :] == own_ids[:, None]).astype(F32) * by_core(weight_f)[None, :]
    in_weight = jnp.sum(point, axis=1)
    hot = (own_label[:, None] == jnp.arange(WIDE, dtype=jnp.int32)[None, :]).astype(F32)
    spread = lambda v: jnp.broadcast_to(v[:, None], (half_batch, LANES))
    extra, g_top, grad_head = head_step(
        devices,
        pooled,
        head_all,
        bias,
        pick,
        point.astype(BF16),
        spread(own_weight),
        spread(in_weight),
        hot,
        jnp.broadcast_to(weight_total, (8, LANES)),
    )
    if head_rows != LANES:
        grad_head = (
            grad_head.transpose(1, 0, 2).reshape(WIDE, devices, head_rows).transpose(1, 0, 2)
        )
    owned_head = lax.psum_scatter(grad_head, "dp", scatter_dimension=0, tiled=False)
    head_grad = lax.psum(owned_head.astype(BF16), "rows").astype(F32)[:CLASSES].T

    no_extra = jnp.zeros_like(extra)
    top = backward_layer(
        devices, True, live_count, 6, field, lows[1], kept[1], weights[3:], g_top, params[1],
        live_rows, extra,
    )
    bottom = backward_layer(
        devices, False, live_count, 7, top[3], lows[0], kept[0], weights[:3], no_extra, params[0],
        live_rows, no_extra,
    )
    small_top, small_bottom = top[4], bottom[3]
    slotted = to_slots(list(bottom[:3]) + list(top[:3]), slot_index, devices)
    tiles = scatter_blocks(slotted)
    conv_grad, stats_new, master_new = shampoo(tiles, conv_master, conv_stats, conv_roots)
    head_one, head_two, head_new = adamw(
        head_master, head_grad, head_moment_one, head_moment_two, RATE_HEAD
    )
    layer_rows = stride // LANES
    grad_bias = small_top[layer_rows : layer_rows + WIDE // LANES].reshape(-1)[:CLASSES]
    loss_sum = small_top[layer_rows + WIDE // LANES, 0]
    grad_small = jnp.concatenate(
        [small_bottom[:layer_rows].reshape(-1), small_top[:layer_rows].reshape(-1), grad_bias]
    )
    small_one, small_two, small_new = adamw(
        small_params, grad_small, small_moment_one, small_moment_two, RATE_SMALL
    )
    return (
        loss_sum,
        weight_total,
        conv_grad,
        stats_new,
        master_new,
        master_new.astype(BF16),
        head_one,
        head_two,
        head_new,
        head_new.astype(BF16),
        small_one,
        small_two,
        small_new,
    )


def solution(mesh):
    in_specs = (
        P("dp", "rows", None, None),
        P("dp"),
        P("dp"),
        P(),
        P(),
        P(),
        P("dp", None),
        P("dp", None, None),
        P("dp", None, None),
        P("dp", None),
        P("dp", None),
        P("dp", None),
        P(),
        P(),
        P(),
    )
    out_specs = (
        P(),
        P(),
        P("dp", None),
        P("dp", None, None),
        P("dp", None),
        P("dp", None),
        P("dp", None),
        P("dp", None),
        P("dp", None),
        P("dp", None),
        P(),
        P(),
        P(),
    )
    return jax.shard_map(body, mesh=mesh, in_specs=in_specs, out_specs=out_specs, check_vma=False)
```

```python
import functools

import jax
import jax.numpy as jnp
from jax import lax
from jax.experimental import pallas as pl
from jax.experimental.pallas import tpu as pltpu
from jax.sharding import PartitionSpec as P

C = 2048
M = 512
CLASSES = 1000
HEIGHT = 7
WIDTH = 7
ROW_SLOTS = 4
LAYERS = 2
BLOCK = 64
STEP = 5


EPS_NORM = 1e-05
MATCH_WEIGHT = 4.0
DECAY_STATS = 0.5
RATE_SHAMPOO = 0.15
RATE_HEAD = 0.03
RATE_SMALL = 0.2
BETA_FIRST = 0.9
BETA_SECOND = 0.95
EPS_ADAM = 1e-08
DECAY_WEIGHT = 0.01


C = 2048
M = 512
CLASSES = 1000
HEIGHT = 7
WIDTH = 7
ROW_SLOTS = 4
LAYERS = 2
BLOCK = 64
STEP = 5


EPS_NORM = 1e-05
MATCH_WEIGHT = 4.0
DECAY_STATS = 0.5
RATE_SHAMPOO = 0.15
RATE_HEAD = 0.03
RATE_SMALL = 0.2
BETA_FIRST = 0.9
BETA_SECOND = 0.95
EPS_ADAM = 1e-08
DECAY_WEIGHT = 0.01


MESH_IDS = pl.DeviceIdType.MESH
HALF = 16
LANES = 128


def bit_split(devices):
    bits = devices.bit_length() - 1
    first = bits // 3
    second = (bits - first) // 2
    return first, second, bits - first - second


def greet(peers):
    barrier = pltpu.get_barrier_semaphore()
    for peer in peers:
        pl.semaphore_signal(barrier, inc=1, device_id=peer, device_id_type=MESH_IDS)
    pl.semaphore_wait(barrier, len(peers))


def axis_masks(devices, core):
    first, second, third = bit_split(devices)
    low = [m for m in range(1, 1 << first)]
    high = [m << first for m in range(1, 1 << second)]
    if first == second:
        one = [jnp.where(core == 0, h, l) for h, l in zip(high, low)]
        two = [jnp.where(core == 0, l, h) for h, l in zip(high, low)]
    else:
        one, two = low, high
    far = [m << (first + second) for m in range(1, 1 << third)]
    return [0] + one, [0] + two, [0] + far


def chunks_of(count):
    for parts in (8, 4, 2):
        if count % parts == 0:
            return parts
    return 1


def slab_shape(shape):
    return (shape[1] // LANES, shape[0], LANES)


def matrix_list():
    shapes = []
    for _ in range(LAYERS):
        shapes += [(C, M), (9 * M, M), (M, C)]
    return shapes


def bring_kernel(devices, parts, idx_ref, m_ref, *refs):
    shapes = matrix_list()
    n = len(shapes)
    outs, bufs, (g_ref, stage, send_sem, recv_sem, out_sem) = refs[:n], refs[n : 2 * n], refs[2 * n :]
    me = lax.axis_index("dp")
    core = lax.axis_index("rows")
    count = m_ref.shape[0]
    per = count // parts
    mid, last, far = axis_masks(devices, core)
    partner = (me, 1 - core)
    peers = [(me ^ m, core) for m in far[1:] + mid[1:] + last[1:]] + [partner]
    barrier = pltpu.get_barrier_semaphore()
    for peer in peers:
        pl.semaphore_signal(barrier, inc=1, device_id=peer, device_id_type=MESH_IDS)

    def spread(first, rows):
        for m in range(HALF):
            one = m_ref[pl.ds(first, rows), m * LANES : (m + 1) * LANES]
            two = m_ref[pl.ds(first, rows), (HALF + m) * LANES : (HALF + m + 1) * LANES]
            h, r = m // (HALF // 2), 2 * (m % (HALF // 2))
            for i in range(2):
                cut = slice(i * BLOCK, (i + 1) * BLOCK)
                stage[h, pl.ds(first * HALF + r + i, rows, stride=HALF)] = jnp.concatenate(
                    [one[:, cut], two[:, cut]], axis=1
                )

    def group(i, carry):
        spread(pl.multiple_of(i * 8, 8), 8)
        return carry

    lax.fori_loop(0, count // 8, group, 0)
    if count % 8:
        spread(count // 8 * 8, count % 8)

    def round_one(k, carry):
        for h in range(2):
            rows = pl.ds(pl.multiple_of(k * HALF, HALF), HALF)
            g_ref[(me * 2 + h) * count + k] = stage[h, rows].astype(jnp.bfloat16)
        return carry

    lax.fori_loop(0, count, round_one, 0)
    pl.semaphore_wait(barrier, len(peers))
    sent = []

    def piece(owner, half, part):
        return g_ref.at[pl.ds((owner * 2 + half) * count + part * per, per)]

    def send(owner, part, device):
        copy = pltpu.make_async_remote_copy(
            src_ref=piece(owner, core, part),
            dst_ref=piece(owner, core, part),
            send_sem=send_sem.at[len(sent)],
            recv_sem=recv_sem.at[owner, core, part],
            device_id=device,
            device_id_type=MESH_IDS,
        )
        copy.start()
        sent.append(copy)

    def arrived(owner, half, part):
        ref = piece(owner, half, part)
        pltpu.make_async_copy(ref, ref, recv_sem.at[owner, half, part]).wait()

    def onward(owner, part, masks):
        arrived(owner, core, part)
        for m in masks:
            send(owner, part, (me ^ m, core))
        send(owner, part, partner)

    early = parts - parts // 4
    for part in range(parts):
        order = far[1:] + last[1:] + mid[1:] if part < early else mid[1:] + far[1:] + last[1:]
        for m in order:
            send(me, part, (me ^ m, core))
    for tick in range(parts + 2):
        part = tick
        if part < parts:
            if part < early:
                for z in far[1:]:
                    onward(me ^ z, part, last[1:] + mid[1:])
            else:
                for m in mid[1:]:
                    onward(me ^ m, part, far[1:] + last[1:])
        part = tick - 1
        if 0 <= part < parts:
            if part < early:
                for m in mid[1:]:
                    for z in far:
                        onward(me ^ m ^ z, part, last[1:])
            else:
                for z in far[1:]:
                    onward(me ^ z, part, last[1:])
                for z in far[1:]:
                    for m in mid[1:]:
                        onward(me ^ z ^ m, part, last[1:])
        part = tick - 2
        if 0 <= part < parts:
            for q in last[1:]:
                for z in far:
                    for m in mid:
                        onward(me ^ q ^ z ^ m, part, [])
    for step in range(1, devices):
        for part in range(parts):
            arrived(me ^ step, 1 - core, part)

    base = 0
    copies = []
    for at, (rows, cols) in enumerate(shapes):
        pairs = cols // LANES
        buf = bufs[at]

        def strip(r, carry, base=base, pairs=pairs, buf=buf):
            for m in range(pairs):
                even = idx_ref[base + r * (2 * pairs) + 2 * m]
                odd = idx_ref[base + r * (2 * pairs) + 2 * m + 1]
                for h in range(2):
                    e = g_ref[even + h * count]
                    o = g_ref[odd + h * count]
                    buf[m, pl.ds(r * BLOCK + h * HALF, HALF)] = jnp.concatenate(
                        [e[:, :BLOCK], o[:, :BLOCK]], axis=1
                    )
                    buf[m, pl.ds(r * BLOCK + 2 * HALF + h * HALF, HALF)] = jnp.concatenate(
                        [e[:, BLOCK:], o[:, BLOCK:]], axis=1
                    )
            return carry

        lax.fori_loop(0, rows // BLOCK, strip, 0, unroll=8 // (pairs // 4))
        copy = pltpu.make_async_copy(buf, outs[at], out_sem.at[at])
        copy.start()
        copies.append(copy)
        base += (rows // BLOCK) * (cols // BLOCK)
    for copy in copies:
        copy.wait()
    for copy in sent:
        copy.wait_send()


def bring_weights(master, index, devices):
    count = master.shape[0]
    parts = chunks_of(count)
    shapes = [slab_shape(s) for s in matrix_list()]
    dma = pltpu.SemaphoreType.DMA
    return pl.pallas_call(
        functools.partial(bring_kernel, devices, parts),
        out_shape=[jax.ShapeDtypeStruct(s, jnp.bfloat16) for s in shapes],
        in_specs=[
            pl.BlockSpec(memory_space=pltpu.SMEM),
            pl.BlockSpec(memory_space=pltpu.VMEM),
        ],
        out_specs=[pl.BlockSpec(memory_space=pl.ANY)] * len(shapes),
        scratch_shapes=[pltpu.VMEM(s, jnp.bfloat16) for s in shapes]
        + [
            pltpu.VMEM((devices * 2 * count, HALF, LANES), jnp.bfloat16),
            pltpu.VMEM((2, count * HALF, LANES), jnp.float32),
            dma((3 * devices * parts,)),
            dma((devices, 2, parts)),
            dma((len(shapes),)),
        ],
        compiler_params=pltpu.CompilerParams(
            collective_id=1, has_side_effects=True, vmem_limit_bytes=56 * 2**20
        ),
    )(index, master)


def deliver_kernel(
    devices, spans, at_ref, odd_ref, head_h, *refs
):
    n = len(matrix_list())
    grads, refs = refs[:n], refs[n:]
    (o_ref, pool, acc, land_last, land_mid, land_far, final) = refs[:7]
    (in_sem, send_sem, last_recv, mid_recv, far_recv, end_send, end_recv, out_sem) = refs[7:]
    me = lax.axis_index("dp")
    core = lax.axis_index("rows")
    count = at_ref.shape[0] // devices
    mid, last, far = axis_masks(devices, core)
    partner = (me, 1 - core)
    peers = [(me ^ m, core) for m in far[1:] + mid[1:] + last[1:]] + [partner]
    barrier = pltpu.get_barrier_semaphore()
    for peer in peers:
        pl.semaphore_signal(barrier, inc=1, device_id=peer, device_id_type=MESH_IDS)
    head = pltpu.make_async_copy(
        head_h, acc.at[:, pl.ds(count, head_h.shape[1])], in_sem.at[n]
    )
    head.start()
    loads = []
    start = 0
    for i, grad in enumerate(grads):
        load = pltpu.make_async_copy(grad, pool.at[pl.ds(start, grad.shape[0])], in_sem.at[i])
        load.start()
        loads.append(load)
        start += grad.shape[0]
    pl.semaphore_wait(barrier, len(peers))
    head.wait()
    sent = []

    def send(owner, span, part, land, sems, at, device):
        copy = pltpu.make_async_remote_copy(
            src_ref=acc.at[owner, span],
            dst_ref=land.at[at, span],
            send_sem=send_sem.at[len(sent)],
            recv_sem=sems.at[at, part],
            device_id=device,
            device_id_type=MESH_IDS,
        )
        copy.start()
        sent.append(copy)

    def arrived(land, sems, at, span, part):
        ref = land.at[at, span]
        pltpu.make_async_copy(ref, ref, sems.at[at, part]).wait()

    def fill(first, size):
        def owner_step(owner, carry):
            def block(k, inner):
                slot = owner * count + first + k
                q = at_ref[slot]
                top = pool[q]
                low = pool[q + 1]
                even = jnp.concatenate([top[:, :BLOCK], low[:, :BLOCK]], axis=1)
                odd = jnp.concatenate([top[:, BLOCK:], low[:, BLOCK:]], axis=1)
                acc[owner, first + k] = jnp.where(odd_ref[slot] == 1, odd, even)
                return inner

            return lax.fori_loop(0, size, block, carry, unroll=True)

        lax.fori_loop(0, devices, owner_step, 0)

    def add(owners, lands, first, size):
        def step(i, carry):
            at = first + i
            for owner, (land, j) in zip(owners, lands):
                acc[owner, at] = (
                    acc[owner, at].astype(jnp.float32) + land[j, at].astype(jnp.float32)
                ).astype(jnp.bfloat16)
            return carry

        lax.fori_loop(0, size, step, 0)

    ends = []
    parts = len(spans)
    for tick in range(parts + 3):
        part = tick
        if part < parts:
            first, size = spans[part]
            span = pl.ds(first, size)
            if part == 1:
                for load in loads:
                    load.wait()
            if part > 0:
                fill(first, size)
            at = 0
            for q in last[1:]:
                for m in mid[::-1]:
                    for z in far[::-1]:
                        send(
                            me ^ q ^ m ^ z, span, part, land_last, last_recv, at, (me ^ q, core)
                        )
                        at += 1
        part = tick - 1
        if 0 <= part < parts:
            first, size = spans[part]
            span = pl.ds(first, size)
            owners, lands = [], []
            per_q = len(mid) * len(far)
            for j in range(len(last) - 1):
                for i, (m, z) in enumerate([(m, z) for m in mid[::-1] for z in far[::-1]]):
                    arrived(land_last, last_recv, j * per_q + i, span, part)
                    owners.append(me ^ m ^ z)
                    lands.append((land_last, j * per_q + i))
            add(owners, lands, first, size)
            at = 0
            for m in mid[1:]:
                for z in far[::-1]:
                    send(me ^ m ^ z, span, part, land_mid, mid_recv, at, (me ^ m, core))
                    at += 1
        part = tick - 2
        if 0 <= part < parts:
            first, size = spans[part]
            span = pl.ds(first, size)
            owners, lands = [], []
            for j in range(len(mid) - 1):
                for i, z in enumerate(far[::-1]):
                    at = j * len(far) + i
                    arrived(land_mid, mid_recv, at, span, part)
                    owners.append(me ^ z)
                    lands.append((land_mid, at))
            add(owners, lands, first, size)
            for at, z in enumerate(far[1:]):
                send(me ^ z, span, part, land_far, far_recv, at, (me ^ z, core))
        part = tick - 3
        if 0 <= part < parts:
            first, size = spans[part]
            span = pl.ds(first, size)
            for at in range(len(far) - 1):
                arrived(land_far, far_recv, at, span, part)

            def finish(i, carry, first=first):
                at = first + i
                total = acc[me, at].astype(jnp.float32)
                for j in range(len(far) - 1):
                    total = total + land_far[j, at].astype(jnp.float32)
                final[core, at] = total.astype(jnp.bfloat16)
                return carry

            lax.fori_loop(0, size, finish, 0)
            copy = pltpu.make_async_remote_copy(
                src_ref=final.at[core, span],
                dst_ref=final.at[core, span],
                send_sem=end_send.at[part],
                recv_sem=end_recv.at[part],
                device_id=partner,
                device_id_type=MESH_IDS,
            )
            copy.start()
            ends.append(copy)
    for part, (first, size) in enumerate(spans):
        ref = final.at[1 - core, pl.ds(first, size)]
        pltpu.make_async_copy(ref, ref, end_recv.at[part]).wait()
    store = pltpu.make_async_copy(final, o_ref, out_sem)
    store.start()
    for copy in sent + ends:
        copy.wait_send()
    store.wait()


def deliver_blocks(grads, head, at, odd, devices):
    count = at.shape[0] // devices
    more = head.shape[1]
    parts = chunks_of(count)
    per = count // parts
    spans = [(count, more)] + [(i * per, per) for i in range(parts)]
    first, second, third = bit_split(devices)
    n_mid, n_last, n_far = 1 << first, 1 << second, 1 << third
    tile = (count + more, HALF, LANES)
    dma = pltpu.SemaphoreType.DMA
    lands = [(n_last - 1) * n_mid * n_far, (n_mid - 1) * n_far, n_far - 1]
    grads = [g.reshape(-1, HALF, LANES) for g in grads]
    any_space = pl.BlockSpec(memory_space=pl.ANY)
    steps = len(spans)
    return pl.pallas_call(
        functools.partial(deliver_kernel, devices, spans),
        out_shape=jax.ShapeDtypeStruct((2,) + tile, jnp.bfloat16),
        in_specs=[pl.BlockSpec(memory_space=pltpu.SMEM)] * 2 + [any_space] * (1 + len(grads)),
        out_specs=any_space,
        scratch_shapes=[
            pltpu.VMEM((sum(g.shape[0] for g in grads), HALF, LANES), jnp.bfloat16),
            pltpu.VMEM((devices,) + tile, jnp.bfloat16),
        ]
        + [pltpu.VMEM((k,) + tile, jnp.bfloat16) for k in lands]
        + [
            pltpu.VMEM((2,) + tile, jnp.bfloat16),
            dma((len(grads) + 1,)),
            dma((sum(lands) * steps,)),
            dma((lands[0], steps)),
            dma((lands[1], steps)),
            dma((lands[2], steps)),
            dma((steps,)),
            dma((steps,)),
            dma(()),
        ],
        compiler_params=pltpu.CompilerParams(
            collective_id=2, has_side_effects=True, vmem_limit_bytes=56 * 2**20
        ),
    )(at, odd, head, *grads)


def block_places(owner_slot):
    places, sides = [], []
    base = 0
    for rows, cols in matrix_list():
        strips, pairs = rows // BLOCK, cols // LANES
        grid = base + 2 * (jnp.arange(pairs)[None, :] * strips + jnp.arange(strips)[:, None])
        places.append(jnp.broadcast_to(grid[:, :, None], (strips, pairs, 2)).reshape(-1))
        sides.append(jnp.broadcast_to(jnp.arange(2)[None, None, :], (strips, pairs, 2)).reshape(-1))
        base += 2 * strips * pairs
    code = (2 * jnp.concatenate(places) + jnp.concatenate(sides)).astype(jnp.int32)
    slots = jnp.arange(owner_slot.shape[0], dtype=jnp.int32)
    found = jnp.sum(
        jnp.where(owner_slot[:, None] == slots[None, :], code[:, None], 0), axis=0, dtype=jnp.int32
    )
    return found // 2, found % 2


ROWS = ROW_SLOTS * WIDTH
N_IN = C // LANES
N_MID = M // LANES
WIDE = 1024
F32 = jnp.float32
BF16 = jnp.bfloat16


def dot(a, b, ca, cb):
    return lax.dot_general(a, b, (((ca,), (cb,)), ((), ())), preferred_element_type=F32)


def lanes_of(ref, first, count):
    return jnp.concatenate([ref[first + i] for i in range(count)], axis=-1)


def half_tanh(v):
    return 0.5 * (1.0 + jnp.tanh(0.5 * v))


class Net:
    def __init__(self, devices):
        first, second, third = bit_split(devices)
        self.me = lax.axis_index("dp")
        self.core = lax.axis_index("rows")
        self.near, self.far = 1 << (first + second), 1 << third
        self.near_at = lax.rem(self.me, self.near)
        self.far_at = self.me // self.near
        self.partner = (self.me, 1 - self.core)
        self.near_peers = [(self.me ^ m, self.core) for m in range(1, self.near)]
        self.near_slots = [self.near_at ^ m for m in range(1, self.near)]
        self.far_peers = [(self.me ^ (m * self.near), self.core) for m in range(1, self.far)]
        self.far_slots = [self.far_at ^ m for m in range(1, self.far)]

    def hello(self):
        barrier = pltpu.get_barrier_semaphore()
        for peer in [self.partner] + self.near_peers + self.far_peers:
            pl.semaphore_signal(barrier, inc=1, device_id=peer, device_id_type=MESH_IDS)

    def ready(self):
        pl.semaphore_wait(
            pltpu.get_barrier_semaphore(), 1 + len(self.near_peers) + len(self.far_peers)
        )


def slots_total(devices):
    first, second, third = bit_split(devices)
    return 2 + (1 << (first + second)) + (1 << third)


def remote(src, dst, send_sem, recv_sem, device):
    copy = pltpu.make_async_remote_copy(
        src_ref=src,
        dst_ref=dst,
        send_sem=send_sem,
        recv_sem=recv_sem,
        device_id=device,
        device_id_type=MESH_IDS,
    )
    copy.start()
    return copy


def landed(ref, sem):
    pltpu.make_async_copy(ref, ref, sem).wait()


def plain_sum(values, counts):
    total = values[0]
    for value in values[1:]:
        total = total + value
    return total


def pooled_moments(rows):
    def merge(values, counts):
        n = counts[0]
        for more in counts[1:]:
            n = n + more
        sums = values[0][:rows]
        spread = values[0][rows:]
        for value in values[1:]:
            sums = sums + value[:rows]
            spread = spread + value[rows:]
        mean = sums / n
        for value, own in zip(values, counts):
            gap = value[:rows] / own - mean
            spread = spread + own * gap * gap
        return jnp.concatenate([sums, spread], axis=0)

    return merge


def reduce_all(net, value, bufs, send_sem, recv_sem, merge, own_count=None, pair_count=0.0, fillers=()):
    fillers = list(fillers) + [None] * 3
    copies = []
    stages = [
        (0, net.core, [net.partner], [1 - net.core], 2),
        (2, net.near_at, net.near_peers, net.near_slots, net.near),
        (2 + net.near, net.far_at, net.far_peers, net.far_slots, net.far),
    ]
    for step, (base, mine, peers, slots, size) in enumerate(stages):
        bufs[base + mine] = value
        for i, peer in enumerate(peers):
            copies.append(
                remote(
                    bufs.at[base + mine],
                    bufs.at[base + mine],
                    send_sem.at[base + i],
                    recv_sem.at[base + mine],
                    peer,
                )
            )
        if fillers[step] is not None:
            fillers[step]()
        for slot in slots:
            landed(bufs.at[base + slot], recv_sem.at[base + slot])
        if own_count is None:
            counts = [None] * size
        elif step == 0:
            rest = pair_count - own_count
            first = net.core == 0
            counts = [jnp.where(first, own_count, rest), jnp.where(first, rest, own_count)]
        else:
            counts = [pair_count * (1 if step == 1 else net.near)] * size
        value = merge([bufs[base + j] for j in range(size)], counts)
    return value, copies


def column_sum(value):
    return jnp.sum(value.reshape(-1, 8, LANES), axis=0)


def local_moments(z, count, live, own_count, stage, masked):
    quarter = z.shape[1] // 4

    def slab(j, carry):
        total = jnp.zeros((8, LANES), F32)
        for q in range(4):
            rows = pl.ds(q * quarter, quarter)
            v = z[j, rows]
            if masked:
                v = v * live[rows]
                z[j, rows] = v
            total = total + column_sum(v)
        sums = jnp.sum(total, axis=0, keepdims=True)
        mean = sums / own_count
        spread = jnp.zeros((8, LANES), F32)
        for q in range(4):
            rows = pl.ds(q * quarter, quarter)
            d = (z[j, rows] - mean) * live[rows]
            spread = spread + column_sum(d * d)
        stage[pl.ds(j, 1)] = sums
        stage[pl.ds(count + j, 1)] = jnp.sum(spread, axis=0, keepdims=True)
        return carry

    lax.fori_loop(0, count, slab, 0)


def window(ref, down, right):
    batch = ref.shape[3]
    parts = [
        ref[j, pl.ds(down, ROW_SLOTS), pl.ds(right, WIDTH)].reshape(ROWS * batch, LANES)
        for j in range(N_MID)
    ]
    return jnp.concatenate(parts, axis=-1)


def clear_edges(ref, core):
    shape = ref.shape
    zero = jnp.zeros((shape[0], 1) + shape[2:], ref.dtype)
    ref[:, pl.ds(jnp.where(core == 0, 0, ROW_SLOTS + 1), 1)] = zero
    column = jnp.zeros(shape[:2] + (1,) + shape[3:], ref.dtype)
    ref[:, :, 0:1] = column
    ref[:, :, WIDTH + 1 : WIDTH + 2] = column


def send_edge(ref, net, send_sem, recv_sem):
    edge = jnp.where(net.core == 0, ROW_SLOTS, 1)
    there = jnp.where(net.core == 0, 0, ROW_SLOTS + 1)
    return remote(
        ref.at[:, edge, pl.ds(1, WIDTH)],
        ref.at[:, there, pl.ds(1, WIDTH)],
        send_sem,
        recv_sem,
        net.partner,
    )


def edge_landed(ref, net, recv_sem):
    here = jnp.where(net.core == 0, ROW_SLOTS + 1, 0)
    landed(ref.at[:, here, pl.ds(1, WIDTH)], recv_sem)


def edge_first(net, fill, send):
    edge = jnp.where(net.core == 0, ROW_SLOTS - 1, 0)
    fill(edge)
    copy = send()
    for step in range(1, ROW_SLOTS):
        fill(lax.rem(edge + step, ROW_SLOTS))
    return copy


def load_all(pairs, sems):
    copies = []
    for i, (src, dst) in enumerate(pairs):
        copy = pltpu.make_async_copy(src, dst, sems.at[i])
        copy.start()
        copies.append(copy)
    return copies


def forward_kernel(devices, top, total_count, *refs):
    refs = list(refs)
    take = lambda n: [refs.pop(0) for _ in range(n)]
    xb_h, xf_h = take(2) if top else [None, None]
    wi_h, wm_h, wo_h = take(3)
    if not top:
        xb, = take(1)
    params, live, count = take(3)
    za_h, hp_h, zb_h, hb_h, zc_h, stat_a, stat_b, stat_c = take(8)
    if top:
        pooled, = take(1)
    else:
        xn_h, xnb_h = take(2)
    if top:
        xb, xf = take(2)
    wi, wm, wo, za, hp, zb, hb, zc = take(8)
    if not top:
        xn, xnb = take(2)
    stage_m, stage_c, buf_a, buf_b, buf_c = take(5)
    in_sem, out_sem, send_sem, recv_sem, halo_sem = take(5)

    net = Net(devices)
    net.hello()
    loads = load_all(
        [(wi_h, wi), (wm_h, wm), (wo_h, wo)] + ([(xb_h, xb), (xf_h, xf)] if top else []), in_sem
    )
    clear_edges(hp, net.core)
    zb[...] = jnp.zeros(zb.shape, F32)
    own_count = count[0:1, :]
    pair_count = total_count / devices
    quarter = za.shape[1] // ROW_SLOTS
    batch = quarter // WIDTH
    stores = []
    sends = []

    def store(src, dst):
        copy = pltpu.make_async_copy(src, dst, out_sem.at[len(stores)])
        copy.start()
        stores.append(copy)

    def norm(z, n, stage, bufs, which, masked, stat):
        local_moments(z, n, live, own_count, stage, masked)
        if which == 0:
            net.ready()
        total, copies = reduce_all(
            net,
            stage[...],
            bufs,
            send_sem.at[which],
            recv_sem.at[which],
            pooled_moments(n),
            own_count,
            pair_count,
        )
        sends.extend(copies)
        stat[0:n] = total[:n] / total_count
        stat[n : 2 * n] = lax.rsqrt(total[n:] / total_count + EPS_NORM)

    def affine(stat, n, gain_at, j):
        mean = stat[pl.ds(j, 1)]
        scale = stat[pl.ds(n + j, 1)] * params[pl.ds(gain_at + j, 1)]
        return mean, scale, params[pl.ds(gain_at + n + j, 1)]

    loads[0].wait()
    if top:
        loads[3].wait()
    product = dot(lanes_of(xb, 0, N_IN) if top else xb[...], lanes_of(wi, 0, N_MID), 1, 0)
    for j in range(N_MID):
        za[j] = product[:, j * LANES : (j + 1) * LANES]
    norm(za, N_MID, stage_m, buf_a, 0, not top, stat_a)
    store(za, za_h)

    def fill_hidden(slot):
        rows = pl.ds(slot * quarter, quarter)

        def slab(j, carry):
            mean, scale, shift = affine(stat_a, N_MID, 0, j)
            y = (za[j, rows] - mean) * scale + shift
            h = (live[rows] * (y * half_tanh(y))).astype(BF16)
            hp[j, pl.ds(slot + 1, 1), pl.ds(1, WIDTH)] = h.reshape(1, WIDTH, batch, LANES)
            return carry

        lax.fori_loop(0, N_MID, slab, 0)

    sends.append(
        edge_first(net, fill_hidden, lambda: send_edge(hp, net, halo_sem.at[0], halo_sem.at[1]))
    )
    loads[1].wait()

    def tap(t):
        k = pl.ds(pl.multiple_of(t * M, M), M)
        part = dot(
            window(hp, t // 3, lax.rem(t, 3)),
            jnp.concatenate([wm[j, k] for j in range(N_MID)], axis=-1),
            1,
            0,
        )
        for j in range(N_MID):
            zb[j] = zb[j] + part[:, j * LANES : (j + 1) * LANES]

    def middle(i, carry):
        tap(i + 3)
        return carry

    def outer(i, carry):
        tap(jnp.where(i < 3, i, i + 3))
        return carry

    lax.fori_loop(0, 3, middle, 0)
    edge_landed(hp, net, halo_sem.at[1])
    store(hp, hp_h)
    lax.fori_loop(0, 6, outer, 0)
    norm(zb, N_MID, stage_m, buf_b, 1, True, stat_b)
    store(zb, zb_h)

    def fill_second(j, carry):
        mean, scale, shift = affine(stat_b, N_MID, 2 * N_MID, j)
        for q in range(4):
            rows = pl.ds(q * quarter, quarter)
            y = (zb[j, rows] - mean) * scale + shift
            hb[j, rows] = (live[rows] * (y * half_tanh(y))).astype(BF16)
        return carry

    lax.fori_loop(0, N_MID, fill_second, 0)
    store(hb, hb_h)
    loads[2].wait()

    def expand(g, carry):
        part = dot(lanes_of(hb, 0, N_MID), lanes_of(wo, g * N_MID, N_MID), 1, 0)
        for j in range(N_MID):
            zc[g * N_MID + j] = part[:, j * LANES : (j + 1) * LANES]
        return carry

    lax.fori_loop(0, N_IN // N_MID, expand, 0)
    store(zc, zc_h)
    norm(zc, N_IN, stage_c, buf_c, 2, False, stat_c)
    if top:
        loads[4].wait()

    def finish(j, carry):
        mean, scale, shift = affine(stat_c, N_IN, 4 * N_MID, j)
        pool = jnp.zeros((batch, LANES), F32)
        for q in range(4):
            rows = pl.ds(q * quarter, quarter)
            if top:
                x = xf[j, rows]
            else:
                x = xb[rows, pl.ds(pl.multiple_of(j * LANES, LANES), LANES)].astype(F32)
            y = (zc[j, rows] - mean) * scale + shift + x
            out = live[rows] * (y * half_tanh(y))
            if top:
                pool = pool + jnp.sum(out.reshape(WIDTH, batch, LANES), axis=0)
            else:
                xn[j, rows] = out
                xnb[j, rows] = out.astype(BF16)
        if top:
            pooled[j] = pool
        return carry

    lax.fori_loop(0, N_IN, finish, 0)
    if not top:
        store(xn, xn_h)
        store(xnb, xnb_h)
    for copy in stores:
        copy.wait()
    for copy in sends:
        copy.wait_send()


def forward_layer(devices, top, total_count, ident, xb, xf, weights, params, live, count):
    rows = live.shape[0]
    batch = rows // ROWS
    shape = jax.ShapeDtypeStruct
    any_space = pl.BlockSpec(memory_space=pl.ANY)
    vmem = pl.BlockSpec(memory_space=pltpu.VMEM)
    fields = [
        shape((N_MID, rows, LANES), F32),
        shape((N_MID, ROW_SLOTS + 2, WIDTH + 2, batch, LANES), BF16),
        shape((N_MID, rows, LANES), F32),
        shape((N_MID, rows, LANES), BF16),
        shape((N_IN, rows, LANES), F32),
    ]
    stats = [shape((2 * n, LANES), F32) for n in (N_MID, N_MID, N_IN)]
    if top:
        last = [shape((N_IN, batch, LANES), F32)]
        last_specs = [vmem]
    else:
        last = [shape((N_IN, rows, LANES), F32), shape((N_IN, rows, LANES), BF16)]
        last_specs = [any_space] * 2
    big = lambda s: pltpu.VMEM(s.shape, s.dtype)
    total = slots_total(devices)
    dma = pltpu.SemaphoreType.DMA
    ins = ([xb, xf] if top else []) + list(weights)
    small_ins = ([] if top else [xb]) + [params, live, count]
    return pl.pallas_call(
        functools.partial(forward_kernel, devices, top, total_count),
        out_shape=fields + stats + last,
        in_specs=[any_space] * len(ins) + [vmem] * len(small_ins),
        out_specs=[any_space] * 5 + [vmem] * 3 + last_specs,
        scratch_shapes=[big(a) for a in ins]
        + [big(s) for s in fields]
        + ([] if top else [big(s) for s in last])
        + [
            pltpu.VMEM((2 * N_MID, LANES), F32),
            pltpu.VMEM((2 * N_IN, LANES), F32),
            pltpu.VMEM((total, 2 * N_MID, LANES), F32),
            pltpu.VMEM((total, 2 * N_MID, LANES), F32),
            pltpu.VMEM((total, 2 * N_IN, LANES), F32),
            dma((5,)),
            dma((8,)),
            dma((3, total)),
            dma((3, total)),
            dma((2,)),
        ],
        compiler_params=pltpu.CompilerParams(
            collective_id=ident, has_side_effects=True, vmem_limit_bytes=60 * 2**20
        ),
    )(*ins, *small_ins)


def head_kernel(
    devices, area, pooled, head_h, bias, pick, point, own_weight, in_weight, hot, total,
    extra, gtop, gh_h,
    head, send_pool, recv_pool, low, logits_all, logits, g_low, gh, gh_there, gh_other, gt,
    in_sem, out_sem, send_sem, recv_sem,
):
    net = Net(devices)
    net.hello()
    load = pltpu.make_async_copy(head_h, head, in_sem)
    load.start()
    half = send_pool.shape[1]
    mine = pl.ds(pl.multiple_of(net.core * half, half), half)
    theirs = pl.ds(pl.multiple_of((1 - net.core) * half, half), half)
    for j in range(N_IN):
        send_pool[j] = pooled[j, theirs].astype(BF16)
    net.ready()
    sends = [remote(send_pool, recv_pool, send_sem.at[0], recv_sem.at[0], net.partner)]
    load.wait()
    landed(recv_pool, recv_sem.at[0])
    for j in range(N_IN):
        low[j] = ((pooled[j, mine] + recv_pool[j].astype(F32)) / area).astype(BF16)
    logits[...] = dot(lanes_of(low, 0, N_IN), lanes_of(head, 0, N_IN), 1, 1) + bias[0:1, :]
    logits_all[net.core, net.me] = logits[...].astype(BF16)
    at = 1
    for peer, slot in zip(net.near_peers, net.near_slots):
        ref = logits_all.at[net.core, net.me]
        sends.append(remote(ref, ref, send_sem.at[at], recv_sem.at[1 + net.near_at], peer))
        at += 1

    own = logits[...]
    keep = lax.broadcasted_iota(jnp.int32, own.shape, 1) < CLASSES
    peak = jnp.max(jnp.where(keep, own, -3.0e38), axis=1, keepdims=True)
    powers = jnp.where(keep, jnp.exp(jnp.where(keep, own - peak, 0.0)), 0.0)
    log_total = peak + jnp.log(jnp.sum(powers, axis=1, keepdims=True))
    softmax = jnp.where(keep, jnp.exp(jnp.where(keep, own - log_total, 0.0)), 0.0)
    picked = jnp.sum(own * hot[...], axis=1, keepdims=True)

    base = net.me - net.near_at
    for slot in net.near_slots:
        landed(logits_all.at[net.core, base + slot], recv_sem.at[1 + slot])
    group = logits_all.at[net.core, pl.ds(base, net.near)]
    for peer in net.far_peers:
        sends.append(
            remote(group, group, send_sem.at[at], recv_sem.at[1 + net.near + net.far_at], peer)
        )
        at += 1
    for slot in net.far_slots:
        landed(
            logits_all.at[net.core, pl.ds(slot * net.near, net.near)],
            recv_sem.at[1 + net.near + slot],
        )
    ref = logits_all.at[net.core]
    sends.append(
        remote(ref, ref, send_sem.at[at], recv_sem.at[1 + net.near + net.far], net.partner)
    )
    at += 1
    landed(logits_all.at[1 - net.core], recv_sem.at[1 + net.near + net.far])
    every = logits_all[...].reshape(-1, WIDE)
    gap = jnp.where(keep, own - dot(pick[...], every, 1, 0), 0.0)
    incoming = dot(point[...], every, 1, 0)
    weight = own_weight[:, 0:1]
    terms = weight * (
        log_total - picked + MATCH_WEIGHT * (jnp.sum(gap * gap, axis=1, keepdims=True) / CLASSES)
    )
    grad = (
        weight * (softmax - hot[...])
        + MATCH_WEIGHT
        * (2.0 / CLASSES)
        * (weight * gap - (incoming - in_weight[:, 0:1] * own))
    ) / total[0:1, 0:1]
    g_low[...] = jnp.where(keep, grad, 0.0).astype(BF16)
    bias_sum = jnp.sum(g_low[...].astype(F32), axis=0, keepdims=True)
    extra[...] = jnp.zeros(extra.shape, F32)
    for j in range(WIDE // LANES):
        extra[j : j + 1] = bias_sum[:, j * LANES : (j + 1) * LANES]
    extra[WIDE // LANES : WIDE // LANES + 1] = jnp.zeros((1, LANES), F32) + jnp.sum(
        terms, axis=0, keepdims=True
    )
    gt_view = gt.at[:, net.core]
    for j in range(N_IN):
        gt[j, net.core] = (dot(g_low[...], head[j], 1, 0) / area).astype(BF16)
    sends.append(
        remote(
            gt_view, gt_view, send_sem.at[at], recv_sem.at[2 + net.near + net.far], net.partner
        )
    )

    at += 1
    block = (WIDE // 2 // HALF, HALF, LANES)
    cut = WIDE // 2
    mine_at = pl.multiple_of(net.core * cut, cut)
    theirs_at = pl.multiple_of((1 - net.core) * cut, cut)

    def grad_there(j, carry):
        part = dot(g_low[:, pl.ds(theirs_at, cut)], low[j], 0, 0)
        gh_there[j] = part.astype(BF16).reshape(block)
        return carry

    lax.fori_loop(0, N_IN, grad_there, 0)
    sends.append(
        remote(gh_there, gh_other, send_sem.at[at], recv_sem.at[3 + net.near + net.far], net.partner)
    )
    landed(gt.at[:, 1 - net.core], recv_sem.at[2 + net.near + net.far])
    for j in range(N_IN):
        gtop[j] = jnp.concatenate([gt[j, 0], gt[j, 1]], axis=0).astype(F32)
    landed(gh_other, recv_sem.at[3 + net.near + net.far])

    def grad_here(j, carry):
        part = dot(g_low[:, pl.ds(mine_at, cut)], low[j], 0, 0)
        gh[j] = (part.reshape(block) + gh_other[j].astype(F32)).astype(BF16)
        return carry

    lax.fori_loop(0, N_IN, grad_here, 0)
    store = pltpu.make_async_copy(gh, gh_h, out_sem)
    store.start()
    store.wait()
    for copy in sends:
        copy.wait_send()


def head_step(devices, pooled, head, bias, pick, point, own_weight, in_weight, hot, total):
    batch = pooled.shape[1]
    half = batch // 2
    shape = jax.ShapeDtypeStruct
    any_space = pl.BlockSpec(memory_space=pl.ANY)
    vmem = pl.BlockSpec(memory_space=pltpu.VMEM)
    dma = pltpu.SemaphoreType.DMA
    count = 4 + slots_total(devices)
    return pl.pallas_call(
        functools.partial(head_kernel, devices, float(HEIGHT * WIDTH)),
        out_shape=[
            shape((16, LANES), F32),
            shape((N_IN, batch, LANES), F32),
            shape((N_IN, WIDE // 2 // HALF, HALF, LANES), BF16),
        ],
        in_specs=[vmem, any_space] + [vmem] * 7,
        out_specs=[vmem, vmem, any_space],
        scratch_shapes=[
            pltpu.VMEM((N_IN, WIDE, LANES), BF16),
            pltpu.VMEM((N_IN, half, LANES), BF16),
            pltpu.VMEM((N_IN, half, LANES), BF16),
            pltpu.VMEM((N_IN, half, LANES), BF16),
            pltpu.VMEM((2, devices, half, WIDE), BF16),
            pltpu.VMEM((half, WIDE), F32),
            pltpu.VMEM((half, WIDE), BF16),
            pltpu.VMEM((N_IN, WIDE // 2 // HALF, HALF, LANES), BF16),
            pltpu.VMEM((N_IN, WIDE // 2 // HALF, HALF, LANES), BF16),
            pltpu.VMEM((N_IN, WIDE // 2 // HALF, HALF, LANES), BF16),
            pltpu.VMEM((N_IN, 2, half, LANES), BF16),
            dma(()),
            dma(()),
            dma((count,)),
            dma((count,)),
        ],
        compiler_params=pltpu.CompilerParams(
            collective_id=5, has_side_effects=True, vmem_limit_bytes=60 * 2**20
        ),
    )(pooled, head, bias, pick, point, own_weight, in_weight, hot, total)


def pieces(part, j):
    return part[:, j * LANES : (j + 1) * LANES].astype(BF16).reshape(-1, 2, HALF, LANES)


def backward_kernel(devices, top, total_count, *refs):
    refs = list(refs)
    take = lambda n: [refs.pop(0) for _ in range(n)]
    field_h = refs.pop(0)
    xb_h, = take(1) if top else [None]
    zc_h, hb_h, hp_h, zb_h, za_h, wi_h, wm_h, wo_h = take(8)
    if not top:
        xb, = take(1)
    gtop, stat_a, stat_b, stat_c, params, live, extra = take(7)
    gi_h, gm_h, go_h = take(3)
    gout_h, = take(1) if top else [None]
    small, = take(1)
    field = refs.pop(0)
    if top:
        xb, = take(1)
    zc, hb, hp, zb, za, wi, wm, wo = take(8)
    gi, gm, go = take(3)
    ri, rm, ro = take(3)
    ec, ep, ea, ub, ua = take(5)
    stage_m, stage_c, buf_a, buf_b, buf_c = take(5)
    in_sem, out_sem, send_sem, recv_sem, halo_sem, pair_sem = take(6)

    net = Net(devices)
    net.hello()
    loads = load_all(
        [
            (zc_h, zc), (field_h, field), (za_h, za), (wo_h, wo), (zb_h, zb), (hb_h, hb),
            (hp_h, hp), (wm_h, wm), (wi_h, wi),
        ]
        + ([(xb_h, xb)] if top else []),
        in_sem,
    )
    clear_edges(ep, net.core)
    quarter = za.shape[1] // ROW_SLOTS
    batch = quarter // WIDTH
    stores = []
    sends = []

    def store(src, dst):
        copy = pltpu.make_async_copy(src, dst, out_sem.at[len(stores)])
        copy.start()
        stores.append(copy)

    def swap(grad, other, at):
        sends.append(
            remote(
                grad.at[:, :, 1 - net.core], other, pair_sem.at[0, at], pair_sem.at[1, at], net.partner
            )
        )

    def fold(grad, other, at, out):
        landed(other, pair_sem.at[1, at])

        def step(i, carry):
            other[:, i] = (grad[:, i, net.core].astype(F32) + other[:, i].astype(F32)).astype(BF16)
            return carry

        lax.fori_loop(0, grad.shape[1], step, 0)
        store(other, out)

    def slope(y):
        sigma = half_tanh(y)
        return sigma * (1.0 + y * (1.0 - sigma))

    def row(ref, j):
        return ref[pl.ds(j, 1)]

    def totals(stage, bufs, which, small_at, n, fillers=()):
        total, copies = reduce_all(
            net, stage[...], bufs, send_sem.at[which], recv_sem.at[which], plain_sum, fillers=fillers
        )
        sends.extend(copies)
        small[small_at : small_at + 2 * n] = total[: 2 * n]
        return total

    loads[0].wait()
    loads[1].wait()

    def slab_c(j, carry):
        mean, scale = row(stat_c, j), row(stat_c, N_IN + j)
        gain, shift = row(params, 4 * N_MID + j), row(params, 4 * N_MID + N_IN + j)
        total = jnp.zeros((8, LANES), F32)
        crossed = jnp.zeros((8, LANES), F32)
        for q in range(4):
            rows = pl.ds(q * quarter, quarter)
            normed = (zc[j, rows] - mean) * scale
            if top:
                x = field[j, rows]
                g = jnp.concatenate([gtop[j]] * WIDTH, axis=0)
            else:
                x = xb[rows, pl.ds(pl.multiple_of(j * LANES, LANES), LANES)].astype(F32)
                g = field[j, rows]
            u = g * live[rows] * slope(normed * gain + shift + x)
            field[j, rows] = u
            total = total + column_sum(u)
            crossed = crossed + column_sum(u * normed)
        stage_c[pl.ds(j, 1)] = jnp.sum(crossed, axis=0, keepdims=True)
        stage_c[pl.ds(N_IN + j, 1)] = jnp.sum(total, axis=0, keepdims=True)
        return carry

    lax.fori_loop(0, N_IN, slab_c, 0)
    stage_c[2 * N_IN :] = extra[...]
    net.ready()
    total_c = totals(stage_c, buf_c, 2, 4 * N_MID, N_IN)
    small[4 * N_MID + 2 * N_IN :] = total_c[2 * N_IN :]

    def back_c(j, carry):
        mean, scale = row(stat_c, j), row(stat_c, N_IN + j)
        gain = row(params, 4 * N_MID + j)
        cross = row(small, 4 * N_MID + j) / total_count
        plain = row(small, 4 * N_MID + N_IN + j) / total_count
        for q in range(4):
            rows = pl.ds(q * quarter, quarter)
            normed = (zc[j, rows] - mean) * scale
            e = live[rows] * ((gain * scale) * (field[j, rows] - plain - normed * cross))
            ec[j, rows] = e.astype(BF16)
        return carry

    lax.fori_loop(0, N_IN, back_c, 0)
    loads[3].wait()
    product = dot(lanes_of(ec, 0, N_IN), lanes_of(wo, 0, N_IN), 1, 1)
    for j in range(N_MID):
        ub[j] = product[:, j * LANES : (j + 1) * LANES]
    loads[4].wait()

    def sums_of(u_ref, z_ref, stat, gain_at, stage):
        def slab(j, carry):
            mean, scale = row(stat, j), row(stat, N_MID + j)
            gain, shift = row(params, gain_at + j), row(params, gain_at + N_MID + j)
            total = jnp.zeros((8, LANES), F32)
            crossed = jnp.zeros((8, LANES), F32)
            for q in range(4):
                rows = pl.ds(q * quarter, quarter)
                normed = (z_ref[j, rows] - mean) * scale
                u = u_ref[j, rows] * live[rows] * slope(normed * gain + shift)
                u_ref[j, rows] = u
                total = total + column_sum(u)
                crossed = crossed + column_sum(u * normed)
            stage[pl.ds(j, 1)] = jnp.sum(crossed, axis=0, keepdims=True)
            stage[pl.ds(N_MID + j, 1)] = jnp.sum(total, axis=0, keepdims=True)
            return carry

        lax.fori_loop(0, N_MID, slab, 0)

    def back_of(u_ref, z_ref, stat, gain_at, small_at, j, rows):
        normed = (z_ref[j, rows] - row(stat, j)) * row(stat, N_MID + j)
        cross = row(small, small_at + j) / total_count
        plain = row(small, small_at + N_MID + j) / total_count
        factor = row(params, gain_at + j) * row(stat, N_MID + j)
        return (live[rows] * (factor * (u_ref[j, rows] - plain - normed * cross))).astype(BF16)

    sums_of(ub, zb, stat_b, 2 * N_MID, stage_m)
    loads[5].wait()

    def grad_out(first, last):
        def group(g, carry):
            part = dot(lanes_of(hb, 0, N_MID), lanes_of(ec, g * N_MID, N_MID), 0, 0)
            for j in range(N_MID):
                go[g * N_MID + j] = pieces(part, j)
            return carry

        return lambda: lax.fori_loop(first, last, group, 0)

    groups = N_IN // N_MID
    totals(
        stage_m, buf_b, 1, 2 * N_MID, N_MID,
        [grad_out(0, 1), grad_out(1, groups - 1), grad_out(groups - 1, groups)],
    )
    swap(go, ro, 0)

    def fill_b(slot):
        rows = pl.ds(slot * quarter, quarter)

        def slab(j, carry):
            e = back_of(ub, zb, stat_b, 2 * N_MID, 2 * N_MID, j, rows)
            ep[j, pl.ds(slot + 1, 1), pl.ds(1, WIDTH)] = e.reshape(1, WIDTH, batch, LANES)
            return carry

        lax.fori_loop(0, N_MID, slab, 0)

    sends.append(
        edge_first(net, fill_b, lambda: send_edge(ep, net, halo_sem.at[0], halo_sem.at[1]))
    )
    loads[6].wait()
    loads[7].wait()
    ua[...] = jnp.zeros(ua.shape, F32)

    def grad_mid(first, last):
        def one(t, carry):
            part = dot(window(hp, t // 3, lax.rem(t, 3)), window(ep, 1, 1), 0, 0)
            for j in range(N_MID):
                gm[j, pl.ds(t * (M // 32), M // 32)] = pieces(part, j)
            return carry

        return lambda: lax.fori_loop(first, last, one, 0)

    def tap(t):
        k = pl.ds(pl.multiple_of(t * M, M), M)
        part = dot(
            window(ep, 2 - t // 3, 2 - lax.rem(t, 3)),
            jnp.concatenate([wm[j, k] for j in range(N_MID)], axis=-1),
            1,
            1,
        )
        for j in range(N_MID):
            ua[j] = ua[j] + part[:, j * LANES : (j + 1) * LANES]

    def middle(i, carry):
        tap(i + 3)
        return carry

    def outer(i, carry):
        tap(jnp.where(i < 3, i, i + 3))
        return carry

    lax.fori_loop(0, 3, middle, 0)
    edge_landed(ep, net, halo_sem.at[1])
    lax.fori_loop(0, 6, outer, 0)
    fold(go, ro, 0, go_h)
    loads[2].wait()
    sums_of(ua, za, stat_a, 0, stage_m)
    totals(
        stage_m, buf_a, 0, 0, N_MID, [grad_mid(0, 2), grad_mid(2, 5), grad_mid(5, 9)]
    )
    swap(gm, rm, 1)

    def fill_a(j, carry):
        for q in range(4):
            rows = pl.ds(q * quarter, quarter)
            ea[j, rows] = back_of(ua, za, stat_a, 0, 0, j, rows)
        return carry

    lax.fori_loop(0, N_MID, fill_a, 0)
    if top:
        loads[9].wait()

    def grad_in(g, carry):
        if top:
            x = lanes_of(xb, g * N_MID, N_MID)
        else:
            x = xb[:, pl.ds(pl.multiple_of(g * M, M), M)]
        part = dot(x, lanes_of(ea, 0, N_MID), 0, 0)
        for j in range(N_MID):
            gi[j, pl.ds(g * (M // 32), M // 32)] = pieces(part, j)
        return carry

    lax.fori_loop(0, groups, grad_in, 0)
    swap(gi, ri, 2)
    loads[8].wait()
    if top:

        def grad_field(g, carry):
            k = pl.ds(pl.multiple_of(g * M, M), M)
            part = dot(
                lanes_of(ea, 0, N_MID),
                jnp.concatenate([wi[j, k] for j in range(N_MID)], axis=-1),
                1,
                1,
            )
            for j in range(N_MID):
                at = g * N_MID + j
                field[at] = field[at] + part[:, j * LANES : (j + 1) * LANES]
            return carry

        lax.fori_loop(0, groups, grad_field, 0)
        store(field, gout_h)
    fold(gm, rm, 1, gm_h)
    fold(gi, ri, 2, gi_h)
    for copy in stores:
        copy.wait()
    for copy in sends:
        copy.wait_send()


def backward_layer(
    devices, top, total_count, ident, field, xb, kept, weights, gtop, params, live, extra
):
    za, hp, zb, hb, zc, stat_a, stat_b, stat_c = kept
    wi, wm, wo = weights
    shape = jax.ShapeDtypeStruct
    any_space = pl.BlockSpec(memory_space=pl.ANY)
    vmem = pl.BlockSpec(memory_space=pltpu.VMEM)
    dma = pltpu.SemaphoreType.DMA
    total = slots_total(devices)
    rows = za.shape[1]
    big = lambda s: pltpu.VMEM(s.shape, s.dtype)
    ins = [field] + ([xb] if top else []) + [zc, hb, hp, zb, za, wi, wm, wo]
    small_ins = ([] if top else [xb]) + [gtop, stat_a, stat_b, stat_c, params, live, extra]
    grads = [shape((w.shape[0], w.shape[1] // 32, HALF, LANES), BF16) for w in weights]
    both = [shape((w.shape[0], w.shape[1] // 32, 2, HALF, LANES), BF16) for w in weights]
    more = [shape(field.shape, F32)] if top else []
    small_rows = 4 * N_MID + 2 * N_IN + extra.shape[0]
    return pl.pallas_call(
        functools.partial(backward_kernel, devices, top, total_count),
        out_shape=grads + more + [shape((small_rows, LANES), F32)],
        in_specs=[any_space] * len(ins) + [vmem] * len(small_ins),
        out_specs=[any_space] * (3 + len(more)) + [vmem],
        scratch_shapes=[big(a) for a in ins]
        + [big(g) for g in both]
        + [big(g) for g in grads]
        + [
            pltpu.VMEM((N_IN, rows, LANES), BF16),
            pltpu.VMEM(hp.shape, BF16),
            pltpu.VMEM((N_MID, rows, LANES), BF16),
            pltpu.VMEM((N_MID, rows, LANES), F32),
            pltpu.VMEM((N_MID, rows, LANES), F32),
            pltpu.VMEM((2 * N_MID, LANES), F32),
            pltpu.VMEM((2 * N_IN + extra.shape[0], LANES), F32),
            pltpu.VMEM((total, 2 * N_MID, LANES), F32),
            pltpu.VMEM((total, 2 * N_MID, LANES), F32),
            pltpu.VMEM((total, 2 * N_IN + extra.shape[0], LANES), F32),
            dma((10,)),
            dma((4,)),
            dma((3, total)),
            dma((3, total)),
            dma((2,)),
            dma((2, 3)),
        ],
        compiler_params=pltpu.CompilerParams(
            collective_id=ident, has_side_effects=True, vmem_limit_bytes=62 * 2**20
        ),
    )(*ins, *small_ins)


def split_two(v):
    high = v.astype(BF16)
    return high, (v - high.astype(F32)).astype(BF16)


def shampoo_kernel(t_ref, m_ref, s_ref, r_ref, g_ref, s_new, m_new, flat, turn):
    group = t_ref.shape[1]
    left = pl.ds(0, BLOCK)
    right = pl.ds(BLOCK, BLOCK)
    for k in range(group):
        rows = pl.ds(k * HALF, HALF)
        parts = [t_ref[h, k].astype(F32) for h in range(2)]
        for h in range(2):
            flat[h, rows] = parts[h]
        tile = jnp.concatenate([p[:, :BLOCK] for p in parts] + [p[:, BLOCK:] for p in parts], axis=0)
        low = tile.astype(BF16)
        old = s_ref[k]
        roots = r_ref[k]
        high, rest = split_two(roots[:, :BLOCK])
        both = dot(jnp.concatenate([high, rest, tile.T.astype(BF16)], axis=0), low, 1, 0)
        s_new[k] = DECAY_STATS * old + (1.0 - DECAY_STATS) * jnp.concatenate(
            [dot(low, low, 1, 1), both[2 * BLOCK :]], axis=1
        )
        turned = both[:BLOCK] + both[BLOCK : 2 * BLOCK]
        t_high, t_rest = split_two(turned)
        high, rest = split_two(roots)
        wide = jnp.concatenate([high[:, BLOCK:], rest[:, BLOCK:]], axis=1)
        both = dot(jnp.concatenate([t_high, t_rest], axis=0), wide, 1, 0)
        turned = both[:BLOCK, :BLOCK] + both[BLOCK:, :BLOCK] + both[:BLOCK, BLOCK:]
        for h in range(2):
            turn[h, rows] = jnp.concatenate(
                [
                    turned[h * HALF : (h + 1) * HALF],
                    turned[2 * HALF + h * HALF : 2 * HALF + (h + 1) * HALF],
                ],
                axis=1,
            )
    for m in range(2 * HALF // 2):
        h, r = m // (HALF // 2), 2 * (m % (HALF // 2))
        grads = [flat[h, pl.ds(r + i, group, stride=HALF)] for i in range(2)]
        steps = [turn[h, pl.ds(r + i, group, stride=HALF)] for i in range(2)]
        for p in range(2):
            lanes = pl.ds(p * (BLOCK * BLOCK // 2) + m * LANES, LANES)
            cut = slice(p * BLOCK, (p + 1) * BLOCK)
            g_ref[:, lanes] = jnp.concatenate([v[:, cut] for v in grads], axis=1)
            m_new[:, lanes] = m_ref[:, lanes] - RATE_SHAMPOO * jnp.concatenate(
                [v[:, cut] for v in steps], axis=1
            )


def shampoo(tiles, master, statistics, root_pairs):
    owned = master.shape[0]
    group = 8
    whole = (owned + group - 1) // group
    shape = jax.ShapeDtypeStruct
    flat_spec = pl.BlockSpec((group, BLOCK * BLOCK), lambda i: (i, 0))
    pair_spec = pl.BlockSpec((group, BLOCK, 2 * BLOCK), lambda i: (i, 0, 0))
    return pl.pallas_call(
        shampoo_kernel,
        grid=(whole,),
        out_shape=[
            shape(master.shape, F32),
            shape(statistics.shape, F32),
            shape(master.shape, F32),
        ],
        in_specs=[
            pl.BlockSpec((2, group, HALF, LANES), lambda i: (0, i, 0, 0)),
            flat_spec,
            pair_spec,
            pair_spec,
        ],
        out_specs=[flat_spec, pair_spec, flat_spec],
        scratch_shapes=[pltpu.VMEM((2, group * HALF, LANES), F32)] * 2,
        compiler_params=pltpu.CompilerParams(vmem_limit_bytes=32 * 2**20),
    )(tiles, master, statistics, root_pairs)


def adamw(values_old, gradient, moment_one, moment_two, step_rate):
    one_new = BETA_FIRST * moment_one + (1.0 - BETA_FIRST) * gradient
    two_new = BETA_SECOND * moment_two + (1.0 - BETA_SECOND) * gradient * gradient
    fixed_one = 1.0 - BETA_FIRST**STEP
    fixed_two = 1.0 - BETA_SECOND**STEP
    update = one_new / fixed_one / (jnp.sqrt(two_new / fixed_two) + EPS_ADAM)
    return (one_new, two_new, values_old - step_rate * (update + DECAY_WEIGHT * values_old))


def body(
    images,
    row_split,
    labels,
    partners,
    image_weight,
    owner_slot,
    conv_master,
    conv_stats,
    conv_roots,
    head_master,
    head_moment_one,
    head_moment_two,
    small_params,
    small_moment_one,
    small_moment_two,
):
    devices = lax.axis_size("dp")
    core_index = lax.axis_index("rows")
    batch_size = images.shape[0]
    half_batch = batch_size // 2
    slot_count = images.shape[1]
    total_images = partners.shape[0]
    live_count = float(total_images * HEIGHT * WIDTH)
    owned = conv_master.shape[0]
    head_rows = head_master.shape[0]

    slot_index = (owner_slot // owned) * (2 * owned) + owner_slot % owned
    weights = list(bring_weights(conv_master, slot_index, devices))
    head_t = jnp.pad(head_master.T.astype(BF16), ((0, WIDE - CLASSES), (0, 0)))
    head_t, weights[0] = lax.optimization_barrier((head_t, weights[0]))
    head_all = lax.all_gather(head_t, "dp", axis=0)
    if head_rows != LANES:
        head_all = head_all.transpose(1, 0, 2).reshape(WIDE, N_IN, LANES).transpose(1, 0, 2)

    slot_ids = core_index * slot_count + jnp.arange(slot_count, dtype=jnp.int32)
    first_live = (ROW_SLOTS - row_split)[:, None]
    live = (slot_ids[None, :] >= first_live) & (slot_ids[None, :] < first_live + HEIGHT)
    own_count = jnp.sum(live.astype(F32)) * WIDTH
    counts = jnp.broadcast_to(own_count, (8, LANES))
    rows = slot_count * WIDTH * batch_size
    live_rows = jnp.broadcast_to(
        live.T.astype(F32)[:, None, :, None], (slot_count, WIDTH, batch_size, LANES)
    ).reshape(rows, LANES)
    first = images.transpose(1, 2, 0, 3).reshape(rows, C)
    stride = 4 * M + 2 * C
    params = [
        small_params[at * stride : (at + 1) * stride].reshape(-1, LANES) for at in range(LAYERS)
    ]
    bias = jnp.broadcast_to(
        jnp.pad(small_params[LAYERS * stride :], (0, WIDE - CLASSES)), (8, WIDE)
    )

    kept = []
    field, low = None, first
    lows = []
    for at in range(LAYERS):
        last = at == LAYERS - 1
        lows.append(low)
        out = forward_layer(
            devices,
            at > 0,
            live_count,
            3 + at,
            low,
            field,
            weights[3 * at : 3 * at + 3],
            params[at],
            live_rows,
            counts,
        )
        kept.append(out[:8])
        if last:
            pooled = out[8]
        else:
            field, low = out[8], out[9]

    def by_core(v):
        return v.reshape(devices, 2, half_batch).transpose(1, 0, 2).reshape(-1)

    weight_f = image_weight.astype(F32)
    weight_total = jnp.sum(weight_f)
    own_start = (lax.axis_index("dp") * 2 + core_index) * half_batch
    own_ids = own_start + jnp.arange(half_batch, dtype=jnp.int32)
    own_weight = lax.dynamic_slice_in_dim(weight_f, own_start, half_batch)
    own_partner = lax.dynamic_slice_in_dim(partners, own_start, half_batch)
    own_label = lax.dynamic_slice_in_dim(labels, core_index * half_batch, half_batch)
    ids = by_core(jnp.arange(total_images, dtype=jnp.int32))
    pick = (own_partner[:, None] == ids[None, :]).astype(BF16)
    point = (by_core(partners)[None, :] == own_ids[:, None]).astype(F32) * by_core(weight_f)[None, :]
    in_weight = jnp.sum(point, axis=1)
    hot = (own_label[:, None] == jnp.arange(WIDE, dtype=jnp.int32)[None, :]).astype(F32)
    spread = lambda v: jnp.broadcast_to(v[:, None], (half_batch, LANES))
    extra, g_top, grad_head = head_step(
        devices,
        pooled,
        head_all,
        bias,
        pick,
        point.astype(BF16),
        spread(own_weight),
        spread(in_weight),
        hot,
        jnp.broadcast_to(weight_total, (8, LANES)),
    )
    head_blocks = head_rows // 4
    if head_rows != LANES:
        grad_head = (
            grad_head.reshape(N_IN, WIDE // 2, LANES)
            .transpose(1, 0, 2)
            .reshape(WIDE // 2, devices, head_rows)
            .transpose(1, 0, 2)
            .reshape(devices, head_blocks, HALF, LANES)
        )
    no_extra = jnp.zeros_like(extra)
    top = backward_layer(
        devices, True, live_count, 6, field, lows[1], kept[1], weights[3:], g_top, params[1],
        live_rows, extra,
    )
    bottom = backward_layer(
        devices, False, live_count, 7, top[3], lows[0], kept[0], weights[:3], no_extra, params[0],
        live_rows, no_extra,
    )
    small_top, small_bottom = top[4], bottom[3]
    places, sides = block_places(owner_slot)
    tiles = deliver_blocks(
        list(bottom[:3]) + list(top[:3]), grad_head, places, sides, devices
    )
    conv_grad, stats_new, master_new = shampoo(tiles, conv_master, conv_stats, conv_roots)
    head_grad = tiles[:, owned:].reshape(WIDE, head_rows)[:CLASSES].T.astype(F32)
    head_one, head_two, head_new = adamw(
        head_master, head_grad, head_moment_one, head_moment_two, RATE_HEAD
    )
    layer_rows = stride // LANES
    grad_bias = small_top[layer_rows : layer_rows + WIDE // LANES].reshape(-1)[:CLASSES]
    loss_sum = small_top[layer_rows + WIDE // LANES, 0]
    grad_small = jnp.concatenate(
        [small_bottom[:layer_rows].reshape(-1), small_top[:layer_rows].reshape(-1), grad_bias]
    )
    small_one, small_two, small_new = adamw(
        small_params, grad_small, small_moment_one, small_moment_two, RATE_SMALL
    )
    return (
        loss_sum,
        weight_total,
        conv_grad,
        stats_new,
        master_new,
        master_new.astype(BF16),
        head_one,
        head_two,
        head_new,
        head_new.astype(BF16),
        small_one,
        small_two,
        small_new,
    )


def solution(mesh):
    in_specs = (
        P("dp", "rows", None, None),
        P("dp"),
        P("dp"),
        P(),
        P(),
        P(),
        P("dp", None),
        P("dp", None, None),
        P("dp", None, None),
        P("dp", None),
        P("dp", None),
        P("dp", None),
        P(),
        P(),
        P(),
    )
    out_specs = (
        P(),
        P(),
        P("dp", None),
        P("dp", None, None),
        P("dp", None),
        P("dp", None),
        P("dp", None),
        P("dp", None),
        P("dp", None),
        P("dp", None),
        P(),
        P(),
        P(),
    )
    return jax.shard_map(body, mesh=mesh, in_specs=in_specs, out_specs=out_specs, check_vma=False)
```

```python
import functools

import jax
import jax.numpy as jnp
import numpy as np
from jax import lax
from jax.experimental import pallas as pl
from jax.experimental.pallas import tpu as pltpu
from jax.sharding import PartitionSpec as P

C = 2048
M = 512
CLASSES = 1000
HEIGHT = 7
WIDTH = 7
ROW_SLOTS = 4
LAYERS = 2
BLOCK = 64
STEP = 5


EPS_NORM = 1e-05
MATCH_WEIGHT = 4.0
DECAY_STATS = 0.5
RATE_SHAMPOO = 0.15
RATE_HEAD = 0.03
RATE_SMALL = 0.2
BETA_FIRST = 0.9
BETA_SECOND = 0.95
EPS_ADAM = 1e-08
DECAY_WEIGHT = 0.01


C = 2048
M = 512
CLASSES = 1000
HEIGHT = 7
WIDTH = 7
ROW_SLOTS = 4
LAYERS = 2
BLOCK = 64
STEP = 5


EPS_NORM = 1e-05
MATCH_WEIGHT = 4.0
DECAY_STATS = 0.5
RATE_SHAMPOO = 0.15
RATE_HEAD = 0.03
RATE_SMALL = 0.2
BETA_FIRST = 0.9
BETA_SECOND = 0.95
EPS_ADAM = 1e-08
DECAY_WEIGHT = 0.01


MESH_IDS = pl.DeviceIdType.MESH
HALF = 16
LANES = 128


def bit_split(devices):
    bits = devices.bit_length() - 1
    first = bits // 3
    second = (bits - first) // 2
    return first, second, bits - first - second


def greet(peers):
    barrier = pltpu.get_barrier_semaphore()
    for peer in peers:
        pl.semaphore_signal(barrier, inc=1, device_id=peer, device_id_type=MESH_IDS)
    pl.semaphore_wait(barrier, len(peers))


def axis_masks(devices, core):
    first, second, third = bit_split(devices)
    low = [m for m in range(1, 1 << first)]
    high = [m << first for m in range(1, 1 << second)]
    if first == second:
        one = [jnp.where(core == 0, h, l) for h, l in zip(high, low)]
        two = [jnp.where(core == 0, l, h) for h, l in zip(high, low)]
    else:
        one, two = low, high
    far = [m << (first + second) for m in range(1, 1 << third)]
    return [0] + one, [0] + two, [0] + far


def even_spans(count):
    parts = 8 if count % 8 == 0 else 1
    return [(i * (count // parts), count // parts) for i in range(parts)]


def spans_of(count):
    spans, at = [], 0
    while at < count:
        rest = count - at
        size = 16 if rest > 8 else rest
        spans.append((at, size))
        at += size
    return spans


def slab_shape(shape):
    return (shape[1] // LANES, shape[0], LANES)


def matrix_list():
    shapes = []
    for _ in range(LAYERS):
        shapes += [(C, M), (9 * M, M), (M, C)]
    return shapes


BRING_LATE = 2


def bring_kernel(devices, spans, idx_ref, m_ref, *refs):
    shapes = matrix_list()
    n = len(shapes)
    outs, bufs, (g_ref, stage, send_sem, recv_sem, out_sem) = refs[:n], refs[n : 2 * n], refs[2 * n :]
    me = lax.axis_index("dp")
    core = lax.axis_index("rows")
    count = m_ref.shape[0]
    parts = len(spans)
    mid, last, far = axis_masks(devices, core)
    partner = (me, 1 - core)
    peers = [(me ^ m, core) for m in far[1:] + mid[1:] + last[1:]] + [partner]
    barrier = pltpu.get_barrier_semaphore()
    for peer in peers:
        pl.semaphore_signal(barrier, inc=1, device_id=peer, device_id_type=MESH_IDS)

    def spread(first, rows):
        for m in range(HALF):
            one = m_ref[pl.ds(first, rows), m * LANES : (m + 1) * LANES]
            two = m_ref[pl.ds(first, rows), (HALF + m) * LANES : (HALF + m + 1) * LANES]
            h, r = m // (HALF // 2), 2 * (m % (HALF // 2))
            for i in range(2):
                cut = slice(i * BLOCK, (i + 1) * BLOCK)
                stage[h, pl.ds(first * HALF + r + i, rows, stride=HALF)] = jnp.concatenate(
                    [one[:, cut], two[:, cut]], axis=1
                )

    def group(i, carry):
        spread(pl.multiple_of(i * 8, 8), 8)
        return carry

    lax.fori_loop(0, count // 8, group, 0)
    if count % 8:
        spread(count // 8 * 8, count % 8)

    def round_one(k, carry):
        for h in range(2):
            rows = pl.ds(pl.multiple_of(k * HALF, HALF), HALF)
            g_ref[(me * 2 + h) * count + k] = stage[h, rows].astype(jnp.bfloat16)
        return carry

    lax.fori_loop(0, count, round_one, 0)
    pl.semaphore_wait(barrier, len(peers))
    sent = []

    def piece(owner, half, part):
        first, size = spans[part]
        return g_ref.at[pl.ds((owner * 2 + half) * count + first, size)]

    def send(owner, part, device):
        copy = pltpu.make_async_remote_copy(
            src_ref=piece(owner, core, part),
            dst_ref=piece(owner, core, part),
            send_sem=send_sem.at[len(sent)],
            recv_sem=recv_sem.at[owner, core, part],
            device_id=device,
            device_id_type=MESH_IDS,
        )
        copy.start()
        sent.append(copy)

    def arrived(owner, half, part):
        ref = piece(owner, half, part)
        pltpu.make_async_copy(ref, ref, recv_sem.at[owner, half, part]).wait()

    def onward(owner, part, masks):
        arrived(owner, core, part)
        for m in masks:
            send(owner, part, (me ^ m, core))
        send(owner, part, partner)

    early = parts - BRING_LATE if parts > BRING_LATE else parts
    for part in range(parts):
        order = far[1:] + last[1:] + mid[1:] if part < early else mid[1:] + far[1:] + last[1:]
        for m in order:
            send(me, part, (me ^ m, core))
    for tick in range(parts + 2):
        part = tick
        if part < parts:
            if part < early:
                for z in far[1:]:
                    onward(me ^ z, part, last[1:] + mid[1:])
            else:
                for m in mid[1:]:
                    onward(me ^ m, part, far[1:] + last[1:])
        part = tick - 1
        if 0 <= part < parts:
            if part < early:
                for m in mid[1:]:
                    for z in far:
                        onward(me ^ m ^ z, part, last[1:])
            else:
                for z in far[1:]:
                    onward(me ^ z, part, last[1:])
                for z in far[1:]:
                    for m in mid[1:]:
                        onward(me ^ z ^ m, part, last[1:])
        part = tick - 2
        if 0 <= part < parts:
            for q in last[1:]:
                for z in far:
                    for m in mid:
                        onward(me ^ q ^ z ^ m, part, [])
    for step in range(1, devices):
        for part in range(parts):
            arrived(me ^ step, 1 - core, part)

    base = 0
    copies = []
    for at, (rows, cols) in enumerate(shapes):
        pairs = cols // LANES
        buf = bufs[at]

        def strip(r, carry, base=base, pairs=pairs, buf=buf):
            for m in range(pairs):
                even = idx_ref[base + r * (2 * pairs) + 2 * m]
                odd = idx_ref[base + r * (2 * pairs) + 2 * m + 1]
                for h in range(2):
                    e = g_ref[even + h * count]
                    o = g_ref[odd + h * count]
                    buf[m, pl.ds(r * BLOCK + h * HALF, HALF)] = jnp.concatenate(
                        [e[:, :BLOCK], o[:, :BLOCK]], axis=1
                    )
                    buf[m, pl.ds(r * BLOCK + 2 * HALF + h * HALF, HALF)] = jnp.concatenate(
                        [e[:, BLOCK:], o[:, BLOCK:]], axis=1
                    )
            return carry

        lax.fori_loop(0, rows // BLOCK, strip, 0, unroll=8 // (pairs // 4))
        copy = pltpu.make_async_copy(buf, outs[at], out_sem.at[at])
        copy.start()
        copies.append(copy)
        base += (rows // BLOCK) * (cols // BLOCK)
    for copy in copies:
        copy.wait()
    for copy in sent:
        copy.wait_send()


def bring_weights(master, index, devices):
    count = master.shape[0]
    spans = even_spans(count)
    parts = len(spans)
    shapes = [slab_shape(s) for s in matrix_list()]
    dma = pltpu.SemaphoreType.DMA
    return pl.pallas_call(
        functools.partial(bring_kernel, devices, spans),
        out_shape=[jax.ShapeDtypeStruct(s, jnp.bfloat16) for s in shapes],
        in_specs=[
            pl.BlockSpec(memory_space=pltpu.SMEM),
            pl.BlockSpec(memory_space=pltpu.VMEM),
        ],
        out_specs=[pl.BlockSpec(memory_space=pl.ANY)] * len(shapes),
        scratch_shapes=[pltpu.VMEM(s, jnp.bfloat16) for s in shapes]
        + [
            pltpu.VMEM((devices * 2 * count, HALF, LANES), jnp.bfloat16),
            pltpu.VMEM((2, count * HALF, LANES), jnp.float32),
            dma((3 * devices * parts,)),
            dma((devices, 2, parts)),
            dma((len(shapes),)),
        ],
        compiler_params=pltpu.CompilerParams(
            collective_id=1, has_side_effects=True, vmem_limit_bytes=56 * 2**20
        ),
    )(index, master)


def split_two(v):
    high = v.astype(BF16)
    return high, (v - high.astype(F32)).astype(BF16)


def shampoo_rows(final, master, stats, roots, grads, flat, turn, first, group):
    for k in range(group):
        rows = pl.ds(k * HALF, HALF)
        parts = [final[h, first + k].astype(F32) for h in range(2)]
        for h in range(2):
            flat[h, rows] = parts[h]
        tile = jnp.concatenate([p[:, :BLOCK] for p in parts] + [p[:, BLOCK:] for p in parts], axis=0)
        low = tile.astype(BF16)
        old = stats[first + k]
        sides = roots[first + k]
        high, rest = split_two(sides[:, :BLOCK])
        both = dot(jnp.concatenate([high, rest, tile.T.astype(BF16)], axis=0), low, 1, 0)
        stats[first + k] = DECAY_STATS * old + (1.0 - DECAY_STATS) * jnp.concatenate(
            [dot(low, low, 1, 1), both[2 * BLOCK :]], axis=1
        )
        turned = both[:BLOCK] + both[BLOCK : 2 * BLOCK]
        t_high, t_rest = split_two(turned)
        high, rest = split_two(sides)
        wide = jnp.concatenate([high[:, BLOCK:], rest[:, BLOCK:]], axis=1)
        both = dot(jnp.concatenate([t_high, t_rest], axis=0), wide, 1, 0)
        turned = both[:BLOCK, :BLOCK] + both[BLOCK:, :BLOCK] + both[:BLOCK, BLOCK:]
        for h in range(2):
            turn[h, rows] = jnp.concatenate(
                [
                    turned[h * HALF : (h + 1) * HALF],
                    turned[2 * HALF + h * HALF : 2 * HALF + (h + 1) * HALF],
                ],
                axis=1,
            )
    here = pl.ds(first if isinstance(first, int) else pl.multiple_of(first, 8), group)
    for m in range(HALF):
        h, r = m // (HALF // 2), 2 * (m % (HALF // 2))
        tiles = [flat[h, pl.ds(r + i, group, stride=HALF)] for i in range(2)]
        steps = [turn[h, pl.ds(r + i, group, stride=HALF)] for i in range(2)]
        for p in range(2):
            lanes = pl.ds(p * (BLOCK * BLOCK // 2) + m * LANES, LANES)
            cut = slice(p * BLOCK, (p + 1) * BLOCK)
            grads[here, lanes] = jnp.concatenate([v[:, cut] for v in tiles], axis=1)
            master[here, lanes] = master[here, lanes] - RATE_SHAMPOO * jnp.concatenate(
                [v[:, cut] for v in steps], axis=1
            )


DELIVER_FAR = ()
AHEAD = 3


def deliver_kernel(devices, spans, code_ref, head_h, *refs):
    n = len(matrix_list())
    grads, refs = refs[:n], refs[n:]
    master_h, stats_h, roots_h, head_out, grad_out, stats_out, master_out = refs[:7]
    pool, acc, land_last, land_mid, land_far, final = refs[7:13]
    master, stats, roots, grad_flat, flat, turn = refs[13:19]
    in_sem, send_sem, last_recv, mid_recv, far_recv, end_send, end_recv, own_sem, out_sem = refs[19:]
    me = lax.axis_index("dp")
    core = lax.axis_index("rows")
    count = code_ref.shape[0] // devices
    mid, last, far = axis_masks(devices, core)
    partner = (me, 1 - core)
    peers = [(me ^ m, core) for m in far[1:] + mid[1:] + last[1:]] + [partner]
    barrier = pltpu.get_barrier_semaphore()
    for peer in peers:
        pl.semaphore_signal(barrier, inc=1, device_id=peer, device_id_type=MESH_IDS)
    head = pltpu.make_async_copy(
        head_h, acc.at[:, pl.ds(count, head_h.shape[1])], in_sem.at[n]
    )
    head.start()
    loads = []
    start = 0
    for i, grad in enumerate(grads):
        load = pltpu.make_async_copy(grad, pool.at[pl.ds(start, grad.shape[0])], in_sem.at[i])
        load.start()
        loads.append(load)
        start += grad.shape[0]
    owned = []
    for i, (src, dst) in enumerate([(stats_h, stats), (roots_h, roots), (master_h, master)]):
        load = pltpu.make_async_copy(src, dst, own_sem.at[i])
        load.start()
        owned.append(load)
    pl.semaphore_wait(barrier, len(peers))
    head.wait()
    sent = []
    stores = []

    def store(src, dst):
        copy = pltpu.make_async_copy(src, dst, out_sem.at[len(stores)])
        copy.start()
        stores.append(copy)

    def send(owner, span, part, land, sems, at, device):
        copy = pltpu.make_async_remote_copy(
            src_ref=acc.at[owner, span],
            dst_ref=land.at[at, span],
            send_sem=send_sem.at[len(sent)],
            recv_sem=sems.at[at, part],
            device_id=device,
            device_id_type=MESH_IDS,
        )
        copy.start()
        sent.append(copy)

    def arrived(land, sems, at, span, part):
        ref = land.at[at, span]
        pltpu.make_async_copy(ref, ref, sems.at[at, part]).wait()

    def fill(first, size):
        def owner_step(owner, carry):
            def block(k, inner):
                slot = owner * count + first + k
                code = code_ref[slot]
                q = lax.shift_right_logical(code, 1)
                top = pool[q]
                low = pool[q + 1]
                even = jnp.concatenate([top[:, :BLOCK], low[:, :BLOCK]], axis=1)
                odd = jnp.concatenate([top[:, BLOCK:], low[:, BLOCK:]], axis=1)
                acc[owner, first + k] = jnp.where(lax.bitwise_and(code, 1) == 1, odd, even)
                return inner

            return lax.fori_loop(0, size, block, carry, unroll=True)

        lax.fori_loop(0, devices, owner_step, 0)

    def add(owners, lands, first, size):
        def step(i, carry):
            at = first + i
            for owner, (land, j) in zip(owners, lands):
                acc[owner, at] = (
                    acc[owner, at].astype(jnp.float32) + land[j, at].astype(jnp.float32)
                ).astype(jnp.bfloat16)
            return carry

        lax.fori_loop(0, size, step, 0)

    ends = []
    parts = len(spans)
    whole_rows = master.shape[0] % 8 != 0

    def far_second(part):
        return part in DELIVER_FAR

    for tick in range(parts + 3 + AHEAD):
        part = tick
        if part < parts:
            first, size = spans[part]
            span = pl.ds(first, size)
            if part == 1:
                for load in loads:
                    load.wait()
            if part > 0:
                fill(first, size)
            at = 0
            for q in last[1:]:
                for m in mid[::-1]:
                    for z in far[::-1]:
                        send(
                            me ^ q ^ m ^ z, span, part, land_last, last_recv, at, (me ^ q, core)
                        )
                        at += 1
        part = tick - AHEAD
        if 0 <= part < parts:
            first, size = spans[part]
            span = pl.ds(first, size)
            pairs = [(m, z) for m in mid[::-1] for z in far[::-1]]
            owners, lands = [], []
            for j in range(len(last) - 1):
                for i, (m, z) in enumerate(pairs):
                    at = j * len(pairs) + i
                    arrived(land_last, last_recv, at, span, part)
                    owners.append(me ^ m ^ z)
                    lands.append((land_last, at))
            add(owners, lands, first, size)
            at = 0
            if far_second(part):
                for z in far[1:]:
                    for m in mid[::-1]:
                        send(me ^ m ^ z, span, part, land_far, far_recv, at, (me ^ z, core))
                        at += 1
            else:
                for m in mid[1:]:
                    for z in far[::-1]:
                        send(me ^ m ^ z, span, part, land_mid, mid_recv, at, (me ^ m, core))
                        at += 1
        part = tick - 1 - AHEAD
        if 0 <= part < parts:
            first, size = spans[part]
            span = pl.ds(first, size)
            owners, lands = [], []
            at = 0
            if far_second(part):
                for z in far[1:]:
                    for m in mid[::-1]:
                        arrived(land_far, far_recv, at, span, part)
                        owners.append(me ^ m)
                        lands.append((land_far, at))
                        at += 1
                add(owners, lands, first, size)
                for at, m in enumerate(mid[1:]):
                    send(me ^ m, span, part, land_mid, mid_recv, at, (me ^ m, core))
            else:
                for m in mid[1:]:
                    for z in far[::-1]:
                        arrived(land_mid, mid_recv, at, span, part)
                        owners.append(me ^ z)
                        lands.append((land_mid, at))
                        at += 1
                add(owners, lands, first, size)
                for at, z in enumerate(far[1:]):
                    send(me ^ z, span, part, land_far, far_recv, at, (me ^ z, core))
        part = tick - 2 - AHEAD
        if 0 <= part < parts:
            first, size = spans[part]
            span = pl.ds(first, size)
            land, sems, width = land_far, far_recv, len(far) - 1
            if far_second(part):
                land, sems, width = land_mid, mid_recv, len(mid) - 1
            for at in range(width):
                arrived(land, sems, at, span, part)

            def finish(i, carry, first=first, land=land, width=width):
                at = first + i
                total = acc[me, at].astype(jnp.float32)
                for j in range(width):
                    total = total + land[j, at].astype(jnp.float32)
                final[core, at] = total.astype(jnp.bfloat16)
                return carry

            lax.fori_loop(0, size, finish, 0)
            copy = pltpu.make_async_remote_copy(
                src_ref=final.at[core, span],
                dst_ref=final.at[core, span],
                send_sem=end_send.at[part],
                recv_sem=end_recv.at[part],
                device_id=partner,
                device_id_type=MESH_IDS,
            )
            copy.start()
            ends.append(copy)
        part = tick - 3 - AHEAD
        if 0 <= part < parts:
            first, size = spans[part]
            ref = final.at[1 - core, pl.ds(first, size)]
            pltpu.make_async_copy(ref, ref, end_recv.at[part]).wait()
            if part == 0:
                store(final.at[:, pl.ds(first, size)], head_out)
                for load in owned:
                    load.wait()
                continue

            def group(i, carry, first=first):
                shampoo_rows(final, master, stats, roots, grad_flat, flat, turn, first + i * 8, 8)
                return carry

            lax.fori_loop(0, size // 8, group, 0)
            if size % 8:
                shampoo_rows(
                    final, master, stats, roots, grad_flat, flat, turn, first + size // 8 * 8, size % 8
                )
            span = pl.ds(first, size)
            store(stats.at[span], stats_out.at[span])
            if not whole_rows:
                store(grad_flat.at[span], grad_out.at[span])
                store(master.at[span], master_out.at[span])
    if whole_rows:
        store(grad_flat, grad_out)
        store(master, master_out)
    for copy in sent + ends:
        copy.wait_send()
    for copy in stores:
        copy.wait()


def deliver_blocks(grads, head, code, master, stats, roots, devices):
    count = code.shape[0] // devices
    more = head.shape[1]
    spans = [(count, more)] + spans_of(count)
    first, second, third = bit_split(devices)
    n_mid, n_last, n_far = 1 << first, 1 << second, 1 << third
    tile = (count + more, HALF, LANES)
    dma = pltpu.SemaphoreType.DMA
    lands = [(n_last - 1) * n_mid * n_far, (n_mid - 1) * n_far, (n_far - 1) * n_mid]
    grads = [g.reshape(-1, HALF, LANES) for g in grads]
    any_space = pl.BlockSpec(memory_space=pl.ANY)
    steps = len(spans)
    return pl.pallas_call(
        functools.partial(deliver_kernel, devices, spans),
        out_shape=[
            jax.ShapeDtypeStruct((2, more, HALF, LANES), BF16),
            jax.ShapeDtypeStruct(master.shape, F32),
            jax.ShapeDtypeStruct(stats.shape, F32),
            jax.ShapeDtypeStruct(master.shape, F32),
        ],
        in_specs=[pl.BlockSpec(memory_space=pltpu.SMEM)] + [any_space] * (4 + len(grads)),
        out_specs=[any_space] * 4,
        scratch_shapes=[
            pltpu.VMEM((sum(g.shape[0] for g in grads), HALF, LANES), jnp.bfloat16),
            pltpu.VMEM((devices,) + tile, jnp.bfloat16),
        ]
        + [pltpu.VMEM((k,) + tile, jnp.bfloat16) for k in lands]
        + [
            pltpu.VMEM((2,) + tile, jnp.bfloat16),
            pltpu.VMEM(master.shape, F32),
            pltpu.VMEM(stats.shape, F32),
            pltpu.VMEM(roots.shape, F32),
            pltpu.VMEM(master.shape, F32),
            pltpu.VMEM((2, 8 * HALF, LANES), F32),
            pltpu.VMEM((2, 8 * HALF, LANES), F32),
            dma((len(grads) + 1,)),
            dma((sum(lands) * steps,)),
            dma((lands[0], steps)),
            dma((lands[1], steps)),
            dma((lands[2], steps)),
            dma((steps,)),
            dma((steps,)),
            dma((3,)),
            dma((3 * steps,)),
        ],
        compiler_params=pltpu.CompilerParams(
            collective_id=2, has_side_effects=True, vmem_limit_bytes=60 * 2**20
        ),
    )(code, head, *grads, master, stats, roots)


def block_places(owner_slot):
    codes = []
    base = 0
    for rows, cols in matrix_list():
        strips, pairs = rows // BLOCK, cols // LANES
        grid = base + 2 * (np.arange(pairs)[None, :] * strips + np.arange(strips)[:, None])
        codes.append((2 * grid[:, :, None] + np.arange(2)[None, None, :]).reshape(-1))
        base += 2 * strips * pairs
    code = np.concatenate(codes).astype(np.int32)
    slots = np.arange(code.shape[0], dtype=np.int32)
    found = jnp.sum(
        jnp.where(owner_slot[:, None] == slots[None, :], code[:, None], 0), axis=0, dtype=jnp.int32
    )
    return found


ROWS = ROW_SLOTS * WIDTH
N_IN = C // LANES
N_MID = M // LANES
WIDE = 1024
F32 = jnp.float32
BF16 = jnp.bfloat16


def dot(a, b, ca, cb):
    return lax.dot_general(a, b, (((ca,), (cb,)), ((), ())), preferred_element_type=F32)


def lanes_of(ref, first, count):
    return jnp.concatenate([ref[first + i] for i in range(count)], axis=-1)


def half_tanh(v):
    return 0.5 * (1.0 + jnp.tanh(0.5 * v))


class Net:
    def __init__(self, devices):
        first, second, third = bit_split(devices)
        self.me = lax.axis_index("dp")
        self.core = lax.axis_index("rows")
        self.near, self.far = 1 << (first + second), 1 << third
        self.near_at = lax.rem(self.me, self.near)
        self.far_at = self.me // self.near
        self.partner = (self.me, 1 - self.core)
        self.near_peers = [(self.me ^ m, self.core) for m in range(1, self.near)]
        self.near_slots = [self.near_at ^ m for m in range(1, self.near)]
        self.far_peers = [(self.me ^ (m * self.near), self.core) for m in range(1, self.far)]
        self.far_slots = [self.far_at ^ m for m in range(1, self.far)]

    def hello(self):
        barrier = pltpu.get_barrier_semaphore()
        for peer in [self.partner] + self.near_peers + self.far_peers:
            pl.semaphore_signal(barrier, inc=1, device_id=peer, device_id_type=MESH_IDS)

    def ready(self):
        pl.semaphore_wait(
            pltpu.get_barrier_semaphore(), 1 + len(self.near_peers) + len(self.far_peers)
        )


def slots_total(devices):
    first, second, third = bit_split(devices)
    return 2 + (1 << (first + second)) + (1 << third)


def remote(src, dst, send_sem, recv_sem, device):
    copy = pltpu.make_async_remote_copy(
        src_ref=src,
        dst_ref=dst,
        send_sem=send_sem,
        recv_sem=recv_sem,
        device_id=device,
        device_id_type=MESH_IDS,
    )
    copy.start()
    return copy


def landed(ref, sem):
    pltpu.make_async_copy(ref, ref, sem).wait()


def plain_sum(values, counts):
    total = values[0]
    for value in values[1:]:
        total = total + value
    return total


def pooled_moments(rows):
    def merge(values, counts):
        n = counts[0]
        for more in counts[1:]:
            n = n + more
        sums = values[0][:rows]
        spread = values[0][rows:]
        for value in values[1:]:
            sums = sums + value[:rows]
            spread = spread + value[rows:]
        mean = sums / n
        for value, own in zip(values, counts):
            gap = value[:rows] / own - mean
            spread = spread + own * gap * gap
        return jnp.concatenate([sums, spread], axis=0)

    return merge


def reduce_all(net, value, bufs, send_sem, recv_sem, merge, own_count=None, pair_count=0.0, fillers=()):
    fillers = list(fillers) + [None] * 3
    copies = []
    stages = [
        (0, net.core, [net.partner], [1 - net.core], 2),
        (2, net.near_at, net.near_peers, net.near_slots, net.near),
        (2 + net.near, net.far_at, net.far_peers, net.far_slots, net.far),
    ]
    for step, (base, mine, peers, slots, size) in enumerate(stages):
        bufs[base + mine] = value
        for i, peer in enumerate(peers):
            copies.append(
                remote(
                    bufs.at[base + mine],
                    bufs.at[base + mine],
                    send_sem.at[base + i],
                    recv_sem.at[base + mine],
                    peer,
                )
            )
        if fillers[step] is not None:
            fillers[step]()
        for slot in slots:
            landed(bufs.at[base + slot], recv_sem.at[base + slot])
        if own_count is None:
            counts = [None] * size
        elif step == 0:
            rest = pair_count - own_count
            first = net.core == 0
            counts = [jnp.where(first, own_count, rest), jnp.where(first, rest, own_count)]
        else:
            counts = [pair_count * (1 if step == 1 else net.near)] * size
        value = merge([bufs[base + j] for j in range(size)], counts)
    return value, copies


def column_sum(value):
    return jnp.sum(value.reshape(-1, 8, LANES), axis=0)


def local_moments(z, count, live, own_count, stage, masked):
    quarter = z.shape[1] // 4

    def slab(j, carry):
        total = jnp.zeros((8, LANES), F32)
        for q in range(4):
            rows = pl.ds(q * quarter, quarter)
            v = z[j, rows]
            if masked:
                v = v * live[rows]
                z[j, rows] = v
            total = total + column_sum(v)
        sums = jnp.sum(total, axis=0, keepdims=True)
        mean = sums / own_count
        spread = jnp.zeros((8, LANES), F32)
        for q in range(4):
            rows = pl.ds(q * quarter, quarter)
            d = (z[j, rows] - mean) * live[rows]
            spread = spread + column_sum(d * d)
        stage[pl.ds(j, 1)] = sums
        stage[pl.ds(count + j, 1)] = jnp.sum(spread, axis=0, keepdims=True)
        return carry

    lax.fori_loop(0, count, slab, 0)


def window(ref, down, right):
    batch = ref.shape[3]
    parts = [
        ref[j, pl.ds(down, ROW_SLOTS), pl.ds(right, WIDTH)].reshape(ROWS * batch, LANES)
        for j in range(N_MID)
    ]
    return jnp.concatenate(parts, axis=-1)


def clear_edges(ref, core):
    shape = ref.shape
    zero = jnp.zeros((shape[0], 1) + shape[2:], ref.dtype)
    ref[:, pl.ds(jnp.where(core == 0, 0, ROW_SLOTS + 1), 1)] = zero
    column = jnp.zeros(shape[:2] + (1,) + shape[3:], ref.dtype)
    ref[:, :, 0:1] = column
    ref[:, :, WIDTH + 1 : WIDTH + 2] = column


def send_edge(ref, net, send_sem, recv_sem):
    edge = jnp.where(net.core == 0, ROW_SLOTS, 1)
    there = jnp.where(net.core == 0, 0, ROW_SLOTS + 1)
    return remote(
        ref.at[:, edge, pl.ds(1, WIDTH)],
        ref.at[:, there, pl.ds(1, WIDTH)],
        send_sem,
        recv_sem,
        net.partner,
    )


def edge_landed(ref, net, recv_sem):
    here = jnp.where(net.core == 0, ROW_SLOTS + 1, 0)
    landed(ref.at[:, here, pl.ds(1, WIDTH)], recv_sem)


def edge_first(net, fill, send):
    edge = jnp.where(net.core == 0, ROW_SLOTS - 1, 0)
    fill(edge)
    copy = send()
    for step in range(1, ROW_SLOTS):
        fill(lax.rem(edge + step, ROW_SLOTS))
    return copy


def load_all(pairs, sems):
    copies = []
    for i, (src, dst) in enumerate(pairs):
        copy = pltpu.make_async_copy(src, dst, sems.at[i])
        copy.start()
        copies.append(copy)
    return copies


def forward_kernel(devices, top, total_count, *refs):
    refs = list(refs)
    take = lambda n: [refs.pop(0) for _ in range(n)]
    xb_h, xf_h = take(2) if top else [None, None]
    wi_h, wm_h, wo_h = take(3)
    if not top:
        xb, = take(1)
    params, live = take(2)
    za_h, hp_h, zb_h, hb_h, zc_h, stat_a, stat_b, stat_c = take(8)
    if top:
        pooled, = take(1)
    else:
        xn_h, xnb_h = take(2)
    if top:
        xb, xf = take(2)
    wi, wm, wo, za, hp, zb, hb, zc = take(8)
    if not top:
        xn, xnb = take(2)
    stage_m, stage_c, buf_a, buf_b, buf_c = take(5)
    in_sem, out_sem, send_sem, recv_sem, halo_sem = take(5)

    net = Net(devices)
    net.hello()
    loads = load_all(
        [(wi_h, wi), (wm_h, wm), (wo_h, wo)] + ([(xb_h, xb), (xf_h, xf)] if top else []), in_sem
    )
    clear_edges(hp, net.core)
    zb[...] = jnp.zeros(zb.shape, F32)
    own_count = jnp.sum(column_sum(live[...]), axis=0, keepdims=True)
    pair_count = total_count / devices
    quarter = za.shape[1] // ROW_SLOTS
    batch = quarter // WIDTH
    stores = []
    sends = []

    def store(src, dst):
        copy = pltpu.make_async_copy(src, dst, out_sem.at[len(stores)])
        copy.start()
        stores.append(copy)

    def norm(z, n, stage, bufs, which, masked, stat):
        local_moments(z, n, live, own_count, stage, masked)
        if which == 0:
            net.ready()
        total, copies = reduce_all(
            net,
            stage[...],
            bufs,
            send_sem.at[which],
            recv_sem.at[which],
            pooled_moments(n),
            own_count,
            pair_count,
        )
        sends.extend(copies)
        stat[0:n] = total[:n] / total_count
        stat[n : 2 * n] = lax.rsqrt(total[n:] / total_count + EPS_NORM)

    def affine(stat, n, gain_at, j):
        mean = stat[pl.ds(j, 1)]
        scale = stat[pl.ds(n + j, 1)] * params[pl.ds(gain_at + j, 1)]
        return mean, scale, params[pl.ds(gain_at + n + j, 1)]

    loads[0].wait()
    if top:
        loads[3].wait()
    product = dot(lanes_of(xb, 0, N_IN) if top else xb[...], lanes_of(wi, 0, N_MID), 1, 0)
    for j in range(N_MID):
        za[j] = product[:, j * LANES : (j + 1) * LANES]
    norm(za, N_MID, stage_m, buf_a, 0, not top, stat_a)
    store(za, za_h)

    def fill_hidden(slot):
        rows = pl.ds(slot * quarter, quarter)

        def slab(j, carry):
            mean, scale, shift = affine(stat_a, N_MID, 0, j)
            y = (za[j, rows] - mean) * scale + shift
            h = (live[rows] * (y * half_tanh(y))).astype(BF16)
            hp[j, pl.ds(slot + 1, 1), pl.ds(1, WIDTH)] = h.reshape(1, WIDTH, batch, LANES)
            return carry

        lax.fori_loop(0, N_MID, slab, 0)

    sends.append(
        edge_first(net, fill_hidden, lambda: send_edge(hp, net, halo_sem.at[0], halo_sem.at[1]))
    )
    loads[1].wait()

    def tap(t):
        k = pl.ds(pl.multiple_of(t * M, M), M)
        part = dot(
            window(hp, t // 3, lax.rem(t, 3)),
            jnp.concatenate([wm[j, k] for j in range(N_MID)], axis=-1),
            1,
            0,
        )
        for j in range(N_MID):
            zb[j] = zb[j] + part[:, j * LANES : (j + 1) * LANES]

    def middle(i, carry):
        tap(i + 3)
        return carry

    def outer(i, carry):
        tap(jnp.where(i < 3, i, i + 3))
        return carry

    lax.fori_loop(0, 3, middle, 0)
    edge_landed(hp, net, halo_sem.at[1])
    store(hp, hp_h)
    lax.fori_loop(0, 6, outer, 0)
    norm(zb, N_MID, stage_m, buf_b, 1, True, stat_b)
    store(zb, zb_h)

    def fill_second(j, carry):
        mean, scale, shift = affine(stat_b, N_MID, 2 * N_MID, j)
        for q in range(4):
            rows = pl.ds(q * quarter, quarter)
            y = (zb[j, rows] - mean) * scale + shift
            hb[j, rows] = (live[rows] * (y * half_tanh(y))).astype(BF16)
        return carry

    lax.fori_loop(0, N_MID, fill_second, 0)
    store(hb, hb_h)
    loads[2].wait()

    def expand(g, carry):
        part = dot(lanes_of(hb, 0, N_MID), lanes_of(wo, g * N_MID, N_MID), 1, 0)
        for j in range(N_MID):
            zc[g * N_MID + j] = part[:, j * LANES : (j + 1) * LANES]
        return carry

    lax.fori_loop(0, N_IN // N_MID, expand, 0)
    store(zc, zc_h)
    norm(zc, N_IN, stage_c, buf_c, 2, False, stat_c)
    if top:
        loads[4].wait()

    def finish(j, carry):
        mean, scale, shift = affine(stat_c, N_IN, 4 * N_MID, j)
        pool = jnp.zeros((batch, LANES), F32)
        for q in range(4):
            rows = pl.ds(q * quarter, quarter)
            if top:
                x = xf[j, rows]
            else:
                x = xb[rows, pl.ds(pl.multiple_of(j * LANES, LANES), LANES)].astype(F32)
            y = (zc[j, rows] - mean) * scale + shift + x
            out = live[rows] * (y * half_tanh(y))
            if top:
                pool = pool + jnp.sum(out.reshape(WIDTH, batch, LANES), axis=0)
            else:
                xn[j, rows] = out
                xnb[j, rows] = out.astype(BF16)
        if top:
            pooled[j] = pool
        return carry

    lax.fori_loop(0, N_IN, finish, 0)
    if not top:
        store(xn, xn_h)
        store(xnb, xnb_h)
    for copy in stores:
        copy.wait()
    for copy in sends:
        copy.wait_send()


def forward_layer(devices, top, total_count, ident, xb, xf, weights, params, live):
    rows = live.shape[0]
    batch = rows // ROWS
    shape = jax.ShapeDtypeStruct
    any_space = pl.BlockSpec(memory_space=pl.ANY)
    vmem = pl.BlockSpec(memory_space=pltpu.VMEM)
    fields = [
        shape((N_MID, rows, LANES), F32),
        shape((N_MID, ROW_SLOTS + 2, WIDTH + 2, batch, LANES), BF16),
        shape((N_MID, rows, LANES), F32),
        shape((N_MID, rows, LANES), BF16),
        shape((N_IN, rows, LANES), F32),
    ]
    stats = [shape((2 * n, LANES), F32) for n in (N_MID, N_MID, N_IN)]
    if top:
        last = [shape((N_IN, batch, LANES), F32)]
        last_specs = [vmem]
    else:
        last = [shape((N_IN, rows, LANES), F32), shape((N_IN, rows, LANES), BF16)]
        last_specs = [any_space] * 2
    big = lambda s: pltpu.VMEM(s.shape, s.dtype)
    total = slots_total(devices)
    dma = pltpu.SemaphoreType.DMA
    ins = ([xb, xf] if top else []) + list(weights)
    small_ins = ([] if top else [xb]) + [params, live]
    return pl.pallas_call(
        functools.partial(forward_kernel, devices, top, total_count),
        out_shape=fields + stats + last,
        in_specs=[any_space] * len(ins) + [vmem] * len(small_ins),
        out_specs=[any_space] * 5 + [vmem] * 3 + last_specs,
        scratch_shapes=[big(a) for a in ins]
        + [big(s) for s in fields]
        + ([] if top else [big(s) for s in last])
        + [
            pltpu.VMEM((2 * N_MID, LANES), F32),
            pltpu.VMEM((2 * N_IN, LANES), F32),
            pltpu.VMEM((total, 2 * N_MID, LANES), F32),
            pltpu.VMEM((total, 2 * N_MID, LANES), F32),
            pltpu.VMEM((total, 2 * N_IN, LANES), F32),
            dma((5,)),
            dma((8,)),
            dma((3, total)),
            dma((3, total)),
            dma((2,)),
        ],
        compiler_params=pltpu.CompilerParams(
            collective_id=ident, has_side_effects=True, vmem_limit_bytes=60 * 2**20
        ),
    )(*ins, *small_ins)


def head_kernel(
    devices, area, pooled, head_h, bias, pick, point, numbers, hot,
    extra, gtop, gh_h,
    head, send_pool, recv_pool, low, logits_all, logits, g_low, gh, gh_there, gh_other, gt,
    in_sem, out_sem, send_sem, recv_sem,
):
    net = Net(devices)
    net.hello()
    load = pltpu.make_async_copy(head_h, head, in_sem)
    load.start()
    half = send_pool.shape[1]
    mine = pl.ds(pl.multiple_of(net.core * half, half), half)
    theirs = pl.ds(pl.multiple_of((1 - net.core) * half, half), half)
    for j in range(N_IN):
        send_pool[j] = pooled[j, theirs].astype(BF16)
    net.ready()
    sends = [remote(send_pool, recv_pool, send_sem.at[0], recv_sem.at[0], net.partner)]
    load.wait()
    landed(recv_pool, recv_sem.at[0])
    for j in range(N_IN):
        low[j] = ((pooled[j, mine] + recv_pool[j].astype(F32)) / area).astype(BF16)
    logits[...] = dot(lanes_of(low, 0, N_IN), lanes_of(head, 0, N_IN), 1, 1) + bias[0:1, :]
    logits_all[net.core, net.far_at, net.near_at] = logits[...].astype(BF16)
    at = 1
    ref = logits_all.at[net.core, net.far_at, net.near_at]
    for peer in net.far_peers:
        sends.append(
            remote(ref, ref, send_sem.at[at], recv_sem.at[1 + net.near + net.far_at], peer)
        )
        at += 1

    own = logits[...]
    keep = lax.broadcasted_iota(jnp.int32, own.shape, 1) < CLASSES
    peak = jnp.max(jnp.where(keep, own, -3.0e38), axis=1, keepdims=True)
    powers = jnp.where(keep, jnp.exp(jnp.where(keep, own - peak, 0.0)), 0.0)
    log_total = peak + jnp.log(jnp.sum(powers, axis=1, keepdims=True))
    softmax = jnp.where(keep, jnp.exp(jnp.where(keep, own - log_total, 0.0)), 0.0)
    picked = jnp.sum(own * hot[...], axis=1, keepdims=True)

    for slot in net.far_slots:
        landed(
            logits_all.at[net.core, slot, net.near_at], recv_sem.at[1 + net.near + slot]
        )
    group = logits_all.at[net.core, :, net.near_at]
    for peer in net.near_peers:
        sends.append(remote(group, group, send_sem.at[at], recv_sem.at[1 + net.near_at], peer))
        at += 1
    for slot in net.near_slots:
        landed(logits_all.at[net.core, :, slot], recv_sem.at[1 + slot])
    ref = logits_all.at[net.core]
    sends.append(
        remote(ref, ref, send_sem.at[at], recv_sem.at[1 + net.near + net.far], net.partner)
    )
    at += 1
    landed(logits_all.at[1 - net.core], recv_sem.at[1 + net.near + net.far])
    every = logits_all[...].reshape(-1, WIDE)
    gap = jnp.where(keep, own - dot(pick[...], every, 1, 0), 0.0)
    incoming = dot(point[...], every, 1, 0)
    weight = numbers[:, 0:1]
    terms = weight * (
        log_total - picked + MATCH_WEIGHT * (jnp.sum(gap * gap, axis=1, keepdims=True) / CLASSES)
    )
    grad = (
        weight * (softmax - hot[...])
        + MATCH_WEIGHT
        * (2.0 / CLASSES)
        * (weight * gap - (incoming - numbers[:, 1:2] * own))
    ) / numbers[:, 2:3]
    g_low[...] = jnp.where(keep, grad, 0.0).astype(BF16)
    bias_sum = jnp.sum(g_low[...].astype(F32), axis=0, keepdims=True)
    extra[...] = jnp.zeros(extra.shape, F32)
    for j in range(WIDE // LANES):
        extra[j : j + 1] = bias_sum[:, j * LANES : (j + 1) * LANES]
    extra[WIDE // LANES : WIDE // LANES + 1] = jnp.zeros((1, LANES), F32) + jnp.sum(
        terms, axis=0, keepdims=True
    )
    gt_view = gt.at[:, net.core]
    for j in range(N_IN):
        gt[j, net.core] = (dot(g_low[...], head[j], 1, 0) / area).astype(BF16)
    sends.append(
        remote(
            gt_view, gt_view, send_sem.at[at], recv_sem.at[2 + net.near + net.far], net.partner
        )
    )

    at += 1
    block = (WIDE // 2 // HALF, HALF, LANES)
    cut = WIDE // 2
    mine_at = pl.multiple_of(net.core * cut, cut)
    theirs_at = pl.multiple_of((1 - net.core) * cut, cut)

    def grad_there(j, carry):
        part = dot(g_low[:, pl.ds(theirs_at, cut)], low[j], 0, 0)
        gh_there[j] = part.astype(BF16).reshape(block)
        return carry

    lax.fori_loop(0, N_IN, grad_there, 0)
    sends.append(
        remote(gh_there, gh_other, send_sem.at[at], recv_sem.at[3 + net.near + net.far], net.partner)
    )
    landed(gt.at[:, 1 - net.core], recv_sem.at[2 + net.near + net.far])
    for j in range(N_IN):
        gtop[j] = jnp.concatenate([gt[j, 0], gt[j, 1]], axis=0).astype(F32)
    landed(gh_other, recv_sem.at[3 + net.near + net.far])

    def grad_here(j, carry):
        part = dot(g_low[:, pl.ds(mine_at, cut)], low[j], 0, 0)
        gh[j] = (part.reshape(block) + gh_other[j].astype(F32)).astype(BF16)
        return carry

    lax.fori_loop(0, N_IN, grad_here, 0)
    store = pltpu.make_async_copy(gh, gh_h, out_sem)
    store.start()
    store.wait()
    for copy in sends:
        copy.wait_send()


def head_step(devices, pooled, head, bias, pick, point, numbers, hot):
    batch = pooled.shape[1]
    half = batch // 2
    shape = jax.ShapeDtypeStruct
    any_space = pl.BlockSpec(memory_space=pl.ANY)
    vmem = pl.BlockSpec(memory_space=pltpu.VMEM)
    dma = pltpu.SemaphoreType.DMA
    count = 4 + slots_total(devices)
    first, second, third = bit_split(devices)
    near, far = 1 << (first + second), 1 << third
    return pl.pallas_call(
        functools.partial(head_kernel, devices, float(HEIGHT * WIDTH)),
        out_shape=[
            shape((16, LANES), F32),
            shape((N_IN, batch, LANES), F32),
            shape((N_IN, WIDE // 2 // HALF, HALF, LANES), BF16),
        ],
        in_specs=[vmem, any_space] + [vmem] * 5,
        out_specs=[vmem, vmem, any_space],
        scratch_shapes=[
            pltpu.VMEM((N_IN, WIDE, LANES), BF16),
            pltpu.VMEM((N_IN, half, LANES), BF16),
            pltpu.VMEM((N_IN, half, LANES), BF16),
            pltpu.VMEM((N_IN, half, LANES), BF16),
            pltpu.VMEM((2, far, near, half, WIDE), BF16),
            pltpu.VMEM((half, WIDE), F32),
            pltpu.VMEM((half, WIDE), BF16),
            pltpu.VMEM((N_IN, WIDE // 2 // HALF, HALF, LANES), BF16),
            pltpu.VMEM((N_IN, WIDE // 2 // HALF, HALF, LANES), BF16),
            pltpu.VMEM((N_IN, WIDE // 2 // HALF, HALF, LANES), BF16),
            pltpu.VMEM((N_IN, 2, half, LANES), BF16),
            dma(()),
            dma(()),
            dma((count,)),
            dma((count,)),
        ],
        compiler_params=pltpu.CompilerParams(
            collective_id=5, has_side_effects=True, vmem_limit_bytes=60 * 2**20
        ),
    )(pooled, head, bias, pick, point, numbers, hot)


def pieces(part, j):
    return part[:, j * LANES : (j + 1) * LANES].astype(BF16).reshape(-1, 2, HALF, LANES)


def backward_kernel(devices, top, total_count, *refs):
    refs = list(refs)
    take = lambda n: [refs.pop(0) for _ in range(n)]
    field_h = refs.pop(0)
    xb_h, = take(1) if top else [None]
    zc_h, hb_h, hp_h, zb_h, za_h, wi_h, wm_h, wo_h = take(8)
    if not top:
        xb, = take(1)
    gtop, stat_a, stat_b, stat_c, params, live, extra = take(7)
    gi_h, gm_h, go_h = take(3)
    gout_h, = take(1) if top else [None]
    small, = take(1)
    field = refs.pop(0)
    if top:
        xb, = take(1)
    zc, hb, hp, zb, za, wi, wm, wo = take(8)
    gi, gm, go = take(3)
    ri, rm, ro = take(3)
    ec, ep, ea, ub, ua = take(5)
    stage_m, stage_c, buf_a, buf_b, buf_c = take(5)
    in_sem, out_sem, send_sem, recv_sem, halo_sem, pair_sem = take(6)

    net = Net(devices)
    net.hello()
    loads = load_all(
        [
            (zc_h, zc), (field_h, field), (za_h, za), (wo_h, wo), (zb_h, zb), (hb_h, hb),
            (hp_h, hp), (wm_h, wm), (wi_h, wi),
        ]
        + ([(xb_h, xb)] if top else []),
        in_sem,
    )
    clear_edges(ep, net.core)
    quarter = za.shape[1] // ROW_SLOTS
    batch = quarter // WIDTH
    stores = []
    sends = []

    def store(src, dst):
        copy = pltpu.make_async_copy(src, dst, out_sem.at[len(stores)])
        copy.start()
        stores.append(copy)

    def swap(grad, other, at):
        sends.append(
            remote(
                grad.at[:, :, 1 - net.core], other, pair_sem.at[0, at], pair_sem.at[1, at], net.partner
            )
        )

    def fold(grad, other, at, out):
        landed(other, pair_sem.at[1, at])

        def step(i, carry):
            other[:, i] = (grad[:, i, net.core].astype(F32) + other[:, i].astype(F32)).astype(BF16)
            return carry

        lax.fori_loop(0, grad.shape[1], step, 0)
        store(other, out)

    def slope(y):
        sigma = half_tanh(y)
        return sigma * (1.0 + y * (1.0 - sigma))

    def row(ref, j):
        return ref[pl.ds(j, 1)]

    def totals(stage, bufs, which, small_at, n, fillers=()):
        total, copies = reduce_all(
            net, stage[...], bufs, send_sem.at[which], recv_sem.at[which], plain_sum, fillers=fillers
        )
        sends.extend(copies)
        small[small_at : small_at + 2 * n] = total[: 2 * n]
        return total

    loads[0].wait()
    loads[1].wait()

    def slab_c(j, carry):
        mean, scale = row(stat_c, j), row(stat_c, N_IN + j)
        gain, shift = row(params, 4 * N_MID + j), row(params, 4 * N_MID + N_IN + j)
        total = jnp.zeros((8, LANES), F32)
        crossed = jnp.zeros((8, LANES), F32)
        for q in range(4):
            rows = pl.ds(q * quarter, quarter)
            normed = (zc[j, rows] - mean) * scale
            if top:
                x = field[j, rows]
                g = jnp.concatenate([gtop[j]] * WIDTH, axis=0)
            else:
                x = xb[rows, pl.ds(pl.multiple_of(j * LANES, LANES), LANES)].astype(F32)
                g = field[j, rows]
            u = g * live[rows] * slope(normed * gain + shift + x)
            field[j, rows] = u
            total = total + column_sum(u)
            crossed = crossed + column_sum(u * normed)
        stage_c[pl.ds(j, 1)] = jnp.sum(crossed, axis=0, keepdims=True)
        stage_c[pl.ds(N_IN + j, 1)] = jnp.sum(total, axis=0, keepdims=True)
        return carry

    lax.fori_loop(0, N_IN, slab_c, 0)
    stage_c[2 * N_IN :] = extra[...]
    net.ready()
    total_c = totals(stage_c, buf_c, 2, 4 * N_MID, N_IN)
    small[4 * N_MID + 2 * N_IN :] = total_c[2 * N_IN :]

    def back_c(j, carry):
        mean, scale = row(stat_c, j), row(stat_c, N_IN + j)
        gain = row(params, 4 * N_MID + j)
        cross = row(small, 4 * N_MID + j) / total_count
        plain = row(small, 4 * N_MID + N_IN + j) / total_count
        for q in range(4):
            rows = pl.ds(q * quarter, quarter)
            normed = (zc[j, rows] - mean) * scale
            e = live[rows] * ((gain * scale) * (field[j, rows] - plain - normed * cross))
            ec[j, rows] = e.astype(BF16)
        return carry

    lax.fori_loop(0, N_IN, back_c, 0)
    loads[3].wait()
    product = dot(lanes_of(ec, 0, N_IN), lanes_of(wo, 0, N_IN), 1, 1)
    for j in range(N_MID):
        ub[j] = product[:, j * LANES : (j + 1) * LANES]
    loads[4].wait()

    def sums_of(u_ref, z_ref, stat, gain_at, stage):
        def slab(j, carry):
            mean, scale = row(stat, j), row(stat, N_MID + j)
            gain, shift = row(params, gain_at + j), row(params, gain_at + N_MID + j)
            total = jnp.zeros((8, LANES), F32)
            crossed = jnp.zeros((8, LANES), F32)
            for q in range(4):
                rows = pl.ds(q * quarter, quarter)
                normed = (z_ref[j, rows] - mean) * scale
                u = u_ref[j, rows] * live[rows] * slope(normed * gain + shift)
                u_ref[j, rows] = u
                total = total + column_sum(u)
                crossed = crossed + column_sum(u * normed)
            stage[pl.ds(j, 1)] = jnp.sum(crossed, axis=0, keepdims=True)
            stage[pl.ds(N_MID + j, 1)] = jnp.sum(total, axis=0, keepdims=True)
            return carry

        lax.fori_loop(0, N_MID, slab, 0)

    def back_of(u_ref, z_ref, stat, gain_at, small_at, j, rows):
        normed = (z_ref[j, rows] - row(stat, j)) * row(stat, N_MID + j)
        cross = row(small, small_at + j) / total_count
        plain = row(small, small_at + N_MID + j) / total_count
        factor = row(params, gain_at + j) * row(stat, N_MID + j)
        return (live[rows] * (factor * (u_ref[j, rows] - plain - normed * cross))).astype(BF16)

    sums_of(ub, zb, stat_b, 2 * N_MID, stage_m)
    loads[5].wait()

    def grad_out(first, last):
        def group(g, carry):
            part = dot(lanes_of(hb, 0, N_MID), lanes_of(ec, g * N_MID, N_MID), 0, 0)
            for j in range(N_MID):
                go[g * N_MID + j] = pieces(part, j)
            return carry

        return lambda: lax.fori_loop(first, last, group, 0)

    groups = N_IN // N_MID
    totals(
        stage_m, buf_b, 1, 2 * N_MID, N_MID,
        [grad_out(0, 1), grad_out(1, groups - 1), grad_out(groups - 1, groups)],
    )
    swap(go, ro, 0)

    def fill_b(slot):
        rows = pl.ds(slot * quarter, quarter)

        def slab(j, carry):
            e = back_of(ub, zb, stat_b, 2 * N_MID, 2 * N_MID, j, rows)
            ep[j, pl.ds(slot + 1, 1), pl.ds(1, WIDTH)] = e.reshape(1, WIDTH, batch, LANES)
            return carry

        lax.fori_loop(0, N_MID, slab, 0)

    sends.append(
        edge_first(net, fill_b, lambda: send_edge(ep, net, halo_sem.at[0], halo_sem.at[1]))
    )
    loads[6].wait()
    loads[7].wait()
    ua[...] = jnp.zeros(ua.shape, F32)

    def grad_mid(first, last):
        def one(t, carry):
            part = dot(window(hp, t // 3, lax.rem(t, 3)), window(ep, 1, 1), 0, 0)
            for j in range(N_MID):
                gm[j, pl.ds(t * (M // 32), M // 32)] = pieces(part, j)
            return carry

        return lambda: lax.fori_loop(first, last, one, 0)

    def tap(t):
        k = pl.ds(pl.multiple_of(t * M, M), M)
        part = dot(
            window(ep, 2 - t // 3, 2 - lax.rem(t, 3)),
            jnp.concatenate([wm[j, k] for j in range(N_MID)], axis=-1),
            1,
            1,
        )
        for j in range(N_MID):
            ua[j] = ua[j] + part[:, j * LANES : (j + 1) * LANES]

    def middle(i, carry):
        tap(i + 3)
        return carry

    def outer(i, carry):
        tap(jnp.where(i < 3, i, i + 3))
        return carry

    lax.fori_loop(0, 3, middle, 0)
    edge_landed(ep, net, halo_sem.at[1])
    lax.fori_loop(0, 6, outer, 0)
    fold(go, ro, 0, go_h)
    loads[2].wait()
    sums_of(ua, za, stat_a, 0, stage_m)
    totals(
        stage_m, buf_a, 0, 0, N_MID, [grad_mid(0, 2), grad_mid(2, 5), grad_mid(5, 9)]
    )
    swap(gm, rm, 1)

    def fill_a(j, carry):
        for q in range(4):
            rows = pl.ds(q * quarter, quarter)
            ea[j, rows] = back_of(ua, za, stat_a, 0, 0, j, rows)
        return carry

    lax.fori_loop(0, N_MID, fill_a, 0)
    if top:
        loads[9].wait()

    def grad_in(g, carry):
        if top:
            x = lanes_of(xb, g * N_MID, N_MID)
        else:
            x = xb[:, pl.ds(pl.multiple_of(g * M, M), M)]
        part = dot(x, lanes_of(ea, 0, N_MID), 0, 0)
        for j in range(N_MID):
            gi[j, pl.ds(g * (M // 32), M // 32)] = pieces(part, j)
        return carry

    lax.fori_loop(0, groups, grad_in, 0)
    swap(gi, ri, 2)
    loads[8].wait()
    if top:

        def grad_field(g, carry):
            k = pl.ds(pl.multiple_of(g * M, M), M)
            part = dot(
                lanes_of(ea, 0, N_MID),
                jnp.concatenate([wi[j, k] for j in range(N_MID)], axis=-1),
                1,
                1,
            )
            for j in range(N_MID):
                at = g * N_MID + j
                field[at] = field[at] + part[:, j * LANES : (j + 1) * LANES]
            return carry

        lax.fori_loop(0, groups, grad_field, 0)
        store(field, gout_h)
    fold(gm, rm, 1, gm_h)
    fold(gi, ri, 2, gi_h)
    for copy in stores:
        copy.wait()
    for copy in sends:
        copy.wait_send()


def backward_layer(
    devices, top, total_count, ident, field, xb, kept, weights, gtop, params, live, extra
):
    za, hp, zb, hb, zc, stat_a, stat_b, stat_c = kept
    wi, wm, wo = weights
    shape = jax.ShapeDtypeStruct
    any_space = pl.BlockSpec(memory_space=pl.ANY)
    vmem = pl.BlockSpec(memory_space=pltpu.VMEM)
    dma = pltpu.SemaphoreType.DMA
    total = slots_total(devices)
    rows = za.shape[1]
    big = lambda s: pltpu.VMEM(s.shape, s.dtype)
    ins = [field] + ([xb] if top else []) + [zc, hb, hp, zb, za, wi, wm, wo]
    small_ins = ([] if top else [xb]) + [gtop, stat_a, stat_b, stat_c, params, live, extra]
    grads = [shape((w.shape[0], w.shape[1] // 32, HALF, LANES), BF16) for w in weights]
    both = [shape((w.shape[0], w.shape[1] // 32, 2, HALF, LANES), BF16) for w in weights]
    more = [shape(field.shape, F32)] if top else []
    small_rows = 4 * N_MID + 2 * N_IN + extra.shape[0]
    return pl.pallas_call(
        functools.partial(backward_kernel, devices, top, total_count),
        out_shape=grads + more + [shape((small_rows, LANES), F32)],
        in_specs=[any_space] * len(ins) + [vmem] * len(small_ins),
        out_specs=[any_space] * (3 + len(more)) + [vmem],
        scratch_shapes=[big(a) for a in ins]
        + [big(g) for g in both]
        + [big(g) for g in grads]
        + [
            pltpu.VMEM((N_IN, rows, LANES), BF16),
            pltpu.VMEM(hp.shape, BF16),
            pltpu.VMEM((N_MID, rows, LANES), BF16),
            pltpu.VMEM((N_MID, rows, LANES), F32),
            pltpu.VMEM((N_MID, rows, LANES), F32),
            pltpu.VMEM((2 * N_MID, LANES), F32),
            pltpu.VMEM((2 * N_IN + extra.shape[0], LANES), F32),
            pltpu.VMEM((total, 2 * N_MID, LANES), F32),
            pltpu.VMEM((total, 2 * N_MID, LANES), F32),
            pltpu.VMEM((total, 2 * N_IN + extra.shape[0], LANES), F32),
            dma((10,)),
            dma((4,)),
            dma((3, total)),
            dma((3, total)),
            dma((2,)),
            dma((2, 3)),
        ],
        compiler_params=pltpu.CompilerParams(
            collective_id=ident, has_side_effects=True, vmem_limit_bytes=62 * 2**20
        ),
    )(*ins, *small_ins)


def adamw(values_old, gradient, moment_one, moment_two, step_rate):
    one_new = BETA_FIRST * moment_one + (1.0 - BETA_FIRST) * gradient
    two_new = BETA_SECOND * moment_two + (1.0 - BETA_SECOND) * gradient * gradient
    fixed_one = 1.0 - BETA_FIRST**STEP
    fixed_two = 1.0 - BETA_SECOND**STEP
    update = one_new / fixed_one / (jnp.sqrt(two_new / fixed_two) + EPS_ADAM)
    return (one_new, two_new, values_old - step_rate * (update + DECAY_WEIGHT * values_old))


def body(
    images,
    row_split,
    labels,
    partners,
    image_weight,
    owner_slot,
    conv_master,
    conv_stats,
    conv_roots,
    head_master,
    head_moment_one,
    head_moment_two,
    small_params,
    small_moment_one,
    small_moment_two,
):
    devices = lax.axis_size("dp")
    core_index = lax.axis_index("rows")
    batch_size = images.shape[0]
    half_batch = batch_size // 2
    slot_count = images.shape[1]
    total_images = partners.shape[0]
    live_count = float(total_images * HEIGHT * WIDTH)
    owned = conv_master.shape[0]
    head_rows = head_master.shape[0]

    slot_index = (owner_slot // owned) * (2 * owned) + owner_slot % owned
    weights = list(bring_weights(conv_master, slot_index, devices))
    head_t = jnp.pad(head_master.T.astype(BF16), ((0, WIDE - CLASSES), (0, 0)))
    head_t, weights[0] = lax.optimization_barrier((head_t, weights[0]))
    head_all = lax.all_gather(head_t, "dp", axis=0)
    if head_rows != LANES:
        head_all = head_all.transpose(1, 0, 2).reshape(WIDE, N_IN, LANES).transpose(1, 0, 2)

    slot_ids = core_index * slot_count + jnp.arange(slot_count, dtype=jnp.int32)
    first_live = (ROW_SLOTS - row_split)[:, None]
    live = (slot_ids[None, :] >= first_live) & (slot_ids[None, :] < first_live + HEIGHT)
    rows = slot_count * WIDTH * batch_size
    live_rows = jnp.broadcast_to(
        live.T.astype(F32)[:, None, :, None], (slot_count, WIDTH, batch_size, LANES)
    ).reshape(rows, LANES)
    first = images.transpose(1, 2, 0, 3).reshape(rows, C)
    stride = 4 * M + 2 * C
    params = [
        small_params[at * stride : (at + 1) * stride].reshape(-1, LANES) for at in range(LAYERS)
    ]
    bias = jnp.pad(small_params[LAYERS * stride :], (0, WIDE - CLASSES))[None, :]

    kept = []
    field, low = None, first
    lows = []
    for at in range(LAYERS):
        last = at == LAYERS - 1
        lows.append(low)
        out = forward_layer(
            devices,
            at > 0,
            live_count,
            3 + at,
            low,
            field,
            weights[3 * at : 3 * at + 3],
            params[at],
            live_rows,
        )
        kept.append(out[:8])
        if last:
            pooled = out[8]
        else:
            field, low = out[8], out[9]

    def by_core(v):
        return v.reshape(devices, 2, half_batch).transpose(1, 0, 2).reshape(-1)

    weight_f = image_weight.astype(F32)
    weight_total = jnp.sum(weight_f)
    own_start = (lax.axis_index("dp") * 2 + core_index) * half_batch
    own_ids = own_start + jnp.arange(half_batch, dtype=jnp.int32)
    own_weight = lax.dynamic_slice_in_dim(weight_f, own_start, half_batch)
    own_partner = lax.dynamic_slice_in_dim(partners, own_start, half_batch)
    own_label = lax.dynamic_slice_in_dim(labels, core_index * half_batch, half_batch)
    ids = by_core(jnp.arange(total_images, dtype=jnp.int32))
    pick = (own_partner[:, None] == ids[None, :]).astype(BF16)
    point = (by_core(partners)[None, :] == own_ids[:, None]).astype(F32) * by_core(weight_f)[None, :]
    in_weight = jnp.sum(point, axis=1)
    hot = (own_label[:, None] == jnp.arange(WIDE, dtype=jnp.int32)[None, :]).astype(F32)
    lane = jnp.arange(LANES)[None, :]
    numbers = jnp.where(
        lane == 0, own_weight[:, None], jnp.where(lane == 1, in_weight[:, None], weight_total)
    )
    extra, g_top, grad_head = head_step(
        devices,
        pooled,
        head_all,
        bias,
        pick,
        point.astype(BF16),
        numbers,
        hot,
    )
    head_blocks = head_rows // 4
    if head_rows != LANES:
        grad_head = (
            grad_head.reshape(N_IN, WIDE // 2, LANES)
            .transpose(1, 0, 2)
            .reshape(WIDE // 2, devices, head_rows)
            .transpose(1, 0, 2)
            .reshape(devices, head_blocks, HALF, LANES)
        )
    no_extra = jnp.zeros_like(extra)
    top = backward_layer(
        devices, True, live_count, 6, field, lows[1], kept[1], weights[3:], g_top, params[1],
        live_rows, extra,
    )
    bottom = backward_layer(
        devices, False, live_count, 7, top[3], lows[0], kept[0], weights[:3], no_extra, params[0],
        live_rows, no_extra,
    )
    small_top, small_bottom = top[4], bottom[3]
    head_sum, conv_grad, stats_new, master_new = deliver_blocks(
        list(bottom[:3]) + list(top[:3]),
        grad_head,
        block_places(owner_slot),
        conv_master,
        conv_stats,
        conv_roots,
        devices,
    )
    head_grad = head_sum.reshape(WIDE, head_rows)[:CLASSES].T.astype(F32)
    head_one, head_two, head_new = adamw(
        head_master, head_grad, head_moment_one, head_moment_two, RATE_HEAD
    )
    layer_rows = stride // LANES
    grad_bias = small_top[layer_rows : layer_rows + WIDE // LANES].reshape(-1)[:CLASSES]
    loss_sum = small_top[layer_rows + WIDE // LANES, 0]
    grad_small = jnp.concatenate(
        [small_bottom[:layer_rows].reshape(-1), small_top[:layer_rows].reshape(-1), grad_bias]
    )
    small_one, small_two, small_new = adamw(
        small_params, grad_small, small_moment_one, small_moment_two, RATE_SMALL
    )
    return (
        loss_sum,
        weight_total,
        conv_grad,
        stats_new,
        master_new,
        master_new.astype(BF16),
        head_one,
        head_two,
        head_new,
        head_new.astype(BF16),
        small_one,
        small_two,
        small_new,
    )


def solution(mesh):
    in_specs = (
        P("dp", "rows", None, None),
        P("dp"),
        P("dp"),
        P(),
        P(),
        P(),
        P("dp", None),
        P("dp", None, None),
        P("dp", None, None),
        P("dp", None),
        P("dp", None),
        P("dp", None),
        P(),
        P(),
        P(),
    )
    out_specs = (
        P(),
        P(),
        P("dp", None),
        P("dp", None, None),
        P("dp", None),
        P("dp", None),
        P("dp", None),
        P("dp", None),
        P("dp", None),
        P("dp", None),
        P(),
        P(),
        P(),
    )
    return jax.shard_map(body, mesh=mesh, in_specs=in_specs, out_specs=out_specs, check_vma=False)
```

```python
import functools

import jax
import jax.numpy as jnp
import numpy as np
from jax import lax
from jax.experimental import pallas as pl
from jax.experimental.pallas import tpu as pltpu
from jax.sharding import PartitionSpec as P

C = 2048
M = 512
CLASSES = 1000
HEIGHT = 7
WIDTH = 7
ROW_SLOTS = 4
LAYERS = 2
BLOCK = 64
STEP = 5


EPS_NORM = 1e-05
MATCH_WEIGHT = 4.0
DECAY_STATS = 0.5
RATE_SHAMPOO = 0.15
RATE_HEAD = 0.03
RATE_SMALL = 0.2
BETA_FIRST = 0.9
BETA_SECOND = 0.95
EPS_ADAM = 1e-08
DECAY_WEIGHT = 0.01


C = 2048
M = 512
CLASSES = 1000
HEIGHT = 7
WIDTH = 7
ROW_SLOTS = 4
LAYERS = 2
BLOCK = 64
STEP = 5


EPS_NORM = 1e-05
MATCH_WEIGHT = 4.0
DECAY_STATS = 0.5
RATE_SHAMPOO = 0.15
RATE_HEAD = 0.03
RATE_SMALL = 0.2
BETA_FIRST = 0.9
BETA_SECOND = 0.95
EPS_ADAM = 1e-08
DECAY_WEIGHT = 0.01


MESH_IDS = pl.DeviceIdType.MESH
HALF = 16
LANES = 128


def bit_split(devices):
    bits = devices.bit_length() - 1
    first = bits // 3
    second = (bits - first) // 2
    return first, second, bits - first - second


def greet(peers):
    barrier = pltpu.get_barrier_semaphore()
    for peer in peers:
        pl.semaphore_signal(barrier, inc=1, device_id=peer, device_id_type=MESH_IDS)
    pl.semaphore_wait(barrier, len(peers))


def axis_masks(devices, core):
    first, second, third = bit_split(devices)
    low = [m for m in range(1, 1 << first)]
    high = [m << first for m in range(1, 1 << second)]
    if first == second:
        one = [jnp.where(core == 0, h, l) for h, l in zip(high, low)]
        two = [jnp.where(core == 0, l, h) for h, l in zip(high, low)]
    else:
        one, two = low, high
    far = [m << (first + second) for m in range(1, 1 << third)]
    return [0] + one, [0] + two, [0] + far


def even_spans(count):
    parts = 8 if count % 8 == 0 else 1
    return [(i * (count // parts), count // parts) for i in range(parts)]


def spans_of(count):
    spans, at = [], 0
    while at < count:
        rest = count - at
        size = 16 if rest > 8 else rest
        spans.append((at, size))
        at += size
    return spans


def slab_shape(shape):
    return (shape[1] // LANES, shape[0], LANES)


def matrix_list():
    shapes = []
    for _ in range(LAYERS):
        shapes += [(C, M), (9 * M, M), (M, C)]
    return shapes


BRING_LATE = 2


def bring_kernel(devices, spans, idx_ref, m_ref, *refs):
    shapes = matrix_list()
    n = len(shapes)
    outs, bufs, (g_ref, stage, send_sem, recv_sem, out_sem) = refs[:n], refs[n : 2 * n], refs[2 * n :]
    me = lax.axis_index("dp")
    core = lax.axis_index("rows")
    count = m_ref.shape[0]
    parts = len(spans)
    mid, last, far = axis_masks(devices, core)
    partner = (me, 1 - core)
    peers = [(me ^ m, core) for m in far[1:] + mid[1:] + last[1:]] + [partner]
    barrier = pltpu.get_barrier_semaphore()
    for peer in peers:
        pl.semaphore_signal(barrier, inc=1, device_id=peer, device_id_type=MESH_IDS)

    def spread(first, rows):
        for m in range(HALF):
            one = m_ref[pl.ds(first, rows), m * LANES : (m + 1) * LANES]
            two = m_ref[pl.ds(first, rows), (HALF + m) * LANES : (HALF + m + 1) * LANES]
            h, r = m // (HALF // 2), 2 * (m % (HALF // 2))
            for i in range(2):
                cut = slice(i * BLOCK, (i + 1) * BLOCK)
                stage[h, pl.ds(first * HALF + r + i, rows, stride=HALF)] = jnp.concatenate(
                    [one[:, cut], two[:, cut]], axis=1
                )

    def group(i, carry):
        spread(pl.multiple_of(i * 8, 8), 8)
        return carry

    lax.fori_loop(0, count // 8, group, 0)
    if count % 8:
        spread(count // 8 * 8, count % 8)

    def round_one(k, carry):
        for h in range(2):
            rows = pl.ds(pl.multiple_of(k * HALF, HALF), HALF)
            g_ref[(me * 2 + h) * count + k] = stage[h, rows].astype(jnp.bfloat16)
        return carry

    lax.fori_loop(0, count, round_one, 0)
    pl.semaphore_wait(barrier, len(peers))
    sent = []

    def piece(owner, half, part):
        first, size = spans[part]
        return g_ref.at[pl.ds((owner * 2 + half) * count + first, size)]

    def send(owner, part, device):
        copy = pltpu.make_async_remote_copy(
            src_ref=piece(owner, core, part),
            dst_ref=piece(owner, core, part),
            send_sem=send_sem.at[len(sent)],
            recv_sem=recv_sem.at[owner, core, part],
            device_id=device,
            device_id_type=MESH_IDS,
        )
        copy.start()
        sent.append(copy)

    def arrived(owner, half, part):
        ref = piece(owner, half, part)
        pltpu.make_async_copy(ref, ref, recv_sem.at[owner, half, part]).wait()

    def onward(owner, part, masks):
        arrived(owner, core, part)
        for m in masks:
            send(owner, part, (me ^ m, core))
        send(owner, part, partner)

    early = parts - BRING_LATE if parts > BRING_LATE else parts
    for part in range(parts):
        order = far[1:] + last[1:] + mid[1:] if part < early else mid[1:] + far[1:] + last[1:]
        for m in order:
            send(me, part, (me ^ m, core))
    for tick in range(parts + 2):
        part = tick
        if part < parts:
            if part < early:
                for z in far[1:]:
                    onward(me ^ z, part, last[1:] + mid[1:])
            else:
                for m in mid[1:]:
                    onward(me ^ m, part, far[1:] + last[1:])
        part = tick - 1
        if 0 <= part < parts:
            if part < early:
                for m in mid[1:]:
                    for z in far:
                        onward(me ^ m ^ z, part, last[1:])
            else:
                for z in far[1:]:
                    onward(me ^ z, part, last[1:])
                for z in far[1:]:
                    for m in mid[1:]:
                        onward(me ^ z ^ m, part, last[1:])
        part = tick - 2
        if 0 <= part < parts:
            for q in last[1:]:
                for z in far:
                    for m in mid:
                        onward(me ^ q ^ z ^ m, part, [])
    for step in range(1, devices):
        for part in range(parts):
            arrived(me ^ step, 1 - core, part)

    base = 0
    copies = []
    for at, (rows, cols) in enumerate(shapes):
        pairs = cols // LANES
        buf = bufs[at]

        def strip(r, carry, base=base, pairs=pairs, buf=buf):
            for m in range(pairs):
                even = idx_ref[base + r * (2 * pairs) + 2 * m]
                odd = idx_ref[base + r * (2 * pairs) + 2 * m + 1]
                for h in range(2):
                    e = g_ref[even + h * count]
                    o = g_ref[odd + h * count]
                    buf[m, pl.ds(r * BLOCK + h * HALF, HALF)] = jnp.concatenate(
                        [e[:, :BLOCK], o[:, :BLOCK]], axis=1
                    )
                    buf[m, pl.ds(r * BLOCK + 2 * HALF + h * HALF, HALF)] = jnp.concatenate(
                        [e[:, BLOCK:], o[:, BLOCK:]], axis=1
                    )
            return carry

        lax.fori_loop(0, rows // BLOCK, strip, 0, unroll=8 // (pairs // 4))
        copy = pltpu.make_async_copy(buf, outs[at], out_sem.at[at])
        copy.start()
        copies.append(copy)
        base += (rows // BLOCK) * (cols // BLOCK)
    for copy in copies:
        copy.wait()
    for copy in sent:
        copy.wait_send()


def bring_weights(master, index, devices):
    count = master.shape[0]
    spans = even_spans(count)
    parts = len(spans)
    shapes = [slab_shape(s) for s in matrix_list()]
    dma = pltpu.SemaphoreType.DMA
    return pl.pallas_call(
        functools.partial(bring_kernel, devices, spans),
        out_shape=[jax.ShapeDtypeStruct(s, jnp.bfloat16) for s in shapes],
        in_specs=[
            pl.BlockSpec(memory_space=pltpu.SMEM),
            pl.BlockSpec(memory_space=pltpu.VMEM),
        ],
        out_specs=[pl.BlockSpec(memory_space=pl.ANY)] * len(shapes),
        scratch_shapes=[pltpu.VMEM(s, jnp.bfloat16) for s in shapes]
        + [
            pltpu.VMEM((devices * 2 * count, HALF, LANES), jnp.bfloat16),
            pltpu.VMEM((2, count * HALF, LANES), jnp.float32),
            dma((3 * devices * parts,)),
            dma((devices, 2, parts)),
            dma((len(shapes),)),
        ],
        compiler_params=pltpu.CompilerParams(
            collective_id=1, has_side_effects=True, vmem_limit_bytes=56 * 2**20
        ),
    )(index, master)


def split_two(v):
    high = v.astype(BF16)
    return high, (v - high.astype(F32)).astype(BF16)


def shampoo_rows(final, master, stats, roots, grads, flat, turn, first, group):
    for k in range(group):
        rows = pl.ds(k * HALF, HALF)
        parts = [final[h, first + k].astype(F32) for h in range(2)]
        for h in range(2):
            flat[h, rows] = parts[h]
        tile = jnp.concatenate([p[:, :BLOCK] for p in parts] + [p[:, BLOCK:] for p in parts], axis=0)
        low = tile.astype(BF16)
        old = stats[first + k]
        sides = roots[first + k]
        high, rest = split_two(sides[:, :BLOCK])
        both = dot(jnp.concatenate([high, rest, tile.T.astype(BF16)], axis=0), low, 1, 0)
        stats[first + k] = DECAY_STATS * old + (1.0 - DECAY_STATS) * jnp.concatenate(
            [dot(low, low, 1, 1), both[2 * BLOCK :]], axis=1
        )
        turned = both[:BLOCK] + both[BLOCK : 2 * BLOCK]
        t_high, t_rest = split_two(turned)
        high, rest = split_two(sides)
        wide = jnp.concatenate([high[:, BLOCK:], rest[:, BLOCK:]], axis=1)
        both = dot(jnp.concatenate([t_high, t_rest], axis=0), wide, 1, 0)
        turned = both[:BLOCK, :BLOCK] + both[BLOCK:, :BLOCK] + both[:BLOCK, BLOCK:]
        for h in range(2):
            turn[h, rows] = jnp.concatenate(
                [
                    turned[h * HALF : (h + 1) * HALF],
                    turned[2 * HALF + h * HALF : 2 * HALF + (h + 1) * HALF],
                ],
                axis=1,
            )
    here = pl.ds(first if isinstance(first, int) else pl.multiple_of(first, 8), group)
    for m in range(HALF):
        h, r = m // (HALF // 2), 2 * (m % (HALF // 2))
        tiles = [flat[h, pl.ds(r + i, group, stride=HALF)] for i in range(2)]
        steps = [turn[h, pl.ds(r + i, group, stride=HALF)] for i in range(2)]
        for p in range(2):
            lanes = pl.ds(p * (BLOCK * BLOCK // 2) + m * LANES, LANES)
            cut = slice(p * BLOCK, (p + 1) * BLOCK)
            grads[here, lanes] = jnp.concatenate([v[:, cut] for v in tiles], axis=1)
            master[here, lanes] = master[here, lanes] - RATE_SHAMPOO * jnp.concatenate(
                [v[:, cut] for v in steps], axis=1
            )


DELIVER_FAR = ()
AHEAD = 3


def deliver_kernel(devices, spans, code_ref, head_h, *refs):
    n = len(matrix_list())
    grads, refs = refs[:n], refs[n:]
    master_h, stats_h, roots_h, head_out, grad_out, stats_out, master_out = refs[:7]
    pool, acc, land_last, land_mid, land_far, final = refs[7:13]
    master, stats, roots, grad_flat, flat, turn = refs[13:19]
    in_sem, send_sem, last_recv, mid_recv, far_recv, end_send, end_recv, own_sem, out_sem = refs[19:]
    me = lax.axis_index("dp")
    core = lax.axis_index("rows")
    count = code_ref.shape[0] // devices
    mid, last, far = axis_masks(devices, core)
    partner = (me, 1 - core)
    peers = [(me ^ m, core) for m in far[1:] + mid[1:] + last[1:]] + [partner]
    barrier = pltpu.get_barrier_semaphore()
    for peer in peers:
        pl.semaphore_signal(barrier, inc=1, device_id=peer, device_id_type=MESH_IDS)
    head = pltpu.make_async_copy(
        head_h, acc.at[:, pl.ds(count, head_h.shape[1])], in_sem.at[n]
    )
    head.start()
    loads = []
    start = 0
    for i, grad in enumerate(grads):
        load = pltpu.make_async_copy(grad, pool.at[pl.ds(start, grad.shape[0])], in_sem.at[i])
        load.start()
        loads.append(load)
        start += grad.shape[0]
    owned = []
    for i, (src, dst) in enumerate([(stats_h, stats), (roots_h, roots), (master_h, master)]):
        load = pltpu.make_async_copy(src, dst, own_sem.at[i])
        load.start()
        owned.append(load)
    pl.semaphore_wait(barrier, len(peers))
    head.wait()
    sent = []
    stores = []

    def store(src, dst):
        copy = pltpu.make_async_copy(src, dst, out_sem.at[len(stores)])
        copy.start()
        stores.append(copy)

    def send(owner, span, part, land, sems, at, device):
        copy = pltpu.make_async_remote_copy(
            src_ref=acc.at[owner, span],
            dst_ref=land.at[at, span],
            send_sem=send_sem.at[len(sent)],
            recv_sem=sems.at[at, part],
            device_id=device,
            device_id_type=MESH_IDS,
        )
        copy.start()
        sent.append(copy)

    def arrived(land, sems, at, span, part):
        ref = land.at[at, span]
        pltpu.make_async_copy(ref, ref, sems.at[at, part]).wait()

    def fill(first, size):
        def owner_step(owner, carry):
            def block(k, inner):
                slot = owner * count + first + k
                code = code_ref[slot]
                q = lax.shift_right_logical(code, 1)
                top = pool[q]
                low = pool[q + 1]
                even = jnp.concatenate([top[:, :BLOCK], low[:, :BLOCK]], axis=1)
                odd = jnp.concatenate([top[:, BLOCK:], low[:, BLOCK:]], axis=1)
                acc[owner, first + k] = jnp.where(lax.bitwise_and(code, 1) == 1, odd, even)
                return inner

            return lax.fori_loop(0, size, block, carry, unroll=True)

        lax.fori_loop(0, devices, owner_step, 0)

    def add(owners, lands, first, size):
        def step(i, carry):
            at = first + i
            for owner, (land, j) in zip(owners, lands):
                acc[owner, at] = (
                    acc[owner, at].astype(jnp.float32) + land[j, at].astype(jnp.float32)
                ).astype(jnp.bfloat16)
            return carry

        lax.fori_loop(0, size, step, 0)

    ends = []
    parts = len(spans)
    whole_rows = master.shape[0] % 8 != 0

    def far_second(part):
        return part in DELIVER_FAR

    for tick in range(parts + 3 + AHEAD):
        part = tick
        if part < parts:
            first, size = spans[part]
            span = pl.ds(first, size)
            if part == 1:
                for load in loads:
                    load.wait()
            if part > 0:
                fill(first, size)
            at = 0
            for q in last[1:]:
                for m in mid[::-1]:
                    for z in far[::-1]:
                        send(
                            me ^ q ^ m ^ z, span, part, land_last, last_recv, at, (me ^ q, core)
                        )
                        at += 1
        part = tick - AHEAD
        if 0 <= part < parts:
            first, size = spans[part]
            span = pl.ds(first, size)
            pairs = [(m, z) for m in mid[::-1] for z in far[::-1]]
            owners, lands = [], []
            for j in range(len(last) - 1):
                for i, (m, z) in enumerate(pairs):
                    at = j * len(pairs) + i
                    arrived(land_last, last_recv, at, span, part)
                    owners.append(me ^ m ^ z)
                    lands.append((land_last, at))
            add(owners, lands, first, size)
            at = 0
            if far_second(part):
                for z in far[1:]:
                    for m in mid[::-1]:
                        send(me ^ m ^ z, span, part, land_far, far_recv, at, (me ^ z, core))
                        at += 1
            else:
                for m in mid[1:]:
                    for z in far[::-1]:
                        send(me ^ m ^ z, span, part, land_mid, mid_recv, at, (me ^ m, core))
                        at += 1
        part = tick - 1 - AHEAD
        if 0 <= part < parts:
            first, size = spans[part]
            span = pl.ds(first, size)
            owners, lands = [], []
            at = 0
            if far_second(part):
                for z in far[1:]:
                    for m in mid[::-1]:
                        arrived(land_far, far_recv, at, span, part)
                        owners.append(me ^ m)
                        lands.append((land_far, at))
                        at += 1
                add(owners, lands, first, size)
                for at, m in enumerate(mid[1:]):
                    send(me ^ m, span, part, land_mid, mid_recv, at, (me ^ m, core))
            else:
                for m in mid[1:]:
                    for z in far[::-1]:
                        arrived(land_mid, mid_recv, at, span, part)
                        owners.append(me ^ z)
                        lands.append((land_mid, at))
                        at += 1
                add(owners, lands, first, size)
                for at, z in enumerate(far[1:]):
                    send(me ^ z, span, part, land_far, far_recv, at, (me ^ z, core))
        part = tick - 2 - AHEAD
        if 0 <= part < parts:
            first, size = spans[part]
            span = pl.ds(first, size)
            land, sems, width = land_far, far_recv, len(far) - 1
            if far_second(part):
                land, sems, width = land_mid, mid_recv, len(mid) - 1
            for at in range(width):
                arrived(land, sems, at, span, part)

            def finish(i, carry, first=first, land=land, width=width):
                at = first + i
                total = acc[me, at].astype(jnp.float32)
                for j in range(width):
                    total = total + land[j, at].astype(jnp.float32)
                final[core, at] = total.astype(jnp.bfloat16)
                return carry

            lax.fori_loop(0, size, finish, 0)
            copy = pltpu.make_async_remote_copy(
                src_ref=final.at[core, span],
                dst_ref=final.at[core, span],
                send_sem=end_send.at[part],
                recv_sem=end_recv.at[part],
                device_id=partner,
                device_id_type=MESH_IDS,
            )
            copy.start()
            ends.append(copy)
        part = tick - 3 - AHEAD
        if 0 <= part < parts:
            first, size = spans[part]
            ref = final.at[1 - core, pl.ds(first, size)]
            pltpu.make_async_copy(ref, ref, end_recv.at[part]).wait()
            if part == 0:
                store(final.at[:, pl.ds(first, size)], head_out)
                for load in owned:
                    load.wait()
                continue

            def group(i, carry, first=first):
                shampoo_rows(final, master, stats, roots, grad_flat, flat, turn, first + i * 8, 8)
                return carry

            lax.fori_loop(0, size // 8, group, 0)
            if size % 8:
                shampoo_rows(
                    final, master, stats, roots, grad_flat, flat, turn, first + size // 8 * 8, size % 8
                )
            span = pl.ds(first, size)
            store(stats.at[span], stats_out.at[span])
            if not whole_rows:
                store(grad_flat.at[span], grad_out.at[span])
                store(master.at[span], master_out.at[span])
    if whole_rows:
        store(grad_flat, grad_out)
        store(master, master_out)
    for copy in sent + ends:
        copy.wait_send()
    for copy in stores:
        copy.wait()


def deliver_blocks(grads, head, code, master, stats, roots, devices):
    count = code.shape[0] // devices
    more = head.shape[1]
    spans = [(count, more)] + spans_of(count)
    first, second, third = bit_split(devices)
    n_mid, n_last, n_far = 1 << first, 1 << second, 1 << third
    tile = (count + more, HALF, LANES)
    dma = pltpu.SemaphoreType.DMA
    lands = [(n_last - 1) * n_mid * n_far, (n_mid - 1) * n_far, (n_far - 1) * n_mid]
    grads = [g.reshape(-1, HALF, LANES) for g in grads]
    any_space = pl.BlockSpec(memory_space=pl.ANY)
    steps = len(spans)
    return pl.pallas_call(
        functools.partial(deliver_kernel, devices, spans),
        out_shape=[
            jax.ShapeDtypeStruct((2, more, HALF, LANES), BF16),
            jax.ShapeDtypeStruct(master.shape, F32),
            jax.ShapeDtypeStruct(stats.shape, F32),
            jax.ShapeDtypeStruct(master.shape, F32),
        ],
        in_specs=[pl.BlockSpec(memory_space=pltpu.SMEM)] + [any_space] * (4 + len(grads)),
        out_specs=[any_space] * 4,
        scratch_shapes=[
            pltpu.VMEM((sum(g.shape[0] for g in grads), HALF, LANES), jnp.bfloat16),
            pltpu.VMEM((devices,) + tile, jnp.bfloat16),
        ]
        + [pltpu.VMEM((k,) + tile, jnp.bfloat16) for k in lands]
        + [
            pltpu.VMEM((2,) + tile, jnp.bfloat16),
            pltpu.VMEM(master.shape, F32),
            pltpu.VMEM(stats.shape, F32),
            pltpu.VMEM(roots.shape, F32),
            pltpu.VMEM(master.shape, F32),
            pltpu.VMEM((2, 8 * HALF, LANES), F32),
            pltpu.VMEM((2, 8 * HALF, LANES), F32),
            dma((len(grads) + 1,)),
            dma((sum(lands) * steps,)),
            dma((lands[0], steps)),
            dma((lands[1], steps)),
            dma((lands[2], steps)),
            dma((steps,)),
            dma((steps,)),
            dma((3,)),
            dma((3 * steps,)),
        ],
        compiler_params=pltpu.CompilerParams(
            collective_id=2, has_side_effects=True, vmem_limit_bytes=60 * 2**20
        ),
    )(code, head, *grads, master, stats, roots)


def block_places(owner_slot):
    codes = []
    base = 0
    for rows, cols in matrix_list():
        strips, pairs = rows // BLOCK, cols // LANES
        grid = base + 2 * (np.arange(pairs)[None, :] * strips + np.arange(strips)[:, None])
        codes.append((2 * grid[:, :, None] + np.arange(2)[None, None, :]).reshape(-1))
        base += 2 * strips * pairs
    code = np.concatenate(codes).astype(np.int32)
    slots = np.arange(code.shape[0], dtype=np.int32)
    found = jnp.sum(
        jnp.where(owner_slot[:, None] == slots[None, :], code[:, None], 0), axis=0, dtype=jnp.int32
    )
    return found


ROWS = ROW_SLOTS * WIDTH
N_IN = C // LANES
N_MID = M // LANES
WIDE = 1024
F32 = jnp.float32
BF16 = jnp.bfloat16


def dot(a, b, ca, cb):
    return lax.dot_general(a, b, (((ca,), (cb,)), ((), ())), preferred_element_type=F32)


def lanes_of(ref, first, count):
    return jnp.concatenate([ref[first + i] for i in range(count)], axis=-1)


def half_tanh(v):
    return 0.5 * (1.0 + jnp.tanh(0.5 * v))


class Net:
    def __init__(self, devices):
        first, second, third = bit_split(devices)
        self.me = lax.axis_index("dp")
        self.core = lax.axis_index("rows")
        self.near, self.far = 1 << (first + second), 1 << third
        self.near_at = lax.rem(self.me, self.near)
        self.far_at = self.me // self.near
        self.partner = (self.me, 1 - self.core)
        self.near_peers = [(self.me ^ m, self.core) for m in range(1, self.near)]
        self.near_slots = [self.near_at ^ m for m in range(1, self.near)]
        self.far_peers = [(self.me ^ (m * self.near), self.core) for m in range(1, self.far)]
        self.far_slots = [self.far_at ^ m for m in range(1, self.far)]

    def hello(self):
        barrier = pltpu.get_barrier_semaphore()
        for peer in [self.partner] + self.near_peers + self.far_peers:
            pl.semaphore_signal(barrier, inc=1, device_id=peer, device_id_type=MESH_IDS)

    def ready(self):
        pl.semaphore_wait(
            pltpu.get_barrier_semaphore(), 1 + len(self.near_peers) + len(self.far_peers)
        )


def slots_total(devices):
    first, second, third = bit_split(devices)
    return 2 + (1 << (first + second)) + (1 << third)


def remote(src, dst, send_sem, recv_sem, device):
    copy = pltpu.make_async_remote_copy(
        src_ref=src,
        dst_ref=dst,
        send_sem=send_sem,
        recv_sem=recv_sem,
        device_id=device,
        device_id_type=MESH_IDS,
    )
    copy.start()
    return copy


def landed(ref, sem):
    pltpu.make_async_copy(ref, ref, sem).wait()


def plain_sum(values, counts):
    total = values[0]
    for value in values[1:]:
        total = total + value
    return total


def pooled_moments(rows):
    def merge(values, counts):
        n = counts[0]
        for more in counts[1:]:
            n = n + more
        sums = values[0][:rows]
        spread = values[0][rows:]
        for value in values[1:]:
            sums = sums + value[:rows]
            spread = spread + value[rows:]
        mean = sums / n
        for value, own in zip(values, counts):
            gap = value[:rows] / own - mean
            spread = spread + own * gap * gap
        return jnp.concatenate([sums, spread], axis=0)

    return merge


def reduce_all(net, value, bufs, send_sem, recv_sem, merge, own_count=None, pair_count=0.0, fillers=()):
    fillers = list(fillers) + [None] * 3
    copies = []
    stages = [
        (0, net.core, [net.partner], [1 - net.core], 2),
        (2, net.near_at, net.near_peers, net.near_slots, net.near),
        (2 + net.near, net.far_at, net.far_peers, net.far_slots, net.far),
    ]
    for step, (base, mine, peers, slots, size) in enumerate(stages):
        bufs[base + mine] = value
        for i, peer in enumerate(peers):
            copies.append(
                remote(
                    bufs.at[base + mine],
                    bufs.at[base + mine],
                    send_sem.at[base + i],
                    recv_sem.at[base + mine],
                    peer,
                )
            )
        if fillers[step] is not None:
            fillers[step]()
        for slot in slots:
            landed(bufs.at[base + slot], recv_sem.at[base + slot])
        if own_count is None:
            counts = [None] * size
        elif step == 0:
            rest = pair_count - own_count
            first = net.core == 0
            counts = [jnp.where(first, own_count, rest), jnp.where(first, rest, own_count)]
        else:
            counts = [pair_count * (1 if step == 1 else net.near)] * size
        value = merge([bufs[base + j] for j in range(size)], counts)
    return value, copies


def column_sum(value):
    return jnp.sum(value.reshape(-1, 8, LANES), axis=0)


def local_moments(z, count, live, own_count, stage, masked):
    quarter = z.shape[1] // 4

    def slab(j, carry):
        total = jnp.zeros((8, LANES), F32)
        for q in range(4):
            rows = pl.ds(q * quarter, quarter)
            v = z[j, rows]
            if masked:
                v = v * live[rows]
                z[j, rows] = v
            total = total + column_sum(v)
        sums = jnp.sum(total, axis=0, keepdims=True)
        mean = sums / own_count
        spread = jnp.zeros((8, LANES), F32)
        for q in range(4):
            rows = pl.ds(q * quarter, quarter)
            d = (z[j, rows] - mean) * live[rows]
            spread = spread + column_sum(d * d)
        stage[pl.ds(j, 1)] = sums
        stage[pl.ds(count + j, 1)] = jnp.sum(spread, axis=0, keepdims=True)
        return carry

    lax.fori_loop(0, count, slab, 0)


def window(ref, down, right):
    batch = ref.shape[3]
    parts = [
        ref[j, pl.ds(down, ROW_SLOTS), pl.ds(right, WIDTH)].reshape(ROWS * batch, LANES)
        for j in range(N_MID)
    ]
    return jnp.concatenate(parts, axis=-1)


def clear_edges(ref, core):
    shape = ref.shape
    zero = jnp.zeros((shape[0], 1) + shape[2:], ref.dtype)
    ref[:, pl.ds(jnp.where(core == 0, 0, ROW_SLOTS + 1), 1)] = zero
    column = jnp.zeros(shape[:2] + (1,) + shape[3:], ref.dtype)
    ref[:, :, 0:1] = column
    ref[:, :, WIDTH + 1 : WIDTH + 2] = column


def send_edge(ref, net, send_sem, recv_sem):
    edge = jnp.where(net.core == 0, ROW_SLOTS, 1)
    there = jnp.where(net.core == 0, 0, ROW_SLOTS + 1)
    return remote(
        ref.at[:, edge, pl.ds(1, WIDTH)],
        ref.at[:, there, pl.ds(1, WIDTH)],
        send_sem,
        recv_sem,
        net.partner,
    )


def edge_landed(ref, net, recv_sem):
    here = jnp.where(net.core == 0, ROW_SLOTS + 1, 0)
    landed(ref.at[:, here, pl.ds(1, WIDTH)], recv_sem)


def edge_first(net, fill, send):
    edge = jnp.where(net.core == 0, ROW_SLOTS - 1, 0)
    fill(edge)
    copy = send()
    for step in range(1, ROW_SLOTS):
        fill(lax.rem(edge + step, ROW_SLOTS))
    return copy


def load_all(pairs, sems):
    copies = []
    for i, (src, dst) in enumerate(pairs):
        copy = pltpu.make_async_copy(src, dst, sems.at[i])
        copy.start()
        copies.append(copy)
    return copies


def forward_kernel(devices, total_count, *refs):
    refs = list(refs)
    take = lambda n: [refs.pop(0) for _ in range(n)]
    w_h = [take(3) for _ in range(LAYERS)]
    x_in, = take(1)
    params_of = take(LAYERS)
    live, = take(1)
    kept_h = [take(5) for _ in range(LAYERS)]
    stats_of = [take(3) for _ in range(LAYERS)]
    xn_h, xnb_h, pooled = take(3)
    wi, wm, wo, za, hp, zb, hb, zc, xn, xnb = take(10)
    stage_m, stage_c = take(2)
    bufs_of = [take(3) for _ in range(LAYERS)]
    in_sem, out_sem, send_sem, recv_sem, halo_sem = take(5)

    net = Net(devices)
    net.hello()
    loading = {}
    places = [wi, wm, wo]

    def start(at, which):
        copy = pltpu.make_async_copy(w_h[at][which], places[which], in_sem.at[at, which])
        copy.start()
        loading[at, which] = copy

    for which in range(3):
        start(0, which)
    clear_edges(hp, net.core)
    own_count = jnp.sum(column_sum(live[...]), axis=0, keepdims=True)
    pair_count = total_count / devices
    quarter = za.shape[1] // ROW_SLOTS
    batch = quarter // WIDTH
    stores = []
    sends = []

    def store(src, dst):
        copy = pltpu.make_async_copy(src, dst, out_sem.at[len(stores)])
        copy.start()
        stores.append(copy)

    def layer(at):
        params = params_of[at]
        stat_a, stat_b, stat_c = stats_of[at]
        za_h, hp_h, zb_h, hb_h, zc_h = kept_h[at]
        later = at + 1 < LAYERS

        def norm(z, n, stage, which, masked, stat):
            local_moments(z, n, live, own_count, stage, masked)
            if at == 0 and which == 0:
                net.ready()
            total, copies = reduce_all(
                net,
                stage[...],
                bufs_of[at][which],
                send_sem.at[3 * at + which],
                recv_sem.at[3 * at + which],
                pooled_moments(n),
                own_count,
                pair_count,
            )
            sends.extend(copies)
            stat[0:n] = total[:n] / total_count
            stat[n : 2 * n] = lax.rsqrt(total[n:] / total_count + EPS_NORM)

        def affine(stat, n, gain_at, j):
            mean = stat[pl.ds(j, 1)]
            scale = stat[pl.ds(n + j, 1)] * params[pl.ds(gain_at + j, 1)]
            return mean, scale, params[pl.ds(gain_at + n + j, 1)]

        loading[at, 0].wait()
        if at:
            for copy in stores[:5]:
                copy.wait()
        x = lanes_of(xnb, 0, N_IN) if at else x_in[...]
        product = dot(x, lanes_of(wi, 0, N_MID), 1, 0)
        for j in range(N_MID):
            za[j] = product[:, j * LANES : (j + 1) * LANES]
        if later:
            start(at + 1, 0)
        norm(za, N_MID, stage_m, 0, at == 0, stat_a)
        store(za, za_h)

        def fill_hidden(slot):
            rows = pl.ds(slot * quarter, quarter)

            def slab(j, carry):
                mean, scale, shift = affine(stat_a, N_MID, 0, j)
                y = (za[j, rows] - mean) * scale + shift
                h = (live[rows] * (y * half_tanh(y))).astype(BF16)
                hp[j, pl.ds(slot + 1, 1), pl.ds(1, WIDTH)] = h.reshape(1, WIDTH, batch, LANES)
                return carry

            lax.fori_loop(0, N_MID, slab, 0)

        edge = edge_first(
            net, fill_hidden, lambda: send_edge(hp, net, halo_sem.at[at, 0], halo_sem.at[at, 1])
        )
        loading[at, 1].wait()
        zb[...] = jnp.zeros(zb.shape, F32)

        def tap(t):
            k = pl.ds(pl.multiple_of(t * M, M), M)
            part = dot(
                window(hp, t // 3, lax.rem(t, 3)),
                jnp.concatenate([wm[j, k] for j in range(N_MID)], axis=-1),
                1,
                0,
            )
            for j in range(N_MID):
                zb[j] = zb[j] + part[:, j * LANES : (j + 1) * LANES]

        def middle(i, carry):
            tap(i + 3)
            return carry

        def outer(i, carry):
            tap(jnp.where(i < 3, i, i + 3))
            return carry

        lax.fori_loop(0, 3, middle, 0)
        edge_landed(hp, net, halo_sem.at[at, 1])
        edge.wait_send()
        store(hp, hp_h)
        lax.fori_loop(0, 6, outer, 0)
        if later:
            start(at + 1, 1)
        norm(zb, N_MID, stage_m, 1, True, stat_b)
        store(zb, zb_h)

        def fill_second(j, carry):
            mean, scale, shift = affine(stat_b, N_MID, 2 * N_MID, j)
            for q in range(4):
                rows = pl.ds(q * quarter, quarter)
                y = (zb[j, rows] - mean) * scale + shift
                hb[j, rows] = (live[rows] * (y * half_tanh(y))).astype(BF16)
            return carry

        lax.fori_loop(0, N_MID, fill_second, 0)
        store(hb, hb_h)
        loading[at, 2].wait()

        def expand(g, carry):
            part = dot(lanes_of(hb, 0, N_MID), lanes_of(wo, g * N_MID, N_MID), 1, 0)
            for j in range(N_MID):
                zc[g * N_MID + j] = part[:, j * LANES : (j + 1) * LANES]
            return carry

        lax.fori_loop(0, N_IN // N_MID, expand, 0)
        if later:
            start(at + 1, 2)
        store(zc, zc_h)
        norm(zc, N_IN, stage_c, 2, False, stat_c)

        def finish(j, carry):
            mean, scale, shift = affine(stat_c, N_IN, 4 * N_MID, j)
            pool = jnp.zeros((batch, LANES), F32)
            for q in range(4):
                rows = pl.ds(q * quarter, quarter)
                if at:
                    x = xn[j, rows]
                else:
                    x = x_in[rows, pl.ds(pl.multiple_of(j * LANES, LANES), LANES)].astype(F32)
                y = (zc[j, rows] - mean) * scale + shift + x
                out = live[rows] * (y * half_tanh(y))
                if later:
                    xn[j, rows] = out
                    xnb[j, rows] = out.astype(BF16)
                else:
                    pool = pool + jnp.sum(out.reshape(WIDTH, batch, LANES), axis=0)
            if not later:
                pooled[j] = pool
            return carry

        lax.fori_loop(0, N_IN, finish, 0)
        if later:
            store(xn, xn_h)
            store(xnb, xnb_h)

    for at in range(LAYERS):
        layer(at)
    for copy in stores[5:]:
        copy.wait()
    for copy in sends:
        copy.wait_send()


def forward_pass(devices, total_count, x, weights, params, live):
    rows = live.shape[0]
    batch = rows // ROWS
    shape = jax.ShapeDtypeStruct
    any_space = pl.BlockSpec(memory_space=pl.ANY)
    vmem = pl.BlockSpec(memory_space=pltpu.VMEM)
    fields = [
        shape((N_MID, rows, LANES), F32),
        shape((N_MID, ROW_SLOTS + 2, WIDTH + 2, batch, LANES), BF16),
        shape((N_MID, rows, LANES), F32),
        shape((N_MID, rows, LANES), BF16),
        shape((N_IN, rows, LANES), F32),
    ]
    stats = [shape((2 * n, LANES), F32) for n in (N_MID, N_MID, N_IN)]
    last = [shape((N_IN, rows, LANES), F32), shape((N_IN, rows, LANES), BF16)]
    big = lambda s: pltpu.VMEM(s.shape, s.dtype)
    total = slots_total(devices)
    dma = pltpu.SemaphoreType.DMA
    small_ins = [x] + list(params) + [live]
    out = pl.pallas_call(
        functools.partial(forward_kernel, devices, total_count),
        out_shape=fields * LAYERS + stats * LAYERS + last + [shape((N_IN, batch, LANES), F32)],
        in_specs=[any_space] * len(weights) + [vmem] * len(small_ins),
        out_specs=[any_space] * (5 * LAYERS) + [vmem] * (3 * LAYERS) + [any_space] * 2 + [vmem],
        scratch_shapes=[big(w) for w in weights[:3]]
        + [big(s) for s in fields + last]
        + [pltpu.VMEM((2 * N_MID, LANES), F32), pltpu.VMEM((2 * N_IN, LANES), F32)]
        + [pltpu.VMEM((total, 2 * n, LANES), F32) for n in (N_MID, N_MID, N_IN)] * LAYERS
        + [
            dma((LAYERS, 3)),
            dma((5 * LAYERS + 2,)),
            dma((3 * LAYERS, total)),
            dma((3 * LAYERS, total)),
            dma((LAYERS, 2)),
        ],
        compiler_params=pltpu.CompilerParams(
            collective_id=3, has_side_effects=True, vmem_limit_bytes=60 * 2**20
        ),
    )(*weights, *small_ins)
    kept = [
        list(out[5 * at : 5 * at + 5]) + list(out[5 * LAYERS + 3 * at : 5 * LAYERS + 3 * at + 3])
        for at in range(LAYERS)
    ]
    return kept, out[-3], out[-2], out[-1]


def head_kernel(
    devices, area, pooled, head_h, bias, pick, point, numbers, hot,
    extra, gtop, gh_h,
    head, send_pool, recv_pool, low, logits_all, logits, g_low, gh, gh_there, gh_other, gt,
    in_sem, out_sem, send_sem, recv_sem,
):
    net = Net(devices)
    net.hello()
    load = pltpu.make_async_copy(head_h, head, in_sem)
    load.start()
    half = send_pool.shape[1]
    mine = pl.ds(pl.multiple_of(net.core * half, half), half)
    theirs = pl.ds(pl.multiple_of((1 - net.core) * half, half), half)
    for j in range(N_IN):
        send_pool[j] = pooled[j, theirs].astype(BF16)
    net.ready()
    sends = [remote(send_pool, recv_pool, send_sem.at[0], recv_sem.at[0], net.partner)]
    load.wait()
    landed(recv_pool, recv_sem.at[0])
    for j in range(N_IN):
        low[j] = ((pooled[j, mine] + recv_pool[j].astype(F32)) / area).astype(BF16)
    logits[...] = dot(lanes_of(low, 0, N_IN), lanes_of(head, 0, N_IN), 1, 1) + bias[0:1, :]
    logits_all[net.core, net.far_at, net.near_at] = logits[...].astype(BF16)
    at = 1
    ref = logits_all.at[net.core, net.far_at, net.near_at]
    for peer in net.far_peers:
        sends.append(
            remote(ref, ref, send_sem.at[at], recv_sem.at[1 + net.near + net.far_at], peer)
        )
        at += 1

    own = logits[...]
    keep = lax.broadcasted_iota(jnp.int32, own.shape, 1) < CLASSES
    peak = jnp.max(jnp.where(keep, own, -3.0e38), axis=1, keepdims=True)
    powers = jnp.where(keep, jnp.exp(jnp.where(keep, own - peak, 0.0)), 0.0)
    log_total = peak + jnp.log(jnp.sum(powers, axis=1, keepdims=True))
    softmax = jnp.where(keep, jnp.exp(jnp.where(keep, own - log_total, 0.0)), 0.0)
    picked = jnp.sum(own * hot[...], axis=1, keepdims=True)

    for slot in net.far_slots:
        landed(
            logits_all.at[net.core, slot, net.near_at], recv_sem.at[1 + net.near + slot]
        )
    group = logits_all.at[net.core, :, net.near_at]
    for peer in net.near_peers:
        sends.append(remote(group, group, send_sem.at[at], recv_sem.at[1 + net.near_at], peer))
        at += 1
    for slot in net.near_slots:
        landed(logits_all.at[net.core, :, slot], recv_sem.at[1 + slot])
    ref = logits_all.at[net.core]
    sends.append(
        remote(ref, ref, send_sem.at[at], recv_sem.at[1 + net.near + net.far], net.partner)
    )
    at += 1
    landed(logits_all.at[1 - net.core], recv_sem.at[1 + net.near + net.far])
    every = logits_all[...].reshape(-1, WIDE)
    gap = jnp.where(keep, own - dot(pick[...], every, 1, 0), 0.0)
    incoming = dot(point[...], every, 1, 0)
    weight = numbers[:, 0:1]
    terms = weight * (
        log_total - picked + MATCH_WEIGHT * (jnp.sum(gap * gap, axis=1, keepdims=True) / CLASSES)
    )
    grad = (
        weight * (softmax - hot[...])
        + MATCH_WEIGHT
        * (2.0 / CLASSES)
        * (weight * gap - (incoming - numbers[:, 1:2] * own))
    ) / numbers[:, 2:3]
    g_low[...] = jnp.where(keep, grad, 0.0).astype(BF16)
    bias_sum = jnp.sum(g_low[...].astype(F32), axis=0, keepdims=True)
    extra[...] = jnp.zeros(extra.shape, F32)
    for j in range(WIDE // LANES):
        extra[j : j + 1] = bias_sum[:, j * LANES : (j + 1) * LANES]
    extra[WIDE // LANES : WIDE // LANES + 1] = jnp.zeros((1, LANES), F32) + jnp.sum(
        terms, axis=0, keepdims=True
    )
    gt_view = gt.at[:, net.core]
    for j in range(N_IN):
        gt[j, net.core] = (dot(g_low[...], head[j], 1, 0) / area).astype(BF16)
    sends.append(
        remote(
            gt_view, gt_view, send_sem.at[at], recv_sem.at[2 + net.near + net.far], net.partner
        )
    )

    at += 1
    block = (WIDE // 2 // HALF, HALF, LANES)
    cut = WIDE // 2
    mine_at = pl.multiple_of(net.core * cut, cut)
    theirs_at = pl.multiple_of((1 - net.core) * cut, cut)

    def grad_there(j, carry):
        part = dot(g_low[:, pl.ds(theirs_at, cut)], low[j], 0, 0)
        gh_there[j] = part.astype(BF16).reshape(block)
        return carry

    lax.fori_loop(0, N_IN, grad_there, 0)
    sends.append(
        remote(gh_there, gh_other, send_sem.at[at], recv_sem.at[3 + net.near + net.far], net.partner)
    )
    landed(gt.at[:, 1 - net.core], recv_sem.at[2 + net.near + net.far])
    for j in range(N_IN):
        gtop[j] = jnp.concatenate([gt[j, 0], gt[j, 1]], axis=0).astype(F32)
    landed(gh_other, recv_sem.at[3 + net.near + net.far])

    def grad_here(j, carry):
        part = dot(g_low[:, pl.ds(mine_at, cut)], low[j], 0, 0)
        gh[j] = (part.reshape(block) + gh_other[j].astype(F32)).astype(BF16)
        return carry

    lax.fori_loop(0, N_IN, grad_here, 0)
    store = pltpu.make_async_copy(gh, gh_h, out_sem)
    store.start()
    store.wait()
    for copy in sends:
        copy.wait_send()


def head_step(devices, pooled, head, bias, pick, point, numbers, hot):
    batch = pooled.shape[1]
    half = batch // 2
    shape = jax.ShapeDtypeStruct
    any_space = pl.BlockSpec(memory_space=pl.ANY)
    vmem = pl.BlockSpec(memory_space=pltpu.VMEM)
    dma = pltpu.SemaphoreType.DMA
    count = 4 + slots_total(devices)
    first, second, third = bit_split(devices)
    near, far = 1 << (first + second), 1 << third
    return pl.pallas_call(
        functools.partial(head_kernel, devices, float(HEIGHT * WIDTH)),
        out_shape=[
            shape((16, LANES), F32),
            shape((N_IN, batch, LANES), F32),
            shape((N_IN, WIDE // 2 // HALF, HALF, LANES), BF16),
        ],
        in_specs=[vmem, any_space] + [vmem] * 5,
        out_specs=[vmem, vmem, any_space],
        scratch_shapes=[
            pltpu.VMEM((N_IN, WIDE, LANES), BF16),
            pltpu.VMEM((N_IN, half, LANES), BF16),
            pltpu.VMEM((N_IN, half, LANES), BF16),
            pltpu.VMEM((N_IN, half, LANES), BF16),
            pltpu.VMEM((2, far, near, half, WIDE), BF16),
            pltpu.VMEM((half, WIDE), F32),
            pltpu.VMEM((half, WIDE), BF16),
            pltpu.VMEM((N_IN, WIDE // 2 // HALF, HALF, LANES), BF16),
            pltpu.VMEM((N_IN, WIDE // 2 // HALF, HALF, LANES), BF16),
            pltpu.VMEM((N_IN, WIDE // 2 // HALF, HALF, LANES), BF16),
            pltpu.VMEM((N_IN, 2, half, LANES), BF16),
            dma(()),
            dma(()),
            dma((count,)),
            dma((count,)),
        ],
        compiler_params=pltpu.CompilerParams(
            collective_id=5, has_side_effects=True, vmem_limit_bytes=60 * 2**20
        ),
    )(pooled, head, bias, pick, point, numbers, hot)


def pieces(part, j):
    return part[:, j * LANES : (j + 1) * LANES].astype(BF16).reshape(-1, 2, HALF, LANES)


def backward_kernel(devices, total_count, *refs):
    refs = list(refs)
    take = lambda n: [refs.pop(0) for _ in range(n)]
    names = ["zc", "hb", "hp", "zb", "za", "wi", "wm", "wo"]
    source = {}
    source["xf", 1], source["xb", 1] = take(2)
    for at in (0, 1):
        for name in names:
            source[name, at] = refs.pop(0)
    x_in, gtop = take(2)
    stats_of = [take(3) for _ in range(LAYERS)]
    params_of = take(LAYERS)
    live, extra = take(2)
    out_of = [take(3) for _ in range(LAYERS)]
    small_of = take(LAYERS)
    field, xb, zc, hb, hp, zb, za, wi, wm, wo = take(10)
    place = dict(xf=field, xb=xb, zc=zc, hb=hb, hp=hp, zb=zb, za=za, wi=wi, wm=wm, wo=wo)
    g_side, g_mid, r_side, r_mid = take(4)
    ec, ep, ea, ub = take(4)
    stage_m, stage_c = take(2)
    bufs_of = [take(3) for _ in range(LAYERS)]
    in_sem, out_sem, send_sem, recv_sem, halo_sem, pair_sem = take(6)

    net = Net(devices)
    net.hello()
    order = ["zc", "xf", "wo", "zb", "hb", "hp", "wm", "za", "wi", "xb"]
    loading = {}

    def start(name, at):
        copy = pltpu.make_async_copy(
            source[name, at], place[name], in_sem.at[at, order.index(name)]
        )
        copy.start()
        loading[name, at] = copy

    def need(name, at):
        loading[name, at].wait()

    for name in order:
        start(name, 1)
    clear_edges(ep, net.core)
    quarter = za.shape[1] // ROW_SLOTS
    batch = quarter // WIDTH
    groups = N_IN // N_MID
    side_rows, mid_rows = M // 32, 9 * M // 32
    sends = []
    stored = []

    def store(src, dst):
        copy = pltpu.make_async_copy(src, dst, out_sem.at[len(stored)])
        copy.start()
        stored.append(copy)
        return copy

    def slope(y):
        sigma = half_tanh(y)
        return sigma * (1.0 + y * (1.0 - sigma))

    def row(ref, j):
        return ref[pl.ds(j, 1)]

    def swap(grad, other, at, which):
        return remote(
            grad.at[:, 1 - net.core],
            other,
            pair_sem.at[at, 0, which],
            pair_sem.at[at, 1, which],
            net.partner,
        )

    def fold(copy, grad, other, at, which, out):
        landed(other, pair_sem.at[at, 1, which])
        copy.wait_send()

        def step(i, carry):
            part = pl.ds(i * 16, 16)
            other[part] = (grad[part, net.core].astype(F32) + other[part].astype(F32)).astype(BF16)
            return carry

        lax.fori_loop(0, grad.shape[0] // 16, step, 0)
        return store(other, out)

    def layer(at, fillers):
        top = at == 1
        stat_a, stat_b, stat_c = stats_of[at]
        params, small = params_of[at], small_of[at]
        gi_h, gm_h, go_h = out_of[at]
        state = {}

        def refill(name):
            if top:
                start(name, 0)

        def totals(stage, which, small_at, n, fillers):
            total, copies = reduce_all(
                net,
                stage[...],
                bufs_of[at][which],
                send_sem.at[3 * at + which],
                recv_sem.at[3 * at + which],
                plain_sum,
                fillers=fillers,
            )
            sends.extend(copies)
            small[small_at : small_at + 2 * n] = total[: 2 * n]
            return total

        need("zc", at)
        if top:
            need("xf", at)

        def slab_c(j, carry):
            mean, scale = row(stat_c, j), row(stat_c, N_IN + j)
            gain, shift = row(params, 4 * N_MID + j), row(params, 4 * N_MID + N_IN + j)
            total = jnp.zeros((8, LANES), F32)
            crossed = jnp.zeros((8, LANES), F32)
            for q in range(4):
                rows = pl.ds(q * quarter, quarter)
                normed = (zc[j, rows] - mean) * scale
                if top:
                    x = field[j, rows]
                    g = jnp.concatenate([gtop[j]] * WIDTH, axis=0)
                else:
                    x = x_in[rows, pl.ds(pl.multiple_of(j * LANES, LANES), LANES)].astype(F32)
                    g = field[j, rows]
                u = g * live[rows] * slope(normed * gain + shift + x)
                field[j, rows] = u
                total = total + column_sum(u)
                crossed = crossed + column_sum(u * normed)
            stage_c[pl.ds(j, 1)] = jnp.sum(crossed, axis=0, keepdims=True)
            stage_c[pl.ds(N_IN + j, 1)] = jnp.sum(total, axis=0, keepdims=True)
            return carry

        lax.fori_loop(0, N_IN, slab_c, 0)
        if top:
            stage_c[2 * N_IN :] = extra[...]
            net.ready()
        else:
            stage_c[2 * N_IN :] = jnp.zeros(extra.shape, F32)
        total_c = totals(stage_c, 2, 4 * N_MID, N_IN, fillers)
        small[4 * N_MID + 2 * N_IN :] = total_c[2 * N_IN :]

        def back_c(j, carry):
            mean, scale = row(stat_c, j), row(stat_c, N_IN + j)
            gain = row(params, 4 * N_MID + j)
            cross = row(small, 4 * N_MID + j) / total_count
            plain = row(small, 4 * N_MID + N_IN + j) / total_count
            for q in range(4):
                rows = pl.ds(q * quarter, quarter)
                normed = (zc[j, rows] - mean) * scale
                e = live[rows] * ((gain * scale) * (field[j, rows] - plain - normed * cross))
                ec[j, rows] = e.astype(BF16)
            return carry

        lax.fori_loop(0, N_IN, back_c, 0)
        refill("zc")
        need("wo", at)
        product = dot(lanes_of(ec, 0, N_IN), lanes_of(wo, 0, N_IN), 1, 1)
        for j in range(N_MID):
            ub[j] = product[:, j * LANES : (j + 1) * LANES]
        refill("wo")
        need("zb", at)

        def sums_of(z_ref, stat, gain_at):
            def slab(j, carry):
                mean, scale = row(stat, j), row(stat, N_MID + j)
                gain, shift = row(params, gain_at + j), row(params, gain_at + N_MID + j)
                total = jnp.zeros((8, LANES), F32)
                crossed = jnp.zeros((8, LANES), F32)
                for q in range(4):
                    rows = pl.ds(q * quarter, quarter)
                    normed = (z_ref[j, rows] - mean) * scale
                    u = ub[j, rows] * live[rows] * slope(normed * gain + shift)
                    ub[j, rows] = u
                    total = total + column_sum(u)
                    crossed = crossed + column_sum(u * normed)
                stage_m[pl.ds(j, 1)] = jnp.sum(crossed, axis=0, keepdims=True)
                stage_m[pl.ds(N_MID + j, 1)] = jnp.sum(total, axis=0, keepdims=True)
                return carry

            lax.fori_loop(0, N_MID, slab, 0)

        def back_of(z_ref, stat, gain_at, j, rows):
            normed = (z_ref[j, rows] - row(stat, j)) * row(stat, N_MID + j)
            cross = row(small, gain_at + j) / total_count
            plain = row(small, gain_at + N_MID + j) / total_count
            factor = row(params, gain_at + j) * row(stat, N_MID + j)
            return (live[rows] * (factor * (ub[j, rows] - plain - normed * cross))).astype(BF16)

        sums_of(zb, stat_b, 2 * N_MID)
        need("hb", at)

        def grad_out(first, last):
            def group(g, carry):
                part = dot(lanes_of(hb, 0, N_MID), lanes_of(ec, g * N_MID, N_MID), 0, 0)
                for j in range(N_MID):
                    g_side[pl.ds((g * N_MID + j) * side_rows, side_rows)] = pieces(part, j)
                return carry

            return lambda: lax.fori_loop(first, last, group, 0)

        totals(
            stage_m, 1, 2 * N_MID, N_MID,
            [grad_out(0, 1), grad_out(1, groups - 1), grad_out(groups - 1, groups)],
        )
        refill("hb")
        out_swap = swap(g_side, r_side, at, 0)

        def fill_b(slot):
            rows = pl.ds(slot * quarter, quarter)

            def slab(j, carry):
                e = back_of(zb, stat_b, 2 * N_MID, j, rows)
                ep[j, pl.ds(slot + 1, 1), pl.ds(1, WIDTH)] = e.reshape(1, WIDTH, batch, LANES)
                return carry

            lax.fori_loop(0, N_MID, slab, 0)

        edge = edge_first(
            net, fill_b, lambda: send_edge(ep, net, halo_sem.at[at, 0], halo_sem.at[at, 1])
        )
        refill("zb")
        need("hp", at)
        need("wm", at)
        ub[...] = jnp.zeros(ub.shape, F32)

        def grad_mid(first, last):
            def one(t, carry):
                part = dot(window(hp, t // 3, lax.rem(t, 3)), window(ep, 1, 1), 0, 0)
                for j in range(N_MID):
                    g_mid[pl.ds(j * mid_rows + t * side_rows, side_rows)] = pieces(part, j)
                return carry

            return lambda: lax.fori_loop(first, last, one, 0)

        def tap(t):
            k = pl.ds(pl.multiple_of(t * M, M), M)
            part = dot(
                window(ep, 2 - t // 3, 2 - lax.rem(t, 3)),
                jnp.concatenate([wm[j, k] for j in range(N_MID)], axis=-1),
                1,
                1,
            )
            for j in range(N_MID):
                ub[j] = ub[j] + part[:, j * LANES : (j + 1) * LANES]

        def middle(i, carry):
            tap(i + 3)
            return carry

        def outer(i, carry):
            tap(jnp.where(i < 3, i, i + 3))
            return carry

        lax.fori_loop(0, 3, middle, 0)
        edge_landed(ep, net, halo_sem.at[at, 1])
        edge.wait_send()
        lax.fori_loop(0, 6, outer, 0)
        refill("wm")
        out_store = fold(out_swap, g_side, r_side, at, 0, go_h)
        need("za", at)
        sums_of(za, stat_a, 0)
        out_store.wait()
        totals(stage_m, 0, 0, N_MID, [grad_mid(0, 2), grad_mid(2, 5), grad_mid(5, 9)])
        refill("hp")
        mid_swap = swap(g_mid, r_mid, at, 1)

        def fill_a(j, carry):
            for q in range(4):
                rows = pl.ds(q * quarter, quarter)
                ea[j, rows] = back_of(za, stat_a, 0, j, rows)
            return carry

        lax.fori_loop(0, N_MID, fill_a, 0)
        refill("za")
        if top:
            need("wi", at)

            def grad_field(g, carry):
                k = pl.ds(pl.multiple_of(g * M, M), M)
                part = dot(
                    lanes_of(ea, 0, N_MID),
                    jnp.concatenate([wi[j, k] for j in range(N_MID)], axis=-1),
                    1,
                    1,
                )
                for j in range(N_MID):
                    slab = g * N_MID + j
                    field[slab] = field[slab] + part[:, j * LANES : (j + 1) * LANES]
                return carry

            lax.fori_loop(0, groups, grad_field, 0)

        def grad_in(g, carry):
            if top:
                x = lanes_of(xb, g * N_MID, N_MID)
            else:
                x = x_in[:, pl.ds(pl.multiple_of(g * M, M), M)]
            part = dot(x, lanes_of(ea, 0, N_MID), 0, 0)
            for j in range(N_MID):
                g_side[pl.ds((j * groups + g) * side_rows, side_rows)] = pieces(part, j)
            return carry

        def first_part():
            if top:
                need("xb", at)
            lax.fori_loop(0, groups, grad_in, 0)
            state["swap"] = swap(g_side, r_side, at, 2)

        def second_part():
            state["mid"] = fold(mid_swap, g_mid, r_mid, at, 1, gm_h)

        def third_part():
            state["in"] = fold(state["swap"], g_side, r_side, at, 2, gi_h)
            state["mid"].wait()
            state["in"].wait()

        return [first_part, second_part, third_part]

    rest = layer(1, [])
    for step in layer(0, rest):
        step()
    for copy in sends:
        copy.wait_send()


def backward_pass(devices, total_count, xf, xb, kept, weights, x, gtop, params, live, extra):
    shape = jax.ShapeDtypeStruct
    any_space = pl.BlockSpec(memory_space=pl.ANY)
    vmem = pl.BlockSpec(memory_space=pltpu.VMEM)
    dma = pltpu.SemaphoreType.DMA
    total = slots_total(devices)
    rows = live.shape[0]
    big = lambda s: pltpu.VMEM(s.shape, s.dtype)
    each = []
    for at in range(LAYERS):
        za, hp, zb, hb, zc = kept[at][:5]
        each.append([zc, hb, hp, zb, za] + list(weights[3 * at : 3 * at + 3]))
    ins = [xf, xb] + each[0] + each[1]
    small_ins = [x, gtop]
    for at in range(LAYERS):
        small_ins += kept[at][5:]
    small_ins += list(params) + [live, extra]
    side = N_IN * M // 32
    middle = N_MID * 9 * M // 32
    small_rows = 4 * N_MID + 2 * N_IN + extra.shape[0]
    stage_rows = [2 * N_MID, 2 * N_MID, 2 * N_IN + extra.shape[0]]
    grads = [shape((n, HALF, LANES), BF16) for n in (side, middle, side)]
    out = pl.pallas_call(
        functools.partial(backward_kernel, devices, total_count),
        out_shape=grads * LAYERS + [shape((small_rows, LANES), F32)] * LAYERS,
        in_specs=[any_space] * len(ins) + [vmem] * len(small_ins),
        out_specs=[any_space] * (3 * LAYERS) + [vmem] * LAYERS,
        scratch_shapes=[big(a) for a in [xf, xb] + each[0]]
        + [
            pltpu.VMEM((side, 2, HALF, LANES), BF16),
            pltpu.VMEM((middle, 2, HALF, LANES), BF16),
            pltpu.VMEM((side, HALF, LANES), BF16),
            pltpu.VMEM((middle, HALF, LANES), BF16),
            pltpu.VMEM((N_IN, rows, LANES), BF16),
            pltpu.VMEM(kept[0][1].shape, BF16),
            pltpu.VMEM((N_MID, rows, LANES), BF16),
            pltpu.VMEM((N_MID, rows, LANES), F32),
            pltpu.VMEM((2 * N_MID, LANES), F32),
            pltpu.VMEM((stage_rows[2], LANES), F32),
        ]
        + [pltpu.VMEM((total, n, LANES), F32) for n in stage_rows] * LAYERS
        + [
            dma((LAYERS, 10)),
            dma((3 * LAYERS,)),
            dma((3 * LAYERS, total)),
            dma((3 * LAYERS, total)),
            dma((LAYERS, 2)),
            dma((LAYERS, 2, 3)),
        ],
        compiler_params=pltpu.CompilerParams(
            collective_id=6, has_side_effects=True, vmem_limit_bytes=62 * 2**20
        ),
    )(*ins, *small_ins)
    return out[: 3 * LAYERS], out[3 * LAYERS :]


def adamw(values_old, gradient, moment_one, moment_two, step_rate):
    one_new = BETA_FIRST * moment_one + (1.0 - BETA_FIRST) * gradient
    two_new = BETA_SECOND * moment_two + (1.0 - BETA_SECOND) * gradient * gradient
    fixed_one = 1.0 - BETA_FIRST**STEP
    fixed_two = 1.0 - BETA_SECOND**STEP
    update = one_new / fixed_one / (jnp.sqrt(two_new / fixed_two) + EPS_ADAM)
    return (one_new, two_new, values_old - step_rate * (update + DECAY_WEIGHT * values_old))


def body(
    images,
    row_split,
    labels,
    partners,
    image_weight,
    owner_slot,
    conv_master,
    conv_stats,
    conv_roots,
    head_master,
    head_moment_one,
    head_moment_two,
    small_params,
    small_moment_one,
    small_moment_two,
):
    devices = lax.axis_size("dp")
    core_index = lax.axis_index("rows")
    batch_size = images.shape[0]
    half_batch = batch_size // 2
    slot_count = images.shape[1]
    total_images = partners.shape[0]
    live_count = float(total_images * HEIGHT * WIDTH)
    owned = conv_master.shape[0]
    head_rows = head_master.shape[0]

    slot_index = (owner_slot // owned) * (2 * owned) + owner_slot % owned
    weights = list(bring_weights(conv_master, slot_index, devices))
    head_t = jnp.pad(head_master.T.astype(BF16), ((0, WIDE - CLASSES), (0, 0)))
    head_t, weights[0] = lax.optimization_barrier((head_t, weights[0]))
    head_all = lax.all_gather(head_t, "dp", axis=0)
    if head_rows != LANES:
        head_all = head_all.transpose(1, 0, 2).reshape(WIDE, N_IN, LANES).transpose(1, 0, 2)

    slot_ids = core_index * slot_count + jnp.arange(slot_count, dtype=jnp.int32)
    first_live = (ROW_SLOTS - row_split)[:, None]
    live = (slot_ids[None, :] >= first_live) & (slot_ids[None, :] < first_live + HEIGHT)
    rows = slot_count * WIDTH * batch_size
    live_rows = jnp.broadcast_to(
        live.T.astype(F32)[:, None, :, None], (slot_count, WIDTH, batch_size, LANES)
    ).reshape(rows, LANES)
    first = images.transpose(1, 2, 0, 3).reshape(rows, C)
    stride = 4 * M + 2 * C
    params = [
        small_params[at * stride : (at + 1) * stride].reshape(-1, LANES) for at in range(LAYERS)
    ]
    bias = jnp.pad(small_params[LAYERS * stride :], (0, WIDE - CLASSES))[None, :]

    kept, field, low, pooled = forward_pass(
        devices, live_count, first, weights, params, live_rows
    )

    def by_core(v):
        return v.reshape(devices, 2, half_batch).transpose(1, 0, 2).reshape(-1)

    weight_f = image_weight.astype(F32)
    weight_total = jnp.sum(weight_f)
    own_start = (lax.axis_index("dp") * 2 + core_index) * half_batch
    own_ids = own_start + jnp.arange(half_batch, dtype=jnp.int32)
    own_weight = lax.dynamic_slice_in_dim(weight_f, own_start, half_batch)
    own_partner = lax.dynamic_slice_in_dim(partners, own_start, half_batch)
    own_label = lax.dynamic_slice_in_dim(labels, core_index * half_batch, half_batch)
    ids = by_core(jnp.arange(total_images, dtype=jnp.int32))
    pick = (own_partner[:, None] == ids[None, :]).astype(BF16)
    point = (by_core(partners)[None, :] == own_ids[:, None]).astype(F32) * by_core(weight_f)[None, :]
    in_weight = jnp.sum(point, axis=1)
    hot = (own_label[:, None] == jnp.arange(WIDE, dtype=jnp.int32)[None, :]).astype(F32)
    lane = jnp.arange(LANES)[None, :]
    numbers = jnp.where(
        lane == 0, own_weight[:, None], jnp.where(lane == 1, in_weight[:, None], weight_total)
    )
    extra, g_top, grad_head = head_step(
        devices,
        pooled,
        head_all,
        bias,
        pick,
        point.astype(BF16),
        numbers,
        hot,
    )
    head_blocks = head_rows // 4
    if head_rows != LANES:
        grad_head = (
            grad_head.reshape(N_IN, WIDE // 2, LANES)
            .transpose(1, 0, 2)
            .reshape(WIDE // 2, devices, head_rows)
            .transpose(1, 0, 2)
            .reshape(devices, head_blocks, HALF, LANES)
        )
    grads, (small_bottom, small_top) = backward_pass(
        devices, live_count, field, low, kept, weights, first, g_top, params, live_rows, extra
    )
    head_sum, conv_grad, stats_new, master_new = deliver_blocks(
        grads,
        grad_head,
        block_places(owner_slot),
        conv_master,
        conv_stats,
        conv_roots,
        devices,
    )
    head_grad = head_sum.reshape(WIDE, head_rows)[:CLASSES].T.astype(F32)
    head_one, head_two, head_new = adamw(
        head_master, head_grad, head_moment_one, head_moment_two, RATE_HEAD
    )
    layer_rows = stride // LANES
    grad_bias = small_top[layer_rows : layer_rows + WIDE // LANES].reshape(-1)[:CLASSES]
    loss_sum = small_top[layer_rows + WIDE // LANES, 0]
    grad_small = jnp.concatenate(
        [small_bottom[:layer_rows].reshape(-1), small_top[:layer_rows].reshape(-1), grad_bias]
    )
    small_one, small_two, small_new = adamw(
        small_params, grad_small, small_moment_one, small_moment_two, RATE_SMALL
    )
    return (
        loss_sum,
        weight_total,
        conv_grad,
        stats_new,
        master_new,
        master_new.astype(BF16),
        head_one,
        head_two,
        head_new,
        head_new.astype(BF16),
        small_one,
        small_two,
        small_new,
    )


def solution(mesh):
    in_specs = (
        P("dp", "rows", None, None),
        P("dp"),
        P("dp"),
        P(),
        P(),
        P(),
        P("dp", None),
        P("dp", None, None),
        P("dp", None, None),
        P("dp", None),
        P("dp", None),
        P("dp", None),
        P(),
        P(),
        P(),
    )
    out_specs = (
        P(),
        P(),
        P("dp", None),
        P("dp", None, None),
        P("dp", None),
        P("dp", None),
        P("dp", None),
        P("dp", None),
        P("dp", None),
        P("dp", None),
        P(),
        P(),
        P(),
    )
    return jax.shard_map(body, mesh=mesh, in_specs=in_specs, out_specs=out_specs, check_vma=False)
```

```python
import functools

import jax
import jax.numpy as jnp
import numpy as np
from jax import lax
from jax.experimental import pallas as pl
from jax.experimental.pallas import tpu as pltpu
from jax.sharding import PartitionSpec as P

C = 2048
M = 512
CLASSES = 1000
HEIGHT = 7
WIDTH = 7
ROW_SLOTS = 4
LAYERS = 2
BLOCK = 64
STEP = 5


EPS_NORM = 1e-05
MATCH_WEIGHT = 4.0
DECAY_STATS = 0.5
RATE_SHAMPOO = 0.15
RATE_HEAD = 0.03
RATE_SMALL = 0.2
BETA_FIRST = 0.9
BETA_SECOND = 0.95
EPS_ADAM = 1e-08
DECAY_WEIGHT = 0.01


C = 2048
M = 512
CLASSES = 1000
HEIGHT = 7
WIDTH = 7
ROW_SLOTS = 4
LAYERS = 2
BLOCK = 64
STEP = 5


EPS_NORM = 1e-05
MATCH_WEIGHT = 4.0
DECAY_STATS = 0.5
RATE_SHAMPOO = 0.15
RATE_HEAD = 0.03
RATE_SMALL = 0.2
BETA_FIRST = 0.9
BETA_SECOND = 0.95
EPS_ADAM = 1e-08
DECAY_WEIGHT = 0.01


MESH_IDS = pl.DeviceIdType.MESH
HALF = 16
LANES = 128


def bit_split(devices):
    bits = devices.bit_length() - 1
    first = bits // 3
    second = (bits - first) // 2
    return first, second, bits - first - second


def greet(peers):
    barrier = pltpu.get_barrier_semaphore()
    for peer in peers:
        pl.semaphore_signal(barrier, inc=1, device_id=peer, device_id_type=MESH_IDS)
    pl.semaphore_wait(barrier, len(peers))


def axis_masks(devices, core):
    first, second, third = bit_split(devices)
    low = [m for m in range(1, 1 << first)]
    high = [m << first for m in range(1, 1 << second)]
    if first == second:
        one = [jnp.where(core == 0, h, l) for h, l in zip(high, low)]
        two = [jnp.where(core == 0, l, h) for h, l in zip(high, low)]
    else:
        one, two = low, high
    far = [m << (first + second) for m in range(1, 1 << third)]
    return [0] + one, [0] + two, [0] + far


def even_spans(count):
    parts = 8 if count % 8 == 0 else 1
    return [(i * (count // parts), count // parts) for i in range(parts)]


def spans_of(count):
    spans, at = [], 0
    while at < count:
        rest = count - at
        size = 16 if rest > 8 else rest
        spans.append((at, size))
        at += size
    return spans


def slab_shape(shape):
    return (shape[1] // LANES, shape[0], LANES)


def matrix_list():
    shapes = []
    for _ in range(LAYERS):
        shapes += [(C, M), (9 * M, M), (M, C)]
    return shapes


BRING_LATE = 2


def bring_kernel(devices, spans, idx_ref, m_ref, *refs):
    shapes = matrix_list()
    n = len(shapes)
    outs, bufs, (g_ref, stage, send_sem, recv_sem, out_sem) = refs[:n], refs[n : 2 * n], refs[2 * n :]
    me = lax.axis_index("dp")
    core = lax.axis_index("rows")
    count = m_ref.shape[0]
    parts = len(spans)
    mid, last, far = axis_masks(devices, core)
    partner = (me, 1 - core)
    peers = [(me ^ m, core) for m in far[1:] + mid[1:] + last[1:]] + [partner]
    barrier = pltpu.get_barrier_semaphore()
    for peer in peers:
        pl.semaphore_signal(barrier, inc=1, device_id=peer, device_id_type=MESH_IDS)

    def spread(first, rows):
        for m in range(HALF):
            one = m_ref[pl.ds(first, rows), m * LANES : (m + 1) * LANES]
            two = m_ref[pl.ds(first, rows), (HALF + m) * LANES : (HALF + m + 1) * LANES]
            h, r = m // (HALF // 2), 2 * (m % (HALF // 2))
            for i in range(2):
                cut = slice(i * BLOCK, (i + 1) * BLOCK)
                stage[h, pl.ds(first * HALF + r + i, rows, stride=HALF)] = jnp.concatenate(
                    [one[:, cut], two[:, cut]], axis=1
                )

    def group(i, carry):
        spread(pl.multiple_of(i * 8, 8), 8)
        return carry

    lax.fori_loop(0, count // 8, group, 0)
    if count % 8:
        spread(count // 8 * 8, count % 8)

    def round_one(k, carry):
        for h in range(2):
            rows = pl.ds(pl.multiple_of(k * HALF, HALF), HALF)
            g_ref[(me * 2 + h) * count + k] = stage[h, rows].astype(jnp.bfloat16)
        return carry

    lax.fori_loop(0, count, round_one, 0)
    pl.semaphore_wait(barrier, len(peers))
    sent = []

    def piece(owner, half, part):
        first, size = spans[part]
        return g_ref.at[pl.ds((owner * 2 + half) * count + first, size)]

    def send(owner, part, device):
        copy = pltpu.make_async_remote_copy(
            src_ref=piece(owner, core, part),
            dst_ref=piece(owner, core, part),
            send_sem=send_sem.at[len(sent)],
            recv_sem=recv_sem.at[owner, core, part],
            device_id=device,
            device_id_type=MESH_IDS,
        )
        copy.start()
        sent.append(copy)

    def arrived(owner, half, part):
        ref = piece(owner, half, part)
        pltpu.make_async_copy(ref, ref, recv_sem.at[owner, half, part]).wait()

    def onward(owner, part, masks):
        arrived(owner, core, part)
        for m in masks:
            send(owner, part, (me ^ m, core))
        send(owner, part, partner)

    early = parts - BRING_LATE if parts > BRING_LATE else parts
    for part in range(parts):
        order = far[1:] + last[1:] + mid[1:] if part < early else mid[1:] + far[1:] + last[1:]
        for m in order:
            send(me, part, (me ^ m, core))
    for tick in range(parts + 2):
        part = tick
        if part < parts:
            if part < early:
                for z in far[1:]:
                    onward(me ^ z, part, last[1:] + mid[1:])
            else:
                for m in mid[1:]:
                    onward(me ^ m, part, far[1:] + last[1:])
        part = tick - 1
        if 0 <= part < parts:
            if part < early:
                for m in mid[1:]:
                    for z in far:
                        onward(me ^ m ^ z, part, last[1:])
            else:
                for z in far[1:]:
                    onward(me ^ z, part, last[1:])
                for z in far[1:]:
                    for m in mid[1:]:
                        onward(me ^ z ^ m, part, last[1:])
        part = tick - 2
        if 0 <= part < parts:
            for q in last[1:]:
                for z in far:
                    for m in mid:
                        onward(me ^ q ^ z ^ m, part, [])
    for step in range(1, devices):
        for part in range(parts):
            arrived(me ^ step, 1 - core, part)

    base = 0
    copies = []
    for at, (rows, cols) in enumerate(shapes):
        pairs = cols // LANES
        buf = bufs[at]

        def strip(r, carry, base=base, pairs=pairs, buf=buf):
            for m in range(pairs):
                even = idx_ref[base + r * (2 * pairs) + 2 * m]
                odd = idx_ref[base + r * (2 * pairs) + 2 * m + 1]
                for h in range(2):
                    e = g_ref[even + h * count]
                    o = g_ref[odd + h * count]
                    buf[m, pl.ds(r * BLOCK + h * HALF, HALF)] = jnp.concatenate(
                        [e[:, :BLOCK], o[:, :BLOCK]], axis=1
                    )
                    buf[m, pl.ds(r * BLOCK + 2 * HALF + h * HALF, HALF)] = jnp.concatenate(
                        [e[:, BLOCK:], o[:, BLOCK:]], axis=1
                    )
            return carry

        lax.fori_loop(0, rows // BLOCK, strip, 0, unroll=8 // (pairs // 4))
        copy = pltpu.make_async_copy(buf, outs[at], out_sem.at[at])
        copy.start()
        copies.append(copy)
        base += (rows // BLOCK) * (cols // BLOCK)
    for copy in copies:
        copy.wait()
    for copy in sent:
        copy.wait_send()


def bring_weights(master, index, devices):
    count = master.shape[0]
    spans = even_spans(count)
    parts = len(spans)
    shapes = [slab_shape(s) for s in matrix_list()]
    dma = pltpu.SemaphoreType.DMA
    return pl.pallas_call(
        functools.partial(bring_kernel, devices, spans),
        out_shape=[jax.ShapeDtypeStruct(s, jnp.bfloat16) for s in shapes],
        in_specs=[
            pl.BlockSpec(memory_space=pltpu.SMEM),
            pl.BlockSpec(memory_space=pltpu.VMEM),
        ],
        out_specs=[pl.BlockSpec(memory_space=pl.ANY)] * len(shapes),
        scratch_shapes=[pltpu.VMEM(s, jnp.bfloat16) for s in shapes]
        + [
            pltpu.VMEM((devices * 2 * count, HALF, LANES), jnp.bfloat16),
            pltpu.VMEM((2, count * HALF, LANES), jnp.float32),
            dma((3 * devices * parts,)),
            dma((devices, 2, parts)),
            dma((len(shapes),)),
        ],
        compiler_params=pltpu.CompilerParams(
            collective_id=1, has_side_effects=True, vmem_limit_bytes=56 * 2**20
        ),
    )(index, master)


def split_two(v):
    high = v.astype(BF16)
    return high, (v - high.astype(F32)).astype(BF16)


def shampoo_rows(final, updates, stats, roots, grads, flat, turn, first, group):
    for k in range(group):
        rows = pl.ds(k * HALF, HALF)
        parts = [final[h, first + k].astype(F32) for h in range(2)]
        for h in range(2):
            flat[h, rows] = parts[h]
        tile = jnp.concatenate([p[:, :BLOCK] for p in parts] + [p[:, BLOCK:] for p in parts], axis=0)
        low = tile.astype(BF16)
        old = stats[first + k]
        sides = roots[first + k]
        high, rest = split_two(sides[:, :BLOCK])
        both = dot(jnp.concatenate([high, rest, tile.T.astype(BF16)], axis=0), low, 1, 0)
        stats[first + k] = DECAY_STATS * old + (1.0 - DECAY_STATS) * jnp.concatenate(
            [dot(low, low, 1, 1), both[2 * BLOCK :]], axis=1
        )
        turned = both[:BLOCK] + both[BLOCK : 2 * BLOCK]
        t_high, t_rest = split_two(turned)
        high, rest = split_two(sides)
        wide = jnp.concatenate([high[:, BLOCK:], rest[:, BLOCK:]], axis=1)
        both = dot(jnp.concatenate([t_high, t_rest], axis=0), wide, 1, 0)
        turned = both[:BLOCK, :BLOCK] + both[BLOCK:, :BLOCK] + both[:BLOCK, BLOCK:]
        for h in range(2):
            turn[h, rows] = jnp.concatenate(
                [
                    turned[h * HALF : (h + 1) * HALF],
                    turned[2 * HALF + h * HALF : 2 * HALF + (h + 1) * HALF],
                ],
                axis=1,
            )
    here = pl.ds(first if isinstance(first, int) else pl.multiple_of(first, 8), group)
    for m in range(HALF):
        h, r = m // (HALF // 2), 2 * (m % (HALF // 2))
        tiles = [flat[h, pl.ds(r + i, group, stride=HALF)] for i in range(2)]
        steps = [turn[h, pl.ds(r + i, group, stride=HALF)] for i in range(2)]
        for p in range(2):
            lanes = pl.ds(p * (BLOCK * BLOCK // 2) + m * LANES, LANES)
            cut = slice(p * BLOCK, (p + 1) * BLOCK)
            grads[here, lanes] = jnp.concatenate([v[:, cut] for v in tiles], axis=1)
            updates[here, lanes] = jnp.concatenate([v[:, cut] for v in steps], axis=1)


DELIVER_FAR = ()
AHEAD = 3


def deliver_kernel(devices, spans, code_ref, head_h, *refs):
    n = len(matrix_list())
    grads, refs = refs[:n], refs[n:]
    stats_h, roots_h, head_out, grad_out, stats_out, step_out = refs[:6]
    pool, acc, land_last, land_mid, land_far, final, head_pair = refs[6:13]
    steps, stats, roots, grad_flat, flat, turn = refs[13:19]
    in_sem, send_sem, last_recv, mid_recv, far_recv, end_send, end_recv, own_sem, out_sem = refs[19:]
    me = lax.axis_index("dp")
    core = lax.axis_index("rows")
    count = code_ref.shape[0] // devices
    mid, last, far = axis_masks(devices, core)
    partner = (me, 1 - core)
    peers = [(me ^ m, core) for m in far[1:] + mid[1:] + last[1:]] + [partner]
    barrier = pltpu.get_barrier_semaphore()
    for peer in peers:
        pl.semaphore_signal(barrier, inc=1, device_id=peer, device_id_type=MESH_IDS)
    head = pltpu.make_async_copy(head_h, head_pair.at[core], in_sem.at[n])
    head.start()
    loads = []
    start = 0
    for i, grad in enumerate(grads):
        load = pltpu.make_async_copy(grad, pool.at[pl.ds(start, grad.shape[0])], in_sem.at[i])
        load.start()
        loads.append(load)
        start += grad.shape[0]
    owned = []
    for i, (src, dst) in enumerate([(stats_h, stats), (roots_h, roots)]):
        load = pltpu.make_async_copy(src, dst, own_sem.at[i])
        load.start()
        owned.append(load)
    pl.semaphore_wait(barrier, len(peers))
    head.wait()
    parts = len(spans)
    sent = [
        remote(
            head_pair.at[core], head_pair.at[core], end_send.at[parts], end_recv.at[parts], partner
        )
    ]
    stores = []

    def store(src, dst):
        copy = pltpu.make_async_copy(src, dst, out_sem.at[len(stores)])
        copy.start()
        stores.append(copy)

    def send(owner, span, part, land, sems, at, device):
        copy = pltpu.make_async_remote_copy(
            src_ref=acc.at[owner, span],
            dst_ref=land.at[at, span],
            send_sem=send_sem.at[len(sent) - 1],
            recv_sem=sems.at[at, part],
            device_id=device,
            device_id_type=MESH_IDS,
        )
        copy.start()
        sent.append(copy)

    def arrived(land, sems, at, span, part):
        ref = land.at[at, span]
        pltpu.make_async_copy(ref, ref, sems.at[at, part]).wait()

    def fill(first, size):
        def owner_step(owner, carry):
            def block(k, inner):
                slot = owner * count + first + k
                code = code_ref[slot]
                q = lax.shift_right_logical(code, 1)
                top = pool[q]
                low = pool[q + 1]
                even = jnp.concatenate([top[:, :BLOCK], low[:, :BLOCK]], axis=1)
                odd = jnp.concatenate([top[:, BLOCK:], low[:, BLOCK:]], axis=1)
                acc[owner, first + k] = jnp.where(lax.bitwise_and(code, 1) == 1, odd, even)
                return inner

            return lax.fori_loop(0, size, block, carry, unroll=True)

        lax.fori_loop(0, devices, owner_step, 0)

    def add(owners, lands, first, size):
        def step(i, carry):
            at = first + i
            for owner, (land, j) in zip(owners, lands):
                acc[owner, at] = (
                    acc[owner, at].astype(jnp.float32) + land[j, at].astype(jnp.float32)
                ).astype(jnp.bfloat16)
            return carry

        lax.fori_loop(0, size, step, 0)

    ends = []
    whole_rows = steps.shape[0] % 8 != 0

    def far_second(part):
        return part in DELIVER_FAR

    for tick in range(parts + 3 + AHEAD):
        part = tick
        if part < parts:
            first, size = spans[part]
            span = pl.ds(first, size)
            if part == 0:
                for load in loads:
                    load.wait()
            fill(first, size)
            at = 0
            for q in last[1:]:
                for m in mid[::-1]:
                    for z in far[::-1]:
                        send(
                            me ^ q ^ m ^ z, span, part, land_last, last_recv, at, (me ^ q, core)
                        )
                        at += 1
        part = tick - AHEAD
        if 0 <= part < parts:
            first, size = spans[part]
            span = pl.ds(first, size)
            pairs = [(m, z) for m in mid[::-1] for z in far[::-1]]
            owners, lands = [], []
            for j in range(len(last) - 1):
                for i, (m, z) in enumerate(pairs):
                    at = j * len(pairs) + i
                    arrived(land_last, last_recv, at, span, part)
                    owners.append(me ^ m ^ z)
                    lands.append((land_last, at))
            add(owners, lands, first, size)
            at = 0
            if far_second(part):
                for z in far[1:]:
                    for m in mid[::-1]:
                        send(me ^ m ^ z, span, part, land_far, far_recv, at, (me ^ z, core))
                        at += 1
            else:
                for m in mid[1:]:
                    for z in far[::-1]:
                        send(me ^ m ^ z, span, part, land_mid, mid_recv, at, (me ^ m, core))
                        at += 1
        part = tick - 1 - AHEAD
        if 0 <= part < parts:
            first, size = spans[part]
            span = pl.ds(first, size)
            owners, lands = [], []
            at = 0
            if far_second(part):
                for z in far[1:]:
                    for m in mid[::-1]:
                        arrived(land_far, far_recv, at, span, part)
                        owners.append(me ^ m)
                        lands.append((land_far, at))
                        at += 1
                add(owners, lands, first, size)
                for at, m in enumerate(mid[1:]):
                    send(me ^ m, span, part, land_mid, mid_recv, at, (me ^ m, core))
            else:
                for m in mid[1:]:
                    for z in far[::-1]:
                        arrived(land_mid, mid_recv, at, span, part)
                        owners.append(me ^ z)
                        lands.append((land_mid, at))
                        at += 1
                add(owners, lands, first, size)
                for at, z in enumerate(far[1:]):
                    send(me ^ z, span, part, land_far, far_recv, at, (me ^ z, core))
        part = tick - 2 - AHEAD
        if 0 <= part < parts:
            first, size = spans[part]
            span = pl.ds(first, size)
            land, sems, width = land_far, far_recv, len(far) - 1
            if far_second(part):
                land, sems, width = land_mid, mid_recv, len(mid) - 1
            for at in range(width):
                arrived(land, sems, at, span, part)

            def finish(i, carry, first=first, land=land, width=width):
                at = first + i
                total = acc[me, at].astype(jnp.float32)
                for j in range(width):
                    total = total + land[j, at].astype(jnp.float32)
                final[core, at] = total.astype(jnp.bfloat16)
                return carry

            lax.fori_loop(0, size, finish, 0)
            copy = pltpu.make_async_remote_copy(
                src_ref=final.at[core, span],
                dst_ref=final.at[core, span],
                send_sem=end_send.at[part],
                recv_sem=end_recv.at[part],
                device_id=partner,
                device_id_type=MESH_IDS,
            )
            copy.start()
            ends.append(copy)
        part = tick - 3 - AHEAD
        if 0 <= part < parts:
            first, size = spans[part]
            ref = final.at[1 - core, pl.ds(first, size)]
            pltpu.make_async_copy(ref, ref, end_recv.at[part]).wait()
            if part == 0:
                landed(head_pair.at[1 - core], end_recv.at[parts])
                store(head_pair, head_out)
                for load in owned:
                    load.wait()

            def group(i, carry, first=first):
                shampoo_rows(final, steps, stats, roots, grad_flat, flat, turn, first + i * 8, 8)
                return carry

            lax.fori_loop(0, size // 8, group, 0)
            if size % 8:
                shampoo_rows(
                    final, steps, stats, roots, grad_flat, flat, turn, first + size // 8 * 8, size % 8
                )
            span = pl.ds(first, size)
            store(stats.at[span], stats_out.at[span])
            if not whole_rows:
                store(grad_flat.at[span], grad_out.at[span])
                store(steps.at[span], step_out.at[span])
    if whole_rows:
        store(grad_flat, grad_out)
        store(steps, step_out)
    for copy in sent + ends:
        copy.wait_send()
    for copy in stores:
        copy.wait()


def deliver_blocks(grads, head, code, stats, roots, devices):
    count = code.shape[0] // devices
    more = head.shape[0]
    spans = spans_of(count)
    flat = (count, BLOCK * BLOCK)
    first, second, third = bit_split(devices)
    n_mid, n_last, n_far = 1 << first, 1 << second, 1 << third
    tile = (count, HALF, LANES)
    dma = pltpu.SemaphoreType.DMA
    lands = [(n_last - 1) * n_mid * n_far, (n_mid - 1) * n_far, (n_far - 1) * n_mid]
    grads = [g.reshape(-1, HALF, LANES) for g in grads]
    any_space = pl.BlockSpec(memory_space=pl.ANY)
    steps = len(spans)
    return pl.pallas_call(
        functools.partial(deliver_kernel, devices, spans),
        out_shape=[
            jax.ShapeDtypeStruct((2, more, HALF, LANES), BF16),
            jax.ShapeDtypeStruct(flat, F32),
            jax.ShapeDtypeStruct(stats.shape, F32),
            jax.ShapeDtypeStruct(flat, F32),
        ],
        in_specs=[pl.BlockSpec(memory_space=pltpu.SMEM)] + [any_space] * (3 + len(grads)),
        out_specs=[any_space] * 4,
        scratch_shapes=[
            pltpu.VMEM((sum(g.shape[0] for g in grads), HALF, LANES), jnp.bfloat16),
            pltpu.VMEM((devices,) + tile, jnp.bfloat16),
        ]
        + [pltpu.VMEM((k,) + tile, jnp.bfloat16) for k in lands]
        + [
            pltpu.VMEM((2,) + tile, jnp.bfloat16),
            pltpu.VMEM((2, more, HALF, LANES), jnp.bfloat16),
            pltpu.VMEM(flat, F32),
            pltpu.VMEM(stats.shape, F32),
            pltpu.VMEM(roots.shape, F32),
            pltpu.VMEM(flat, F32),
            pltpu.VMEM((2, 8 * HALF, LANES), F32),
            pltpu.VMEM((2, 8 * HALF, LANES), F32),
            dma((len(grads) + 1,)),
            dma((sum(lands) * steps,)),
            dma((lands[0], steps)),
            dma((lands[1], steps)),
            dma((lands[2], steps)),
            dma((steps + 1,)),
            dma((steps + 1,)),
            dma((2,)),
            dma((3 * steps + 3,)),
        ],
        compiler_params=pltpu.CompilerParams(
            collective_id=2, has_side_effects=True, vmem_limit_bytes=60 * 2**20
        ),
    )(code, head, *grads, stats, roots)


def block_places(owner_slot):
    codes = []
    base = 0
    for rows, cols in matrix_list():
        strips, pairs = rows // BLOCK, cols // LANES
        grid = base + 2 * (np.arange(pairs)[None, :] * strips + np.arange(strips)[:, None])
        codes.append((2 * grid[:, :, None] + np.arange(2)[None, None, :]).reshape(-1))
        base += 2 * strips * pairs
    code = np.concatenate(codes).astype(np.int32)
    slots = np.arange(code.shape[0], dtype=np.int32)
    found = jnp.sum(
        jnp.where(owner_slot[:, None] == slots[None, :], code[:, None], 0), axis=0, dtype=jnp.int32
    )
    return found


ROWS = ROW_SLOTS * WIDTH
N_IN = C // LANES
N_MID = M // LANES
WIDE = 1024
F32 = jnp.float32
BF16 = jnp.bfloat16


def dot(a, b, ca, cb):
    return lax.dot_general(a, b, (((ca,), (cb,)), ((), ())), preferred_element_type=F32)


def lanes_of(ref, first, count):
    return jnp.concatenate([ref[first + i] for i in range(count)], axis=-1)


def half_tanh(v):
    return 0.5 * (1.0 + jnp.tanh(0.5 * v))


class Net:
    def __init__(self, devices):
        first, second, third = bit_split(devices)
        self.me = lax.axis_index("dp")
        self.core = lax.axis_index("rows")
        self.near, self.far = 1 << (first + second), 1 << third
        self.near_at = lax.rem(self.me, self.near)
        self.far_at = self.me // self.near
        self.partner = (self.me, 1 - self.core)
        self.near_peers = [(self.me ^ m, self.core) for m in range(1, self.near)]
        self.near_slots = [self.near_at ^ m for m in range(1, self.near)]
        self.far_peers = [(self.me ^ (m * self.near), self.core) for m in range(1, self.far)]
        self.far_slots = [self.far_at ^ m for m in range(1, self.far)]
        self.direct = devices <= DIRECT
        self.all_slots = [self.me ^ m for m in range(1, devices)]
        self.all_peers = [(slot, self.core) for slot in self.all_slots]
        self.devices = devices

    def known(self):
        if self.direct:
            return [self.partner] + self.all_peers
        return [self.partner] + self.near_peers + self.far_peers

    def hello(self):
        barrier = pltpu.get_barrier_semaphore()
        for peer in self.known():
            pl.semaphore_signal(barrier, inc=1, device_id=peer, device_id_type=MESH_IDS)

    def ready(self):
        pl.semaphore_wait(pltpu.get_barrier_semaphore(), len(self.known()))


DIRECT = 16


def slots_total(devices):
    first, second, third = bit_split(devices)
    staged = 2 + (1 << (first + second)) + (1 << third)
    return max(staged, 2 + devices) if devices <= DIRECT else staged


def remote(src, dst, send_sem, recv_sem, device):
    copy = pltpu.make_async_remote_copy(
        src_ref=src,
        dst_ref=dst,
        send_sem=send_sem,
        recv_sem=recv_sem,
        device_id=device,
        device_id_type=MESH_IDS,
    )
    copy.start()
    return copy


def landed(ref, sem):
    pltpu.make_async_copy(ref, ref, sem).wait()


def plain_sum(values, counts):
    total = values[0]
    for value in values[1:]:
        total = total + value
    return total


def pooled_moments(rows):
    def merge(values, counts):
        n = counts[0]
        for more in counts[1:]:
            n = n + more
        sums = values[0][:rows]
        spread = values[0][rows:]
        for value in values[1:]:
            sums = sums + value[:rows]
            spread = spread + value[rows:]
        mean = sums / n
        for value, own in zip(values, counts):
            gap = value[:rows] / own - mean
            spread = spread + own * gap * gap
        return jnp.concatenate([sums, spread], axis=0)

    return merge


def reduce_all(net, value, bufs, send_sem, recv_sem, merge, own_count=None, pair_count=0.0, fillers=()):
    fillers = list(fillers) + [None] * 3
    fillers_after = fillers[1:]
    copies = []
    stages = [
        (0, net.core, [net.partner], [1 - net.core], 2),
        (2, net.near_at, net.near_peers, net.near_slots, net.near),
        (2 + net.near, net.far_at, net.far_peers, net.far_slots, net.far),
    ]
    if net.direct and value.shape[0] <= 2 * N_MID:
        stages = stages[:1] + [(2, net.me, net.all_peers, net.all_slots, net.devices)]
        fillers = [fillers[0], lambda: [more() for more in fillers_after if more is not None]]
    for step, (base, mine, peers, slots, size) in enumerate(stages):
        bufs[base + mine] = value
        for i, peer in enumerate(peers):
            copies.append(
                remote(
                    bufs.at[base + mine],
                    bufs.at[base + mine],
                    send_sem.at[base + i],
                    recv_sem.at[base + mine],
                    peer,
                )
            )
        if fillers[step] is not None:
            fillers[step]()
        for slot in slots:
            landed(bufs.at[base + slot], recv_sem.at[base + slot])
        if own_count is None:
            counts = [None] * size
        elif step == 0:
            rest = pair_count - own_count
            first = net.core == 0
            counts = [jnp.where(first, own_count, rest), jnp.where(first, rest, own_count)]
        else:
            counts = [pair_count * (1 if step == 1 else net.near)] * size
        value = merge([bufs[base + j] for j in range(size)], counts)
    return value, copies


def column_sum(value):
    return jnp.sum(value.reshape(-1, 8, LANES), axis=0)


def local_moments(z, count, live, own_count, stage, masked):
    quarter = z.shape[1] // 4

    def slab(j, carry):
        total = jnp.zeros((8, LANES), F32)
        for q in range(4):
            rows = pl.ds(q * quarter, quarter)
            v = z[j, rows]
            if masked:
                v = v * live[rows]
                z[j, rows] = v
            total = total + column_sum(v)
        sums = jnp.sum(total, axis=0, keepdims=True)
        mean = sums / own_count
        spread = jnp.zeros((8, LANES), F32)
        for q in range(4):
            rows = pl.ds(q * quarter, quarter)
            d = (z[j, rows] - mean) * live[rows]
            spread = spread + column_sum(d * d)
        stage[pl.ds(j, 1)] = sums
        stage[pl.ds(count + j, 1)] = jnp.sum(spread, axis=0, keepdims=True)
        return carry

    lax.fori_loop(0, count, slab, 0)


def window(ref, down, right):
    batch = ref.shape[3]
    parts = [
        ref[j, pl.ds(down, ROW_SLOTS), pl.ds(right, WIDTH)].reshape(ROWS * batch, LANES)
        for j in range(N_MID)
    ]
    return jnp.concatenate(parts, axis=-1)


def clear_edges(ref, core):
    shape = ref.shape
    zero = jnp.zeros((shape[0], 1) + shape[2:], ref.dtype)
    ref[:, pl.ds(jnp.where(core == 0, 0, ROW_SLOTS + 1), 1)] = zero
    column = jnp.zeros(shape[:2] + (1,) + shape[3:], ref.dtype)
    ref[:, :, 0:1] = column
    ref[:, :, WIDTH + 1 : WIDTH + 2] = column


def send_edge(ref, net, send_sem, recv_sem):
    edge = jnp.where(net.core == 0, ROW_SLOTS, 1)
    there = jnp.where(net.core == 0, 0, ROW_SLOTS + 1)
    return remote(
        ref.at[:, edge, pl.ds(1, WIDTH)],
        ref.at[:, there, pl.ds(1, WIDTH)],
        send_sem,
        recv_sem,
        net.partner,
    )


def edge_landed(ref, net, recv_sem):
    here = jnp.where(net.core == 0, ROW_SLOTS + 1, 0)
    landed(ref.at[:, here, pl.ds(1, WIDTH)], recv_sem)


def edge_first(net, fill, send):
    edge = jnp.where(net.core == 0, ROW_SLOTS - 1, 0)
    fill(edge)
    copy = send()
    for step in range(1, ROW_SLOTS):
        fill(lax.rem(edge + step, ROW_SLOTS))
    return copy


def load_all(pairs, sems):
    copies = []
    for i, (src, dst) in enumerate(pairs):
        copy = pltpu.make_async_copy(src, dst, sems.at[i])
        copy.start()
        copies.append(copy)
    return copies


def forward_kernel(devices, total_count, *refs):
    refs = list(refs)
    take = lambda n: [refs.pop(0) for _ in range(n)]
    w_h = [take(3) for _ in range(LAYERS)]
    x_in, = take(1)
    params_of = take(LAYERS)
    live, = take(1)
    kept_h = [take(5) for _ in range(LAYERS)]
    stats_of = [take(3) for _ in range(LAYERS)]
    xn_h, xnb_h, pooled = take(3)
    wi, wm, wo, za, hp, zb, hb, zc, xn, xnb = take(10)
    stage_m, stage_c = take(2)
    bufs_of = [take(3) for _ in range(LAYERS)]
    in_sem, out_sem, send_sem, recv_sem, halo_sem = take(5)

    net = Net(devices)
    net.hello()
    loading = {}
    places = [wi, wm, wo]

    def start(at, which):
        copy = pltpu.make_async_copy(w_h[at][which], places[which], in_sem.at[at, which])
        copy.start()
        loading[at, which] = copy

    for which in range(3):
        start(0, which)
    clear_edges(hp, net.core)
    own_count = jnp.sum(column_sum(live[...]), axis=0, keepdims=True)
    pair_count = total_count / devices
    quarter = za.shape[1] // ROW_SLOTS
    batch = quarter // WIDTH
    stores = []
    sends = []

    def store(src, dst):
        copy = pltpu.make_async_copy(src, dst, out_sem.at[len(stores)])
        copy.start()
        stores.append(copy)

    def layer(at):
        params = params_of[at]
        stat_a, stat_b, stat_c = stats_of[at]
        za_h, hp_h, zb_h, hb_h, zc_h = kept_h[at]
        later = at + 1 < LAYERS

        def norm(z, n, stage, which, masked, stat):
            local_moments(z, n, live, own_count, stage, masked)
            if at == 0 and which == 0:
                net.ready()
            total, copies = reduce_all(
                net,
                stage[...],
                bufs_of[at][which],
                send_sem.at[3 * at + which],
                recv_sem.at[3 * at + which],
                pooled_moments(n),
                own_count,
                pair_count,
            )
            sends.extend(copies)
            stat[0:n] = total[:n] / total_count
            stat[n : 2 * n] = lax.rsqrt(total[n:] / total_count + EPS_NORM)

        def affine(stat, n, gain_at, j):
            mean = stat[pl.ds(j, 1)]
            scale = stat[pl.ds(n + j, 1)] * params[pl.ds(gain_at + j, 1)]
            return mean, scale, params[pl.ds(gain_at + n + j, 1)]

        loading[at, 0].wait()
        if at:
            for copy in stores[:5]:
                copy.wait()
        x = lanes_of(xnb, 0, N_IN) if at else x_in[...]
        product = dot(x, lanes_of(wi, 0, N_MID), 1, 0)
        for j in range(N_MID):
            za[j] = product[:, j * LANES : (j + 1) * LANES]
        if later:
            start(at + 1, 0)
        norm(za, N_MID, stage_m, 0, at == 0, stat_a)
        store(za, za_h)

        def fill_hidden(slot):
            rows = pl.ds(slot * quarter, quarter)

            def slab(j, carry):
                mean, scale, shift = affine(stat_a, N_MID, 0, j)
                y = (za[j, rows] - mean) * scale + shift
                h = (live[rows] * (y * half_tanh(y))).astype(BF16)
                hp[j, pl.ds(slot + 1, 1), pl.ds(1, WIDTH)] = h.reshape(1, WIDTH, batch, LANES)
                return carry

            lax.fori_loop(0, N_MID, slab, 0)

        edge = edge_first(
            net, fill_hidden, lambda: send_edge(hp, net, halo_sem.at[at, 0], halo_sem.at[at, 1])
        )
        loading[at, 1].wait()
        zb[...] = jnp.zeros(zb.shape, F32)

        def tap(t):
            k = pl.ds(pl.multiple_of(t * M, M), M)
            part = dot(
                window(hp, t // 3, lax.rem(t, 3)),
                jnp.concatenate([wm[j, k] for j in range(N_MID)], axis=-1),
                1,
                0,
            )
            for j in range(N_MID):
                zb[j] = zb[j] + part[:, j * LANES : (j + 1) * LANES]

        def middle(i, carry):
            tap(i + 3)
            return carry

        def outer(i, carry):
            tap(jnp.where(i < 3, i, i + 3))
            return carry

        lax.fori_loop(0, 3, middle, 0)
        edge_landed(hp, net, halo_sem.at[at, 1])
        edge.wait_send()
        store(hp, hp_h)
        lax.fori_loop(0, 6, outer, 0)
        if later:
            start(at + 1, 1)
        norm(zb, N_MID, stage_m, 1, True, stat_b)
        store(zb, zb_h)

        def fill_second(j, carry):
            mean, scale, shift = affine(stat_b, N_MID, 2 * N_MID, j)
            for q in range(4):
                rows = pl.ds(q * quarter, quarter)
                y = (zb[j, rows] - mean) * scale + shift
                hb[j, rows] = (live[rows] * (y * half_tanh(y))).astype(BF16)
            return carry

        lax.fori_loop(0, N_MID, fill_second, 0)
        store(hb, hb_h)
        loading[at, 2].wait()

        def expand(g, carry):
            part = dot(lanes_of(hb, 0, N_MID), lanes_of(wo, g * N_MID, N_MID), 1, 0)
            for j in range(N_MID):
                zc[g * N_MID + j] = part[:, j * LANES : (j + 1) * LANES]
            return carry

        lax.fori_loop(0, N_IN // N_MID, expand, 0)
        if later:
            start(at + 1, 2)
        store(zc, zc_h)
        norm(zc, N_IN, stage_c, 2, False, stat_c)

        def finish(j, carry):
            mean, scale, shift = affine(stat_c, N_IN, 4 * N_MID, j)
            pool = jnp.zeros((batch, LANES), F32)
            for q in range(4):
                rows = pl.ds(q * quarter, quarter)
                if at:
                    x = xn[j, rows]
                else:
                    x = x_in[rows, pl.ds(pl.multiple_of(j * LANES, LANES), LANES)].astype(F32)
                y = (zc[j, rows] - mean) * scale + shift + x
                out = live[rows] * (y * half_tanh(y))
                if later:
                    xn[j, rows] = out
                    xnb[j, rows] = out.astype(BF16)
                else:
                    pool = pool + jnp.sum(out.reshape(WIDTH, batch, LANES), axis=0)
            if not later:
                pooled[j] = pool
            return carry

        lax.fori_loop(0, N_IN, finish, 0)
        if later:
            store(xn, xn_h)
            store(xnb, xnb_h)

    for at in range(LAYERS):
        layer(at)
    for copy in stores[5:]:
        copy.wait()
    for copy in sends:
        copy.wait_send()


def forward_pass(devices, total_count, x, weights, params, live):
    rows = live.shape[0]
    batch = rows // ROWS
    shape = jax.ShapeDtypeStruct
    any_space = pl.BlockSpec(memory_space=pl.ANY)
    vmem = pl.BlockSpec(memory_space=pltpu.VMEM)
    fields = [
        shape((N_MID, rows, LANES), F32),
        shape((N_MID, ROW_SLOTS + 2, WIDTH + 2, batch, LANES), BF16),
        shape((N_MID, rows, LANES), F32),
        shape((N_MID, rows, LANES), BF16),
        shape((N_IN, rows, LANES), F32),
    ]
    stats = [shape((2 * n, LANES), F32) for n in (N_MID, N_MID, N_IN)]
    last = [shape((N_IN, rows, LANES), F32), shape((N_IN, rows, LANES), BF16)]
    big = lambda s: pltpu.VMEM(s.shape, s.dtype)
    total = slots_total(devices)
    dma = pltpu.SemaphoreType.DMA
    small_ins = [x] + list(params) + [live]
    out = pl.pallas_call(
        functools.partial(forward_kernel, devices, total_count),
        out_shape=fields * LAYERS + stats * LAYERS + last + [shape((N_IN, batch, LANES), F32)],
        in_specs=[any_space] * len(weights) + [vmem] * len(small_ins),
        out_specs=[any_space] * (5 * LAYERS) + [vmem] * (3 * LAYERS) + [any_space] * 2 + [vmem],
        scratch_shapes=[big(w) for w in weights[:3]]
        + [big(s) for s in fields + last]
        + [pltpu.VMEM((2 * N_MID, LANES), F32), pltpu.VMEM((2 * N_IN, LANES), F32)]
        + [pltpu.VMEM((total, 2 * n, LANES), F32) for n in (N_MID, N_MID, N_IN)] * LAYERS
        + [
            dma((LAYERS, 3)),
            dma((5 * LAYERS + 2,)),
            dma((3 * LAYERS, total)),
            dma((3 * LAYERS, total)),
            dma((LAYERS, 2)),
        ],
        compiler_params=pltpu.CompilerParams(
            collective_id=3, has_side_effects=True, vmem_limit_bytes=60 * 2**20
        ),
    )(*weights, *small_ins)
    kept = [
        list(out[5 * at : 5 * at + 5]) + list(out[5 * LAYERS + 3 * at : 5 * LAYERS + 3 * at + 3])
        for at in range(LAYERS)
    ]
    return kept, out[-3], out[-2], out[-1]


def head_kernel(
    devices, area, pooled, head_h, bias, pick, point, numbers, hot,
    extra, gtop, gh_h,
    head, send_pool, recv_pool, low, logits_all, logits, g_low, gh, gh_there, gh_other, gt,
    in_sem, out_sem, send_sem, recv_sem,
):
    net = Net(devices)
    net.hello()
    load = pltpu.make_async_copy(head_h, head, in_sem)
    load.start()
    half = send_pool.shape[1]
    mine = pl.ds(pl.multiple_of(net.core * half, half), half)
    theirs = pl.ds(pl.multiple_of((1 - net.core) * half, half), half)
    for j in range(N_IN):
        send_pool[j] = pooled[j, theirs].astype(BF16)
    net.ready()
    sends = [remote(send_pool, recv_pool, send_sem.at[0], recv_sem.at[0], net.partner)]
    load.wait()
    landed(recv_pool, recv_sem.at[0])
    for j in range(N_IN):
        low[j] = ((pooled[j, mine] + recv_pool[j].astype(F32)) / area).astype(BF16)
    logits[...] = dot(lanes_of(low, 0, N_IN), lanes_of(head, 0, N_IN), 1, 1) + bias[0:1, :]
    logits_all[net.core, net.far_at, net.near_at] = logits[...].astype(BF16)
    at = 1
    ref = logits_all.at[net.core, net.far_at, net.near_at]
    for peer in net.far_peers:
        sends.append(
            remote(ref, ref, send_sem.at[at], recv_sem.at[1 + net.near + net.far_at], peer)
        )
        at += 1

    own = logits[...]
    keep = lax.broadcasted_iota(jnp.int32, own.shape, 1) < CLASSES
    peak = jnp.max(jnp.where(keep, own, -3.0e38), axis=1, keepdims=True)
    powers = jnp.where(keep, jnp.exp(jnp.where(keep, own - peak, 0.0)), 0.0)
    log_total = peak + jnp.log(jnp.sum(powers, axis=1, keepdims=True))
    softmax = jnp.where(keep, jnp.exp(jnp.where(keep, own - log_total, 0.0)), 0.0)
    picked = jnp.sum(own * hot[...], axis=1, keepdims=True)

    for slot in net.far_slots:
        landed(
            logits_all.at[net.core, slot, net.near_at], recv_sem.at[1 + net.near + slot]
        )
    group = logits_all.at[net.core, :, net.near_at]
    for peer in net.near_peers:
        sends.append(remote(group, group, send_sem.at[at], recv_sem.at[1 + net.near_at], peer))
        at += 1
    for slot in net.near_slots:
        landed(logits_all.at[net.core, :, slot], recv_sem.at[1 + slot])
    ref = logits_all.at[net.core]
    sends.append(
        remote(ref, ref, send_sem.at[at], recv_sem.at[1 + net.near + net.far], net.partner)
    )
    at += 1
    landed(logits_all.at[1 - net.core], recv_sem.at[1 + net.near + net.far])
    every = logits_all[...].reshape(-1, WIDE)
    gap = jnp.where(keep, own - dot(pick[...], every, 1, 0), 0.0)
    incoming = dot(point[...], every, 1, 0)
    weight = numbers[:, 0:1]
    terms = weight * (
        log_total - picked + MATCH_WEIGHT * (jnp.sum(gap * gap, axis=1, keepdims=True) / CLASSES)
    )
    grad = (
        weight * (softmax - hot[...])
        + MATCH_WEIGHT
        * (2.0 / CLASSES)
        * (weight * gap - (incoming - numbers[:, 1:2] * own))
    ) / numbers[:, 2:3]
    g_low[...] = jnp.where(keep, grad, 0.0).astype(BF16)
    bias_sum = jnp.sum(g_low[...].astype(F32), axis=0, keepdims=True)
    extra[...] = jnp.zeros(extra.shape, F32)
    for j in range(WIDE // LANES):
        extra[j : j + 1] = bias_sum[:, j * LANES : (j + 1) * LANES]
    extra[WIDE // LANES : WIDE // LANES + 1] = jnp.zeros((1, LANES), F32) + jnp.sum(
        terms, axis=0, keepdims=True
    )
    gt_view = gt.at[:, net.core]
    for j in range(N_IN):
        gt[j, net.core] = (dot(g_low[...], head[j], 1, 0) / area).astype(BF16)
    sends.append(
        remote(
            gt_view, gt_view, send_sem.at[at], recv_sem.at[2 + net.near + net.far], net.partner
        )
    )

    at += 1
    block = (WIDE // 2 // HALF, HALF, LANES)
    cut = WIDE // 2
    mine_at = pl.multiple_of(net.core * cut, cut)
    theirs_at = pl.multiple_of((1 - net.core) * cut, cut)

    def grad_there(j, carry):
        part = dot(g_low[:, pl.ds(theirs_at, cut)], low[j], 0, 0)
        gh_there[j] = part.astype(BF16).reshape(block)
        return carry

    lax.fori_loop(0, N_IN, grad_there, 0)
    sends.append(
        remote(gh_there, gh_other, send_sem.at[at], recv_sem.at[3 + net.near + net.far], net.partner)
    )
    landed(gt.at[:, 1 - net.core], recv_sem.at[2 + net.near + net.far])
    for j in range(N_IN):
        gtop[j] = jnp.concatenate([gt[j, 0], gt[j, 1]], axis=0).astype(F32)
    landed(gh_other, recv_sem.at[3 + net.near + net.far])

    def grad_here(j, carry):
        part = dot(g_low[:, pl.ds(mine_at, cut)], low[j], 0, 0)
        gh[j] = (part.reshape(block) + gh_other[j].astype(F32)).astype(BF16)
        return carry

    lax.fori_loop(0, N_IN, grad_here, 0)
    store = pltpu.make_async_copy(gh, gh_h, out_sem)
    store.start()
    store.wait()
    for copy in sends:
        copy.wait_send()


def head_step(devices, pooled, head, bias, pick, point, numbers, hot):
    batch = pooled.shape[1]
    half = batch // 2
    shape = jax.ShapeDtypeStruct
    any_space = pl.BlockSpec(memory_space=pl.ANY)
    vmem = pl.BlockSpec(memory_space=pltpu.VMEM)
    dma = pltpu.SemaphoreType.DMA
    count = 4 + slots_total(devices)
    first, second, third = bit_split(devices)
    near, far = 1 << (first + second), 1 << third
    return pl.pallas_call(
        functools.partial(head_kernel, devices, float(HEIGHT * WIDTH)),
        out_shape=[
            shape((16, LANES), F32),
            shape((N_IN, batch, LANES), F32),
            shape((N_IN, WIDE // 2 // HALF, HALF, LANES), BF16),
        ],
        in_specs=[vmem, any_space] + [vmem] * 5,
        out_specs=[vmem, vmem, any_space],
        scratch_shapes=[
            pltpu.VMEM((N_IN, WIDE, LANES), BF16),
            pltpu.VMEM((N_IN, half, LANES), BF16),
            pltpu.VMEM((N_IN, half, LANES), BF16),
            pltpu.VMEM((N_IN, half, LANES), BF16),
            pltpu.VMEM((2, far, near, half, WIDE), BF16),
            pltpu.VMEM((half, WIDE), F32),
            pltpu.VMEM((half, WIDE), BF16),
            pltpu.VMEM((N_IN, WIDE // 2 // HALF, HALF, LANES), BF16),
            pltpu.VMEM((N_IN, WIDE // 2 // HALF, HALF, LANES), BF16),
            pltpu.VMEM((N_IN, WIDE // 2 // HALF, HALF, LANES), BF16),
            pltpu.VMEM((N_IN, 2, half, LANES), BF16),
            dma(()),
            dma(()),
            dma((count,)),
            dma((count,)),
        ],
        compiler_params=pltpu.CompilerParams(
            collective_id=5, has_side_effects=True, vmem_limit_bytes=60 * 2**20
        ),
    )(pooled, head, bias, pick, point, numbers, hot)


def pieces(part, j):
    return part[:, j * LANES : (j + 1) * LANES].astype(BF16).reshape(-1, 2, HALF, LANES)


def backward_kernel(devices, total_count, *refs):
    refs = list(refs)
    take = lambda n: [refs.pop(0) for _ in range(n)]
    names = ["zc", "hb", "hp", "zb", "za", "wi", "wm", "wo"]
    source = {}
    head_h, = take(1)
    source["xf", 1], source["xb", 1] = take(2)
    for at in (0, 1):
        for name in names:
            source[name, at] = refs.pop(0)
    x_in, gtop = take(2)
    stats_of = [take(3) for _ in range(LAYERS)]
    params_of = take(LAYERS)
    live, extra = take(2)
    out_of = [take(3) for _ in range(LAYERS)]
    head_out, = take(1)
    small_of = take(LAYERS)
    field, xb, zc, hb, hp, zb, za, wi, wm, wo = take(10)
    place = dict(xf=field, xb=xb, zc=zc, hb=hb, hp=hp, zb=zb, za=za, wi=wi, wm=wm, wo=wo)
    g_side, g_mid, r_side, r_mid = take(4)
    ec, ep, ea, ub = take(4)
    head, land_last, land_mid, land_far = take(4)
    stage_m, stage_c = take(2)
    bufs_of = [take(3) for _ in range(LAYERS)]
    in_sem, out_sem, send_sem, recv_sem, halo_sem, pair_sem = take(6)
    head_in, head_send, last_recv, mid_recv, far_recv = take(5)

    net = Net(devices)
    net.hello()
    order = ["zc", "xf", "wo", "zb", "hb", "hp", "wm", "za", "wi", "xb"]
    loading = {}

    def start(name, at):
        copy = pltpu.make_async_copy(
            source[name, at], place[name], in_sem.at[at, order.index(name)]
        )
        copy.start()
        loading[name, at] = copy

    def need(name, at):
        loading[name, at].wait()

    for name in order:
        start(name, 1)
    head_load = pltpu.make_async_copy(head_h, head, head_in)
    head_load.start()
    clear_edges(ep, net.core)
    quarter = za.shape[1] // ROW_SLOTS
    batch = quarter // WIDTH
    groups = N_IN // N_MID
    side_rows, mid_rows = M // 32, 9 * M // 32
    sends = []
    stored = []

    def store(src, dst):
        copy = pltpu.make_async_copy(src, dst, out_sem.at[len(stored)])
        copy.start()
        stored.append(copy)
        return copy

    def slope(y):
        sigma = half_tanh(y)
        return sigma * (1.0 + y * (1.0 - sigma))

    def row(ref, j):
        return ref[pl.ds(j, 1)]

    def swap(grad, other, at, which):
        return remote(
            grad.at[:, 1 - net.core],
            other,
            pair_sem.at[at, 0, which],
            pair_sem.at[at, 1, which],
            net.partner,
        )

    def fold(copy, grad, other, at, which, out):
        landed(other, pair_sem.at[at, 1, which])
        copy.wait_send()

        def step(i, carry):
            part = pl.ds(i * 16, 16)
            other[part] = (grad[part, net.core].astype(F32) + other[part].astype(F32)).astype(BF16)
            return carry

        lax.fori_loop(0, grad.shape[0] // 16, step, 0)
        return store(other, out)

    mid, last, far = axis_masks(devices, net.core)
    me, core = net.me, net.core
    head_sent = []

    def head_copy(owner, land, sems, slot, device):
        head_sent.append(
            remote(head.at[owner], land.at[slot], head_send.at[len(head_sent)], sems.at[slot], device)
        )

    def head_add(owners, land, sems):
        for slot in range(len(owners)):
            landed(land.at[slot], sems.at[slot])

        def step(i, carry):
            for slot, owner in enumerate(owners):
                head[owner, i] = (
                    head[owner, i].astype(F32) + land[slot, i].astype(F32)
                ).astype(BF16)
            return carry

        lax.fori_loop(0, head.shape[1], step, 0)

    def head_first():
        head_load.wait()
        slot = 0
        for q in last[1:]:
            for m in mid:
                for z in far:
                    head_copy(me ^ q ^ m ^ z, land_last, last_recv, slot, (me ^ q, core))
                    slot += 1

    def head_second():
        owners = [me ^ m ^ z for m in mid for z in far]
        for j in range(len(last) - 1):
            view = pl.ds(j * len(owners), len(owners))
            head_add(owners, land_last.at[view], last_recv.at[view])
        slot = 0
        for m in mid[1:]:
            for z in far:
                head_copy(me ^ m ^ z, land_mid, mid_recv, slot, (me ^ m, core))
                slot += 1

    def head_third():
        owners = [me ^ z for z in far]
        for j in range(len(mid) - 1):
            view = pl.ds(j * len(owners), len(owners))
            head_add(owners, land_mid.at[view], mid_recv.at[view])
        for slot, z in enumerate(far[1:]):
            head_copy(me ^ z, land_far, far_recv, slot, (me ^ z, core))

    def head_last():
        for slot in range(len(far) - 1):
            landed(land_far.at[slot], far_recv.at[slot])

        def step(i, carry):
            total = head[me, i].astype(F32)
            for slot in range(len(far) - 1):
                total = total + land_far[slot, i].astype(F32)
            head[me, i] = total.astype(BF16)
            return carry

        lax.fori_loop(0, head.shape[1], step, 0)
        for copy in head_sent:
            copy.wait_send()
        return store(head.at[me], head_out)

    def layer(at, fillers):
        top = at == 1
        stat_a, stat_b, stat_c = stats_of[at]
        params, small = params_of[at], small_of[at]
        gi_h, gm_h, go_h = out_of[at]
        state = {}

        def refill(name):
            if top:
                start(name, 0)

        def totals(stage, which, small_at, n, fillers):
            total, copies = reduce_all(
                net,
                stage[...],
                bufs_of[at][which],
                send_sem.at[3 * at + which],
                recv_sem.at[3 * at + which],
                plain_sum,
                fillers=fillers,
            )
            sends.extend(copies)
            small[small_at : small_at + 2 * n] = total[: 2 * n]
            return total

        need("zc", at)
        if top:
            need("xf", at)

        def slab_c(j, carry):
            mean, scale = row(stat_c, j), row(stat_c, N_IN + j)
            gain, shift = row(params, 4 * N_MID + j), row(params, 4 * N_MID + N_IN + j)
            total = jnp.zeros((8, LANES), F32)
            crossed = jnp.zeros((8, LANES), F32)
            for q in range(4):
                rows = pl.ds(q * quarter, quarter)
                normed = (zc[j, rows] - mean) * scale
                if top:
                    x = field[j, rows]
                    g = jnp.concatenate([gtop[j]] * WIDTH, axis=0)
                else:
                    x = x_in[rows, pl.ds(pl.multiple_of(j * LANES, LANES), LANES)].astype(F32)
                    g = field[j, rows]
                u = g * live[rows] * slope(normed * gain + shift + x)
                field[j, rows] = u
                total = total + column_sum(u)
                crossed = crossed + column_sum(u * normed)
            stage_c[pl.ds(j, 1)] = jnp.sum(crossed, axis=0, keepdims=True)
            stage_c[pl.ds(N_IN + j, 1)] = jnp.sum(total, axis=0, keepdims=True)
            return carry

        lax.fori_loop(0, N_IN, slab_c, 0)
        if top:
            stage_c[2 * N_IN :] = extra[...]
            net.ready()
        else:
            stage_c[2 * N_IN :] = jnp.zeros(extra.shape, F32)
        total_c = totals(stage_c, 2, 4 * N_MID, N_IN, fillers)
        small[4 * N_MID + 2 * N_IN :] = total_c[2 * N_IN :]
        if not top:
            head_third()

        def back_c(j, carry):
            mean, scale = row(stat_c, j), row(stat_c, N_IN + j)
            gain = row(params, 4 * N_MID + j)
            cross = row(small, 4 * N_MID + j) / total_count
            plain = row(small, 4 * N_MID + N_IN + j) / total_count
            for q in range(4):
                rows = pl.ds(q * quarter, quarter)
                normed = (zc[j, rows] - mean) * scale
                e = live[rows] * ((gain * scale) * (field[j, rows] - plain - normed * cross))
                ec[j, rows] = e.astype(BF16)
            return carry

        lax.fori_loop(0, N_IN, back_c, 0)
        refill("zc")
        need("wo", at)
        product = dot(lanes_of(ec, 0, N_IN), lanes_of(wo, 0, N_IN), 1, 1)
        for j in range(N_MID):
            ub[j] = product[:, j * LANES : (j + 1) * LANES]
        refill("wo")
        need("zb", at)

        def sums_of(z_ref, stat, gain_at):
            def slab(j, carry):
                mean, scale = row(stat, j), row(stat, N_MID + j)
                gain, shift = row(params, gain_at + j), row(params, gain_at + N_MID + j)
                total = jnp.zeros((8, LANES), F32)
                crossed = jnp.zeros((8, LANES), F32)
                for q in range(4):
                    rows = pl.ds(q * quarter, quarter)
                    normed = (z_ref[j, rows] - mean) * scale
                    u = ub[j, rows] * live[rows] * slope(normed * gain + shift)
                    ub[j, rows] = u
                    total = total + column_sum(u)
                    crossed = crossed + column_sum(u * normed)
                stage_m[pl.ds(j, 1)] = jnp.sum(crossed, axis=0, keepdims=True)
                stage_m[pl.ds(N_MID + j, 1)] = jnp.sum(total, axis=0, keepdims=True)
                return carry

            lax.fori_loop(0, N_MID, slab, 0)

        def back_of(z_ref, stat, gain_at, j, rows):
            normed = (z_ref[j, rows] - row(stat, j)) * row(stat, N_MID + j)
            cross = row(small, gain_at + j) / total_count
            plain = row(small, gain_at + N_MID + j) / total_count
            factor = row(params, gain_at + j) * row(stat, N_MID + j)
            return (live[rows] * (factor * (ub[j, rows] - plain - normed * cross))).astype(BF16)

        sums_of(zb, stat_b, 2 * N_MID)
        need("hb", at)

        def grad_out(first, last):
            def group(g, carry):
                part = dot(lanes_of(hb, 0, N_MID), lanes_of(ec, g * N_MID, N_MID), 0, 0)
                for j in range(N_MID):
                    g_side[pl.ds((g * N_MID + j) * side_rows, side_rows)] = pieces(part, j)
                return carry

            return lambda: lax.fori_loop(first, last, group, 0)

        totals(
            stage_m, 1, 2 * N_MID, N_MID,
            [grad_out(0, 1), grad_out(1, groups - 1), grad_out(groups - 1, groups)],
        )
        refill("hb")
        out_swap = swap(g_side, r_side, at, 0)
        if top:
            head_first()

        def fill_b(slot):
            rows = pl.ds(slot * quarter, quarter)

            def slab(j, carry):
                e = back_of(zb, stat_b, 2 * N_MID, j, rows)
                ep[j, pl.ds(slot + 1, 1), pl.ds(1, WIDTH)] = e.reshape(1, WIDTH, batch, LANES)
                return carry

            lax.fori_loop(0, N_MID, slab, 0)

        edge = edge_first(
            net, fill_b, lambda: send_edge(ep, net, halo_sem.at[at, 0], halo_sem.at[at, 1])
        )
        refill("zb")
        need("hp", at)
        need("wm", at)
        ub[...] = jnp.zeros(ub.shape, F32)

        def grad_mid(first, last):
            def one(t, carry):
                part = dot(window(hp, t // 3, lax.rem(t, 3)), window(ep, 1, 1), 0, 0)
                for j in range(N_MID):
                    g_mid[pl.ds(j * mid_rows + t * side_rows, side_rows)] = pieces(part, j)
                return carry

            return lambda: lax.fori_loop(first, last, one, 0)

        def tap(t):
            k = pl.ds(pl.multiple_of(t * M, M), M)
            part = dot(
                window(ep, 2 - t // 3, 2 - lax.rem(t, 3)),
                jnp.concatenate([wm[j, k] for j in range(N_MID)], axis=-1),
                1,
                1,
            )
            for j in range(N_MID):
                ub[j] = ub[j] + part[:, j * LANES : (j + 1) * LANES]

        def middle(i, carry):
            tap(i + 3)
            return carry

        def outer(i, carry):
            tap(jnp.where(i < 3, i, i + 3))
            return carry

        lax.fori_loop(0, 3, middle, 0)
        edge_landed(ep, net, halo_sem.at[at, 1])
        edge.wait_send()
        lax.fori_loop(0, 6, outer, 0)
        refill("wm")
        out_store = fold(out_swap, g_side, r_side, at, 0, go_h)
        need("za", at)
        sums_of(za, stat_a, 0)
        out_store.wait()
        totals(stage_m, 0, 0, N_MID, [grad_mid(0, 2), grad_mid(2, 5), grad_mid(5, 9)])
        refill("hp")
        mid_swap = swap(g_mid, r_mid, at, 1)
        if top:
            head_second()

        def fill_a(j, carry):
            for q in range(4):
                rows = pl.ds(q * quarter, quarter)
                ea[j, rows] = back_of(za, stat_a, 0, j, rows)
            return carry

        lax.fori_loop(0, N_MID, fill_a, 0)
        refill("za")
        if top:
            need("wi", at)

            def grad_field(g, carry):
                k = pl.ds(pl.multiple_of(g * M, M), M)
                part = dot(
                    lanes_of(ea, 0, N_MID),
                    jnp.concatenate([wi[j, k] for j in range(N_MID)], axis=-1),
                    1,
                    1,
                )
                for j in range(N_MID):
                    slab = g * N_MID + j
                    field[slab] = field[slab] + part[:, j * LANES : (j + 1) * LANES]
                return carry

            lax.fori_loop(0, groups, grad_field, 0)

        def grad_in(g, carry):
            if top:
                x = lanes_of(xb, g * N_MID, N_MID)
            else:
                x = x_in[:, pl.ds(pl.multiple_of(g * M, M), M)]
            part = dot(x, lanes_of(ea, 0, N_MID), 0, 0)
            for j in range(N_MID):
                g_side[pl.ds((j * groups + g) * side_rows, side_rows)] = pieces(part, j)
            return carry

        def first_part():
            if top:
                need("xb", at)
            lax.fori_loop(0, groups, grad_in, 0)
            state["swap"] = swap(g_side, r_side, at, 2)

        def second_part():
            state["mid"] = fold(mid_swap, g_mid, r_mid, at, 1, gm_h)

        def third_part():
            state["in"] = fold(state["swap"], g_side, r_side, at, 2, gi_h)
            state["mid"].wait()
            state["in"].wait()

        return [first_part, second_part, third_part]

    rest = layer(1, [])
    final = layer(0, rest)
    head_store = head_last()
    for step in final:
        step()
    head_store.wait()
    for copy in sends:
        copy.wait_send()


def backward_pass(devices, total_count, head, xf, xb, kept, weights, x, gtop, params, live, extra):
    shape = jax.ShapeDtypeStruct
    any_space = pl.BlockSpec(memory_space=pl.ANY)
    vmem = pl.BlockSpec(memory_space=pltpu.VMEM)
    dma = pltpu.SemaphoreType.DMA
    total = slots_total(devices)
    rows = live.shape[0]
    big = lambda s: pltpu.VMEM(s.shape, s.dtype)
    each = []
    for at in range(LAYERS):
        za, hp, zb, hb, zc = kept[at][:5]
        each.append([zc, hb, hp, zb, za] + list(weights[3 * at : 3 * at + 3]))
    ins = [head, xf, xb] + each[0] + each[1]
    small_ins = [x, gtop]
    for at in range(LAYERS):
        small_ins += kept[at][5:]
    small_ins += list(params) + [live, extra]
    first, second, third = bit_split(devices)
    n_mid, n_last, n_far = 1 << first, 1 << second, 1 << third
    lands = [(n_last - 1) * n_mid * n_far, (n_mid - 1) * n_far, n_far - 1]
    side = N_IN * M // 32
    middle = N_MID * 9 * M // 32
    small_rows = 4 * N_MID + 2 * N_IN + extra.shape[0]
    stage_rows = [2 * N_MID, 2 * N_MID, 2 * N_IN + extra.shape[0]]
    grads = [shape((n, HALF, LANES), BF16) for n in (side, middle, side)]
    out = pl.pallas_call(
        functools.partial(backward_kernel, devices, total_count),
        out_shape=grads * LAYERS
        + [shape(head.shape[1:], BF16)]
        + [shape((small_rows, LANES), F32)] * LAYERS,
        in_specs=[any_space] * len(ins) + [vmem] * len(small_ins),
        out_specs=[any_space] * (3 * LAYERS + 1) + [vmem] * LAYERS,
        scratch_shapes=[big(a) for a in [xf, xb] + each[0]]
        + [
            pltpu.VMEM((side, 2, HALF, LANES), BF16),
            pltpu.VMEM((middle, 2, HALF, LANES), BF16),
            pltpu.VMEM((side, HALF, LANES), BF16),
            pltpu.VMEM((middle, HALF, LANES), BF16),
            pltpu.VMEM((N_IN, rows, LANES), BF16),
            pltpu.VMEM(kept[0][1].shape, BF16),
            pltpu.VMEM((N_MID, rows, LANES), BF16),
            pltpu.VMEM((N_MID, rows, LANES), F32),
            big(head),
        ]
        + [pltpu.VMEM((n,) + head.shape[1:], BF16) for n in lands]
        + [
            pltpu.VMEM((2 * N_MID, LANES), F32),
            pltpu.VMEM((stage_rows[2], LANES), F32),
        ]
        + [pltpu.VMEM((total, n, LANES), F32) for n in stage_rows] * LAYERS
        + [
            dma((LAYERS, 10)),
            dma((3 * LAYERS + 1,)),
            dma((3 * LAYERS, total)),
            dma((3 * LAYERS, total)),
            dma((LAYERS, 2)),
            dma((LAYERS, 2, 3)),
            dma(()),
            dma((sum(lands),)),
            dma((lands[0],)),
            dma((lands[1],)),
            dma((lands[2],)),
        ],
        compiler_params=pltpu.CompilerParams(
            collective_id=6, has_side_effects=True, vmem_limit_bytes=62 * 2**20
        ),
    )(*ins, *small_ins)
    return out[: 3 * LAYERS], out[3 * LAYERS], out[3 * LAYERS + 1 :]


def adamw(values_old, gradient, moment_one, moment_two, step_rate):
    one_new = BETA_FIRST * moment_one + (1.0 - BETA_FIRST) * gradient
    two_new = BETA_SECOND * moment_two + (1.0 - BETA_SECOND) * gradient * gradient
    fixed_one = 1.0 - BETA_FIRST**STEP
    fixed_two = 1.0 - BETA_SECOND**STEP
    update = one_new / fixed_one / (jnp.sqrt(two_new / fixed_two) + EPS_ADAM)
    return (one_new, two_new, values_old - step_rate * (update + DECAY_WEIGHT * values_old))


def body(
    images,
    row_split,
    labels,
    partners,
    image_weight,
    owner_slot,
    conv_master,
    conv_stats,
    conv_roots,
    head_master,
    head_moment_one,
    head_moment_two,
    small_params,
    small_moment_one,
    small_moment_two,
):
    devices = lax.axis_size("dp")
    core_index = lax.axis_index("rows")
    batch_size = images.shape[0]
    half_batch = batch_size // 2
    slot_count = images.shape[1]
    total_images = partners.shape[0]
    live_count = float(total_images * HEIGHT * WIDTH)
    owned = conv_master.shape[0]
    head_rows = head_master.shape[0]

    slot_index = (owner_slot // owned) * (2 * owned) + owner_slot % owned
    weights = list(bring_weights(conv_master, slot_index, devices))
    head_t = jnp.pad(head_master.T.astype(BF16), ((0, WIDE - CLASSES), (0, 0)))
    head_t, weights[0] = lax.optimization_barrier((head_t, weights[0]))
    head_all = lax.all_gather(head_t, "dp", axis=0)
    if head_rows != LANES:
        head_all = head_all.transpose(1, 0, 2).reshape(WIDE, N_IN, LANES).transpose(1, 0, 2)

    slot_ids = core_index * slot_count + jnp.arange(slot_count, dtype=jnp.int32)
    first_live = (ROW_SLOTS - row_split)[:, None]
    live = (slot_ids[None, :] >= first_live) & (slot_ids[None, :] < first_live + HEIGHT)
    rows = slot_count * WIDTH * batch_size
    live_rows = jnp.broadcast_to(
        live.T.astype(F32)[:, None, :, None], (slot_count, WIDTH, batch_size, LANES)
    ).reshape(rows, LANES)
    first = images.transpose(1, 2, 0, 3).reshape(rows, C)
    stride = 4 * M + 2 * C
    params = [
        small_params[at * stride : (at + 1) * stride].reshape(-1, LANES) for at in range(LAYERS)
    ]
    bias = jnp.pad(small_params[LAYERS * stride :], (0, WIDE - CLASSES))[None, :]

    kept, field, low, pooled = forward_pass(
        devices, live_count, first, weights, params, live_rows
    )

    def by_core(v):
        return v.reshape(devices, 2, half_batch).transpose(1, 0, 2).reshape(-1)

    weight_f = image_weight.astype(F32)
    weight_total = jnp.sum(weight_f)
    own_start = (lax.axis_index("dp") * 2 + core_index) * half_batch
    own_ids = own_start + jnp.arange(half_batch, dtype=jnp.int32)
    own_weight = lax.dynamic_slice_in_dim(weight_f, own_start, half_batch)
    own_partner = lax.dynamic_slice_in_dim(partners, own_start, half_batch)
    own_label = lax.dynamic_slice_in_dim(labels, core_index * half_batch, half_batch)
    ids = by_core(jnp.arange(total_images, dtype=jnp.int32))
    pick = (own_partner[:, None] == ids[None, :]).astype(BF16)
    point = (by_core(partners)[None, :] == own_ids[:, None]).astype(F32) * by_core(weight_f)[None, :]
    in_weight = jnp.sum(point, axis=1)
    hot = (own_label[:, None] == jnp.arange(WIDE, dtype=jnp.int32)[None, :]).astype(F32)
    lane = jnp.arange(LANES)[None, :]
    numbers = jnp.where(
        lane == 0, own_weight[:, None], jnp.where(lane == 1, in_weight[:, None], weight_total)
    )
    extra, g_top, grad_head = head_step(
        devices,
        pooled,
        head_all,
        bias,
        pick,
        point.astype(BF16),
        numbers,
        hot,
    )
    head_blocks = head_rows // 4
    if head_rows != LANES:
        grad_head = (
            grad_head.reshape(N_IN, WIDE // 2, LANES)
            .transpose(1, 0, 2)
            .reshape(WIDE // 2, devices, head_rows)
            .transpose(1, 0, 2)
            .reshape(devices, head_blocks, HALF, LANES)
        )
    grads, head_mine, (small_bottom, small_top) = backward_pass(
        devices, live_count, grad_head, field, low, kept, weights, first, g_top, params, live_rows, extra
    )
    head_sum, conv_grad, stats_new, step = deliver_blocks(
        grads,
        head_mine,
        block_places(owner_slot),
        conv_stats,
        conv_roots,
        devices,
    )
    master_new = conv_master - RATE_SHAMPOO * step
    head_grad = head_sum.reshape(WIDE, head_rows)[:CLASSES].T.astype(F32)
    head_one, head_two, head_new = adamw(
        head_master, head_grad, head_moment_one, head_moment_two, RATE_HEAD
    )
    layer_rows = stride // LANES
    grad_bias = small_top[layer_rows : layer_rows + WIDE // LANES].reshape(-1)[:CLASSES]
    loss_sum = small_top[layer_rows + WIDE // LANES, 0]
    grad_small = jnp.concatenate(
        [small_bottom[:layer_rows].reshape(-1), small_top[:layer_rows].reshape(-1), grad_bias]
    )
    small_one, small_two, small_new = adamw(
        small_params, grad_small, small_moment_one, small_moment_two, RATE_SMALL
    )
    return (
        loss_sum,
        weight_total,
        conv_grad,
        stats_new,
        master_new,
        master_new.astype(BF16),
        head_one,
        head_two,
        head_new,
        head_new.astype(BF16),
        small_one,
        small_two,
        small_new,
    )


def solution(mesh):
    in_specs = (
        P("dp", "rows", None, None),
        P("dp"),
        P("dp"),
        P(),
        P(),
        P(),
        P("dp", None),
        P("dp", None, None),
        P("dp", None, None),
        P("dp", None),
        P("dp", None),
        P("dp", None),
        P(),
        P(),
        P(),
    )
    out_specs = (
        P(),
        P(),
        P("dp", None),
        P("dp", None, None),
        P("dp", None),
        P("dp", None),
        P("dp", None),
        P("dp", None),
        P("dp", None),
        P("dp", None),
        P(),
        P(),
        P(),
    )
    return jax.shard_map(body, mesh=mesh, in_specs=in_specs, out_specs=out_specs, check_vma=False)
```

```python
import functools

import jax
import jax.numpy as jnp
import numpy as np
from jax import lax
from jax.experimental import pallas as pl
from jax.experimental.pallas import tpu as pltpu
from jax.sharding import PartitionSpec as P

C = 2048
M = 512
CLASSES = 1000
HEIGHT = 7
WIDTH = 7
ROW_SLOTS = 4
LAYERS = 2
BLOCK = 64
STEP = 5


EPS_NORM = 1e-05
MATCH_WEIGHT = 4.0
DECAY_STATS = 0.5
RATE_SHAMPOO = 0.15
RATE_HEAD = 0.03
RATE_SMALL = 0.2
BETA_FIRST = 0.9
BETA_SECOND = 0.95
EPS_ADAM = 1e-08
DECAY_WEIGHT = 0.01


C = 2048
M = 512
CLASSES = 1000
HEIGHT = 7
WIDTH = 7
ROW_SLOTS = 4
LAYERS = 2
BLOCK = 64
STEP = 5


EPS_NORM = 1e-05
MATCH_WEIGHT = 4.0
DECAY_STATS = 0.5
RATE_SHAMPOO = 0.15
RATE_HEAD = 0.03
RATE_SMALL = 0.2
BETA_FIRST = 0.9
BETA_SECOND = 0.95
EPS_ADAM = 1e-08
DECAY_WEIGHT = 0.01


MESH_IDS = pl.DeviceIdType.MESH
HALF = 16
LANES = 128


def bit_split(devices):
    bits = devices.bit_length() - 1
    first = bits // 3
    second = (bits - first) // 2
    return first, second, bits - first - second


def greet(peers):
    barrier = pltpu.get_barrier_semaphore()
    for peer in peers:
        pl.semaphore_signal(barrier, inc=1, device_id=peer, device_id_type=MESH_IDS)
    pl.semaphore_wait(barrier, len(peers))


def axis_masks(devices, core):
    first, second, third = bit_split(devices)
    low = [m for m in range(1, 1 << first)]
    high = [m << first for m in range(1, 1 << second)]
    if first == second:
        one = [jnp.where(core == 0, h, l) for h, l in zip(high, low)]
        two = [jnp.where(core == 0, l, h) for h, l in zip(high, low)]
    else:
        one, two = low, high
    far = [m << (first + second) for m in range(1, 1 << third)]
    return [0] + one, [0] + two, [0] + far


def even_spans(count):
    parts = 8 if count % 8 == 0 else 1
    return [(i * (count // parts), count // parts) for i in range(parts)]


def spans_of(count):
    spans, at = [], 0
    while at < count:
        rest = count - at
        size = 16 if rest > 8 else rest
        spans.append((at, size))
        at += size
    return spans


def slab_shape(shape):
    return (shape[1] // LANES, shape[0], LANES)


def matrix_list():
    shapes = []
    for _ in range(LAYERS):
        shapes += [(C, M), (9 * M, M), (M, C)]
    return shapes


BRING_LATE = 2


def bring_kernel(devices, spans, idx_ref, m_ref, *refs):
    shapes = matrix_list()
    n = len(shapes)
    outs, bufs, (g_ref, stage, send_sem, recv_sem, out_sem) = refs[:n], refs[n : 2 * n], refs[2 * n :]
    me = lax.axis_index("dp")
    core = lax.axis_index("rows")
    count = m_ref.shape[0]
    parts = len(spans)
    mid, last, far = axis_masks(devices, core)
    partner = (me, 1 - core)
    peers = [(me ^ m, core) for m in far[1:] + mid[1:] + last[1:]] + [partner]
    barrier = pltpu.get_barrier_semaphore()
    for peer in peers:
        pl.semaphore_signal(barrier, inc=1, device_id=peer, device_id_type=MESH_IDS)

    def spread(first, rows):
        for m in range(HALF):
            one = m_ref[pl.ds(first, rows), m * LANES : (m + 1) * LANES]
            two = m_ref[pl.ds(first, rows), (HALF + m) * LANES : (HALF + m + 1) * LANES]
            h, r = m // (HALF // 2), 2 * (m % (HALF // 2))
            for i in range(2):
                cut = slice(i * BLOCK, (i + 1) * BLOCK)
                stage[h, pl.ds(first * HALF + r + i, rows, stride=HALF)] = jnp.concatenate(
                    [one[:, cut], two[:, cut]], axis=1
                )

    def group(i, carry):
        spread(pl.multiple_of(i * 8, 8), 8)
        return carry

    lax.fori_loop(0, count // 8, group, 0)
    if count % 8:
        spread(count // 8 * 8, count % 8)

    def round_one(k, carry):
        for h in range(2):
            rows = pl.ds(pl.multiple_of(k * HALF, HALF), HALF)
            g_ref[(me * 2 + h) * count + k] = stage[h, rows].astype(jnp.bfloat16)
        return carry

    lax.fori_loop(0, count, round_one, 0)
    pl.semaphore_wait(barrier, len(peers))
    sent = []

    def piece(owner, half, part):
        first, size = spans[part]
        return g_ref.at[pl.ds((owner * 2 + half) * count + first, size)]

    def send(owner, part, device):
        copy = pltpu.make_async_remote_copy(
            src_ref=piece(owner, core, part),
            dst_ref=piece(owner, core, part),
            send_sem=send_sem.at[len(sent)],
            recv_sem=recv_sem.at[owner, core, part],
            device_id=device,
            device_id_type=MESH_IDS,
        )
        copy.start()
        sent.append(copy)

    def arrived(owner, half, part):
        ref = piece(owner, half, part)
        pltpu.make_async_copy(ref, ref, recv_sem.at[owner, half, part]).wait()

    def onward(owner, part, masks):
        arrived(owner, core, part)
        for m in masks:
            send(owner, part, (me ^ m, core))
        send(owner, part, partner)

    early = parts - BRING_LATE if parts > BRING_LATE else parts
    for part in range(parts):
        order = far[1:] + last[1:] + mid[1:] if part < early else mid[1:] + far[1:] + last[1:]
        for m in order:
            send(me, part, (me ^ m, core))
    for tick in range(parts + 2):
        part = tick
        if part < parts:
            if part < early:
                for z in far[1:]:
                    onward(me ^ z, part, last[1:] + mid[1:])
            else:
                for m in mid[1:]:
                    onward(me ^ m, part, far[1:] + last[1:])
        part = tick - 1
        if 0 <= part < parts:
            if part < early:
                for m in mid[1:]:
                    for z in far:
                        onward(me ^ m ^ z, part, last[1:])
            else:
                for z in far[1:]:
                    onward(me ^ z, part, last[1:])
                for z in far[1:]:
                    for m in mid[1:]:
                        onward(me ^ z ^ m, part, last[1:])
        part = tick - 2
        if 0 <= part < parts:
            for q in last[1:]:
                for z in far:
                    for m in mid:
                        onward(me ^ q ^ z ^ m, part, [])
    for step in range(1, devices):
        for part in range(parts):
            arrived(me ^ step, 1 - core, part)

    base = 0
    copies = []
    for at, (rows, cols) in enumerate(shapes):
        pairs = cols // LANES
        buf = bufs[at]

        def strip(r, carry, base=base, pairs=pairs, buf=buf):
            for m in range(pairs):
                even = idx_ref[base + r * (2 * pairs) + 2 * m]
                odd = idx_ref[base + r * (2 * pairs) + 2 * m + 1]
                for h in range(2):
                    e = g_ref[even + h * count]
                    o = g_ref[odd + h * count]
                    buf[m, pl.ds(r * BLOCK + h * HALF, HALF)] = jnp.concatenate(
                        [e[:, :BLOCK], o[:, :BLOCK]], axis=1
                    )
                    buf[m, pl.ds(r * BLOCK + 2 * HALF + h * HALF, HALF)] = jnp.concatenate(
                        [e[:, BLOCK:], o[:, BLOCK:]], axis=1
                    )
            return carry

        lax.fori_loop(0, rows // BLOCK, strip, 0, unroll=8 // (pairs // 4))
        copy = pltpu.make_async_copy(buf, outs[at], out_sem.at[at])
        copy.start()
        copies.append(copy)
        base += (rows // BLOCK) * (cols // BLOCK)
    for copy in copies:
        copy.wait()
    for copy in sent:
        copy.wait_send()


def bring_weights(master, index, devices):
    count = master.shape[0]
    spans = even_spans(count)
    parts = len(spans)
    shapes = [slab_shape(s) for s in matrix_list()]
    dma = pltpu.SemaphoreType.DMA
    return pl.pallas_call(
        functools.partial(bring_kernel, devices, spans),
        out_shape=[jax.ShapeDtypeStruct(s, jnp.bfloat16) for s in shapes],
        in_specs=[
            pl.BlockSpec(memory_space=pltpu.SMEM),
            pl.BlockSpec(memory_space=pltpu.VMEM),
        ],
        out_specs=[pl.BlockSpec(memory_space=pl.ANY)] * len(shapes),
        scratch_shapes=[pltpu.VMEM(s, jnp.bfloat16) for s in shapes]
        + [
            pltpu.VMEM((devices * 2 * count, HALF, LANES), jnp.bfloat16),
            pltpu.VMEM((2, count * HALF, LANES), jnp.float32),
            dma((3 * devices * parts,)),
            dma((devices, 2, parts)),
            dma((len(shapes),)),
        ],
        compiler_params=pltpu.CompilerParams(
            collective_id=1, has_side_effects=True, vmem_limit_bytes=56 * 2**20
        ),
    )(index, master)


def split_two(v):
    high = v.astype(BF16)
    return high, (v - high.astype(F32)).astype(BF16)


def shampoo_rows(final, updates, stats, roots, grads, flat, turn, first, group):
    for k in range(group):
        rows = pl.ds(k * HALF, HALF)
        parts = [final[h, first + k].astype(F32) for h in range(2)]
        for h in range(2):
            flat[h, rows] = parts[h]
        tile = jnp.concatenate([p[:, :BLOCK] for p in parts] + [p[:, BLOCK:] for p in parts], axis=0)
        low = tile.astype(BF16)
        old = stats[first + k]
        sides = roots[first + k]
        high, rest = split_two(sides[:, :BLOCK])
        both = dot(jnp.concatenate([high, rest, tile.T.astype(BF16)], axis=0), low, 1, 0)
        stats[first + k] = DECAY_STATS * old + (1.0 - DECAY_STATS) * jnp.concatenate(
            [dot(low, low, 1, 1), both[2 * BLOCK :]], axis=1
        )
        turned = both[:BLOCK] + both[BLOCK : 2 * BLOCK]
        t_high, t_rest = split_two(turned)
        high, rest = split_two(sides)
        wide = jnp.concatenate([high[:, BLOCK:], rest[:, BLOCK:]], axis=1)
        both = dot(jnp.concatenate([t_high, t_rest], axis=0), wide, 1, 0)
        turned = both[:BLOCK, :BLOCK] + both[BLOCK:, :BLOCK] + both[:BLOCK, BLOCK:]
        for h in range(2):
            turn[h, rows] = jnp.concatenate(
                [
                    turned[h * HALF : (h + 1) * HALF],
                    turned[2 * HALF + h * HALF : 2 * HALF + (h + 1) * HALF],
                ],
                axis=1,
            )
    here = pl.ds(first if isinstance(first, int) else pl.multiple_of(first, 8), group)
    for m in range(HALF):
        h, r = m // (HALF // 2), 2 * (m % (HALF // 2))
        tiles = [flat[h, pl.ds(r + i, group, stride=HALF)] for i in range(2)]
        steps = [turn[h, pl.ds(r + i, group, stride=HALF)] for i in range(2)]
        for p in range(2):
            lanes = pl.ds(p * (BLOCK * BLOCK // 2) + m * LANES, LANES)
            cut = slice(p * BLOCK, (p + 1) * BLOCK)
            grads[here, lanes] = jnp.concatenate([v[:, cut] for v in tiles], axis=1)
            updates[here, lanes] = jnp.concatenate([v[:, cut] for v in steps], axis=1)


DELIVER_FAR = ()
AHEAD = 3


def deliver_kernel(devices, spans, code_ref, head_h, *refs):
    n = len(matrix_list())
    grads, refs = refs[:n], refs[n:]
    stats_h, roots_h, head_out, grad_out, stats_out, step_out = refs[:6]
    pool, acc, land_last, land_mid, land_far, final, head_pair = refs[6:13]
    steps, stats, roots, grad_flat, flat, turn = refs[13:19]
    in_sem, send_sem, last_recv, mid_recv, far_recv, end_send, end_recv, own_sem, out_sem = refs[19:]
    me = lax.axis_index("dp")
    core = lax.axis_index("rows")
    count = code_ref.shape[0] // devices
    mid, last, far = axis_masks(devices, core)
    partner = (me, 1 - core)
    peers = [(me ^ m, core) for m in far[1:] + mid[1:] + last[1:]] + [partner]
    barrier = pltpu.get_barrier_semaphore()
    for peer in peers:
        pl.semaphore_signal(barrier, inc=1, device_id=peer, device_id_type=MESH_IDS)
    head = pltpu.make_async_copy(head_h, head_pair.at[core], in_sem.at[n])
    head.start()
    loads = []
    start = 0
    for i, grad in enumerate(grads):
        load = pltpu.make_async_copy(grad, pool.at[pl.ds(start, grad.shape[0])], in_sem.at[i])
        load.start()
        loads.append(load)
        start += grad.shape[0]
    owned = []
    for i, (src, dst) in enumerate([(stats_h, stats), (roots_h, roots)]):
        load = pltpu.make_async_copy(src, dst, own_sem.at[i])
        load.start()
        owned.append(load)
    pl.semaphore_wait(barrier, len(peers))
    head.wait()
    parts = len(spans)
    sent = [
        remote(
            head_pair.at[core], head_pair.at[core], end_send.at[parts], end_recv.at[parts], partner
        )
    ]
    stores = []

    def store(src, dst):
        copy = pltpu.make_async_copy(src, dst, out_sem.at[len(stores)])
        copy.start()
        stores.append(copy)

    def send(owner, span, part, land, sems, at, device):
        copy = pltpu.make_async_remote_copy(
            src_ref=acc.at[owner, span],
            dst_ref=land.at[at, span],
            send_sem=send_sem.at[len(sent) - 1],
            recv_sem=sems.at[at, part],
            device_id=device,
            device_id_type=MESH_IDS,
        )
        copy.start()
        sent.append(copy)

    def arrived(land, sems, at, span, part):
        ref = land.at[at, span]
        pltpu.make_async_copy(ref, ref, sems.at[at, part]).wait()

    def fill(first, size):
        def owner_step(owner, carry):
            def block(k, inner):
                slot = owner * count + first + k
                code = code_ref[slot]
                q = lax.shift_right_logical(code, 1)
                top = pool[q]
                low = pool[q + 1]
                even = jnp.concatenate([top[:, :BLOCK], low[:, :BLOCK]], axis=1)
                odd = jnp.concatenate([top[:, BLOCK:], low[:, BLOCK:]], axis=1)
                acc[owner, first + k] = jnp.where(lax.bitwise_and(code, 1) == 1, odd, even)
                return inner

            return lax.fori_loop(0, size, block, carry, unroll=True)

        lax.fori_loop(0, devices, owner_step, 0)

    def add(owners, lands, first, size):
        def step(i, carry):
            at = first + i
            for owner, (land, j) in zip(owners, lands):
                acc[owner, at] = (
                    acc[owner, at].astype(jnp.float32) + land[j, at].astype(jnp.float32)
                ).astype(jnp.bfloat16)
            return carry

        lax.fori_loop(0, size, step, 0)

    ends = []
    whole_rows = steps.shape[0] % 8 != 0

    def far_second(part):
        return part in DELIVER_FAR

    for tick in range(parts + 3 + AHEAD):
        part = tick
        if part < parts:
            first, size = spans[part]
            span = pl.ds(first, size)
            if part == 0:
                for load in loads:
                    load.wait()
            fill(first, size)
            at = 0
            for q in last[1:]:
                for m in mid[::-1]:
                    for z in far[::-1]:
                        send(
                            me ^ q ^ m ^ z, span, part, land_last, last_recv, at, (me ^ q, core)
                        )
                        at += 1
        part = tick - AHEAD
        if 0 <= part < parts:
            first, size = spans[part]
            span = pl.ds(first, size)
            pairs = [(m, z) for m in mid[::-1] for z in far[::-1]]
            owners, lands = [], []
            for j in range(len(last) - 1):
                for i, (m, z) in enumerate(pairs):
                    at = j * len(pairs) + i
                    arrived(land_last, last_recv, at, span, part)
                    owners.append(me ^ m ^ z)
                    lands.append((land_last, at))
            add(owners, lands, first, size)
            at = 0
            if far_second(part):
                for z in far[1:]:
                    for m in mid[::-1]:
                        send(me ^ m ^ z, span, part, land_far, far_recv, at, (me ^ z, core))
                        at += 1
            else:
                for m in mid[1:]:
                    for z in far[::-1]:
                        send(me ^ m ^ z, span, part, land_mid, mid_recv, at, (me ^ m, core))
                        at += 1
        part = tick - 1 - AHEAD
        if 0 <= part < parts:
            first, size = spans[part]
            span = pl.ds(first, size)
            owners, lands = [], []
            at = 0
            if far_second(part):
                for z in far[1:]:
                    for m in mid[::-1]:
                        arrived(land_far, far_recv, at, span, part)
                        owners.append(me ^ m)
                        lands.append((land_far, at))
                        at += 1
                add(owners, lands, first, size)
                for at, m in enumerate(mid[1:]):
                    send(me ^ m, span, part, land_mid, mid_recv, at, (me ^ m, core))
            else:
                for m in mid[1:]:
                    for z in far[::-1]:
                        arrived(land_mid, mid_recv, at, span, part)
                        owners.append(me ^ z)
                        lands.append((land_mid, at))
                        at += 1
                add(owners, lands, first, size)
                for at, z in enumerate(far[1:]):
                    send(me ^ z, span, part, land_far, far_recv, at, (me ^ z, core))
        part = tick - 2 - AHEAD
        if 0 <= part < parts:
            first, size = spans[part]
            span = pl.ds(first, size)
            land, sems, width = land_far, far_recv, len(far) - 1
            if far_second(part):
                land, sems, width = land_mid, mid_recv, len(mid) - 1
            for at in range(width):
                arrived(land, sems, at, span, part)

            def finish(i, carry, first=first, land=land, width=width):
                at = first + i
                total = acc[me, at].astype(jnp.float32)
                for j in range(width):
                    total = total + land[j, at].astype(jnp.float32)
                final[core, at] = total.astype(jnp.bfloat16)
                return carry

            lax.fori_loop(0, size, finish, 0)
            copy = pltpu.make_async_remote_copy(
                src_ref=final.at[core, span],
                dst_ref=final.at[core, span],
                send_sem=end_send.at[part],
                recv_sem=end_recv.at[part],
                device_id=partner,
                device_id_type=MESH_IDS,
            )
            copy.start()
            ends.append(copy)
        part = tick - 3 - AHEAD
        if 0 <= part < parts:
            first, size = spans[part]
            ref = final.at[1 - core, pl.ds(first, size)]
            pltpu.make_async_copy(ref, ref, end_recv.at[part]).wait()
            if part == 0:
                landed(head_pair.at[1 - core], end_recv.at[parts])
                store(head_pair, head_out)
                for load in owned:
                    load.wait()

            def group(i, carry, first=first):
                shampoo_rows(final, steps, stats, roots, grad_flat, flat, turn, first + i * 8, 8)
                return carry

            lax.fori_loop(0, size // 8, group, 0)
            if size % 8:
                shampoo_rows(
                    final, steps, stats, roots, grad_flat, flat, turn, first + size // 8 * 8, size % 8
                )
            span = pl.ds(first, size)
            store(stats.at[span], stats_out.at[span])
            if not whole_rows:
                store(grad_flat.at[span], grad_out.at[span])
                store(steps.at[span], step_out.at[span])
    if whole_rows:
        store(grad_flat, grad_out)
        store(steps, step_out)
    for copy in sent + ends:
        copy.wait_send()
    for copy in stores:
        copy.wait()


def deliver_blocks(grads, head, code, stats, roots, devices):
    count = code.shape[0] // devices
    more = head.shape[0]
    spans = spans_of(count)
    flat = (count, BLOCK * BLOCK)
    first, second, third = bit_split(devices)
    n_mid, n_last, n_far = 1 << first, 1 << second, 1 << third
    tile = (count, HALF, LANES)
    dma = pltpu.SemaphoreType.DMA
    lands = [(n_last - 1) * n_mid * n_far, (n_mid - 1) * n_far, (n_far - 1) * n_mid]
    grads = [g.reshape(-1, HALF, LANES) for g in grads]
    any_space = pl.BlockSpec(memory_space=pl.ANY)
    steps = len(spans)
    return pl.pallas_call(
        functools.partial(deliver_kernel, devices, spans),
        out_shape=[
            jax.ShapeDtypeStruct((2, more, HALF, LANES), BF16),
            jax.ShapeDtypeStruct(flat, F32),
            jax.ShapeDtypeStruct(stats.shape, F32),
            jax.ShapeDtypeStruct(flat, F32),
        ],
        in_specs=[pl.BlockSpec(memory_space=pltpu.SMEM)] + [any_space] * (3 + len(grads)),
        out_specs=[any_space] * 4,
        scratch_shapes=[
            pltpu.VMEM((sum(g.shape[0] for g in grads), HALF, LANES), jnp.bfloat16),
            pltpu.VMEM((devices,) + tile, jnp.bfloat16),
        ]
        + [pltpu.VMEM((k,) + tile, jnp.bfloat16) for k in lands]
        + [
            pltpu.VMEM((2,) + tile, jnp.bfloat16),
            pltpu.VMEM((2, more, HALF, LANES), jnp.bfloat16),
            pltpu.VMEM(flat, F32),
            pltpu.VMEM(stats.shape, F32),
            pltpu.VMEM(roots.shape, F32),
            pltpu.VMEM(flat, F32),
            pltpu.VMEM((2, 8 * HALF, LANES), F32),
            pltpu.VMEM((2, 8 * HALF, LANES), F32),
            dma((len(grads) + 1,)),
            dma((sum(lands) * steps,)),
            dma((lands[0], steps)),
            dma((lands[1], steps)),
            dma((lands[2], steps)),
            dma((steps + 1,)),
            dma((steps + 1,)),
            dma((2,)),
            dma((3 * steps + 3,)),
        ],
        compiler_params=pltpu.CompilerParams(
            collective_id=2, has_side_effects=True, vmem_limit_bytes=60 * 2**20
        ),
    )(code, head, *grads, stats, roots)


def block_places(owner_slot):
    codes = []
    base = 0
    for rows, cols in matrix_list():
        strips, pairs = rows // BLOCK, cols // LANES
        grid = base + 2 * (np.arange(pairs)[None, :] * strips + np.arange(strips)[:, None])
        codes.append((2 * grid[:, :, None] + np.arange(2)[None, None, :]).reshape(-1))
        base += 2 * strips * pairs
    code = np.concatenate(codes).astype(np.int32)
    slots = np.arange(code.shape[0], dtype=np.int32)
    found = jnp.sum(
        jnp.where(owner_slot[:, None] == slots[None, :], code[:, None], 0), axis=0, dtype=jnp.int32
    )
    return found


ROWS = ROW_SLOTS * WIDTH
N_IN = C // LANES
N_MID = M // LANES
WIDE = 1024
F32 = jnp.float32
BF16 = jnp.bfloat16


def dot(a, b, ca, cb):
    return lax.dot_general(a, b, (((ca,), (cb,)), ((), ())), preferred_element_type=F32)


def lanes_of(ref, first, count):
    return jnp.concatenate([ref[first + i] for i in range(count)], axis=-1)


def half_tanh(v):
    return 0.5 * (1.0 + jnp.tanh(0.5 * v))


class Net:
    def __init__(self, devices):
        first, second, third = bit_split(devices)
        self.me = lax.axis_index("dp")
        self.core = lax.axis_index("rows")
        self.near, self.far = 1 << (first + second), 1 << third
        self.near_at = lax.rem(self.me, self.near)
        self.far_at = self.me // self.near
        self.partner = (self.me, 1 - self.core)
        self.near_peers = [(self.me ^ m, self.core) for m in range(1, self.near)]
        self.near_slots = [self.near_at ^ m for m in range(1, self.near)]
        self.far_peers = [(self.me ^ (m * self.near), self.core) for m in range(1, self.far)]
        self.far_slots = [self.far_at ^ m for m in range(1, self.far)]
        self.direct = devices <= DIRECT
        self.all_slots = [self.me ^ m for m in range(1, devices)]
        self.all_peers = [(slot, self.core) for slot in self.all_slots]
        self.devices = devices

    def known(self):
        if self.direct:
            return [self.partner] + self.all_peers
        return [self.partner] + self.near_peers + self.far_peers

    def hello(self):
        barrier = pltpu.get_barrier_semaphore()
        for peer in self.known():
            pl.semaphore_signal(barrier, inc=1, device_id=peer, device_id_type=MESH_IDS)

    def ready(self):
        pl.semaphore_wait(pltpu.get_barrier_semaphore(), len(self.known()))


DIRECT = 16


def slots_total(devices):
    first, second, third = bit_split(devices)
    staged = 2 + (1 << (first + second)) + (1 << third)
    return max(staged, 2 + devices) if devices <= DIRECT else staged


def remote(src, dst, send_sem, recv_sem, device):
    copy = pltpu.make_async_remote_copy(
        src_ref=src,
        dst_ref=dst,
        send_sem=send_sem,
        recv_sem=recv_sem,
        device_id=device,
        device_id_type=MESH_IDS,
    )
    copy.start()
    return copy


def landed(ref, sem):
    pltpu.make_async_copy(ref, ref, sem).wait()


def plain_sum(values, counts):
    total = values[0]
    for value in values[1:]:
        total = total + value
    return total


def pooled_moments(rows):
    def merge(values, counts):
        n = counts[0]
        for more in counts[1:]:
            n = n + more
        sums = values[0][:rows]
        spread = values[0][rows:]
        for value in values[1:]:
            sums = sums + value[:rows]
            spread = spread + value[rows:]
        mean = sums / n
        for value, own in zip(values, counts):
            gap = value[:rows] / own - mean
            spread = spread + own * gap * gap
        return jnp.concatenate([sums, spread], axis=0)

    return merge


def reduce_all(net, value, bufs, send_sem, recv_sem, merge, own_count=None, pair_count=0.0, fillers=()):
    fillers = list(fillers) + [None] * 3
    fillers_after = fillers[1:]
    copies = []
    stages = [
        (0, net.core, [net.partner], [1 - net.core], 2),
        (2, net.near_at, net.near_peers, net.near_slots, net.near),
        (2 + net.near, net.far_at, net.far_peers, net.far_slots, net.far),
    ]
    if net.direct and value.shape[0] <= 2 * N_MID:
        stages = stages[:1] + [(2, net.me, net.all_peers, net.all_slots, net.devices)]
        fillers = [fillers[0], lambda: [more() for more in fillers_after if more is not None]]
    for step, (base, mine, peers, slots, size) in enumerate(stages):
        bufs[base + mine] = value
        for i, peer in enumerate(peers):
            copies.append(
                remote(
                    bufs.at[base + mine],
                    bufs.at[base + mine],
                    send_sem.at[base + i],
                    recv_sem.at[base + mine],
                    peer,
                )
            )
        if fillers[step] is not None:
            fillers[step]()
        for slot in slots:
            landed(bufs.at[base + slot], recv_sem.at[base + slot])
        if own_count is None:
            counts = [None] * size
        elif step == 0:
            rest = pair_count - own_count
            first = net.core == 0
            counts = [jnp.where(first, own_count, rest), jnp.where(first, rest, own_count)]
        else:
            counts = [pair_count * (1 if step == 1 else net.near)] * size
        value = merge([bufs[base + j] for j in range(size)], counts)
    return value, copies


def column_sum(value):
    return jnp.sum(value.reshape(-1, 8, LANES), axis=0)


def local_moments(z, count, live, own_count, stage, masked):
    quarter = z.shape[1] // 4

    def slab(j, carry):
        total = jnp.zeros((8, LANES), F32)
        for q in range(4):
            rows = pl.ds(q * quarter, quarter)
            v = z[j, rows]
            if masked:
                v = v * live[rows]
                z[j, rows] = v
            total = total + column_sum(v)
        sums = jnp.sum(total, axis=0, keepdims=True)
        mean = sums / own_count
        spread = jnp.zeros((8, LANES), F32)
        for q in range(4):
            rows = pl.ds(q * quarter, quarter)
            d = (z[j, rows] - mean) * live[rows]
            spread = spread + column_sum(d * d)
        stage[pl.ds(j, 1)] = sums
        stage[pl.ds(count + j, 1)] = jnp.sum(spread, axis=0, keepdims=True)
        return carry

    lax.fori_loop(0, count, slab, 0)


def window(ref, down, right):
    batch = ref.shape[3]
    parts = [
        ref[j, pl.ds(down, ROW_SLOTS), pl.ds(right, WIDTH)].reshape(ROWS * batch, LANES)
        for j in range(N_MID)
    ]
    return jnp.concatenate(parts, axis=-1)


def clear_edges(ref, core):
    shape = ref.shape
    zero = jnp.zeros((shape[0], 1) + shape[2:], ref.dtype)
    ref[:, pl.ds(jnp.where(core == 0, 0, ROW_SLOTS + 1), 1)] = zero
    column = jnp.zeros(shape[:2] + (1,) + shape[3:], ref.dtype)
    ref[:, :, 0:1] = column
    ref[:, :, WIDTH + 1 : WIDTH + 2] = column


def send_edge(ref, net, send_sem, recv_sem):
    edge = jnp.where(net.core == 0, ROW_SLOTS, 1)
    there = jnp.where(net.core == 0, 0, ROW_SLOTS + 1)
    return remote(
        ref.at[:, edge, pl.ds(1, WIDTH)],
        ref.at[:, there, pl.ds(1, WIDTH)],
        send_sem,
        recv_sem,
        net.partner,
    )


def edge_landed(ref, net, recv_sem):
    here = jnp.where(net.core == 0, ROW_SLOTS + 1, 0)
    landed(ref.at[:, here, pl.ds(1, WIDTH)], recv_sem)


def edge_first(net, fill, send):
    edge = jnp.where(net.core == 0, ROW_SLOTS - 1, 0)
    fill(edge)
    copy = send()
    for step in range(1, ROW_SLOTS):
        fill(lax.rem(edge + step, ROW_SLOTS))
    return copy


def load_all(pairs, sems):
    copies = []
    for i, (src, dst) in enumerate(pairs):
        copy = pltpu.make_async_copy(src, dst, sems.at[i])
        copy.start()
        copies.append(copy)
    return copies


def forward_kernel(devices, total_count, *refs):
    refs = list(refs)
    take = lambda n: [refs.pop(0) for _ in range(n)]
    w_h = [take(3) for _ in range(LAYERS)]
    x_in, = take(1)
    params_of = take(LAYERS)
    live, = take(1)
    kept_h = [take(5) for _ in range(LAYERS)]
    stats_of = [take(3) for _ in range(LAYERS)]
    xn_h, xnb_h, pooled = take(3)
    wi, wm, wo, za, hp, zb, hb, zc, xn, xnb = take(10)
    stage_m, stage_c = take(2)
    bufs_of = [take(3) for _ in range(LAYERS)]
    in_sem, out_sem, send_sem, recv_sem, halo_sem = take(5)

    net = Net(devices)
    net.hello()
    loading = {}
    places = [wi, wm, wo]

    def start(at, which):
        copy = pltpu.make_async_copy(w_h[at][which], places[which], in_sem.at[at, which])
        copy.start()
        loading[at, which] = copy

    for which in range(3):
        start(0, which)
    clear_edges(hp, net.core)
    own_count = jnp.sum(column_sum(live[...]), axis=0, keepdims=True)
    pair_count = total_count / devices
    quarter = za.shape[1] // ROW_SLOTS
    batch = quarter // WIDTH
    stores = []
    sends = []

    def store(src, dst):
        copy = pltpu.make_async_copy(src, dst, out_sem.at[len(stores)])
        copy.start()
        stores.append(copy)

    def layer(at):
        params = params_of[at]
        stat_a, stat_b, stat_c = stats_of[at]
        za_h, hp_h, zb_h, hb_h, zc_h = kept_h[at]
        later = at + 1 < LAYERS

        def norm(z, n, stage, which, masked, stat):
            local_moments(z, n, live, own_count, stage, masked)
            if at == 0 and which == 0:
                net.ready()
            total, copies = reduce_all(
                net,
                stage[...],
                bufs_of[at][which],
                send_sem.at[3 * at + which],
                recv_sem.at[3 * at + which],
                pooled_moments(n),
                own_count,
                pair_count,
            )
            sends.extend(copies)
            stat[0:n] = total[:n] / total_count
            stat[n : 2 * n] = lax.rsqrt(total[n:] / total_count + EPS_NORM)

        def affine(stat, n, gain_at, j):
            mean = stat[pl.ds(j, 1)]
            scale = stat[pl.ds(n + j, 1)] * params[pl.ds(gain_at + j, 1)]
            return mean, scale, params[pl.ds(gain_at + n + j, 1)]

        loading[at, 0].wait()
        if at:
            for copy in stores[:5]:
                copy.wait()
        x = lanes_of(xnb, 0, N_IN) if at else x_in[...]
        product = dot(x, lanes_of(wi, 0, N_MID), 1, 0)
        for j in range(N_MID):
            za[j] = product[:, j * LANES : (j + 1) * LANES]
        if later:
            start(at + 1, 0)
        norm(za, N_MID, stage_m, 0, at == 0, stat_a)
        store(za, za_h)

        def fill_hidden(slot):
            rows = pl.ds(slot * quarter, quarter)

            def slab(j, carry):
                mean, scale, shift = affine(stat_a, N_MID, 0, j)
                y = (za[j, rows] - mean) * scale + shift
                h = (live[rows] * (y * half_tanh(y))).astype(BF16)
                hp[j, pl.ds(slot + 1, 1), pl.ds(1, WIDTH)] = h.reshape(1, WIDTH, batch, LANES)
                return carry

            lax.fori_loop(0, N_MID, slab, 0)

        edge = edge_first(
            net, fill_hidden, lambda: send_edge(hp, net, halo_sem.at[at, 0], halo_sem.at[at, 1])
        )
        loading[at, 1].wait()
        zb[...] = jnp.zeros(zb.shape, F32)

        def tap(t):
            k = pl.ds(pl.multiple_of(t * M, M), M)
            part = dot(
                window(hp, t // 3, lax.rem(t, 3)),
                jnp.concatenate([wm[j, k] for j in range(N_MID)], axis=-1),
                1,
                0,
            )
            for j in range(N_MID):
                zb[j] = zb[j] + part[:, j * LANES : (j + 1) * LANES]

        def middle(i, carry):
            tap(i + 3)
            return carry

        def outer(i, carry):
            tap(jnp.where(i < 3, i, i + 3))
            return carry

        lax.fori_loop(0, 3, middle, 0)
        edge_landed(hp, net, halo_sem.at[at, 1])
        edge.wait_send()
        store(hp, hp_h)
        lax.fori_loop(0, 6, outer, 0)
        if later:
            start(at + 1, 1)
        norm(zb, N_MID, stage_m, 1, True, stat_b)
        store(zb, zb_h)

        def fill_second(j, carry):
            mean, scale, shift = affine(stat_b, N_MID, 2 * N_MID, j)
            for q in range(4):
                rows = pl.ds(q * quarter, quarter)
                y = (zb[j, rows] - mean) * scale + shift
                hb[j, rows] = (live[rows] * (y * half_tanh(y))).astype(BF16)
            return carry

        lax.fori_loop(0, N_MID, fill_second, 0)
        store(hb, hb_h)
        loading[at, 2].wait()

        def expand(g, carry):
            part = dot(lanes_of(hb, 0, N_MID), lanes_of(wo, g * N_MID, N_MID), 1, 0)
            for j in range(N_MID):
                zc[g * N_MID + j] = part[:, j * LANES : (j + 1) * LANES]
            return carry

        lax.fori_loop(0, N_IN // N_MID, expand, 0)
        if later:
            start(at + 1, 2)
        store(zc, zc_h)
        norm(zc, N_IN, stage_c, 2, False, stat_c)

        def finish(j, carry):
            mean, scale, shift = affine(stat_c, N_IN, 4 * N_MID, j)
            pool = jnp.zeros((batch, LANES), F32)
            for q in range(4):
                rows = pl.ds(q * quarter, quarter)
                if at:
                    x = xn[j, rows]
                else:
                    x = x_in[rows, pl.ds(pl.multiple_of(j * LANES, LANES), LANES)].astype(F32)
                y = (zc[j, rows] - mean) * scale + shift + x
                out = live[rows] * (y * half_tanh(y))
                if later:
                    xn[j, rows] = out
                    xnb[j, rows] = out.astype(BF16)
                else:
                    pool = pool + jnp.sum(out.reshape(WIDTH, batch, LANES), axis=0)
            if not later:
                pooled[j] = pool
            return carry

        lax.fori_loop(0, N_IN, finish, 0)
        if later:
            store(xn, xn_h)
            store(xnb, xnb_h)

    for at in range(LAYERS):
        layer(at)
    for copy in stores[5:]:
        copy.wait()
    for copy in sends:
        copy.wait_send()


def forward_pass(devices, total_count, x, weights, params, live):
    rows = live.shape[0]
    batch = rows // ROWS
    shape = jax.ShapeDtypeStruct
    any_space = pl.BlockSpec(memory_space=pl.ANY)
    vmem = pl.BlockSpec(memory_space=pltpu.VMEM)
    fields = [
        shape((N_MID, rows, LANES), F32),
        shape((N_MID, ROW_SLOTS + 2, WIDTH + 2, batch, LANES), BF16),
        shape((N_MID, rows, LANES), F32),
        shape((N_MID, rows, LANES), BF16),
        shape((N_IN, rows, LANES), F32),
    ]
    stats = [shape((2 * n, LANES), F32) for n in (N_MID, N_MID, N_IN)]
    last = [shape((N_IN, rows, LANES), F32), shape((N_IN, rows, LANES), BF16)]
    big = lambda s: pltpu.VMEM(s.shape, s.dtype)
    total = slots_total(devices)
    dma = pltpu.SemaphoreType.DMA
    small_ins = [x] + list(params) + [live]
    out = pl.pallas_call(
        functools.partial(forward_kernel, devices, total_count),
        out_shape=fields * LAYERS + stats * LAYERS + last + [shape((N_IN, batch, LANES), F32)],
        in_specs=[any_space] * len(weights) + [vmem] * len(small_ins),
        out_specs=[any_space] * (5 * LAYERS) + [vmem] * (3 * LAYERS) + [any_space] * 2 + [vmem],
        scratch_shapes=[big(w) for w in weights[:3]]
        + [big(s) for s in fields + last]
        + [pltpu.VMEM((2 * N_MID, LANES), F32), pltpu.VMEM((2 * N_IN, LANES), F32)]
        + [pltpu.VMEM((total, 2 * n, LANES), F32) for n in (N_MID, N_MID, N_IN)] * LAYERS
        + [
            dma((LAYERS, 3)),
            dma((5 * LAYERS + 2,)),
            dma((3 * LAYERS, total)),
            dma((3 * LAYERS, total)),
            dma((LAYERS, 2)),
        ],
        compiler_params=pltpu.CompilerParams(
            collective_id=3, has_side_effects=True, vmem_limit_bytes=60 * 2**20
        ),
    )(*weights, *small_ins)
    kept = [
        list(out[5 * at : 5 * at + 5]) + list(out[5 * LAYERS + 3 * at : 5 * LAYERS + 3 * at + 3])
        for at in range(LAYERS)
    ]
    return kept, out[-3], out[-2], out[-1]


def head_kernel(
    devices, area, emit, pooled, head_h, bias, pick, point, numbers, hot, extra, gtop, *refs
):
    outs, refs = (refs[:1], refs[1:]) if emit else (refs[:2], refs[2:])
    (
    head, send_pool, recv_pool, low, logits_all, logits, g_low, gh, gh_there, gh_other, gt,
    in_sem, out_sem, send_sem, recv_sem,
    ) = refs
    net = Net(devices)
    net.hello()
    load = pltpu.make_async_copy(head_h, head, in_sem)
    load.start()
    half = send_pool.shape[1]
    mine = pl.ds(pl.multiple_of(net.core * half, half), half)
    theirs = pl.ds(pl.multiple_of((1 - net.core) * half, half), half)
    for j in range(N_IN):
        send_pool[j] = pooled[j, theirs].astype(BF16)
    net.ready()
    sends = [remote(send_pool, recv_pool, send_sem.at[0], recv_sem.at[0], net.partner)]
    load.wait()
    landed(recv_pool, recv_sem.at[0])
    for j in range(N_IN):
        low[j] = ((pooled[j, mine] + recv_pool[j].astype(F32)) / area).astype(BF16)
    logits[...] = dot(lanes_of(low, 0, N_IN), lanes_of(head, 0, N_IN), 1, 1) + bias[0:1, :]
    logits_all[net.core, net.far_at, net.near_at] = logits[...].astype(BF16)
    at = 1
    ref = logits_all.at[net.core, net.far_at, net.near_at]
    for peer in net.far_peers:
        sends.append(
            remote(ref, ref, send_sem.at[at], recv_sem.at[1 + net.near + net.far_at], peer)
        )
        at += 1

    own = logits[...]
    keep = lax.broadcasted_iota(jnp.int32, own.shape, 1) < CLASSES
    peak = jnp.max(jnp.where(keep, own, -3.0e38), axis=1, keepdims=True)
    powers = jnp.where(keep, jnp.exp(jnp.where(keep, own - peak, 0.0)), 0.0)
    log_total = peak + jnp.log(jnp.sum(powers, axis=1, keepdims=True))
    softmax = jnp.where(keep, jnp.exp(jnp.where(keep, own - log_total, 0.0)), 0.0)
    picked = jnp.sum(own * hot[...], axis=1, keepdims=True)

    for slot in net.far_slots:
        landed(
            logits_all.at[net.core, slot, net.near_at], recv_sem.at[1 + net.near + slot]
        )
    group = logits_all.at[net.core, :, net.near_at]
    for peer in net.near_peers:
        sends.append(remote(group, group, send_sem.at[at], recv_sem.at[1 + net.near_at], peer))
        at += 1
    for slot in net.near_slots:
        landed(logits_all.at[net.core, :, slot], recv_sem.at[1 + slot])
    ref = logits_all.at[net.core]
    sends.append(
        remote(ref, ref, send_sem.at[at], recv_sem.at[1 + net.near + net.far], net.partner)
    )
    at += 1
    landed(logits_all.at[1 - net.core], recv_sem.at[1 + net.near + net.far])
    every = logits_all[...].reshape(-1, WIDE)
    gap = jnp.where(keep, own - dot(pick[...], every, 1, 0), 0.0)
    incoming = dot(point[...], every, 1, 0)
    weight = numbers[:, 0:1]
    terms = weight * (
        log_total - picked + MATCH_WEIGHT * (jnp.sum(gap * gap, axis=1, keepdims=True) / CLASSES)
    )
    grad = (
        weight * (softmax - hot[...])
        + MATCH_WEIGHT
        * (2.0 / CLASSES)
        * (weight * gap - (incoming - numbers[:, 1:2] * own))
    ) / numbers[:, 2:3]
    g_low[...] = jnp.where(keep, grad, 0.0).astype(BF16)
    bias_sum = jnp.sum(g_low[...].astype(F32), axis=0, keepdims=True)
    extra[...] = jnp.zeros(extra.shape, F32)
    for j in range(WIDE // LANES):
        extra[j : j + 1] = bias_sum[:, j * LANES : (j + 1) * LANES]
    extra[WIDE // LANES : WIDE // LANES + 1] = jnp.zeros((1, LANES), F32) + jnp.sum(
        terms, axis=0, keepdims=True
    )
    gt_view = gt.at[:, net.core]
    for j in range(N_IN):
        gt[j, net.core] = (dot(g_low[...], head[j], 1, 0) / area).astype(BF16)
    sends.append(
        remote(
            gt_view, gt_view, send_sem.at[at], recv_sem.at[2 + net.near + net.far], net.partner
        )
    )

    if emit:
        at += 1
        block = (WIDE // 2 // HALF, HALF, LANES)
        cut = WIDE // 2
        mine_at = pl.multiple_of(net.core * cut, cut)
        theirs_at = pl.multiple_of((1 - net.core) * cut, cut)

        def grad_there(j, carry):
            part = dot(g_low[:, pl.ds(theirs_at, cut)], low[j], 0, 0)
            gh_there[j] = part.astype(BF16).reshape(block)
            return carry

        lax.fori_loop(0, N_IN, grad_there, 0)
        sends.append(
            remote(
                gh_there, gh_other, send_sem.at[at], recv_sem.at[3 + net.near + net.far], net.partner
            )
        )
    else:
        outs[0][...] = low[...].astype(F32)
        outs[1][...] = g_low[...].astype(F32)
    landed(gt.at[:, 1 - net.core], recv_sem.at[2 + net.near + net.far])
    for j in range(N_IN):
        gtop[j] = jnp.concatenate([gt[j, 0], gt[j, 1]], axis=0).astype(F32)
    if emit:
        landed(gh_other, recv_sem.at[3 + net.near + net.far])

        def grad_here(j, carry):
            part = dot(g_low[:, pl.ds(mine_at, cut)], low[j], 0, 0)
            gh[j] = (part.reshape(block) + gh_other[j].astype(F32)).astype(BF16)
            return carry

        lax.fori_loop(0, N_IN, grad_here, 0)
        store = pltpu.make_async_copy(gh, outs[0], out_sem)
        store.start()
        store.wait()
    for copy in sends:
        copy.wait_send()


def head_step(devices, emit, pooled, head, bias, pick, point, numbers, hot):
    batch = pooled.shape[1]
    half = batch // 2
    shape = jax.ShapeDtypeStruct
    any_space = pl.BlockSpec(memory_space=pl.ANY)
    vmem = pl.BlockSpec(memory_space=pltpu.VMEM)
    dma = pltpu.SemaphoreType.DMA
    count = 4 + slots_total(devices)
    first, second, third = bit_split(devices)
    near, far = 1 << (first + second), 1 << third
    return pl.pallas_call(
        functools.partial(head_kernel, devices, float(HEIGHT * WIDTH), emit),
        out_shape=[
            shape((16, LANES), F32),
            shape((N_IN, batch, LANES), F32),
        ]
        + (
            [shape((N_IN, WIDE // 2 // HALF, HALF, LANES), BF16)]
            if emit
            else [shape((N_IN, half, LANES), F32), shape((half, WIDE), F32)]
        ),
        in_specs=[vmem, any_space] + [vmem] * 5,
        out_specs=[vmem, vmem] + ([any_space] if emit else [vmem, vmem]),
        scratch_shapes=[
            pltpu.VMEM((N_IN, WIDE, LANES), BF16),
            pltpu.VMEM((N_IN, half, LANES), BF16),
            pltpu.VMEM((N_IN, half, LANES), BF16),
            pltpu.VMEM((N_IN, half, LANES), BF16),
            pltpu.VMEM((2, far, near, half, WIDE), BF16),
            pltpu.VMEM((half, WIDE), F32),
            pltpu.VMEM((half, WIDE), BF16),
            pltpu.VMEM((N_IN, WIDE // 2 // HALF, HALF, LANES), BF16),
            pltpu.VMEM((N_IN, WIDE // 2 // HALF, HALF, LANES), BF16),
            pltpu.VMEM((N_IN, WIDE // 2 // HALF, HALF, LANES), BF16),
            pltpu.VMEM((N_IN, 2, half, LANES), BF16),
            dma(()),
            dma(()),
            dma((count,)),
            dma((count,)),
        ],
        compiler_params=pltpu.CompilerParams(
            collective_id=5, has_side_effects=True, vmem_limit_bytes=60 * 2**20
        ),
    )(pooled, head, bias, pick, point, numbers, hot)


def pieces(part, j):
    return part[:, j * LANES : (j + 1) * LANES].astype(BF16).reshape(-1, 2, HALF, LANES)


def backward_kernel(devices, total_count, inside, *refs):
    refs = list(refs)
    take = lambda n: [refs.pop(0) for _ in range(n)]
    names = ["zc", "hb", "hp", "zb", "za", "wi", "wm", "wo"]
    source = {}
    head_h, = [None] if inside else take(1)
    source["xf", 1], source["xb", 1] = take(2)
    for at in (0, 1):
        for name in names:
            source[name, at] = refs.pop(0)
    x_in, gtop = take(2)
    stats_of = [take(3) for _ in range(LAYERS)]
    params_of = take(LAYERS)
    live, extra = take(2)
    low, g_low = take(2) if inside else [None, None]
    out_of = [take(3) for _ in range(LAYERS)]
    head_out, = take(1)
    small_of = take(LAYERS)
    field, xb, zc, hb, hp, zb, za, wi, wm, wo = take(10)
    place = dict(xf=field, xb=xb, zc=zc, hb=hb, hp=hp, zb=zb, za=za, wi=wi, wm=wm, wo=wo)
    g_side, g_mid, r_side, r_mid = take(4)
    ec, ep, ea, ub = take(4)
    head, land_last, land_mid, land_far = take(4)
    stage_m, stage_c = take(2)
    bufs_of = [take(3) for _ in range(LAYERS)]
    in_sem, out_sem, send_sem, recv_sem, halo_sem, pair_sem = take(6)
    head_in, head_send, last_recv, mid_recv, far_recv, swap_sem = take(6)

    net = Net(devices)
    net.hello()
    order = ["zc", "xf", "wo", "zb", "hb", "hp", "wm", "za", "wi", "xb"]
    loading = {}

    def start(name, at):
        copy = pltpu.make_async_copy(
            source[name, at], place[name], in_sem.at[at, order.index(name)]
        )
        copy.start()
        loading[name, at] = copy

    def need(name, at):
        loading[name, at].wait()

    for name in order:
        start(name, 1)
    if not inside:
        head_load = pltpu.make_async_copy(head_h, head, head_in)
        head_load.start()
    clear_edges(ep, net.core)
    quarter = za.shape[1] // ROW_SLOTS
    batch = quarter // WIDTH
    groups = N_IN // N_MID
    side_rows, mid_rows = M // 32, 9 * M // 32
    sends = []
    stored = []

    def store(src, dst):
        copy = pltpu.make_async_copy(src, dst, out_sem.at[len(stored)])
        copy.start()
        stored.append(copy)
        return copy

    def slope(y):
        sigma = half_tanh(y)
        return sigma * (1.0 + y * (1.0 - sigma))

    def row(ref, j):
        return ref[pl.ds(j, 1)]

    def swap(grad, other, at, which):
        return remote(
            grad.at[:, 1 - net.core],
            other,
            pair_sem.at[at, 0, which],
            pair_sem.at[at, 1, which],
            net.partner,
        )

    def fold(copy, grad, other, at, which, out):
        landed(other, pair_sem.at[at, 1, which])
        copy.wait_send()

        def step(i, carry):
            part = pl.ds(i * 16, 16)
            other[part] = (grad[part, net.core].astype(F32) + other[part].astype(F32)).astype(BF16)
            return carry

        lax.fori_loop(0, grad.shape[0] // 16, step, 0)
        return store(other, out)

    mid, last, far = axis_masks(devices, net.core)
    me, core = net.me, net.core
    head_sent = []

    def head_copy(owner, land, sems, slot, device):
        head_sent.append(
            remote(head.at[owner], land.at[slot], head_send.at[len(head_sent)], sems.at[slot], device)
        )

    def head_add(owners, land, sems):
        for slot in range(len(owners)):
            landed(land.at[slot], sems.at[slot])

        def step(i, carry):
            for slot, owner in enumerate(owners):
                head[owner, i] = (
                    head[owner, i].astype(F32) + land[slot, i].astype(F32)
                ).astype(BF16)
            return carry

        lax.fori_loop(0, head.shape[1], step, 0)

    cut = WIDE // 2
    lot = cut // (2 * HALF)
    state = {}

    def head_part(j, which):
        classes = pl.ds(pl.multiple_of(which * cut, cut), cut)
        return dot(g_low[:, classes].astype(BF16), low[j].astype(BF16), 0, 0)

    def head_there():
        def step(j, carry):
            part = head_part(j, 1 - core).astype(BF16)
            g_mid[pl.ds(j * lot, lot)] = part.reshape(lot, 2, HALF, LANES)
            return carry

        lax.fori_loop(0, N_IN, step, 0)
        state["there"] = remote(
            g_mid.at[pl.ds(0, N_IN * lot)],
            g_mid.at[pl.ds(N_IN * lot, N_IN * lot)],
            swap_sem.at[0],
            swap_sem.at[1],
            net.partner,
        )

    def head_here():
        landed(g_mid.at[pl.ds(N_IN * lot, N_IN * lot)], swap_sem.at[1])

        def step(j, carry):
            other = g_mid[pl.ds((N_IN + j) * lot, lot)].astype(F32)
            part = head_part(j, core).reshape(lot, 2, HALF, LANES) + other
            head[j] = part.astype(BF16).reshape(2 * lot, HALF, LANES)
            return carry

        lax.fori_loop(0, N_IN, step, 0)
        state["there"].wait_send()

    def head_first():
        if not inside:
            head_load.wait()
        slot = 0
        for q in last[1:]:
            for m in mid:
                for z in far:
                    head_copy(me ^ q ^ m ^ z, land_last, last_recv, slot, (me ^ q, core))
                    slot += 1

    def head_second():
        owners = [me ^ m ^ z for m in mid for z in far]
        for j in range(len(last) - 1):
            view = pl.ds(j * len(owners), len(owners))
            head_add(owners, land_last.at[view], last_recv.at[view])
        slot = 0
        for m in mid[1:]:
            for z in far:
                head_copy(me ^ m ^ z, land_mid, mid_recv, slot, (me ^ m, core))
                slot += 1

    def head_third():
        owners = [me ^ z for z in far]
        for j in range(len(mid) - 1):
            view = pl.ds(j * len(owners), len(owners))
            head_add(owners, land_mid.at[view], mid_recv.at[view])
        for slot, z in enumerate(far[1:]):
            head_copy(me ^ z, land_far, far_recv, slot, (me ^ z, core))

    def head_last():
        for slot in range(len(far) - 1):
            landed(land_far.at[slot], far_recv.at[slot])

        def step(i, carry):
            total = head[me, i].astype(F32)
            for slot in range(len(far) - 1):
                total = total + land_far[slot, i].astype(F32)
            head[me, i] = total.astype(BF16)
            return carry

        lax.fori_loop(0, head.shape[1], step, 0)
        for copy in head_sent:
            copy.wait_send()
        return store(head.at[me], head_out)

    def layer(at, fillers):
        top = at == 1
        stat_a, stat_b, stat_c = stats_of[at]
        params, small = params_of[at], small_of[at]
        gi_h, gm_h, go_h = out_of[at]
        state = {}

        def refill(name):
            if top:
                start(name, 0)

        def totals(stage, which, small_at, n, fillers):
            total, copies = reduce_all(
                net,
                stage[...],
                bufs_of[at][which],
                send_sem.at[3 * at + which],
                recv_sem.at[3 * at + which],
                plain_sum,
                fillers=fillers,
            )
            sends.extend(copies)
            small[small_at : small_at + 2 * n] = total[: 2 * n]
            return total

        need("zc", at)
        if top:
            need("xf", at)

        def slab_c(j, carry):
            mean, scale = row(stat_c, j), row(stat_c, N_IN + j)
            gain, shift = row(params, 4 * N_MID + j), row(params, 4 * N_MID + N_IN + j)
            total = jnp.zeros((8, LANES), F32)
            crossed = jnp.zeros((8, LANES), F32)
            for q in range(4):
                rows = pl.ds(q * quarter, quarter)
                normed = (zc[j, rows] - mean) * scale
                if top:
                    x = field[j, rows]
                    g = jnp.concatenate([gtop[j]] * WIDTH, axis=0)
                else:
                    x = x_in[rows, pl.ds(pl.multiple_of(j * LANES, LANES), LANES)].astype(F32)
                    g = field[j, rows]
                u = g * live[rows] * slope(normed * gain + shift + x)
                field[j, rows] = u
                total = total + column_sum(u)
                crossed = crossed + column_sum(u * normed)
            stage_c[pl.ds(j, 1)] = jnp.sum(crossed, axis=0, keepdims=True)
            stage_c[pl.ds(N_IN + j, 1)] = jnp.sum(total, axis=0, keepdims=True)
            return carry

        lax.fori_loop(0, N_IN, slab_c, 0)
        if top:
            stage_c[2 * N_IN :] = extra[...]
            net.ready()
        else:
            stage_c[2 * N_IN :] = jnp.zeros(extra.shape, F32)
        total_c = totals(stage_c, 2, 4 * N_MID, N_IN, fillers)
        small[4 * N_MID + 2 * N_IN :] = total_c[2 * N_IN :]
        if not top:
            head_third()

        def back_c(j, carry):
            mean, scale = row(stat_c, j), row(stat_c, N_IN + j)
            gain = row(params, 4 * N_MID + j)
            cross = row(small, 4 * N_MID + j) / total_count
            plain = row(small, 4 * N_MID + N_IN + j) / total_count
            for q in range(4):
                rows = pl.ds(q * quarter, quarter)
                normed = (zc[j, rows] - mean) * scale
                e = live[rows] * ((gain * scale) * (field[j, rows] - plain - normed * cross))
                ec[j, rows] = e.astype(BF16)
            return carry

        lax.fori_loop(0, N_IN, back_c, 0)
        refill("zc")
        need("wo", at)
        product = dot(lanes_of(ec, 0, N_IN), lanes_of(wo, 0, N_IN), 1, 1)
        for j in range(N_MID):
            ub[j] = product[:, j * LANES : (j + 1) * LANES]
        refill("wo")
        need("zb", at)

        def sums_of(z_ref, stat, gain_at):
            def slab(j, carry):
                mean, scale = row(stat, j), row(stat, N_MID + j)
                gain, shift = row(params, gain_at + j), row(params, gain_at + N_MID + j)
                total = jnp.zeros((8, LANES), F32)
                crossed = jnp.zeros((8, LANES), F32)
                for q in range(4):
                    rows = pl.ds(q * quarter, quarter)
                    normed = (z_ref[j, rows] - mean) * scale
                    u = ub[j, rows] * live[rows] * slope(normed * gain + shift)
                    ub[j, rows] = u
                    total = total + column_sum(u)
                    crossed = crossed + column_sum(u * normed)
                stage_m[pl.ds(j, 1)] = jnp.sum(crossed, axis=0, keepdims=True)
                stage_m[pl.ds(N_MID + j, 1)] = jnp.sum(total, axis=0, keepdims=True)
                return carry

            lax.fori_loop(0, N_MID, slab, 0)

        def back_of(z_ref, stat, gain_at, j, rows):
            normed = (z_ref[j, rows] - row(stat, j)) * row(stat, N_MID + j)
            cross = row(small, gain_at + j) / total_count
            plain = row(small, gain_at + N_MID + j) / total_count
            factor = row(params, gain_at + j) * row(stat, N_MID + j)
            return (live[rows] * (factor * (ub[j, rows] - plain - normed * cross))).astype(BF16)

        sums_of(zb, stat_b, 2 * N_MID)
        need("hb", at)

        def grad_out(first, last):
            def group(g, carry):
                part = dot(lanes_of(hb, 0, N_MID), lanes_of(ec, g * N_MID, N_MID), 0, 0)
                for j in range(N_MID):
                    g_side[pl.ds((g * N_MID + j) * side_rows, side_rows)] = pieces(part, j)
                return carry

            return lambda: lax.fori_loop(first, last, group, 0)

        totals(
            stage_m, 1, 2 * N_MID, N_MID,
            [grad_out(0, 1), grad_out(1, groups - 1), grad_out(groups - 1, groups)],
        )
        refill("hb")
        out_swap = swap(g_side, r_side, at, 0)
        if top:
            head_first()

        def fill_b(slot):
            rows = pl.ds(slot * quarter, quarter)

            def slab(j, carry):
                e = back_of(zb, stat_b, 2 * N_MID, j, rows)
                ep[j, pl.ds(slot + 1, 1), pl.ds(1, WIDTH)] = e.reshape(1, WIDTH, batch, LANES)
                return carry

            lax.fori_loop(0, N_MID, slab, 0)

        edge = edge_first(
            net, fill_b, lambda: send_edge(ep, net, halo_sem.at[at, 0], halo_sem.at[at, 1])
        )
        refill("zb")
        need("hp", at)
        need("wm", at)
        ub[...] = jnp.zeros(ub.shape, F32)

        def grad_mid(first, last):
            def one(t, carry):
                part = dot(window(hp, t // 3, lax.rem(t, 3)), window(ep, 1, 1), 0, 0)
                for j in range(N_MID):
                    g_mid[pl.ds(j * mid_rows + t * side_rows, side_rows)] = pieces(part, j)
                return carry

            return lambda: lax.fori_loop(first, last, one, 0)

        def tap(t):
            k = pl.ds(pl.multiple_of(t * M, M), M)
            part = dot(
                window(ep, 2 - t // 3, 2 - lax.rem(t, 3)),
                jnp.concatenate([wm[j, k] for j in range(N_MID)], axis=-1),
                1,
                1,
            )
            for j in range(N_MID):
                ub[j] = ub[j] + part[:, j * LANES : (j + 1) * LANES]

        def middle(i, carry):
            tap(i + 3)
            return carry

        def outer(i, carry):
            tap(jnp.where(i < 3, i, i + 3))
            return carry

        lax.fori_loop(0, 3, middle, 0)
        edge_landed(ep, net, halo_sem.at[at, 1])
        edge.wait_send()
        lax.fori_loop(0, 6, outer, 0)
        refill("wm")
        out_store = fold(out_swap, g_side, r_side, at, 0, go_h)
        need("za", at)
        sums_of(za, stat_a, 0)
        out_store.wait()
        totals(stage_m, 0, 0, N_MID, [grad_mid(0, 2), grad_mid(2, 5), grad_mid(5, 9)])
        refill("hp")
        mid_swap = swap(g_mid, r_mid, at, 1)
        if top:
            head_second()

        def fill_a(j, carry):
            for q in range(4):
                rows = pl.ds(q * quarter, quarter)
                ea[j, rows] = back_of(za, stat_a, 0, j, rows)
            return carry

        lax.fori_loop(0, N_MID, fill_a, 0)
        refill("za")
        if top:
            need("wi", at)

            def grad_field(g, carry):
                k = pl.ds(pl.multiple_of(g * M, M), M)
                part = dot(
                    lanes_of(ea, 0, N_MID),
                    jnp.concatenate([wi[j, k] for j in range(N_MID)], axis=-1),
                    1,
                    1,
                )
                for j in range(N_MID):
                    slab = g * N_MID + j
                    field[slab] = field[slab] + part[:, j * LANES : (j + 1) * LANES]
                return carry

            lax.fori_loop(0, groups, grad_field, 0)

        def grad_in(g, carry):
            if top:
                x = lanes_of(xb, g * N_MID, N_MID)
            else:
                x = x_in[:, pl.ds(pl.multiple_of(g * M, M), M)]
            part = dot(x, lanes_of(ea, 0, N_MID), 0, 0)
            for j in range(N_MID):
                g_side[pl.ds((j * groups + g) * side_rows, side_rows)] = pieces(part, j)
            return carry

        def first_part():
            if top:
                need("xb", at)
            lax.fori_loop(0, groups, grad_in, 0)
            state["swap"] = swap(g_side, r_side, at, 2)

        def second_part():
            state["mid"] = fold(mid_swap, g_mid, r_mid, at, 1, gm_h)

        def third_part():
            state["in"] = fold(state["swap"], g_side, r_side, at, 2, gi_h)
            state["mid"].wait()
            state["in"].wait()

        return [first_part, second_part, third_part]

    rest = layer(1, [head_there, None, head_here] if inside else [])
    final = layer(0, rest)
    head_store = head_last()
    for step in final:
        step()
    head_store.wait()
    for copy in sends:
        copy.wait_send()


def backward_pass(devices, total_count, head, xf, xb, kept, weights, x, gtop, params, live, extra):
    shape = jax.ShapeDtypeStruct
    any_space = pl.BlockSpec(memory_space=pl.ANY)
    vmem = pl.BlockSpec(memory_space=pltpu.VMEM)
    dma = pltpu.SemaphoreType.DMA
    total = slots_total(devices)
    rows = live.shape[0]
    big = lambda s: pltpu.VMEM(s.shape, s.dtype)
    each = []
    for at in range(LAYERS):
        za, hp, zb, hb, zc = kept[at][:5]
        each.append([zc, hb, hp, zb, za] + list(weights[3 * at : 3 * at + 3]))
    inside = len(head) == 2
    head_shape = shape((devices, WIDE // 2 // HALF, HALF, LANES), BF16)
    if not inside:
        head_shape = shape(head[0].shape, BF16)
    ins = ([] if inside else list(head)) + [xf, xb] + each[0] + each[1]
    small_ins = [x, gtop]
    for at in range(LAYERS):
        small_ins += kept[at][5:]
    small_ins += list(params) + [live, extra] + (list(head) if inside else [])
    first, second, third = bit_split(devices)
    n_mid, n_last, n_far = 1 << first, 1 << second, 1 << third
    lands = [(n_last - 1) * n_mid * n_far, (n_mid - 1) * n_far, n_far - 1]
    side = N_IN * M // 32
    middle = N_MID * 9 * M // 32
    small_rows = 4 * N_MID + 2 * N_IN + extra.shape[0]
    stage_rows = [2 * N_MID, 2 * N_MID, 2 * N_IN + extra.shape[0]]
    grads = [shape((n, HALF, LANES), BF16) for n in (side, middle, side)]
    out = pl.pallas_call(
        functools.partial(backward_kernel, devices, total_count, inside),
        out_shape=grads * LAYERS
        + [shape(head_shape.shape[1:], BF16)]
        + [shape((small_rows, LANES), F32)] * LAYERS,
        in_specs=[any_space] * len(ins) + [vmem] * len(small_ins),
        out_specs=[any_space] * (3 * LAYERS + 1) + [vmem] * LAYERS,
        scratch_shapes=[big(a) for a in [xf, xb] + each[0]]
        + [
            pltpu.VMEM((side, 2, HALF, LANES), BF16),
            pltpu.VMEM((middle, 2, HALF, LANES), BF16),
            pltpu.VMEM((side, HALF, LANES), BF16),
            pltpu.VMEM((middle, HALF, LANES), BF16),
            pltpu.VMEM((N_IN, rows, LANES), BF16),
            pltpu.VMEM(kept[0][1].shape, BF16),
            pltpu.VMEM((N_MID, rows, LANES), BF16),
            pltpu.VMEM((N_MID, rows, LANES), F32),
            big(head_shape),
        ]
        + [pltpu.VMEM((n,) + head_shape.shape[1:], BF16) for n in lands]
        + [
            pltpu.VMEM((2 * N_MID, LANES), F32),
            pltpu.VMEM((stage_rows[2], LANES), F32),
        ]
        + [pltpu.VMEM((total, n, LANES), F32) for n in stage_rows] * LAYERS
        + [
            dma((LAYERS, 10)),
            dma((3 * LAYERS + 1,)),
            dma((3 * LAYERS, total)),
            dma((3 * LAYERS, total)),
            dma((LAYERS, 2)),
            dma((LAYERS, 2, 3)),
            dma(()),
            dma((sum(lands),)),
            dma((lands[0],)),
            dma((lands[1],)),
            dma((lands[2],)),
            dma((2,)),
        ],
        compiler_params=pltpu.CompilerParams(
            collective_id=6, has_side_effects=True, vmem_limit_bytes=62 * 2**20
        ),
    )(*ins, *small_ins)
    return out[: 3 * LAYERS], out[3 * LAYERS], out[3 * LAYERS + 1 :]


def adamw(values_old, gradient, moment_one, moment_two, step_rate):
    one_new = BETA_FIRST * moment_one + (1.0 - BETA_FIRST) * gradient
    two_new = BETA_SECOND * moment_two + (1.0 - BETA_SECOND) * gradient * gradient
    fixed_one = 1.0 - BETA_FIRST**STEP
    fixed_two = 1.0 - BETA_SECOND**STEP
    update = one_new / fixed_one / (jnp.sqrt(two_new / fixed_two) + EPS_ADAM)
    return (one_new, two_new, values_old - step_rate * (update + DECAY_WEIGHT * values_old))


def body(
    images,
    row_split,
    labels,
    partners,
    image_weight,
    owner_slot,
    conv_master,
    conv_stats,
    conv_roots,
    head_master,
    head_moment_one,
    head_moment_two,
    small_params,
    small_moment_one,
    small_moment_two,
):
    devices = lax.axis_size("dp")
    core_index = lax.axis_index("rows")
    batch_size = images.shape[0]
    half_batch = batch_size // 2
    slot_count = images.shape[1]
    total_images = partners.shape[0]
    live_count = float(total_images * HEIGHT * WIDTH)
    owned = conv_master.shape[0]
    head_rows = head_master.shape[0]

    slot_index = (owner_slot // owned) * (2 * owned) + owner_slot % owned
    weights = list(bring_weights(conv_master, slot_index, devices))
    head_t = jnp.pad(head_master.T.astype(BF16), ((0, WIDE - CLASSES), (0, 0)))
    head_t, weights[0] = lax.optimization_barrier((head_t, weights[0]))
    head_all = lax.all_gather(head_t, "dp", axis=0)
    if head_rows != LANES:
        head_all = head_all.transpose(1, 0, 2).reshape(WIDE, N_IN, LANES).transpose(1, 0, 2)

    slot_ids = core_index * slot_count + jnp.arange(slot_count, dtype=jnp.int32)
    first_live = (ROW_SLOTS - row_split)[:, None]
    live = (slot_ids[None, :] >= first_live) & (slot_ids[None, :] < first_live + HEIGHT)
    rows = slot_count * WIDTH * batch_size
    live_rows = jnp.broadcast_to(
        live.T.astype(F32)[:, None, :, None], (slot_count, WIDTH, batch_size, LANES)
    ).reshape(rows, LANES)
    first = images.transpose(1, 2, 0, 3).reshape(rows, C)
    stride = 4 * M + 2 * C
    params = [
        small_params[at * stride : (at + 1) * stride].reshape(-1, LANES) for at in range(LAYERS)
    ]
    bias = jnp.pad(small_params[LAYERS * stride :], (0, WIDE - CLASSES))[None, :]

    kept, field, low, pooled = forward_pass(
        devices, live_count, first, weights, params, live_rows
    )

    def by_core(v):
        return v.reshape(devices, 2, half_batch).transpose(1, 0, 2).reshape(-1)

    weight_f = image_weight.astype(F32)
    weight_total = jnp.sum(weight_f)
    own_start = (lax.axis_index("dp") * 2 + core_index) * half_batch
    own_ids = own_start + jnp.arange(half_batch, dtype=jnp.int32)
    own_weight = lax.dynamic_slice_in_dim(weight_f, own_start, half_batch)
    own_partner = lax.dynamic_slice_in_dim(partners, own_start, half_batch)
    own_label = lax.dynamic_slice_in_dim(labels, core_index * half_batch, half_batch)
    ids = by_core(jnp.arange(total_images, dtype=jnp.int32))
    pick = (own_partner[:, None] == ids[None, :]).astype(BF16)
    point = (by_core(partners)[None, :] == own_ids[:, None]).astype(F32) * by_core(weight_f)[None, :]
    in_weight = jnp.sum(point, axis=1)
    hot = (own_label[:, None] == jnp.arange(WIDE, dtype=jnp.int32)[None, :]).astype(F32)
    lane = jnp.arange(LANES)[None, :]
    numbers = jnp.where(
        lane == 0, own_weight[:, None], jnp.where(lane == 1, in_weight[:, None], weight_total)
    )
    emit = head_rows != LANES
    extra, g_top, *grad_head = head_step(
        devices,
        emit,
        pooled,
        head_all,
        bias,
        pick,
        point.astype(BF16),
        numbers,
        hot,
    )
    head_blocks = head_rows // 4
    if emit:
        grad_head[0] = (
            grad_head[0].reshape(N_IN, WIDE // 2, LANES)
            .transpose(1, 0, 2)
            .reshape(WIDE // 2, devices, head_rows)
            .transpose(1, 0, 2)
            .reshape(devices, head_blocks, HALF, LANES)
        )
    grads, head_mine, (small_bottom, small_top) = backward_pass(
        devices, live_count, grad_head, field, low, kept, weights, first, g_top, params, live_rows, extra
    )
    head_sum, conv_grad, stats_new, step = deliver_blocks(
        grads,
        head_mine,
        block_places(owner_slot),
        conv_stats,
        conv_roots,
        devices,
    )
    master_new = conv_master - RATE_SHAMPOO * step
    head_grad = head_sum.reshape(WIDE, head_rows)[:CLASSES].T.astype(F32)
    head_one, head_two, head_new = adamw(
        head_master, head_grad, head_moment_one, head_moment_two, RATE_HEAD
    )
    layer_rows = stride // LANES
    grad_bias = small_top[layer_rows : layer_rows + WIDE // LANES].reshape(-1)[:CLASSES]
    loss_sum = small_top[layer_rows + WIDE // LANES, 0]
    grad_small = jnp.concatenate(
        [small_bottom[:layer_rows].reshape(-1), small_top[:layer_rows].reshape(-1), grad_bias]
    )
    small_one, small_two, small_new = adamw(
        small_params, grad_small, small_moment_one, small_moment_two, RATE_SMALL
    )
    return (
        loss_sum,
        weight_total,
        conv_grad,
        stats_new,
        master_new,
        master_new.astype(BF16),
        head_one,
        head_two,
        head_new,
        head_new.astype(BF16),
        small_one,
        small_two,
        small_new,
    )


def solution(mesh):
    in_specs = (
        P("dp", "rows", None, None),
        P("dp"),
        P("dp"),
        P(),
        P(),
        P(),
        P("dp", None),
        P("dp", None, None),
        P("dp", None, None),
        P("dp", None),
        P("dp", None),
        P("dp", None),
        P(),
        P(),
        P(),
    )
    out_specs = (
        P(),
        P(),
        P("dp", None),
        P("dp", None, None),
        P("dp", None),
        P("dp", None),
        P("dp", None),
        P("dp", None),
        P("dp", None),
        P("dp", None),
        P(),
        P(),
        P(),
    )
    return jax.shard_map(body, mesh=mesh, in_specs=in_specs, out_specs=out_specs, check_vma=False)
```
